32 devices in a mesh: section: 2 (over x), ctx: 8 (over z, core), tp: 2 (over y).
Axes of the slice: x: 2, y: 2, z: 4, core: 2. Of those that a mesh axis runs over, the one named last changes fastest.
Arguments:
- inputs: bfloat16 [2, 1024, 1024], P(None, 'ctx'), may hold values from -6 to 6
- cotangent: bfloat16 [2, 1024, 1024], P(None, 'ctx'), may hold values from -6 to 6
- ln1_gain: bfloat16 [2, 1024], P('section'), may hold values from 0.25 to 1.75
- ln1_bias: bfloat16 [2, 1024], P('section'), may hold values from -1.75 to 1.75
- ln2_gain: bfloat16 [2, 1024], P('section'), may hold values from 0.25 to 1.75
- ln2_bias: bfloat16 [2, 1024], P('section'), may hold values from -1.75 to 1.75
- qkv_weight: bfloat16 [2, 3, 1024, 1024], P('section', None, None, 'tp'), may hold values from -0.1875 to 0.1875
- qkv_bias: bfloat16 [2, 3, 1024], P('section', None, 'tp'), may hold values from -3 to 3
- out_weight: bfloat16 [2, 1024, 1024], P('section', 'tp'), may hold values from -0.75 to 0.75
- up_weight: bfloat16 [2, 1024, 4096], P('section', None, 'tp'), may hold values from -0.1875 to 0.1875
- up_bias: bfloat16 [2, 4096], P('section', 'tp'), may hold values from -3 to 3
- down_weight: bfloat16 [2, 4096, 1024], P('section', 'tp'), may hold values from -0.09375 to 0.09375
- branch_bias: bfloat16 [2, 1024], P('section'), may hold values from -3 to 3
Outputs:
- acts: bfloat16 [2, 2, 1024, 1024], P('section', None, 'ctx')
- in_grads: bfloat16 [2, 2, 1024, 1024], P('section', None, 'ctx')
- ln1_gain_grad: float32 [2, 1024], P('section')
- ln1_bias_grad: float32 [2, 1024], P('section')
- ln2_gain_grad: float32 [2, 1024], P('section')
- ln2_bias_grad: float32 [2, 1024], P('section')
- qkv_weight_grad: float32 [2, 3, 1024, 1024], P('section', None, 'ctx', 'tp')
- qkv_bias_grad: float32 [2, 3, 1024], P('section', None, 'tp')
- out_weight_grad: float32 [2, 1024, 1024], P('section', 'tp', 'ctx')
- up_weight_grad: float32 [2, 1024, 4096], P('section', 'ctx', 'tp')
- up_bias_grad: float32 [2, 4096], P('section', 'tp')
- down_weight_grad: float32 [2, 4096, 1024], P('section', 'tp', 'ctx')
- branch_bias_grad: float32 [2, 1024], P('section')
The draws below stay inside these ranges and needn't reach their ends.
All inputs are finite; a program needn't handle non-finite values.
Results may differ from the reference program's by a relative error of at most 0.015.
Values may be sent and summed in bfloat16 or wider, within the bound.
No kernel may reach another device: no remote copies, remote signals or barrier semaphores. Data moves between devices by JAX's collectives and lax.ppermute only.
A program may use at most 320 MiB of HBM per device.

```python
import math
import jax
import jax.numpy as jnp
from jax import lax

D = 1024
HEADS = 16
HD = 64
ROT = 16
FF = 4096
MICRO = 2
SEQ = 1024


def shard_levels(key, dims, split, least, largest):
    level, own = 1.0, jax.random.fold_in(key, 6)
    for axis_at, parts in split:
        steps = jnp.exp(jax.random.uniform(jax.random.fold_in(own, axis_at), (parts,), jnp.float32, least / len(split), largest / len(split)))
        level = level * jnp.repeat(steps, dims[axis_at] // parts).reshape([-1 if axis == axis_at else 1 for axis in range(len(dims))])
    return level


def bell_draw(own_key, dims, scale, most, pieces=(), held_as=jnp.bfloat16):
    values = scale * jax.random.normal(own_key, dims, jnp.float32)
    if pieces:
        values = values * shard_levels(own_key, dims, pieces, -0.22, 0.18)
    return jnp.clip(values, -most, most).astype(held_as)


def setup_inputs(seed: int = 0) -> dict:
    key_list = jax.random.split(jax.random.key(seed), 14)
    return {
        "inputs": bell_draw(key_list[0], (MICRO, SEQ, D), 1.0, 6.0, ((1, 8),)),
        "cotangent": bell_draw(key_list[1], (MICRO, SEQ, D), 1.0, 6.0, ((1, 8),)),
        "ln1_gain": jnp.clip(1.0 + 0.15 * jax.random.normal(key_list[2], (2, D), jnp.float32), 0.25, 1.75).astype(jnp.bfloat16),
        "ln1_bias": bell_draw(key_list[3], (2, D), 0.3, 1.75, ((0, 2),)),
        "ln2_gain": jnp.clip(1.0 + 0.15 * jax.random.normal(key_list[4], (2, D), jnp.float32), 0.25, 1.75).astype(jnp.bfloat16),
        "ln2_bias": bell_draw(key_list[5], (2, D), 0.3, 1.75, ((0, 2),)),
        "qkv_weight": bell_draw(key_list[6], (2, 3, D, D), D ** -0.5, 0.1875, ((0, 2), (3, 2))),
        "qkv_bias": bell_draw(key_list[7], (2, 3, D), 0.5, 3.0, ((0, 2), (2, 2))),
        "out_weight": bell_draw(key_list[8], (2, D, D), (D * 64 // SEQ) ** -0.5, 0.75, ((0, 2), (1, 2))),
        "up_weight": bell_draw(key_list[9], (2, D, FF), D ** -0.5, 0.1875, ((0, 2), (2, 2))),
        "up_bias": bell_draw(key_list[10], (2, FF), 0.5, 3.0, ((0, 2), (1, 2))),
        "down_weight": bell_draw(key_list[11], (2, FF, D), FF ** -0.5, 0.09375, ((0, 2), (1, 2))),
        "branch_bias": bell_draw(key_list[12], (2, D), 0.5, 3.0, ((0, 2),)),
    }


@jax.custom_vjp
def low(v):
    return lax.optimization_barrier(v.astype(jnp.bfloat16)).astype(jnp.float32)

@jax.custom_vjp
def low_back(v):
    return v

def low_keep(v):
    return (low(v), None)

def low_pass(kept, grad):
    return (grad,)

def back_keep(v):
    return (v, None)

def back_low(kept, grad):
    return (low(grad),)
low.defvjp(low_keep, low_pass)
low_back.defvjp(back_keep, back_low)
highest = lax.Precision.HIGHEST

def tables(positions):
    freqs = 1.0 / 10000.0 ** (jnp.arange(0, ROT, 2).astype(jnp.float32) / ROT)
    angles = positions.astype(jnp.float32)[:, None] * freqs[None, :]
    return (jnp.cos(angles)[:, None, :], jnp.sin(angles)[:, None, :])

def rotate(field, cosine, sine):
    half_rot = ROT // 2
    front = field[..., :half_rot]
    second = field[..., half_rot:ROT]
    return jnp.concatenate([front * cosine - second * sine, second * cosine + front * sine, field[..., ROT:]], axis=-1)

def layer(hidden_in, params):
    gain_one, shift_one, gain_two, shift_two, w_qkv, b_qkv, w_out, w_up, b_up, w_down, b_branch = params
    hidden_in = low_back(hidden_in)
    centre = hidden_in - lax.optimization_barrier(jnp.mean(hidden_in, axis=-1, keepdims=True))
    normed = centre * lax.rsqrt(lax.optimization_barrier(jnp.mean(centre * centre, axis=-1, keepdims=True)) + 1e-05)
    attn_in = low(normed * gain_one + shift_one)
    mlp_in = low(normed * gain_two + shift_two)
    projected = jnp.einsum('td,cdf->tcf', attn_in, w_qkv, precision=highest) + b_qkv
    positions = jnp.arange(SEQ, dtype=jnp.int32)
    cosine, sine = tables(positions)
    head_shape = (SEQ, HEADS, HD)
    queries = low(rotate(low_back(projected[:, 0]).reshape(head_shape), cosine, sine))
    keys = low(rotate(low_back(projected[:, 1]).reshape(head_shape), cosine, sine))
    values = low(low_back(projected[:, 2])).reshape(head_shape)
    block_rows = 512 if SEQ % 512 == 0 else SEQ
    score_scale = 1.0 / math.sqrt(HD)

    def attend(start):
        query_rows = lax.dynamic_slice_in_dim(queries, start, block_rows, 0)
        raw = low_back(jnp.einsum('qhd,khd->hqk', query_rows, keys, precision=highest))
        query_pos = start + jnp.arange(block_rows, dtype=jnp.int32)
        scores = jnp.where(positions[None, None, :] <= query_pos[None, :, None], raw * score_scale, -1000000000.0)
        probability = jax.nn.softmax(scores, axis=-1)
        return jnp.einsum('hqk,khd->qhd', low(probability), values, precision=highest)
    starts = (jnp.arange(SEQ // block_rows) * block_rows).astype(jnp.int32)
    mixed = lax.map(jax.checkpoint(attend), starts).reshape(SEQ, HEADS * HD)
    mixed = low_back(low(mixed))
    attn_out = jnp.dot(mixed, w_out, precision=highest)
    up_value = low_back(jnp.dot(mlp_in, w_up, precision=highest) + b_up)
    active = low(jax.nn.gelu(up_value, approximate=False))
    mlp_out = jnp.dot(active, w_down, precision=highest)
    return low(hidden_in + attn_out + mlp_out + b_branch)

def reference(inputs, cotangent, ln1_gain, ln1_bias, ln2_gain, ln2_bias, qkv_weight, qkv_bias, out_weight, up_weight, up_bias, down_weight, branch_bias):
    weight_list = [w.astype(jnp.float32) for w in (ln1_gain, ln1_bias, ln2_gain, ln2_bias, qkv_weight, qkv_bias, out_weight, up_weight, up_bias, down_weight, branch_bias)]
    section_params = [tuple((w[section_index] for w in weight_list)) for section_index in range(2)]
    totals = [tuple((jnp.zeros_like(w) for w in params)) for params in section_params]
    first_acts, second_acts, first_grads, second_grads = ([], [], [], [])
    for batch_index in range(MICRO):
        first_out, first_back = jax.vjp(layer, inputs[batch_index].astype(jnp.float32), section_params[0])
        second_out, second_back = jax.vjp(layer, first_out, section_params[1])
        middle_grad, grads_two = second_back(cotangent[batch_index].astype(jnp.float32))
        input_grad, grads_one = first_back(middle_grad)
        totals[0] = tuple((a + b for a, b in zip(totals[0], grads_one)))
        totals[1] = tuple((a + b for a, b in zip(totals[1], grads_two)))
        first_acts.append(first_out)
        second_acts.append(second_out)
        first_grads.append(input_grad)
        second_grads.append(middle_grad)
    acts = jnp.stack([jnp.stack(first_acts), jnp.stack(second_acts)]).astype(jnp.bfloat16)
    in_grads = jnp.stack([jnp.stack(first_grads), jnp.stack(second_grads)]).astype(jnp.bfloat16)
    stacked = [jnp.stack([totals[0][i], totals[1][i]]).astype(jnp.float32) for i in range(11)]
    return (acts, in_grads, stacked[0], stacked[1], stacked[2], stacked[3], stacked[4], stacked[5], stacked[6], stacked[7], stacked[8], stacked[9], stacked[10])
```

```python
import math

import jax
import jax.numpy as jnp
from jax import lax
from jax.sharding import PartitionSpec as P

HD = 64
ROT = 16


def shifted(shard, axis, by):
    peers = lax.axis_size(axis)
    pairs = [(i, i + by) for i in range(peers) if 0 <= i + by < peers]
    return lax.ppermute(shard, axis, pairs)


def tables(positions):
    freqs = 1.0 / 10000.0 ** (jnp.arange(0, ROT, 2).astype(jnp.float32) / ROT)
    angles = positions.astype(jnp.float32)[:, None] * freqs[None, :]
    return (jnp.cos(angles)[:, None, :], jnp.sin(angles)[:, None, :])


def rotate(field, cosine, sine):
    half_rot = ROT // 2
    front = field[..., :half_rot]
    second = field[..., half_rot:ROT]
    return jnp.concatenate(
        [front * cosine - second * sine, second * cosine + front * sine, field[..., ROT:]], axis=-1
    )


def norms(hidden, gain_one, shift_one, gain_two, shift_two):
    centre = hidden - jnp.mean(hidden, axis=-1, keepdims=True)
    normed = centre * lax.rsqrt(jnp.mean(centre * centre, axis=-1, keepdims=True) + 1e-05)
    return (normed * gain_one + shift_one, normed * gain_two + shift_two)


def gelu_exact(value):
    return jax.nn.gelu(value, approximate=False)


def scores_of(queries, keys, query_pos, score_scale):
    raw = jnp.einsum("qhd,khd->hqk", queries, keys, preferred_element_type=jnp.float32)
    key_pos = jnp.arange(keys.shape[0], dtype=jnp.int32)
    return jnp.where(
        key_pos[None, None, :] <= query_pos[None, :, None], raw * score_scale, -1000000000.0
    )


def forward_layer(layer_in, weights, query_pos, cosine, sine):
    gains, w_qkv, b_qkv, w_out, w_up, b_up, w_down, b_branch = weights
    hidden = layer_in.astype(jnp.float32)
    attn_norm, mlp_norm = norms(hidden, gains[0], gains[1], gains[2], gains[3])
    attn_in = attn_norm.astype(jnp.bfloat16)
    mlp_in = mlp_norm.astype(jnp.bfloat16)
    projected = (
        jnp.einsum("td,cdf->tcf", attn_in, w_qkv, preferred_element_type=jnp.float32) + b_qkv
    )
    row_count = hidden.shape[0]
    feat_width = projected.shape[2]
    head_count = feat_width // HD
    queries = rotate(projected[:, 0].reshape(row_count, head_count, HD), cosine, sine).astype(
        jnp.bfloat16
    )
    key_flat = (
        rotate(projected[:, 1].reshape(row_count, head_count, HD), cosine, sine)
        .astype(jnp.bfloat16)
        .reshape(row_count, feat_width)
    )
    value_flat = projected[:, 2].astype(jnp.bfloat16)
    all_keys, all_values = (
        lax.all_gather(key_flat, "ctx", axis=0, tiled=True),
        lax.all_gather(value_flat, "ctx", axis=0, tiled=True),
    )
    key_count = all_keys.shape[0]
    score_scale = 1.0 / math.sqrt(HD)
    scores = scores_of(queries, all_keys.reshape(key_count, head_count, HD), query_pos, score_scale)
    row_max = jnp.max(scores, axis=-1, keepdims=True)
    exponent = jnp.exp(scores - row_max)
    summed = jnp.sum(exponent, axis=-1, keepdims=True)
    probability = (exponent / summed).astype(jnp.bfloat16)
    log_total = row_max + jnp.log(summed)
    mixed = jnp.einsum(
        "hqk,khd->qhd",
        probability,
        all_values.reshape(key_count, head_count, HD),
        preferred_element_type=jnp.float32,
    )
    mixed = mixed.reshape(row_count, feat_width).astype(jnp.bfloat16)
    partial_out = jnp.dot(mixed, w_out, preferred_element_type=jnp.float32)
    up_value = jnp.dot(mlp_in, w_up, preferred_element_type=jnp.float32) + b_up
    active = gelu_exact(up_value).astype(jnp.bfloat16)
    partial_out = partial_out + jnp.dot(active, w_down, preferred_element_type=jnp.float32)
    branches = lax.psum(partial_out, "tp")
    layer_out = (hidden + branches + b_branch).astype(jnp.bfloat16)
    stored = (key_flat, value_flat)
    saved = (layer_in, queries, stored, log_total, mixed, up_value, active)
    return (layer_out, saved)


def backward_layer(grad_out, saved, weights, query_pos, cosine, sine):
    gains, w_qkv, b_qkv, w_out, w_up, b_up, w_down, b_branch = weights
    layer_in, queries, stored, log_total, mixed, up_value, active = saved
    grad_full = grad_out.astype(jnp.float32)
    row_count, feat_width = mixed.shape
    head_count = feat_width // HD
    hidden = layer_in.astype(jnp.float32)
    norm_pair, norm_back = jax.vjp(norms, hidden, gains[0], gains[1], gains[2], gains[3])
    attn_in = norm_pair[0].astype(jnp.bfloat16)
    mlp_in = norm_pair[1].astype(jnp.bfloat16)
    active_grad = jnp.einsum("td,fd->tf", grad_out, w_down, preferred_element_type=jnp.float32)
    grad_down = jnp.einsum("tf,td->fd", active, grad_out, preferred_element_type=jnp.float32)
    gelu_back = jax.vjp(gelu_exact, up_value)[1]
    up_grad = gelu_back(active_grad)[0].astype(jnp.bfloat16)
    grad_up_bias = jnp.sum(up_grad.astype(jnp.float32), axis=0)
    grad_up = jnp.einsum("td,tf->df", mlp_in, up_grad, preferred_element_type=jnp.float32)
    mlp_in_grad = jnp.einsum("tf,df->td", up_grad, w_up, preferred_element_type=jnp.float32)
    mixed_grad = jnp.einsum(
        "td,fd->tf", grad_out, w_out, preferred_element_type=jnp.float32
    ).astype(jnp.bfloat16)
    grad_out_weight = jnp.einsum("tf,td->fd", mixed, grad_out, preferred_element_type=jnp.float32)
    all_keys, all_values = (
        lax.all_gather(stored[0], "ctx", axis=0, tiled=True),
        lax.all_gather(stored[1], "ctx", axis=0, tiled=True),
    )
    key_count = all_keys.shape[0]
    keys_heads = all_keys.reshape(key_count, head_count, HD)
    values_heads = all_values.reshape(key_count, head_count, HD)
    score_scale = 1.0 / math.sqrt(HD)
    scores = scores_of(queries, keys_heads, query_pos, score_scale)
    probability = jnp.exp(scores - log_total)
    heads_grad = mixed_grad.reshape(row_count, head_count, HD)
    prob_grad = jnp.einsum(
        "qhd,khd->hqk", heads_grad, values_heads, preferred_element_type=jnp.float32
    )
    centre = jnp.sum(probability * prob_grad, axis=-1, keepdims=True)
    score_grad = (score_scale * probability * (prob_grad - centre)).astype(jnp.bfloat16)
    query_grad = jnp.einsum(
        "hqk,khd->qhd", score_grad, keys_heads, preferred_element_type=jnp.float32
    )
    value_terms = jnp.einsum(
        "hqk,qhd->khd",
        probability.astype(jnp.bfloat16),
        heads_grad,
        preferred_element_type=jnp.float32,
    )
    key_terms = jnp.einsum("hqk,qhd->khd", score_grad, queries, preferred_element_type=jnp.float32)
    key_grad, value_grad = (
        lax.psum_scatter(
            key_terms.reshape(key_count, feat_width), "ctx", scatter_dimension=0, tiled=True
        ),
        lax.psum_scatter(
            value_terms.reshape(key_count, feat_width), "ctx", scatter_dimension=0, tiled=True
        ),
    )
    query_grad = rotate(query_grad, cosine, -sine).reshape(row_count, feat_width)
    key_grad = rotate(key_grad.reshape(row_count, head_count, HD), cosine, -sine).reshape(
        row_count, feat_width
    )
    qkv_grad = jnp.stack([query_grad, key_grad, value_grad], axis=1).astype(jnp.bfloat16)
    grad_qkv_bias = jnp.sum(qkv_grad.astype(jnp.float32), axis=0)
    grad_qkv = jnp.einsum("td,tcf->cdf", attn_in, qkv_grad, preferred_element_type=jnp.float32)
    attn_in_grad = jnp.einsum("tcf,cdf->td", qkv_grad, w_qkv, preferred_element_type=jnp.float32)
    attn_in_grad, mlp_in_grad = lax.psum((attn_in_grad, mlp_in_grad), "tp")
    hidden_grad, gain_one_grad, shift_one_grad, gain_two_grad, shift_two_grad = norm_back(
        (attn_in_grad, mlp_in_grad)
    )
    input_grad = (grad_full + hidden_grad).astype(jnp.bfloat16)
    grad_branch = jnp.sum(grad_full, axis=0)
    grads = (
        gain_one_grad,
        shift_one_grad,
        gain_two_grad,
        shift_two_grad,
        grad_qkv,
        grad_qkv_bias,
        grad_out_weight,
        grad_up,
        grad_up_bias,
        grad_down,
        grad_branch,
    )
    return (input_grad, grads)


def per_device(
    inputs,
    cotangent,
    ln1_gain,
    ln1_bias,
    ln2_gain,
    ln2_bias,
    qkv_weight,
    qkv_bias,
    out_weight,
    up_weight,
    up_bias,
    down_weight,
    branch_bias,
):
    gains = (
        ln1_gain[0].astype(jnp.float32),
        ln1_bias[0].astype(jnp.float32),
        ln2_gain[0].astype(jnp.float32),
        ln2_bias[0].astype(jnp.float32),
    )
    weights = (
        gains,
        qkv_weight[0],
        qkv_bias[0].astype(jnp.float32),
        out_weight[0],
        up_weight[0],
        up_bias[0].astype(jnp.float32),
        down_weight[0],
        branch_bias[0].astype(jnp.float32),
    )
    micro_count = inputs.shape[0]
    row_count = inputs.shape[1]
    query_pos = lax.axis_index("ctx") * row_count + jnp.arange(row_count, dtype=jnp.int32)
    cosine, sine = tables(query_pos)
    at_first = lax.axis_index("section") == 0
    blank = jnp.zeros_like(inputs[0])
    received = blank
    outputs_list = []
    saved_list = []
    for step_index in range(micro_count + 1):
        fresh = inputs[step_index] if step_index < micro_count else blank
        layer_in = jnp.where(at_first, fresh, received)
        layer_out, saved = forward_layer(layer_in, weights, query_pos, cosine, sine)
        outputs_list.append(layer_out)
        saved_list.append(saved)
        if step_index < micro_count:
            received = shifted(layer_out, "section", 1)
    returned = blank
    grad_list = []
    sums = None
    for back_index in range(micro_count + 1):
        batch_index = micro_count - 1 - back_index
        given = cotangent[batch_index] if batch_index >= 0 else blank
        grad_in = jnp.where(at_first, returned, given)
        input_grad, grads = backward_layer(
            grad_in, saved_list[micro_count - back_index], weights, query_pos, cosine, sine
        )
        sums = grads if sums is None else jax.tree.map(jnp.add, sums, grads)
        grad_list.append(input_grad)
        if back_index < micro_count:
            returned = shifted(input_grad, "section", -1)
    acts = jnp.stack(
        [jnp.where(at_first, outputs_list[j], outputs_list[j + 1]) for j in range(micro_count)]
    )[None]
    in_grads = jnp.stack(
        [
            jnp.where(at_first, grad_list[micro_count - j], grad_list[micro_count - 1 - j])
            for j in range(micro_count)
        ]
    )[None]
    (
        gain_one_grad,
        shift_one_grad,
        gain_two_grad,
        shift_two_grad,
        grad_qkv,
        grad_qkv_bias,
        grad_out_weight,
        grad_up,
        grad_up_bias,
        grad_down,
        grad_branch,
    ) = sums
    qkv_part, out_part, up_part, down_part = (
        lax.psum_scatter(
            grad_qkv[None].astype(jnp.bfloat16), "ctx", scatter_dimension=2, tiled=True
        ).astype(jnp.float32),
        lax.psum_scatter(
            grad_out_weight[None].astype(jnp.bfloat16), "ctx", scatter_dimension=2, tiled=True
        ).astype(jnp.float32),
        lax.psum_scatter(
            grad_up[None].astype(jnp.bfloat16), "ctx", scatter_dimension=1, tiled=True
        ).astype(jnp.float32),
        lax.psum_scatter(
            grad_down[None].astype(jnp.bfloat16), "ctx", scatter_dimension=2, tiled=True
        ).astype(jnp.float32),
    )
    small_sums = (
        lax.psum(gain_one_grad[None].astype(jnp.bfloat16), "ctx").astype(jnp.float32),
        lax.psum(shift_one_grad[None].astype(jnp.bfloat16), "ctx").astype(jnp.float32),
        lax.psum(gain_two_grad[None].astype(jnp.bfloat16), "ctx").astype(jnp.float32),
        lax.psum(shift_two_grad[None].astype(jnp.bfloat16), "ctx").astype(jnp.float32),
        lax.psum(grad_qkv_bias[None].astype(jnp.bfloat16), "ctx").astype(jnp.float32),
        lax.psum(grad_up_bias[None].astype(jnp.bfloat16), "ctx").astype(jnp.float32),
        lax.psum(grad_branch[None].astype(jnp.bfloat16), "ctx").astype(jnp.float32),
    )
    return (
        acts,
        in_grads,
        small_sums[0],
        small_sums[1],
        small_sums[2],
        small_sums[3],
        qkv_part,
        small_sums[4],
        out_part,
        up_part,
        small_sums[5],
        down_part,
        small_sums[6],
    )


ALL = ("section", "ctx", "tp")
SECTION, HALF, NEAR, CORE, SIDE = 16, 8, 4, 2, 1
CHIPS = (0, SIDE, NEAR, NEAR | SIDE, SECTION, SECTION | SIDE, SECTION | NEAR, SECTION | NEAR | SIDE)


def swapped(array, mask, only=None):
    pairs = [(i, i ^ mask) for i in range(32) if only is None or only(i)]
    return lax.ppermute(array, ALL, pairs)


def pick(array, index, axis=0):
    return lax.dynamic_index_in_dim(array, index, axis, keepdims=False)


def part(array, index, size, axis):
    return lax.dynamic_slice_in_dim(array, index * size, size, axis)


def in_order(relative, index):
    pieces = list(relative)
    bit = 1
    while bit < len(pieces):
        flip = (index & bit) != 0
        pieces = [jnp.where(flip, pieces[j ^ bit], pieces[j]) for j in range(len(pieces))]
        bit *= 2
    return jnp.stack(pieces)


class Place:
    def __init__(self):
        self.section = lax.axis_index("section")
        self.ctx = lax.axis_index("ctx")
        self.side = lax.axis_index("tp")
        self.half = self.ctx // 4
        self.near = (self.ctx // 2) % 2
        self.core = self.ctx % 2
        self.chip = 4 * self.section + 2 * self.near + self.side


def gather_start(array, at):
    mine = pick(array, at.half)
    other = pick(array, 1 - at.half)
    width = other.shape[-1] // 2
    strip = part(other, at.side, width, 1)
    near = swapped(mine, NEAR)
    far = jnp.stack([swapped(strip, HALF), swapped(strip, HALF | NEAR)])
    rest = swapped(far, SIDE)
    first = jnp.where(at.side == 0, far, rest)
    second = jnp.where(at.side == 0, rest, far)
    far = jnp.concatenate([first, second], axis=-1)
    return in_order([mine, near, far[0], far[1]], 2 * at.half + at.near)


def shard_weights(section_weights, at):
    gains, w_qkv, b_qkv, w_out, w_up, b_up, w_down, b_branch = section_weights

    def cut(index):
        return (
            part(w_qkv, index, w_qkv.shape[2] // 4, 2),
            part(w_up, index, w_up.shape[1] // 4, 1),
            part(w_out, index, w_out.shape[0] // 4, 0),
            part(w_down, index, w_down.shape[0] // 4, 0),
            jnp.concatenate(
                list(gains)
                + [b_branch]
                + [part(b_qkv, index, b_qkv.shape[1] // 4, 1).reshape(-1)]
                + [part(b_up, index, b_up.shape[0] // 4, 0)]
            )[None],
        )

    own = cut(2 * at.section + at.near)
    give = cut(2 * (1 - at.section) + at.near)

    def exchange(array, axis):
        size = array.shape[axis] // 2
        got = swapped(part(array, at.core, size, axis), SECTION)
        rest = swapped(got, CORE)
        low = jnp.where(at.core == 0, got, rest)
        high = jnp.where(at.core == 0, rest, got)
        return jnp.concatenate([low, high], axis=axis)

    taken = (
        exchange(give[0], 1),
        exchange(give[1], 0),
        exchange(give[2], 0),
        exchange(give[3], 0),
        swapped(give[4], SECTION),
    )
    layers = []
    for layer in range(2):
        qkv, up, out, down, small = [
            jnp.where(at.section == layer, a, b) for a, b in zip(own, taken)
        ]
        small = small[0].astype(jnp.float32)
        dim = w_up.shape[0]
        heads = qkv.shape[2]
        layers.append(
            dict(
                gains=[small[i * dim : (i + 1) * dim] for i in range(4)],
                branch=small[4 * dim : 5 * dim],
                b_qkv=small[5 * dim : 5 * dim + 3 * heads].reshape(3, heads),
                b_up=small[5 * dim + 3 * heads :],
                qkv=qkv,
                up=up,
                out=out,
                down=down,
            )
        )
    return layers


def turn(flat, cosine, sine):
    rows, width = flat.shape
    return rotate(flat.reshape(rows, width // HD, HD), cosine, sine).reshape(rows, width)


def normal(x):
    hidden = x.astype(jnp.float32)
    centre = hidden - jnp.mean(hidden, axis=-1, keepdims=True)
    scale = lax.rsqrt(jnp.mean(centre * centre, axis=-1, keepdims=True) + 1e-05)
    return centre * scale, scale


def forward_part(x, w, own_pos, other_pos, cosine, sine):
    normed, _ = normal(x)
    g = w["gains"]
    attn_in = (normed * g[0] + g[1]).astype(jnp.bfloat16)
    mlp_in = (normed * g[2] + g[3]).astype(jnp.bfloat16)
    projected = (
        jnp.einsum("td,cdf->ctf", attn_in, w["qkv"], preferred_element_type=jnp.float32)
        + w["b_qkv"][:, None]
    )
    q = turn(projected[0], cosine, sine).astype(jnp.bfloat16)
    k = turn(projected[1], cosine, sine).astype(jnp.bfloat16)
    v = projected[2].astype(jnp.bfloat16)
    kv = jnp.stack([k, v])
    kv = jnp.concatenate([kv, swapped(kv, CORE)], axis=1)
    rows, width = q.shape
    heads = width // HD
    keys = kv[0].reshape(-1, heads, HD)
    values = kv[1].reshape(-1, heads, HD)
    raw = jnp.einsum(
        "qhd,khd->hqk", q.reshape(rows, heads, HD), keys, preferred_element_type=jnp.float32
    )
    key_pos = jnp.concatenate([own_pos, other_pos])
    allowed = key_pos[None, None, :] <= own_pos[None, :, None]
    scores = jnp.where(allowed, raw * (1.0 / math.sqrt(HD)), -1e9)
    row_max = jnp.max(scores, axis=-1, keepdims=True)
    exponent = jnp.exp(scores - row_max)
    prob = exponent / jnp.sum(exponent, axis=-1, keepdims=True)
    mixed = jnp.einsum(
        "hqk,khd->qhd", prob.astype(jnp.bfloat16), values, preferred_element_type=jnp.float32
    )
    mixed = mixed.reshape(rows, width).astype(jnp.bfloat16)
    up = jnp.dot(mlp_in, w["up"], preferred_element_type=jnp.float32) + w["b_up"]
    active = gelu_exact(up).astype(jnp.bfloat16)
    partial = jnp.dot(mixed, w["out"], preferred_element_type=jnp.float32) + jnp.dot(
        active, w["down"], preferred_element_type=jnp.float32
    )
    saved = dict(
        x=x, normed=normed, attn_in=attn_in, mlp_in=mlp_in, q=q, keys=keys, values=values,
        prob=prob, mixed=mixed, up=up, active=active,
    )
    return partial, saved


def backward_part(g, saved, w, cosine, sine):
    f32 = jnp.float32
    active_grad = jnp.einsum("td,fd->tf", g, w["down"], preferred_element_type=f32)
    up_grad = jax.vjp(gelu_exact, saved["up"])[1](active_grad)[0].astype(jnp.bfloat16)
    d_down = jnp.einsum("tf,td->fd", saved["active"], g, preferred_element_type=f32)
    d_up = jnp.einsum("td,tf->df", saved["mlp_in"], up_grad, preferred_element_type=f32)
    mlp_in_grad = jnp.einsum("tf,df->td", up_grad, w["up"], preferred_element_type=f32)
    mixed_grad = jnp.einsum("td,fd->tf", g, w["out"], preferred_element_type=f32)
    mixed_grad = mixed_grad.astype(jnp.bfloat16)
    d_out = jnp.einsum("tf,td->fd", saved["mixed"], g, preferred_element_type=f32)
    rows, width = mixed_grad.shape
    heads = width // HD
    q = saved["q"].reshape(rows, heads, HD)
    mg = mixed_grad.reshape(rows, heads, HD)
    prob = saved["prob"]
    prob_grad = jnp.einsum("qhd,khd->hqk", mg, saved["values"], preferred_element_type=f32)
    delta = jnp.sum(prob * prob_grad, axis=-1, keepdims=True)
    score_grad = (prob * (prob_grad - delta) * (1.0 / math.sqrt(HD))).astype(jnp.bfloat16)
    dq = jnp.einsum("hqk,khd->qhd", score_grad, saved["keys"], preferred_element_type=f32)
    dk = jnp.einsum("hqk,qhd->khd", score_grad, q, preferred_element_type=f32)
    dv = jnp.einsum("hqk,qhd->khd", prob.astype(jnp.bfloat16), mg, preferred_element_type=f32)
    dkv = jnp.stack([dk.reshape(-1, width), dv.reshape(-1, width)])
    dkv = dkv[:, :rows] + swapped(dkv[:, rows:], CORE)
    dq = turn(dq.reshape(rows, width), cosine, -sine)
    dk = turn(dkv[0], cosine, -sine)
    qkv_grad = jnp.stack([dq, dk, dkv[1]]).astype(jnp.bfloat16)
    attn_in_grad = jnp.einsum("ctf,cdf->td", qkv_grad, w["qkv"], preferred_element_type=f32)
    d_qkv = jnp.einsum("td,ctf->cdf", saved["attn_in"], qkv_grad, preferred_element_type=f32)
    normed = saved["normed"]
    small = dict(
        lines=[
            jnp.sum(attn_in_grad * normed, axis=0),
            jnp.sum(attn_in_grad, axis=0),
            jnp.sum(mlp_in_grad * normed, axis=0),
            jnp.sum(mlp_in_grad, axis=0),
        ],
        qkv=jnp.sum(qkv_grad.astype(f32), axis=1),
        up=jnp.sum(up_grad.astype(f32), axis=0),
        branch=jnp.sum(g.astype(f32), axis=0),
    )
    dn = attn_in_grad * w["gains"][0] + mlp_in_grad * w["gains"][2]
    return dn, dict(qkv=d_qkv, up=d_up, out=d_out, down=d_down), small


def scatter_sum(partial, at):
    rows = partial.shape[0] // 8
    pieces = partial.astype(jnp.bfloat16).reshape(8, rows, partial.shape[1])
    total = part(partial, at.chip, rows, 0)
    got = [swapped(pick(pieces, at.chip ^ j), CHIPS[j]) for j in range(1, 8)]
    for piece in got:
        total = total + piece.astype(jnp.float32)
    return total


def gather_rows(piece, at):
    got = [piece] + [swapped(piece, CHIPS[j]) for j in range(1, 8)]
    return in_order(got, at.chip).reshape(-1, piece.shape[1])


def spread_rows(full, at):
    blocks = full.reshape(4, -1, full.shape[1])
    mine = pick(blocks, 2 * at.half + at.near)
    got = swapped(pick(blocks, 2 * (1 - at.half) + at.near), HALF)
    return jnp.where(at.half == 0, jnp.stack([mine, got]), jnp.stack([got, mine]))


def deliver_rows(piece, layer, at):
    got = swapped(piece, SECTION)
    both = jnp.where(at.section == 0, jnp.stack([piece, got]), jnp.stack([got, piece]))
    rest = swapped(both, SIDE)
    low = jnp.where(at.side == 0, both, rest)
    high = jnp.where(at.side == 0, rest, both)
    blocks = jnp.concatenate([low, high], axis=1)
    mine = pick(blocks, at.half)
    got = swapped(pick(blocks, 1 - at.half), HALF)
    return jnp.where(at.half == 0, jnp.stack([mine, got]), jnp.stack([got, mine]))


def matrix_grads(grads, layer, at):
    f32, b16 = jnp.float32, jnp.bfloat16

    def reduce(array, axis, join):
        shape = array.shape
        cut = shape[:axis] + (2, 2, 2, shape[axis] // 8) + shape[axis + 1 :]
        array = array.reshape(cut)
        give = pick(array, 1 - at.core, axis + 2).astype(b16)
        array = pick(array, at.core, axis + 2) + swapped(give, CORE).astype(f32)
        give = pick(array, 1 - at.half, axis).astype(b16)
        array = pick(array, at.half, axis) + swapped(give, HALF).astype(f32)
        array = array.astype(b16)
        mine = pick(array, at.near, axis)
        give = pick(array, 1 - at.near, axis)
        near = swapped(give, NEAR, lambda i: i // 16 == layer)
        far = swapped(mine, SECTION, lambda i: i // 16 != layer)
        cross = swapped(give, SECTION | NEAR, lambda i: i // 16 != layer)
        first = [jnp.where(at.near == 0, mine, near), jnp.where(at.near == 0, near, mine)]
        second = [jnp.where(at.near == 0, far, cross), jnp.where(at.near == 0, cross, far)]
        order = first + second if layer == 0 else second + first
        return jnp.concatenate(order, axis=join)

    return dict(
        qkv=reduce(grads["qkv"], 1, 2),
        up=reduce(grads["up"], 0, 1),
        out=reduce(grads["out"], 1, 0),
        down=reduce(grads["down"], 1, 0),
    )


def vector_grads(small, at, tp_parts):
    index = 2 * at.section + at.near
    f32 = jnp.float32

    def placed(array, axis):
        size = array.shape[axis]
        shape = array.shape[:axis] + (size * 4 * tp_parts,) + array.shape[axis + 1 :]
        return lax.dynamic_update_slice_in_dim(
            jnp.zeros(shape, f32), array, (at.side * 4 + index) * size, axis
        )

    branch = jnp.where(at.chip == 0, small["branch"], 0.0)
    qkv = placed(small["qkv"], 1)
    up = placed(small["up"], 0)
    packed = jnp.concatenate(small["lines"] + [branch, qkv.reshape(-1), up])
    packed = lax.psum(packed, ALL)
    dim = branch.shape[0]
    lines = [packed[i * dim : (i + 1) * dim] for i in range(5)]
    qkv = packed[5 * dim : 5 * dim + qkv.size].reshape(qkv.shape)
    up = packed[5 * dim + qkv.size :]
    return lines, part(qkv, at.side, qkv.shape[1] // tp_parts, 1), part(
        up, at.side, up.shape[0] // tp_parts, 0
    )


def cube_device(
    inputs, cotangent, ln1_gain, ln1_bias, ln2_gain, ln2_bias, qkv_weight, qkv_bias,
    out_weight, up_weight, up_bias, down_weight, branch_bias,
):
    at = Place()
    rows = inputs.shape[1]
    x = gather_start(inputs, at)
    layers = shard_weights(
        (
            (ln1_gain[0], ln1_bias[0], ln2_gain[0], ln2_bias[0]),
            qkv_weight[0], qkv_bias[0], out_weight[0], up_weight[0], up_bias[0],
            down_weight[0], branch_bias[0],
        ),
        at,
    )
    g = gather_start(cotangent, at)
    dim = inputs.shape[2]
    x = x.reshape(-1, dim)
    g = g.reshape(-1, dim)
    place = jnp.arange(4 * rows, dtype=jnp.int32)
    own_pos = (2 * (place // rows) + at.core) * rows + place % rows
    other_pos = (2 * (place // rows) + 1 - at.core) * rows + place % rows
    cosine, sine = tables(own_pos)
    eighth = 4 * rows // 8

    partial, saved_first = forward_part(x, layers[0], own_pos, other_pos, cosine, sine)
    total = scatter_sum(partial, at)
    x_piece = part(x, at.chip, eighth, 0).astype(jnp.float32)
    piece = (x_piece + total + layers[0]["branch"]).astype(jnp.bfloat16)
    middle = gather_rows(piece, at)
    acts_first = spread_rows(middle, at)

    partial, saved_second = forward_part(middle, layers[1], own_pos, other_pos, cosine, sine)
    total = scatter_sum(partial, at)
    last = (piece.astype(jnp.float32) + total + layers[1]["branch"]).astype(jnp.bfloat16)
    acts_second = deliver_rows(last, 1, at)

    def input_grad(dn, g_piece, x_piece):
        total = scatter_sum(dn, at)
        normed, scale = normal(x_piece)
        inner = (
            total
            - jnp.mean(total, axis=-1, keepdims=True)
            - normed * jnp.mean(total * normed, axis=-1, keepdims=True)
        )
        return (g_piece.astype(jnp.float32) + scale * inner).astype(jnp.bfloat16)

    dn, grads_second, small_second = backward_part(g, saved_second, layers[1], cosine, sine)
    g_piece = input_grad(dn, part(g, at.chip, eighth, 0), piece)
    g_middle = gather_rows(g_piece, at)
    in_second = spread_rows(g_middle, at)
    done_second = matrix_grads(grads_second, 1, at)
    vectors_second = vector_grads(small_second, at, 2)

    dn, grads_first, small_first = backward_part(g_middle, saved_first, layers[0], cosine, sine)
    g_last = input_grad(dn, g_piece, part(x, at.chip, eighth, 0))
    in_first = deliver_rows(g_last, 0, at)
    done_first = matrix_grads(grads_first, 0, at)
    vectors_first = vector_grads(small_first, at, 2)

    def choose(a, b):
        return jnp.where(at.section == 0, a, b)[None]

    def matrix(name):
        return choose(done_first[name], done_second[name]).astype(jnp.float32)

    lines = [choose(a, b) for a, b in zip(vectors_first[0], vectors_second[0])]
    return (
        choose(acts_first, acts_second),
        choose(in_first, in_second),
        lines[0],
        lines[1],
        lines[2],
        lines[3],
        matrix("qkv"),
        choose(vectors_first[1], vectors_second[1]),
        matrix("out"),
        matrix("up"),
        choose(vectors_first[2], vectors_second[2]),
        matrix("down"),
        lines[4],
    )


def placed_program(mesh, device_program):
    placed = (
        P(None, "ctx", None),
        P(None, "ctx", None),
        P("section", None),
        P("section", None),
        P("section", None),
        P("section", None),
        P("section", None, None, "tp"),
        P("section", None, "tp"),
        P("section", "tp", None),
        P("section", None, "tp"),
        P("section", "tp"),
        P("section", "tp", None),
        P("section", None),
    )
    return jax.shard_map(
        device_program,
        mesh=mesh,
        in_specs=placed,
        out_specs=(
            P("section", None, "ctx", None),
            P("section", None, "ctx", None),
            P("section", None),
            P("section", None),
            P("section", None),
            P("section", None),
            P("section", None, "ctx", "tp"),
            P("section", None, "tp"),
            P("section", "tp", "ctx"),
            P("section", "ctx", "tp"),
            P("section", "tp"),
            P("section", "tp", "ctx"),
            P("section", None),
        ),
        check_vma=False,
    )


def solution(mesh):
    sizes = dict(mesh.shape)
    if sizes["section"] == 2 and sizes["tp"] == 2 and sizes["ctx"] == 8:
        return placed_program(mesh, cube_device)
    return placed_program(mesh, per_device)
```

```python
import math

import jax
import jax.numpy as jnp
from jax import lax
from jax.experimental import pallas as pl
from jax.experimental.pallas import tpu as pltpu
from jax.sharding import PartitionSpec as P

HD = 64
ROT = 16


def shifted(shard, axis, by):
    peers = lax.axis_size(axis)
    pairs = [(i, i + by) for i in range(peers) if 0 <= i + by < peers]
    return lax.ppermute(shard, axis, pairs)


def tables(positions):
    freqs = 1.0 / 10000.0 ** (jnp.arange(0, ROT, 2).astype(jnp.float32) / ROT)
    angles = positions.astype(jnp.float32)[:, None] * freqs[None, :]
    return (jnp.cos(angles)[:, None, :], jnp.sin(angles)[:, None, :])


def rotate(field, cosine, sine):
    half_rot = ROT // 2
    front = field[..., :half_rot]
    second = field[..., half_rot:ROT]
    return jnp.concatenate(
        [front * cosine - second * sine, second * cosine + front * sine, field[..., ROT:]], axis=-1
    )


def norms(hidden, gain_one, shift_one, gain_two, shift_two):
    centre = hidden - jnp.mean(hidden, axis=-1, keepdims=True)
    normed = centre * lax.rsqrt(jnp.mean(centre * centre, axis=-1, keepdims=True) + 1e-05)
    return (normed * gain_one + shift_one, normed * gain_two + shift_two)


def gelu_exact(value):
    return jax.nn.gelu(value, approximate=False)


def scores_of(queries, keys, query_pos, score_scale):
    raw = jnp.einsum("qhd,khd->hqk", queries, keys, preferred_element_type=jnp.float32)
    key_pos = jnp.arange(keys.shape[0], dtype=jnp.int32)
    return jnp.where(
        key_pos[None, None, :] <= query_pos[None, :, None], raw * score_scale, -1000000000.0
    )


def forward_layer(layer_in, weights, query_pos, cosine, sine):
    gains, w_qkv, b_qkv, w_out, w_up, b_up, w_down, b_branch = weights
    hidden = layer_in.astype(jnp.float32)
    attn_norm, mlp_norm = norms(hidden, gains[0], gains[1], gains[2], gains[3])
    attn_in = attn_norm.astype(jnp.bfloat16)
    mlp_in = mlp_norm.astype(jnp.bfloat16)
    projected = (
        jnp.einsum("td,cdf->tcf", attn_in, w_qkv, preferred_element_type=jnp.float32) + b_qkv
    )
    row_count = hidden.shape[0]
    feat_width = projected.shape[2]
    head_count = feat_width // HD
    queries = rotate(projected[:, 0].reshape(row_count, head_count, HD), cosine, sine).astype(
        jnp.bfloat16
    )
    key_flat = (
        rotate(projected[:, 1].reshape(row_count, head_count, HD), cosine, sine)
        .astype(jnp.bfloat16)
        .reshape(row_count, feat_width)
    )
    value_flat = projected[:, 2].astype(jnp.bfloat16)
    all_keys, all_values = (
        lax.all_gather(key_flat, "ctx", axis=0, tiled=True),
        lax.all_gather(value_flat, "ctx", axis=0, tiled=True),
    )
    key_count = all_keys.shape[0]
    score_scale = 1.0 / math.sqrt(HD)
    scores = scores_of(queries, all_keys.reshape(key_count, head_count, HD), query_pos, score_scale)
    row_max = jnp.max(scores, axis=-1, keepdims=True)
    exponent = jnp.exp(scores - row_max)
    summed = jnp.sum(exponent, axis=-1, keepdims=True)
    probability = (exponent / summed).astype(jnp.bfloat16)
    log_total = row_max + jnp.log(summed)
    mixed = jnp.einsum(
        "hqk,khd->qhd",
        probability,
        all_values.reshape(key_count, head_count, HD),
        preferred_element_type=jnp.float32,
    )
    mixed = mixed.reshape(row_count, feat_width).astype(jnp.bfloat16)
    partial_out = jnp.dot(mixed, w_out, preferred_element_type=jnp.float32)
    up_value = jnp.dot(mlp_in, w_up, preferred_element_type=jnp.float32) + b_up
    active = gelu_exact(up_value).astype(jnp.bfloat16)
    partial_out = partial_out + jnp.dot(active, w_down, preferred_element_type=jnp.float32)
    branches = lax.psum(partial_out, "tp")
    layer_out = (hidden + branches + b_branch).astype(jnp.bfloat16)
    stored = (key_flat, value_flat)
    saved = (layer_in, queries, stored, log_total, mixed, up_value, active)
    return (layer_out, saved)


def backward_layer(grad_out, saved, weights, query_pos, cosine, sine):
    gains, w_qkv, b_qkv, w_out, w_up, b_up, w_down, b_branch = weights
    layer_in, queries, stored, log_total, mixed, up_value, active = saved
    grad_full = grad_out.astype(jnp.float32)
    row_count, feat_width = mixed.shape
    head_count = feat_width // HD
    hidden = layer_in.astype(jnp.float32)
    norm_pair, norm_back = jax.vjp(norms, hidden, gains[0], gains[1], gains[2], gains[3])
    attn_in = norm_pair[0].astype(jnp.bfloat16)
    mlp_in = norm_pair[1].astype(jnp.bfloat16)
    active_grad = jnp.einsum("td,fd->tf", grad_out, w_down, preferred_element_type=jnp.float32)
    grad_down = jnp.einsum("tf,td->fd", active, grad_out, preferred_element_type=jnp.float32)
    gelu_back = jax.vjp(gelu_exact, up_value)[1]
    up_grad = gelu_back(active_grad)[0].astype(jnp.bfloat16)
    grad_up_bias = jnp.sum(up_grad.astype(jnp.float32), axis=0)
    grad_up = jnp.einsum("td,tf->df", mlp_in, up_grad, preferred_element_type=jnp.float32)
    mlp_in_grad = jnp.einsum("tf,df->td", up_grad, w_up, preferred_element_type=jnp.float32)
    mixed_grad = jnp.einsum(
        "td,fd->tf", grad_out, w_out, preferred_element_type=jnp.float32
    ).astype(jnp.bfloat16)
    grad_out_weight = jnp.einsum("tf,td->fd", mixed, grad_out, preferred_element_type=jnp.float32)
    all_keys, all_values = (
        lax.all_gather(stored[0], "ctx", axis=0, tiled=True),
        lax.all_gather(stored[1], "ctx", axis=0, tiled=True),
    )
    key_count = all_keys.shape[0]
    keys_heads = all_keys.reshape(key_count, head_count, HD)
    values_heads = all_values.reshape(key_count, head_count, HD)
    score_scale = 1.0 / math.sqrt(HD)
    scores = scores_of(queries, keys_heads, query_pos, score_scale)
    probability = jnp.exp(scores - log_total)
    heads_grad = mixed_grad.reshape(row_count, head_count, HD)
    prob_grad = jnp.einsum(
        "qhd,khd->hqk", heads_grad, values_heads, preferred_element_type=jnp.float32
    )
    centre = jnp.sum(probability * prob_grad, axis=-1, keepdims=True)
    score_grad = (score_scale * probability * (prob_grad - centre)).astype(jnp.bfloat16)
    query_grad = jnp.einsum(
        "hqk,khd->qhd", score_grad, keys_heads, preferred_element_type=jnp.float32
    )
    value_terms = jnp.einsum(
        "hqk,qhd->khd",
        probability.astype(jnp.bfloat16),
        heads_grad,
        preferred_element_type=jnp.float32,
    )
    key_terms = jnp.einsum("hqk,qhd->khd", score_grad, queries, preferred_element_type=jnp.float32)
    key_grad, value_grad = (
        lax.psum_scatter(
            key_terms.reshape(key_count, feat_width), "ctx", scatter_dimension=0, tiled=True
        ),
        lax.psum_scatter(
            value_terms.reshape(key_count, feat_width), "ctx", scatter_dimension=0, tiled=True
        ),
    )
    query_grad = rotate(query_grad, cosine, -sine).reshape(row_count, feat_width)
    key_grad = rotate(key_grad.reshape(row_count, head_count, HD), cosine, -sine).reshape(
        row_count, feat_width
    )
    qkv_grad = jnp.stack([query_grad, key_grad, value_grad], axis=1).astype(jnp.bfloat16)
    grad_qkv_bias = jnp.sum(qkv_grad.astype(jnp.float32), axis=0)
    grad_qkv = jnp.einsum("td,tcf->cdf", attn_in, qkv_grad, preferred_element_type=jnp.float32)
    attn_in_grad = jnp.einsum("tcf,cdf->td", qkv_grad, w_qkv, preferred_element_type=jnp.float32)
    attn_in_grad, mlp_in_grad = lax.psum((attn_in_grad, mlp_in_grad), "tp")
    hidden_grad, gain_one_grad, shift_one_grad, gain_two_grad, shift_two_grad = norm_back(
        (attn_in_grad, mlp_in_grad)
    )
    input_grad = (grad_full + hidden_grad).astype(jnp.bfloat16)
    grad_branch = jnp.sum(grad_full, axis=0)
    grads = (
        gain_one_grad,
        shift_one_grad,
        gain_two_grad,
        shift_two_grad,
        grad_qkv,
        grad_qkv_bias,
        grad_out_weight,
        grad_up,
        grad_up_bias,
        grad_down,
        grad_branch,
    )
    return (input_grad, grads)


def per_device(
    inputs,
    cotangent,
    ln1_gain,
    ln1_bias,
    ln2_gain,
    ln2_bias,
    qkv_weight,
    qkv_bias,
    out_weight,
    up_weight,
    up_bias,
    down_weight,
    branch_bias,
):
    gains = (
        ln1_gain[0].astype(jnp.float32),
        ln1_bias[0].astype(jnp.float32),
        ln2_gain[0].astype(jnp.float32),
        ln2_bias[0].astype(jnp.float32),
    )
    weights = (
        gains,
        qkv_weight[0],
        qkv_bias[0].astype(jnp.float32),
        out_weight[0],
        up_weight[0],
        up_bias[0].astype(jnp.float32),
        down_weight[0],
        branch_bias[0].astype(jnp.float32),
    )
    micro_count = inputs.shape[0]
    row_count = inputs.shape[1]
    query_pos = lax.axis_index("ctx") * row_count + jnp.arange(row_count, dtype=jnp.int32)
    cosine, sine = tables(query_pos)
    at_first = lax.axis_index("section") == 0
    blank = jnp.zeros_like(inputs[0])
    received = blank
    outputs_list = []
    saved_list = []
    for step_index in range(micro_count + 1):
        fresh = inputs[step_index] if step_index < micro_count else blank
        layer_in = jnp.where(at_first, fresh, received)
        layer_out, saved = forward_layer(layer_in, weights, query_pos, cosine, sine)
        outputs_list.append(layer_out)
        saved_list.append(saved)
        if step_index < micro_count:
            received = shifted(layer_out, "section", 1)
    returned = blank
    grad_list = []
    sums = None
    for back_index in range(micro_count + 1):
        batch_index = micro_count - 1 - back_index
        given = cotangent[batch_index] if batch_index >= 0 else blank
        grad_in = jnp.where(at_first, returned, given)
        input_grad, grads = backward_layer(
            grad_in, saved_list[micro_count - back_index], weights, query_pos, cosine, sine
        )
        sums = grads if sums is None else jax.tree.map(jnp.add, sums, grads)
        grad_list.append(input_grad)
        if back_index < micro_count:
            returned = shifted(input_grad, "section", -1)
    acts = jnp.stack(
        [jnp.where(at_first, outputs_list[j], outputs_list[j + 1]) for j in range(micro_count)]
    )[None]
    in_grads = jnp.stack(
        [
            jnp.where(at_first, grad_list[micro_count - j], grad_list[micro_count - 1 - j])
            for j in range(micro_count)
        ]
    )[None]
    (
        gain_one_grad,
        shift_one_grad,
        gain_two_grad,
        shift_two_grad,
        grad_qkv,
        grad_qkv_bias,
        grad_out_weight,
        grad_up,
        grad_up_bias,
        grad_down,
        grad_branch,
    ) = sums
    qkv_part, out_part, up_part, down_part = (
        lax.psum_scatter(
            grad_qkv[None].astype(jnp.bfloat16), "ctx", scatter_dimension=2, tiled=True
        ).astype(jnp.float32),
        lax.psum_scatter(
            grad_out_weight[None].astype(jnp.bfloat16), "ctx", scatter_dimension=2, tiled=True
        ).astype(jnp.float32),
        lax.psum_scatter(
            grad_up[None].astype(jnp.bfloat16), "ctx", scatter_dimension=1, tiled=True
        ).astype(jnp.float32),
        lax.psum_scatter(
            grad_down[None].astype(jnp.bfloat16), "ctx", scatter_dimension=2, tiled=True
        ).astype(jnp.float32),
    )
    small_sums = (
        lax.psum(gain_one_grad[None].astype(jnp.bfloat16), "ctx").astype(jnp.float32),
        lax.psum(shift_one_grad[None].astype(jnp.bfloat16), "ctx").astype(jnp.float32),
        lax.psum(gain_two_grad[None].astype(jnp.bfloat16), "ctx").astype(jnp.float32),
        lax.psum(shift_two_grad[None].astype(jnp.bfloat16), "ctx").astype(jnp.float32),
        lax.psum(grad_qkv_bias[None].astype(jnp.bfloat16), "ctx").astype(jnp.float32),
        lax.psum(grad_up_bias[None].astype(jnp.bfloat16), "ctx").astype(jnp.float32),
        lax.psum(grad_branch[None].astype(jnp.bfloat16), "ctx").astype(jnp.float32),
    )
    return (
        acts,
        in_grads,
        small_sums[0],
        small_sums[1],
        small_sums[2],
        small_sums[3],
        qkv_part,
        small_sums[4],
        out_part,
        up_part,
        small_sums[5],
        down_part,
        small_sums[6],
    )


ALL = ("section", "ctx", "tp")
SECTION, HALF, NEAR, CORE, SIDE = 16, 8, 4, 2, 1
CHIPS = (0, SIDE, NEAR, NEAR | SIDE, SECTION, SECTION | SIDE, SECTION | NEAR, SECTION | NEAR | SIDE)
F32, B16 = jnp.float32, jnp.bfloat16
ONE = 128
S_SECTION, S_HALF, S_NEAR, S_CORE, S_SIDE, S_CHIP, S_OWN, S_GIVE = range(8)


def swapped(array, mask):
    return lax.ppermute(array, ALL, [(i, i ^ mask) for i in range(32)])


def where_am_i():
    section = lax.axis_index("section")
    ctx = lax.axis_index("ctx")
    side = lax.axis_index("tp")
    half, near, core = ctx // 4, (ctx // 2) % 2, ctx % 2
    chip = 4 * section + 2 * near + side
    own, give = 2 * section + near, 2 * (1 - section) + near
    return jnp.stack([section, half, near, core, side, chip, own, give]).astype(jnp.int32)


def kernel_call(body, outs, at, *arrays, scratch=(), flops=0, exps=0):
    moved = sum(a.size * a.dtype.itemsize for a in arrays)
    moved += sum(math.prod(s) * jnp.dtype(d).itemsize for s, d in outs)
    return pl.pallas_call(
        body,
        out_shape=[jax.ShapeDtypeStruct(s, d) for s, d in outs],
        in_specs=[pl.BlockSpec(memory_space=pltpu.SMEM)]
        + [pl.BlockSpec(memory_space=pltpu.VMEM)] * len(arrays),
        out_specs=[pl.BlockSpec(memory_space=pltpu.VMEM)] * len(outs),
        scratch_shapes=list(scratch),
        compiler_params=pltpu.CompilerParams(vmem_limit_bytes=VMEM_BYTES),
        cost_estimate=pl.CostEstimate(flops=flops, bytes_accessed=moved, transcendentals=exps),
    )(at, *arrays)


VMEM_BYTES = 40 * 1024 * 1024


def nn(a, b):
    return jnp.dot(a, b, preferred_element_type=F32)


def nt(a, b):
    return lax.dot_general(a, b, (((1,), (1,)), ((), ())), preferred_element_type=F32)


def tn(a, b):
    return lax.dot_general(a, b, (((0,), (0,)), ((), ())), preferred_element_type=F32)


def pack_tokens(at, array):
    _, rows, dim = array.shape

    def body(at, mine, strip, mine_out, strip_out):
        mine_out[...] = mine[0]
        strip_out[...] = strip[0]

    return pl.pallas_call(
        body,
        out_shape=[
            jax.ShapeDtypeStruct((rows, dim), B16),
            jax.ShapeDtypeStruct((rows, dim // 2), B16),
        ],
        grid_spec=pltpu.PrefetchScalarGridSpec(
            num_scalar_prefetch=1,
            grid=(1,),
            in_specs=[
                pl.BlockSpec((1, rows, dim), lambda i, at: (at[S_HALF], 0, 0)),
                pl.BlockSpec((1, rows, dim // 2), lambda i, at: (1 - at[S_HALF], 0, at[S_SIDE])),
            ],
            out_specs=[
                pl.BlockSpec((rows, dim), lambda i, at: (0, 0)),
                pl.BlockSpec((rows, dim // 2), lambda i, at: (0, 0)),
            ],
        ),
    )(at, array, array)


def start_tokens(at, array):
    mine, strip = pack_tokens(at, array)
    near = swapped(mine, NEAR)
    far = swapped(strip, HALF)
    far_near = swapped(strip, HALF | NEAR)
    return mine, near, far, far_near, swapped(far, SIDE), swapped(far_near, SIDE)


def start_loader(at, refs):
    mine, near, far, far_near, far_rest, far_near_rest = refs
    first = at[S_SIDE] == 0
    index = 2 * at[S_HALF] + at[S_NEAR]

    def whole(strip, rest):
        a, b = strip[...], rest[...]
        return jnp.concatenate([jnp.where(first, a, b), jnp.where(first, b, a)], axis=1)

    yield index, mine[...]
    yield index ^ 1, near[...]
    yield index ^ 2, whole(far, far_rest)
    yield index ^ 3, whole(far_near, far_near_rest)


def piece_loader(at, refs):
    for j, ref in enumerate(refs):
        yield at[S_CHIP] ^ j, ref[...]


def pack_weights(at, small, w_qkv, w_up, w_out, w_down):
    _, three, dim, wide = w_qkv.shape
    heads = wide // 4
    units = w_up.shape[2] // 4
    side = dim // 2

    def body(at, qkv, up, out, down, small, a, b, c):
        for i in range(three):
            a[i * side : (i + 1) * side] = qkv[0, i]
        a[three * side :] = small[...]
        b[...] = up[0]
        c[: units // 2] = down[0]
        c[units // 2 :] = out[0]

    shapes = [(three * side + small.shape[0], ONE), (side, units), ((units + heads) // 2, dim)]
    return pl.pallas_call(
        body,
        out_shape=[jax.ShapeDtypeStruct(s, B16) for s in shapes],
        grid_spec=pltpu.PrefetchScalarGridSpec(
            num_scalar_prefetch=1,
            grid=(1,),
            in_specs=[
                pl.BlockSpec(
                    (1, three, side, heads), lambda i, at: (0, 0, at[S_CORE], at[S_GIVE])
                ),
                pl.BlockSpec((1, side, units), lambda i, at: (0, at[S_CORE], at[S_GIVE])),
                pl.BlockSpec(
                    (1, heads // 2, dim), lambda i, at: (0, 2 * at[S_GIVE] + at[S_CORE], 0)
                ),
                pl.BlockSpec(
                    (1, units // 2, dim), lambda i, at: (0, 2 * at[S_GIVE] + at[S_CORE], 0)
                ),
                pl.BlockSpec(small.shape, lambda i, at: (0, 0)),
            ],
            out_specs=[pl.BlockSpec(s, lambda i, at: (0, 0)) for s in shapes],
        ),
        compiler_params=pltpu.CompilerParams(vmem_limit_bytes=VMEM_BYTES),
    )(at, w_qkv, w_up, w_out, w_down, small)


def small_weights(index, gains, b_branch, b_up, b_qkv):
    units, heads = b_up.shape[1] // 4, b_qkv.shape[2] // 4
    rows = [v.reshape(-1, ONE) for v in list(gains) + [b_branch]]
    rows.append(lax.dynamic_slice_in_dim(b_up[0], index * units, units, 0).reshape(-1, ONE))
    rows.append(lax.dynamic_slice_in_dim(b_qkv[0], index * heads, heads, 1).reshape(-1, ONE))
    rows.append(jnp.zeros((1, ONE), B16))
    return jnp.concatenate(rows, axis=0)


def own_specs(index_maps, shapes):
    return [pl.BlockSpec(s, m) for s, m in zip(shapes, index_maps)]


def choose_weights(at, own_specs, owns, got, rest, outs, body):
    whole = [
        pl.BlockSpec(a.shape, lambda i, at, n=a.ndim: (0,) * n) for a in list(got) + list(rest)
    ]
    return pl.pallas_call(
        body,
        out_shape=[jax.ShapeDtypeStruct(s, d) for s, d in outs],
        grid_spec=pltpu.PrefetchScalarGridSpec(
            num_scalar_prefetch=1,
            grid=(1,),
            in_specs=list(own_specs) + whole,
            out_specs=[pl.BlockSpec(s, lambda i, at, n=len(s): (0,) * n) for s, _ in outs],
        ),
        compiler_params=pltpu.CompilerParams(vmem_limit_bytes=VMEM_BYTES),
    )(at, *owns, *got, *rest)


def both_layers(at, own, got, rest, low):
    taken = jnp.where((at[S_CORE] == 0) == low, got, rest)
    mine = at[S_SECTION] == 0
    return jnp.where(mine, own, taken), jnp.where(mine, taken, own)


def layer_weights(at, small_own, w_qkv, w_up, w_out, w_down, sent):
    _, three, dim, wide = w_qkv.shape
    heads, units, side = wide // 4, w_up.shape[2] // 4, dim // 2
    got = [swapped(array, SECTION) for array in sent]
    rest = [swapped(array, CORE) for array in got]

    def qkv_body(at, own, own_small, got, rest, qkv0, qkv1, rows0, rows1):
        for low, first in ((True, 0), (False, side)):
            for i in range(three):
                source = slice(i * side, (i + 1) * side)
                target = (slice(first, first + side), slice(i * heads, (i + 1) * heads))
                a, b = both_layers(
                    at, own[0, i, first : first + side], got[source], rest[source], low
                )
                qkv0[target] = a
                qkv1[target] = b
        taken, mine = got[three * side :].astype(F32), own_small[...].astype(F32)
        is_first = at[S_SECTION] == 0
        for rows, table in (
            (rows0, jnp.where(is_first, mine, taken)),
            (rows1, jnp.where(is_first, taken, mine)),
        ):
            rows[...] = jnp.zeros_like(rows)
            line = 0
            for r, tiles in enumerate([dim // ONE] * 5 + [units // ONE, three * heads // ONE]):
                for i in range(tiles):
                    rows[r : r + 1, i * ONE : (i + 1) * ONE] = table[line : line + 1]
                    line += 1

    qkv0, qkv1, rows0, rows1 = choose_weights(
        at,
        [
            pl.BlockSpec((1, three, dim, heads), lambda i, at: (0, 0, 0, at[S_OWN])),
            pl.BlockSpec(small_own.shape, lambda i, at: (0, 0)),
        ],
        [w_qkv, small_own],
        got[:1],
        rest[:1],
        [((dim, three * heads), B16)] * 2 + [((8, dim), F32)] * 2,
        qkv_body,
    )

    def up_body(at, own, got, rest, up0, up1):
        for low, first in ((True, 0), (False, side)):
            a, b = both_layers(at, own[0, first : first + side], got[...], rest[...], low)
            up0[first : first + side] = a
            up1[first : first + side] = b

    up0, up1 = choose_weights(
        at,
        [pl.BlockSpec((1, dim, units), lambda i, at: (0, 0, at[S_OWN]))],
        [w_up],
        got[1:2],
        rest[1:2],
        [((dim, units), B16)] * 2,
        up_body,
    )

    def down_body(at, own_down, own_out, got, rest, down0, down1, out0, out1):
        for own, size, source, first, second in (
            (own_down, units // 2, 0, down0, down1),
            (own_out, heads // 2, units // 2, out0, out1),
        ):
            for low, start in ((True, 0), (False, size)):
                rows = slice(start, start + size)
                span = slice(source, source + size)
                a, b = both_layers(at, own[0, rows], got[span], rest[span], low)
                first[rows] = a
                second[rows] = b

    down0, down1, out0, out1 = choose_weights(
        at,
        [
            pl.BlockSpec((1, units, dim), lambda i, at: (0, at[S_OWN], 0)),
            pl.BlockSpec((1, heads, dim), lambda i, at: (0, at[S_OWN], 0)),
        ],
        [w_down, w_out],
        got[2:],
        rest[2:],
        [((units, dim), B16)] * 2 + [((heads, dim), B16)] * 2,
        down_body,
    )
    return (
        dict(qkv=qkv0, rows=rows0, up=up0, down=down0, out=out0),
        dict(qkv=qkv1, rows=rows1, up=up1, down=down1, out=out1),
    )


def turn_tables(at, rows):
    place = jnp.arange(rows, dtype=jnp.int32)
    positions = (2 * (place // ONE) + at[S_CORE]) * ONE + place % ONE
    freqs = 1.0 / 10000.0 ** (jnp.arange(0, ROT, 2).astype(F32) / ROT)
    half_rot = ROT // 2
    lane = jnp.arange(ONE, dtype=jnp.int32) % HD
    angles = positions.astype(F32)[:, None] * jnp.tile(freqs, ONE // half_rot)[None, :]
    sine = jnp.sin(angles)
    return jnp.stack(
        [
            jnp.where(lane < ROT, jnp.cos(angles), 1.0),
            jnp.where((lane >= half_rot) & (lane < ROT), sine, 0.0),
            jnp.where(lane < half_rot, -sine, 0.0),
        ]
    )


def front(at, loader, sources, w, turns, with_piece):
    dim = w["qkv"].shape[0]
    rows = turns.shape[1]
    count = len(sources)

    def body(at, *refs):
        given = refs[:count]
        qkv, vectors, turns = refs[count : count + 3]
        attn_in, mlp_in, normed_out, q, kv = refs[count + 3 : count + 8]
        gains = [vectors[i : i + 1] for i in range(4)]
        for place, block in loader(at, given):
            size = block.shape[0]
            hidden = block.astype(F32)
            mean = jnp.sum(hidden, axis=1, keepdims=True) * (1.0 / dim)
            centre = hidden - mean
            var = jnp.sum(centre * centre, axis=1, keepdims=True) * (1.0 / dim)
            normed = centre * lax.rsqrt(var + 1e-05)
            span = pl.ds(pl.multiple_of(place * size, size), size)
            attn_in[span] = (normed * gains[0] + gains[1]).astype(B16)
            mlp_in[span] = (normed * gains[2] + gains[3]).astype(B16)
            normed_out[span] = normed.astype(B16)
            if with_piece:
                refs[count + 9][span] = block
        bias = vectors[6:7, : 3 * ONE]
        step = 256
        for first in range(0, rows, step):
            span = slice(first, first + step)
            projected = nn(attn_in[span], qkv[...]) + bias
            cosine, second, first_half = turns[0, span], turns[1, span], turns[2, span]
            for i, target in ((0, q), (1, kv.at[0])):
                flat = projected[:, i * ONE : (i + 1) * ONE]
                flat = (
                    flat * cosine
                    + pltpu.roll(flat, ROT // 2, 1) * second
                    + pltpu.roll(flat, ONE - ROT // 2, 1) * first_half
                )
                target[span] = flat.astype(B16)
            kv[1, span] = projected[:, 2 * ONE :].astype(B16)
        if with_piece:
            size = rows // 8
            span = pl.ds(pl.multiple_of(at[S_CHIP] * size, size), size)
            refs[count + 8][...] = refs[count + 9][span]

    outs = [((rows, dim), B16)] * 3 + [((rows, ONE), B16), ((2, rows, ONE), B16)]
    scratch = []
    if with_piece:
        outs.append(((rows // 8, dim), B16))
        scratch.append(pltpu.VMEM((rows, dim), B16))
    return kernel_call(
        body, outs, at, *sources, w["qkv"], w["rows"], turns,
        scratch=scratch, flops=2 * rows * dim * 3 * ONE + 20 * rows * dim,
    )


def units_forward(at, mlp_in, w):
    rows, dim = mlp_in.shape
    units = w["up"].shape[1]

    def body(at, mlp_in, up, vectors, active, slope):
        bias = vectors[5:6, :units]
        step = 128
        for first in range(0, rows, step):
            span = slice(first, first + step)
            value = nn(mlp_in[span], up[...]) + bias
            cdf = 0.5 + 0.5 * lax.erf(value * (1.0 / math.sqrt(2.0)))
            pdf = jnp.exp(value * value * -0.5) * (1.0 / math.sqrt(2.0 * math.pi))
            active[span] = (value * cdf).astype(B16)
            slope[span] = (cdf + value * pdf).astype(B16)

    return kernel_call(
        body, [((rows, units), B16)] * 2, at, mlp_in, w["up"], w["rows"],
        flops=2 * rows * dim * units + 40 * rows * units, exps=rows * units,
    )


def head_lanes():
    return lax.broadcasted_iota(jnp.int32, (1, ONE), 1) < HD


def allowed_keys(at, first, step, count):
    row = lax.broadcasted_iota(jnp.int32, (step, count), 0) + first
    column = lax.broadcasted_iota(jnp.int32, (step, count), 1)
    return column <= row, column < (row // ONE + at[S_CORE]) * ONE


def pieces_out(at, total, pieces):
    size = total.shape[0] // 8
    for j, piece in enumerate(pieces):
        span = pl.ds(pl.multiple_of((at[S_CHIP] ^ j) * size, size), size)
        piece[...] = total[span].astype(piece.dtype)


def attention_forward(at, q, kv, kv_other, active, w):
    rows = q.shape[0]
    units, dim = w["down"].shape
    scale = 1.0 / math.sqrt(HD)

    def body(at, q, kv, kv_other, active, out, down, mixed, lse, *rest):
        pieces, total = rest[:8], rest[8]
        first_head = head_lanes()
        step = 256
        for first in range(0, rows, step):
            span = slice(first, first + step)
            count = first + step
            queries = q[span]
            masks = allowed_keys(at, first, step, count)
            results, totals = [], []
            for head in range(2):
                lanes = first_head if head == 0 else jnp.logical_not(first_head)
                one = jnp.where(lanes, queries, jnp.zeros_like(queries))
                scores = [
                    jnp.where(mask, nt(one, keys[0, :count]) * scale, -1e9)
                    for mask, keys in zip(masks, (kv, kv_other))
                ]
                most = jnp.maximum(
                    jnp.max(scores[0], axis=1, keepdims=True),
                    jnp.max(scores[1], axis=1, keepdims=True),
                )
                exponents = [jnp.exp(s - most) for s in scores]
                summed = jnp.sum(exponents[0], axis=1, keepdims=True) + jnp.sum(
                    exponents[1], axis=1, keepdims=True
                )
                inverse = 1.0 / summed
                results.append(
                    nn((exponents[0] * inverse).astype(B16), kv[1, :count])
                    + nn((exponents[1] * inverse).astype(B16), kv_other[1, :count])
                )
                totals.append(most + jnp.log(summed))
            mixed[span] = jnp.where(first_head, results[0], results[1]).astype(B16)
            lse[span] = jnp.where(first_head, totals[0], totals[1])
            total[span] = nn(mixed[span], out[...]) + nn(active[span], down[...])
        pieces_out(at, total, pieces)

    outs = [((rows, ONE), B16), ((rows, ONE), F32), ((rows // 8, dim), F32)]
    outs += [((rows // 8, dim), B16)] * 7
    return kernel_call(
        body, outs, at, q, kv, kv_other, active, w["out"], w["down"],
        scratch=[pltpu.VMEM((rows, dim), F32)],
        flops=2 * rows * dim * (units + ONE) + 8 * rows * rows * ONE * 2,
        exps=2 * rows * rows * 2,
    )


def units_backward(at, loader, sources, slope, w, with_piece):
    rows, units = slope.shape
    dim = w["up"].shape[0]
    count = len(sources)

    def body(at, *refs):
        given = refs[:count]
        slope, down, out = refs[count : count + 3]
        g, up_grad, mixed_grad = refs[count + 3 : count + 6]
        for place, block in loader(at, given):
            size = block.shape[0]
            g[pl.ds(pl.multiple_of(place * size, size), size)] = block
        step = 256
        for first in range(0, rows, step):
            span = slice(first, first + step)
            up_grad[span] = (nt(g[span], down[...]) * slope[span].astype(F32)).astype(B16)
            mixed_grad[span] = nt(g[span], out[...]).astype(B16)
        if with_piece:
            size = rows // 8
            refs[count + 6][...] = g[pl.ds(pl.multiple_of(at[S_CHIP] * size, size), size)]

    outs = [((rows, dim), B16), ((rows, units), B16), ((rows, ONE), B16)]
    if with_piece:
        outs.append(((rows // 8, dim), B16))
    return kernel_call(
        body, outs, at, *sources, slope, w["down"], w["out"],
        flops=2 * rows * dim * (units + ONE),
    )


def attention_backward(at, q, kv, kv_other, lse, mixed_grad):
    rows = q.shape[0]
    scale = 1.0 / math.sqrt(HD)

    def body(at, q, kv, kv_other, lse, mixed_grad, dq, dkv, dkv_other):
        first_head = head_lanes()
        step = 256
        dkv[...] = jnp.zeros_like(dkv)
        dkv_other[...] = jnp.zeros_like(dkv_other)
        for first in range(0, rows, step):
            span = slice(first, first + step)
            count = first + step
            queries, back = q[span], mixed_grad[span]
            masks = allowed_keys(at, first, step, count)
            sides = ((masks[0], kv, dkv), (masks[1], kv_other, dkv_other))
            results = []
            for head in range(2):
                lanes = first_head if head == 0 else jnp.logical_not(first_head)
                one = jnp.where(lanes, queries, jnp.zeros_like(queries))
                one_back = jnp.where(lanes, back, jnp.zeros_like(back))
                level = lse[span, head * HD : head * HD + 1]
                probs, grads = [], []
                for mask, keys, _ in sides:
                    scores = nt(one, keys[0, :count]) * scale
                    probs.append(jnp.exp(jnp.where(mask, scores, -1e9) - level))
                    grads.append(nt(one_back, keys[1, :count]))
                delta = jnp.sum(probs[0] * grads[0], axis=1, keepdims=True) + jnp.sum(
                    probs[1] * grads[1], axis=1, keepdims=True
                )
                result = 0.0
                for (_, keys, target), prob, grad in zip(sides, probs, grads):
                    score_grad = (prob * (grad - delta) * scale).astype(B16)
                    result = result + nn(score_grad, keys[0, :count])
                    target[0, :count] += tn(score_grad, one)
                    target[1, :count] += tn(prob.astype(B16), one_back)
                results.append(result)
            dq[span] = jnp.where(first_head, results[0], results[1])

    return kernel_call(
        body, [((rows, ONE), F32), ((2, rows, ONE), F32), ((2, rows, ONE), F32)],
        at, q, kv, kv_other, lse, mixed_grad,
        flops=20 * rows * rows * ONE * 2, exps=2 * rows * rows * 2,
    )


def inputs_backward(at, dq, dkv, dkv_got, up_grad, normed, g, turns, w):
    rows, dim = normed.shape
    units = up_grad.shape[1]

    def body(at, dq, dkv, dkv_got, up_grad, normed, g, turns, qkv, up, vectors, *rest):
        qkv_grad, table = rest[:2]
        pieces, total, lines = rest[2:10], rest[10], rest[11]
        gain_one, gain_two = vectors[0:1], vectors[2:3]
        step = 128
        sums = None
        for first in range(0, rows, step):
            span = slice(first, first + step)
            cosine, second, first_half = turns[0, span], turns[1, span], turns[2, span]
            parts = []
            for flat in (dq[span], dkv[0, span] + dkv_got[0, span]):
                parts.append(
                    flat * cosine
                    - pltpu.roll(flat, ROT // 2, 1) * second
                    - pltpu.roll(flat, ONE - ROT // 2, 1) * first_half
                )
            parts.append(dkv[1, span] + dkv_got[1, span])
            both = jnp.concatenate([p.astype(B16) for p in parts], axis=1)
            qkv_grad[span] = both
            attn = nt(both, qkv[...])
            mlp = nt(up_grad[span], up[...])
            total[span] = attn * gain_one + mlp * gain_two
            unit = normed[span].astype(F32)
            new = [
                jnp.sum(v, axis=0, keepdims=True)
                for v in (
                    attn * unit, attn, mlp * unit, mlp, g[span].astype(F32),
                    up_grad[span].astype(F32), both.astype(F32),
                )
            ]
            sums = new if sums is None else [a + b for a, b in zip(sums, new)]
        pieces_out(at, total, pieces)
        lines[...] = jnp.zeros_like(lines)
        line = 0
        for value in sums:
            for i in range(value.shape[1] // ONE):
                lines[line : line + 1] = value[:, i * ONE : (i + 1) * ONE]
                line += 1
        table[...] = lines[...].astype(B16)

    outs = [((rows, 3 * ONE), B16), ((LINES, ONE), B16), ((rows // 8, dim), F32)]
    outs += [((rows // 8, dim), B16)] * 7
    return kernel_call(
        body, outs, at, dq, dkv, dkv_got, up_grad, normed, g, turns, w["qkv"], w["up"], w["rows"],
        scratch=[pltpu.VMEM((rows, dim), F32), pltpu.VMEM((LINES, ONE), F32)],
        flops=2 * rows * dim * (units + 3 * ONE) + 12 * rows * dim,
    )


LINES = 64


def join_forward(at, x_piece, parts, w):
    def body(at, x, vectors, own, *rest):
        total = x[...].astype(F32) + own[...] + vectors[4:5]
        for piece in rest[:-1]:
            total = total + piece[...].astype(F32)
        rest[-1][...] = total.astype(B16)

    return kernel_call(body, [(x_piece.shape, B16)], at, x_piece, w["rows"], *parts)[0]


def join_backward(at, g_piece, x_piece, parts):
    dim = x_piece.shape[1]

    def body(at, g, x, own, *rest):
        total = own[...]
        for piece in rest[:-1]:
            total = total + piece[...].astype(F32)
        hidden = x[...].astype(F32)
        centre = hidden - jnp.sum(hidden, axis=1, keepdims=True) * (1.0 / dim)
        var = jnp.sum(centre * centre, axis=1, keepdims=True) * (1.0 / dim)
        scale = lax.rsqrt(var + 1e-05)
        normed = centre * scale
        inner = (
            total
            - jnp.sum(total, axis=1, keepdims=True) * (1.0 / dim)
            - normed * (jnp.sum(total * normed, axis=1, keepdims=True) * (1.0 / dim))
        )
        rest[-1][...] = (g[...].astype(F32) + scale * inner).astype(B16)

    return kernel_call(body, [(x_piece.shape, B16)], at, g_piece, x_piece, *parts)[0]


def exchanged(pieces):
    return [pieces[0]] + [swapped(pieces[j], CHIPS[j]) for j in range(1, 8)]


def gathered(piece):
    return [piece] + [swapped(piece, CHIPS[j]) for j in range(1, 8)]


def columns(at, ref, core, high):
    which = at[S_CORE] ^ core
    return jnp.concatenate(
        [
            ref[:, pl.ds(pl.multiple_of((4 * high + 2 * low + which) * ONE, ONE), ONE)]
            for low in range(2)
        ],
        axis=1,
    )


def early_grads(at, active, mixed, mlp_in, up_grad, g):
    rows, dim = g.shape
    units = active.shape[1]
    tiles = units // ONE

    def body(at, active, mixed, mlp_in, up_grad, g, keep, give):
        for core, target in ((0, keep), (1, give)):
            for high in range(2):
                strip = columns(at, g, core, high)
                down = tn(active[...], strip).astype(B16)
                out = tn(mixed[...], strip).astype(B16)
                up = tn(columns(at, mlp_in, core, high), up_grad[...]).astype(B16)
                for low in range(2):
                    lanes = slice(low * ONE, (low + 1) * ONE)
                    where = (at[S_HALF] ^ high, at[S_NEAR] ^ low)
                    target[where[0], where[1], :units] = down[:, lanes]
                    target[where[0], where[1], units : units + ONE] = out[:, lanes]
                    for i in range(tiles):
                        base = units + (1 + i) * ONE
                        target[where[0], where[1], base : base + ONE] = up[
                            lanes, i * ONE : (i + 1) * ONE
                        ]

    shape = (2, 2, 2 * units + ONE, ONE)
    return kernel_call(
        body, [(shape, B16)] * 2, at, active, mixed, mlp_in, up_grad, g,
        flops=2 * rows * dim * (2 * units + ONE),
    )


def late_grads(at, attn_in, qkv_grad, table):
    rows, dim = attn_in.shape

    def body(at, attn_in, qkv_grad, table, keep, give):
        for core, target in ((0, keep), (1, give)):
            for high in range(2):
                qkv = tn(columns(at, attn_in, core, high), qkv_grad[...]).astype(B16)
                for low in range(2):
                    where = (at[S_HALF] ^ high, at[S_NEAR] ^ low)
                    for i in range(3):
                        target[where[0], where[1], i * ONE : (i + 1) * ONE] = qkv[
                            low * ONE : (low + 1) * ONE, i * ONE : (i + 1) * ONE
                        ]
                    target[where[0], where[1], 3 * ONE :] = table[...]

    shape = (2, 2, 3 * ONE + LINES, ONE)
    return kernel_call(
        body, [(shape, B16)] * 2, at, attn_in, qkv_grad, table,
        flops=2 * rows * dim * 3 * ONE,
    )


def plus(a, b):
    return (a.astype(F32) + b.astype(F32)).astype(B16)


def summed_halves(keep, give):
    got = swapped(give, CORE)
    mine = plus(keep[0], got[0])
    other = plus(keep[1], got[1])
    return plus(mine, swapped(other, HALF))


def at_owner(section, first, second):
    own = jnp.where(section == 0, first, second)
    got = swapped(jnp.where(section == 0, second, first), SECTION)
    near = swapped(jnp.stack([own[1], got[1]]), NEAR)
    return own[0], got[0], near[0], near[1]


def unpack_grads(at, early, late, sizes):
    dim_part, units, heads = ONE, sizes["units"], ONE

    def body(at, *refs):
        early, late = refs[:4], refs[4:8]
        qkv, out, up, down, lines, b_qkv, b_up, branch = refs[8:]
        index = at[S_OWN]
        total = 0.0
        for j, (wide, narrow) in enumerate(zip(early, late)):
            source = index ^ (2 * (j % 2) + j // 2)
            place = pl.multiple_of(source * units, units)
            small = pl.multiple_of(source * ONE, ONE)
            down[pl.ds(place, units)] = wide[:units].astype(F32)
            out[pl.ds(small, ONE)] = wide[units : units + ONE].astype(F32)
            for i in range(units // ONE):
                base = units + (1 + i) * ONE
                up[:, pl.ds(place + i * ONE, ONE)] = wide[base : base + ONE].astype(F32)
            for i in range(3):
                qkv[i, :, pl.ds(small, ONE)] = narrow[i * ONE : (i + 1) * ONE].astype(F32)
            table = narrow[3 * ONE :].astype(F32)
            total = total + table[:32]
            for i in range(units // ONE):
                b_up[:, pl.ds(place + i * ONE, ONE)] = table[40 + i : 41 + i]
            for i in range(3):
                b_qkv[i : i + 1, pl.ds(small, ONE)] = table[40 + units // ONE + i :][:1]
            if j == 0:
                branch[...] = table[32:40]
        lines[...] = total

    outs = [
        ((3, dim_part, 4 * heads), F32),
        ((4 * heads, dim_part), F32),
        ((dim_part, 4 * units), F32),
        ((4 * units, dim_part), F32),
        ((32, ONE), F32),
        ((3, 4 * heads), F32),
        ((1, 4 * units), F32),
        ((8, ONE), F32),
    ]
    return kernel_call(body, outs, at, *early, *late)


def cube_device(
    inputs, cotangent, ln1_gain, ln1_bias, ln2_gain, ln2_bias, qkv_weight, qkv_bias,
    out_weight, up_weight, up_bias, down_weight, branch_bias,
):
    at = where_am_i()
    section, half, near, core, side, chip, own, give = [at[i] for i in range(8)]
    dim = inputs.shape[2]
    rows = 4 * inputs.shape[1]
    vectors = (ln1_gain, ln1_bias, ln2_gain, ln2_bias)
    small_own = small_weights(own, vectors, branch_bias, up_bias, qkv_bias)
    small_give = small_weights(give, vectors, branch_bias, up_bias, qkv_bias)

    x_parts = start_tokens(at, inputs)
    sent = pack_weights(at, small_give, qkv_weight, up_weight, out_weight, down_weight)
    first, second = layer_weights(
        at, small_own, qkv_weight, up_weight, out_weight, down_weight, sent
    )
    turns = turn_tables(at, rows)
    g_parts = start_tokens(at, cotangent)

    def forward(loader, sources, w, with_piece):
        got = front(at, loader, sources, w, turns, with_piece)
        attn_in, mlp_in, normed, q, kv = got[:5]
        kv_other = swapped(kv, CORE)
        active, slope = units_forward(at, mlp_in, w)
        made = attention_forward(at, q, kv, kv_other, active, w)
        mixed, lse, pieces = made[0], made[1], made[2:]
        saved = dict(
            attn_in=attn_in, mlp_in=mlp_in, normed=normed, q=q, kv=kv, kv_other=kv_other,
            active=active, slope=slope, mixed=mixed, lse=lse,
        )
        return exchanged(pieces), saved, got[5:]

    def backward(loader, sources, saved, w, with_piece):
        made = units_backward(at, loader, sources, saved["slope"], w, with_piece)
        g, up_grad, mixed_grad = made[:3]
        dq, dkv, dkv_other = attention_backward(
            at, saved["q"], saved["kv"], saved["kv_other"], saved["lse"], mixed_grad
        )
        dkv_got = swapped(dkv_other, CORE)
        early = early_grads(at, saved["active"], saved["mixed"], saved["mlp_in"], up_grad, g)
        out = inputs_backward(at, dq, dkv, dkv_got, up_grad, saved["normed"], g, turns, w)
        qkv_grad, table, pieces = out[0], out[1], out[2:]
        late = late_grads(at, saved["attn_in"], qkv_grad, table)
        return exchanged(pieces), early, late, made[3:]

    parts, saved_first, (x_piece,) = forward(start_loader, x_parts, first, True)
    piece = join_forward(at, x_piece, parts, first)
    middle = gathered(piece)

    parts_last, saved_second, _ = forward(piece_loader, middle, second, False)
    last = join_forward(at, piece, parts_last, second)

    parts, early_second, late_second, (g_piece,) = backward(
        start_loader, g_parts, saved_second, second, True
    )
    back = join_backward(at, g_piece, piece, parts)
    g_middle = gathered(back)
    early_second = summed_halves(*early_second)
    late_second = summed_halves(*late_second)

    parts, early_first, late_first, _ = backward(
        piece_loader, g_middle, saved_first, first, False
    )
    back_last = join_backward(at, back, x_piece, parts)
    early_first = summed_halves(*early_first)
    late_first = summed_halves(*late_first)

    early = at_owner(section, early_first, early_second)
    late = at_owner(section, late_first, late_second)
    sizes = dict(units=up_weight.shape[2] // 4)
    qkv, out, up, down, lines, b_qkv, b_up, branch = unpack_grads(at, early, late, sizes)
    lines = lines + swapped(lines, SIDE)

    def halves(mine, got):
        return jnp.where(half == 0, jnp.stack([mine, got]), jnp.stack([got, mine]))

    def relative(pieces, index):
        pair = [lax.dynamic_index_in_dim(pieces, 2 * index + i ^ chip, 0, False) for i in range(2)]
        return jnp.concatenate(pair, axis=0)

    known = jnp.where(section == 0, jnp.stack(middle), jnp.stack(g_middle))
    known_mine = relative(known, 2 * half + near)
    known_got = swapped(relative(known, 2 * (1 - half) + near), HALF)
    known = halves(known_mine, known_got)

    mine = jnp.where(section == 0, back_last, last)
    got = swapped(jnp.where(section == 0, last, back_last), SECTION)
    both = jnp.where(section == 0, jnp.stack([mine, got]), jnp.stack([got, mine]))
    rest = swapped(both, SIDE)
    blocks = jnp.where(
        side == 0, jnp.concatenate([both, rest], axis=1), jnp.concatenate([rest, both], axis=1)
    )
    mine = lax.dynamic_index_in_dim(blocks, half, 0, False)
    got = swapped(lax.dynamic_index_in_dim(blocks, 1 - half, 0, False), HALF)
    new = halves(mine, got)
    acts = jnp.where(section == 0, known, new)
    in_grads = jnp.where(section == 0, new, known)

    lines = lines.reshape(4, dim)
    return (
        acts[None],
        in_grads[None],
        lines[0:1],
        lines[1:2],
        lines[2:3],
        lines[3:4],
        qkv[None],
        b_qkv[None],
        out[None],
        up[None],
        b_up,
        down[None],
        branch.reshape(1, dim),
    )


def placed_program(mesh, device_program):
    placed = (
        P(None, "ctx", None),
        P(None, "ctx", None),
        P("section", None),
        P("section", None),
        P("section", None),
        P("section", None),
        P("section", None, None, "tp"),
        P("section", None, "tp"),
        P("section", "tp", None),
        P("section", None, "tp"),
        P("section", "tp"),
        P("section", "tp", None),
        P("section", None),
    )
    return jax.shard_map(
        device_program,
        mesh=mesh,
        in_specs=placed,
        out_specs=(
            P("section", None, "ctx", None),
            P("section", None, "ctx", None),
            P("section", None),
            P("section", None),
            P("section", None),
            P("section", None),
            P("section", None, "ctx", "tp"),
            P("section", None, "tp"),
            P("section", "tp", "ctx"),
            P("section", "ctx", "tp"),
            P("section", "tp"),
            P("section", "tp", "ctx"),
            P("section", None),
        ),
        check_vma=False,
    )


def solution(mesh):
    sizes = dict(mesh.shape)
    if sizes["section"] == 2 and sizes["tp"] == 2 and sizes["ctx"] == 8:
        return placed_program(mesh, cube_device)
    return placed_program(mesh, per_device)
```

```python
import math

import jax
import jax.numpy as jnp
from jax import lax
from jax.experimental import pallas as pl
from jax.experimental.pallas import tpu as pltpu
from jax.sharding import PartitionSpec as P

HD = 64
ROT = 16


def shifted(shard, axis, by):
    peers = lax.axis_size(axis)
    pairs = [(i, i + by) for i in range(peers) if 0 <= i + by < peers]
    return lax.ppermute(shard, axis, pairs)


def tables(positions):
    freqs = 1.0 / 10000.0 ** (jnp.arange(0, ROT, 2).astype(jnp.float32) / ROT)
    angles = positions.astype(jnp.float32)[:, None] * freqs[None, :]
    return (jnp.cos(angles)[:, None, :], jnp.sin(angles)[:, None, :])


def rotate(field, cosine, sine):
    half_rot = ROT // 2
    front = field[..., :half_rot]
    second = field[..., half_rot:ROT]
    return jnp.concatenate(
        [front * cosine - second * sine, second * cosine + front * sine, field[..., ROT:]], axis=-1
    )


def norms(hidden, gain_one, shift_one, gain_two, shift_two):
    centre = hidden - jnp.mean(hidden, axis=-1, keepdims=True)
    normed = centre * lax.rsqrt(jnp.mean(centre * centre, axis=-1, keepdims=True) + 1e-05)
    return (normed * gain_one + shift_one, normed * gain_two + shift_two)


def gelu_exact(value):
    return jax.nn.gelu(value, approximate=False)


def scores_of(queries, keys, query_pos, score_scale):
    raw = jnp.einsum("qhd,khd->hqk", queries, keys, preferred_element_type=jnp.float32)
    key_pos = jnp.arange(keys.shape[0], dtype=jnp.int32)
    return jnp.where(
        key_pos[None, None, :] <= query_pos[None, :, None], raw * score_scale, -1000000000.0
    )


def forward_layer(layer_in, weights, query_pos, cosine, sine):
    gains, w_qkv, b_qkv, w_out, w_up, b_up, w_down, b_branch = weights
    hidden = layer_in.astype(jnp.float32)
    attn_norm, mlp_norm = norms(hidden, gains[0], gains[1], gains[2], gains[3])
    attn_in = attn_norm.astype(jnp.bfloat16)
    mlp_in = mlp_norm.astype(jnp.bfloat16)
    projected = (
        jnp.einsum("td,cdf->tcf", attn_in, w_qkv, preferred_element_type=jnp.float32) + b_qkv
    )
    row_count = hidden.shape[0]
    feat_width = projected.shape[2]
    head_count = feat_width // HD
    queries = rotate(projected[:, 0].reshape(row_count, head_count, HD), cosine, sine).astype(
        jnp.bfloat16
    )
    key_flat = (
        rotate(projected[:, 1].reshape(row_count, head_count, HD), cosine, sine)
        .astype(jnp.bfloat16)
        .reshape(row_count, feat_width)
    )
    value_flat = projected[:, 2].astype(jnp.bfloat16)
    all_keys, all_values = (
        lax.all_gather(key_flat, "ctx", axis=0, tiled=True),
        lax.all_gather(value_flat, "ctx", axis=0, tiled=True),
    )
    key_count = all_keys.shape[0]
    score_scale = 1.0 / math.sqrt(HD)
    scores = scores_of(queries, all_keys.reshape(key_count, head_count, HD), query_pos, score_scale)
    row_max = jnp.max(scores, axis=-1, keepdims=True)
    exponent = jnp.exp(scores - row_max)
    summed = jnp.sum(exponent, axis=-1, keepdims=True)
    probability = (exponent / summed).astype(jnp.bfloat16)
    log_total = row_max + jnp.log(summed)
    mixed = jnp.einsum(
        "hqk,khd->qhd",
        probability,
        all_values.reshape(key_count, head_count, HD),
        preferred_element_type=jnp.float32,
    )
    mixed = mixed.reshape(row_count, feat_width).astype(jnp.bfloat16)
    partial_out = jnp.dot(mixed, w_out, preferred_element_type=jnp.float32)
    up_value = jnp.dot(mlp_in, w_up, preferred_element_type=jnp.float32) + b_up
    active = gelu_exact(up_value).astype(jnp.bfloat16)
    partial_out = partial_out + jnp.dot(active, w_down, preferred_element_type=jnp.float32)
    branches = lax.psum(partial_out, "tp")
    layer_out = (hidden + branches + b_branch).astype(jnp.bfloat16)
    stored = (key_flat, value_flat)
    saved = (layer_in, queries, stored, log_total, mixed, up_value, active)
    return (layer_out, saved)


def backward_layer(grad_out, saved, weights, query_pos, cosine, sine):
    gains, w_qkv, b_qkv, w_out, w_up, b_up, w_down, b_branch = weights
    layer_in, queries, stored, log_total, mixed, up_value, active = saved
    grad_full = grad_out.astype(jnp.float32)
    row_count, feat_width = mixed.shape
    head_count = feat_width // HD
    hidden = layer_in.astype(jnp.float32)
    norm_pair, norm_back = jax.vjp(norms, hidden, gains[0], gains[1], gains[2], gains[3])
    attn_in = norm_pair[0].astype(jnp.bfloat16)
    mlp_in = norm_pair[1].astype(jnp.bfloat16)
    active_grad = jnp.einsum("td,fd->tf", grad_out, w_down, preferred_element_type=jnp.float32)
    grad_down = jnp.einsum("tf,td->fd", active, grad_out, preferred_element_type=jnp.float32)
    gelu_back = jax.vjp(gelu_exact, up_value)[1]
    up_grad = gelu_back(active_grad)[0].astype(jnp.bfloat16)
    grad_up_bias = jnp.sum(up_grad.astype(jnp.float32), axis=0)
    grad_up = jnp.einsum("td,tf->df", mlp_in, up_grad, preferred_element_type=jnp.float32)
    mlp_in_grad = jnp.einsum("tf,df->td", up_grad, w_up, preferred_element_type=jnp.float32)
    mixed_grad = jnp.einsum(
        "td,fd->tf", grad_out, w_out, preferred_element_type=jnp.float32
    ).astype(jnp.bfloat16)
    grad_out_weight = jnp.einsum("tf,td->fd", mixed, grad_out, preferred_element_type=jnp.float32)
    all_keys, all_values = (
        lax.all_gather(stored[0], "ctx", axis=0, tiled=True),
        lax.all_gather(stored[1], "ctx", axis=0, tiled=True),
    )
    key_count = all_keys.shape[0]
    keys_heads = all_keys.reshape(key_count, head_count, HD)
    values_heads = all_values.reshape(key_count, head_count, HD)
    score_scale = 1.0 / math.sqrt(HD)
    scores = scores_of(queries, keys_heads, query_pos, score_scale)
    probability = jnp.exp(scores - log_total)
    heads_grad = mixed_grad.reshape(row_count, head_count, HD)
    prob_grad = jnp.einsum(
        "qhd,khd->hqk", heads_grad, values_heads, preferred_element_type=jnp.float32
    )
    centre = jnp.sum(probability * prob_grad, axis=-1, keepdims=True)
    score_grad = (score_scale * probability * (prob_grad - centre)).astype(jnp.bfloat16)
    query_grad = jnp.einsum(
        "hqk,khd->qhd", score_grad, keys_heads, preferred_element_type=jnp.float32
    )
    value_terms = jnp.einsum(
        "hqk,qhd->khd",
        probability.astype(jnp.bfloat16),
        heads_grad,
        preferred_element_type=jnp.float32,
    )
    key_terms = jnp.einsum("hqk,qhd->khd", score_grad, queries, preferred_element_type=jnp.float32)
    key_grad, value_grad = (
        lax.psum_scatter(
            key_terms.reshape(key_count, feat_width), "ctx", scatter_dimension=0, tiled=True
        ),
        lax.psum_scatter(
            value_terms.reshape(key_count, feat_width), "ctx", scatter_dimension=0, tiled=True
        ),
    )
    query_grad = rotate(query_grad, cosine, -sine).reshape(row_count, feat_width)
    key_grad = rotate(key_grad.reshape(row_count, head_count, HD), cosine, -sine).reshape(
        row_count, feat_width
    )
    qkv_grad = jnp.stack([query_grad, key_grad, value_grad], axis=1).astype(jnp.bfloat16)
    grad_qkv_bias = jnp.sum(qkv_grad.astype(jnp.float32), axis=0)
    grad_qkv = jnp.einsum("td,tcf->cdf", attn_in, qkv_grad, preferred_element_type=jnp.float32)
    attn_in_grad = jnp.einsum("tcf,cdf->td", qkv_grad, w_qkv, preferred_element_type=jnp.float32)
    attn_in_grad, mlp_in_grad = lax.psum((attn_in_grad, mlp_in_grad), "tp")
    hidden_grad, gain_one_grad, shift_one_grad, gain_two_grad, shift_two_grad = norm_back(
        (attn_in_grad, mlp_in_grad)
    )
    input_grad = (grad_full + hidden_grad).astype(jnp.bfloat16)
    grad_branch = jnp.sum(grad_full, axis=0)
    grads = (
        gain_one_grad,
        shift_one_grad,
        gain_two_grad,
        shift_two_grad,
        grad_qkv,
        grad_qkv_bias,
        grad_out_weight,
        grad_up,
        grad_up_bias,
        grad_down,
        grad_branch,
    )
    return (input_grad, grads)


def per_device(
    inputs,
    cotangent,
    ln1_gain,
    ln1_bias,
    ln2_gain,
    ln2_bias,
    qkv_weight,
    qkv_bias,
    out_weight,
    up_weight,
    up_bias,
    down_weight,
    branch_bias,
):
    gains = (
        ln1_gain[0].astype(jnp.float32),
        ln1_bias[0].astype(jnp.float32),
        ln2_gain[0].astype(jnp.float32),
        ln2_bias[0].astype(jnp.float32),
    )
    weights = (
        gains,
        qkv_weight[0],
        qkv_bias[0].astype(jnp.float32),
        out_weight[0],
        up_weight[0],
        up_bias[0].astype(jnp.float32),
        down_weight[0],
        branch_bias[0].astype(jnp.float32),
    )
    micro_count = inputs.shape[0]
    row_count = inputs.shape[1]
    query_pos = lax.axis_index("ctx") * row_count + jnp.arange(row_count, dtype=jnp.int32)
    cosine, sine = tables(query_pos)
    at_first = lax.axis_index("section") == 0
    blank = jnp.zeros_like(inputs[0])
    received = blank
    outputs_list = []
    saved_list = []
    for step_index in range(micro_count + 1):
        fresh = inputs[step_index] if step_index < micro_count else blank
        layer_in = jnp.where(at_first, fresh, received)
        layer_out, saved = forward_layer(layer_in, weights, query_pos, cosine, sine)
        outputs_list.append(layer_out)
        saved_list.append(saved)
        if step_index < micro_count:
            received = shifted(layer_out, "section", 1)
    returned = blank
    grad_list = []
    sums = None
    for back_index in range(micro_count + 1):
        batch_index = micro_count - 1 - back_index
        given = cotangent[batch_index] if batch_index >= 0 else blank
        grad_in = jnp.where(at_first, returned, given)
        input_grad, grads = backward_layer(
            grad_in, saved_list[micro_count - back_index], weights, query_pos, cosine, sine
        )
        sums = grads if sums is None else jax.tree.map(jnp.add, sums, grads)
        grad_list.append(input_grad)
        if back_index < micro_count:
            returned = shifted(input_grad, "section", -1)
    acts = jnp.stack(
        [jnp.where(at_first, outputs_list[j], outputs_list[j + 1]) for j in range(micro_count)]
    )[None]
    in_grads = jnp.stack(
        [
            jnp.where(at_first, grad_list[micro_count - j], grad_list[micro_count - 1 - j])
            for j in range(micro_count)
        ]
    )[None]
    (
        gain_one_grad,
        shift_one_grad,
        gain_two_grad,
        shift_two_grad,
        grad_qkv,
        grad_qkv_bias,
        grad_out_weight,
        grad_up,
        grad_up_bias,
        grad_down,
        grad_branch,
    ) = sums
    qkv_part, out_part, up_part, down_part = (
        lax.psum_scatter(
            grad_qkv[None].astype(jnp.bfloat16), "ctx", scatter_dimension=2, tiled=True
        ).astype(jnp.float32),
        lax.psum_scatter(
            grad_out_weight[None].astype(jnp.bfloat16), "ctx", scatter_dimension=2, tiled=True
        ).astype(jnp.float32),
        lax.psum_scatter(
            grad_up[None].astype(jnp.bfloat16), "ctx", scatter_dimension=1, tiled=True
        ).astype(jnp.float32),
        lax.psum_scatter(
            grad_down[None].astype(jnp.bfloat16), "ctx", scatter_dimension=2, tiled=True
        ).astype(jnp.float32),
    )
    small_sums = (
        lax.psum(gain_one_grad[None].astype(jnp.bfloat16), "ctx").astype(jnp.float32),
        lax.psum(shift_one_grad[None].astype(jnp.bfloat16), "ctx").astype(jnp.float32),
        lax.psum(gain_two_grad[None].astype(jnp.bfloat16), "ctx").astype(jnp.float32),
        lax.psum(shift_two_grad[None].astype(jnp.bfloat16), "ctx").astype(jnp.float32),
        lax.psum(grad_qkv_bias[None].astype(jnp.bfloat16), "ctx").astype(jnp.float32),
        lax.psum(grad_up_bias[None].astype(jnp.bfloat16), "ctx").astype(jnp.float32),
        lax.psum(grad_branch[None].astype(jnp.bfloat16), "ctx").astype(jnp.float32),
    )
    return (
        acts,
        in_grads,
        small_sums[0],
        small_sums[1],
        small_sums[2],
        small_sums[3],
        qkv_part,
        small_sums[4],
        out_part,
        up_part,
        small_sums[5],
        down_part,
        small_sums[6],
    )


ALL = ("section", "ctx", "tp")
SECTION, HALF, NEAR, CORE, SIDE = 16, 8, 4, 2, 1
CHIPS = (0, SIDE, NEAR, NEAR | SIDE, SECTION, SECTION | SIDE, SECTION | NEAR, SECTION | NEAR | SIDE)
F32, B16 = jnp.float32, jnp.bfloat16
ONE = 128
S_SECTION, S_HALF, S_NEAR, S_CORE, S_SIDE, S_CHIP, S_OWN, S_GIVE = range(8)


def swapped(array, mask, section=None):
    pairs = [(i, i ^ mask) for i in range(32) if section is None or i // 16 == section]
    return lax.ppermute(array, ALL, pairs)


def after(array, *earlier):
    return lax.optimization_barrier((array,) + earlier)[0]


def where_am_i():
    section = lax.axis_index("section")
    ctx = lax.axis_index("ctx")
    side = lax.axis_index("tp")
    half, near, core = ctx // 4, (ctx // 2) % 2, ctx % 2
    chip = 4 * section + 2 * near + side
    own, give = 2 * section + near, 2 * (1 - section) + near
    return jnp.stack([section, half, near, core, side, chip, own, give]).astype(jnp.int32)


def in_hbm(arrays):
    return [pltpu.with_memory_space_constraint(a, pltpu.HBM) for a in arrays]


def kernel_call(body, outs, at, *arrays, hbm=(), scratch=(), flops=0, exps=0, name=None, keep=True):
    moved = sum(a.size * a.dtype.itemsize for a in arrays)
    moved += sum(math.prod(s) * jnp.dtype(d).itemsize for s, d in outs)
    return pl.pallas_call(
        body,
        name=name,
        out_shape=[(pltpu.VMEM if keep else jax.ShapeDtypeStruct)(s, d) for s, d in outs],
        in_specs=[pl.BlockSpec(memory_space=pltpu.SMEM)]
        + [pl.BlockSpec(memory_space=pltpu.VMEM)] * len(arrays)
        + [pl.BlockSpec(memory_space=pltpu.HBM)] * len(hbm),
        out_specs=[pl.BlockSpec(memory_space=pltpu.VMEM)] * len(outs),
        scratch_shapes=list(scratch),
        compiler_params=pltpu.CompilerParams(vmem_limit_bytes=VMEM_BYTES),
        cost_estimate=pl.CostEstimate(flops=0, bytes_accessed=0, transcendentals=0),
    )(at, *arrays, *in_hbm(hbm))


VMEM_BYTES = 12 * 1024 * 1024


def kernel_call_named(name, *args, **kwargs):
    return kernel_call(*args, name=name, **kwargs)


def by_rows(rows, step, do):
    def one(i, _):
        do(pl.ds(pl.multiple_of(i * step, step), step))
        return 0

    lax.fori_loop(0, rows // step, one, 0)


def nn(a, b):
    return jnp.dot(a, b, preferred_element_type=F32)


def nt(a, b):
    return lax.dot_general(a, b, (((1,), (1,)), ((), ())), preferred_element_type=F32)


def tn(a, b):
    return lax.dot_general(a, b, (((0,), (0,)), ((), ())), preferred_element_type=F32)


def copy_kernel(name, body, outs, at, arrays, scratch):
    return pl.pallas_call(
        body,
        name=name,
        out_shape=[jax.ShapeDtypeStruct(s, B16) for s in outs],
        in_specs=[pl.BlockSpec(memory_space=pltpu.SMEM)]
        + [pl.BlockSpec(memory_space=pltpu.HBM)] * len(arrays),
        out_specs=[pl.BlockSpec(memory_space=pltpu.HBM)] * len(outs),
        scratch_shapes=list(scratch),
        compiler_params=pltpu.CompilerParams(vmem_limit_bytes=VMEM_BYTES),
        cost_estimate=pl.CostEstimate(flops=0, bytes_accessed=0, transcendentals=0),
    )(at, *in_hbm(arrays))


def token_copies(at, array, mine, strip, sems):
    width = strip.shape[1]
    lanes = pl.ds(pl.multiple_of(at[S_SIDE] * width, width), width)
    return [
        pltpu.make_async_copy(array.at[at[S_HALF]], mine, sems.at[0]),
        pltpu.make_async_copy(array.at[1 - at[S_HALF], :, lanes], strip, sems.at[1]),
    ]


def token_shapes(array):
    _, rows, dim = array.shape
    return [(rows, dim), (rows, dim // 2)]


def send_tokens(mine, strip):
    near = swapped(mine, NEAR)
    far = swapped(strip, HALF)
    far_near = swapped(strip, HALF | NEAR)
    return mine, near, far, far_near, swapped(far, SIDE), swapped(far_near, SIDE)


def start_loader(at, refs):
    mine, near, far, far_near, far_rest, far_near_rest = refs
    first = at[S_SIDE] == 0
    index = 2 * at[S_HALF] + at[S_NEAR]

    def whole(strip, rest):
        a, b = strip[...], rest[...]
        return jnp.concatenate([jnp.where(first, a, b), jnp.where(first, b, a)], axis=1)

    yield index, mine[...]
    yield index ^ 1, near[...]
    yield index ^ 2, whole(far, far_rest)
    yield index ^ 3, whole(far_near, far_near_rest)


def piece_loader(at, refs):
    for step, ref in zip(STEPS, refs):
        for i in range(2):
            yield at[S_CHIP] ^ (step | 2 * i), ref[i]


def run_copies(copies):
    for copy in copies:
        copy.start()
    for copy in copies:
        copy.wait()


def pack_first(at, tokens, vectors, w_qkv):
    _, three, dim, wide = w_qkv.shape
    heads, side = wide // 4, dim // 2
    count = len(vectors)

    def body(at, tokens, w_qkv, *refs):
        lines = refs[:count]
        mine, strip, packed, table, rounded, sems = refs[count : count + 6]
        held = refs[count + 6 :]
        rows = pl.ds(pl.multiple_of(at[S_CORE] * side, side), side)
        lanes = pl.ds(pl.multiple_of(at[S_GIVE] * heads, heads), heads)
        copies = token_copies(at, tokens, mine, strip, sems)
        for i in range(three):
            copies.append(
                pltpu.make_async_copy(
                    w_qkv.at[0, i, rows, lanes], packed.at[i * side : (i + 1) * side], sems.at[2 + i]
                )
            )
        loads = [
            pltpu.make_async_copy(line, hold, sems.at[6 + i])
            for i, (line, hold) in enumerate(zip(lines, held))
        ]
        for copy in copies:
            copy.start()
        run_copies(loads)
        fill_table(table, at[S_GIVE], held)
        rounded[...] = table[...].astype(B16)
        run_copies([pltpu.make_async_copy(rounded, packed.at[three * side :], sems.at[5])])
        for copy in copies:
            copy.wait()

    return copy_kernel(
        "pack_first", body, token_shapes(tokens) + [(three * side + TABLE, ONE)], at,
        [tokens, w_qkv, *vectors],
        [pltpu.VMEM((TABLE, ONE), F32), pltpu.VMEM((TABLE, ONE), B16), pltpu.SemaphoreType.DMA((6 + count,))]
        + [pltpu.VMEM(v.shape, B16) for v in vectors],
    )


def pack_second(at, tokens, w_up, w_out, w_down):
    dim, units, heads = w_up.shape[1], w_up.shape[2] // 4, w_out.shape[1] // 4
    side = dim // 2

    def body(at, tokens, w_up, w_out, w_down, mine, strip, up, down, sems):
        copies = token_copies(at, tokens, mine, strip, sems)
        rows = pl.ds(pl.multiple_of(at[S_CORE] * side, side), side)
        lanes = pl.ds(pl.multiple_of(at[S_GIVE] * units, units), units)
        copies.append(pltpu.make_async_copy(w_up.at[0, rows, lanes], up, sems.at[2]))
        part = 2 * at[S_GIVE] + at[S_CORE]
        for i, (source, size, start) in enumerate(
            ((w_down, units // 2, 0), (w_out, heads // 2, units // 2))
        ):
            rows = pl.ds(pl.multiple_of(part * size, size), size)
            copies.append(
                pltpu.make_async_copy(
                    source.at[0, rows], down.at[start : start + size], sems.at[3 + i]
                )
            )
        run_copies(copies)

    return copy_kernel(
        "pack_second", body, token_shapes(tokens) + [(side, units), ((units + heads) // 2, dim)], at,
        [tokens, w_up, w_out, w_down], [pltpu.SemaphoreType.DMA((5,))],
    )


def fill_table(table, index, vectors):
    *lines, b_up, b_qkv = vectors
    units, heads = b_up.shape[1] // 4, b_qkv.shape[2] // 4
    table[...] = jnp.zeros_like(table)
    row = 0
    for line in lines:
        for i in range(line.shape[1] // ONE):
            table[row : row + 1] = line[:, i * ONE : (i + 1) * ONE].astype(F32)
            row += 1
    for i in range(units // ONE):
        lanes = pl.ds(pl.multiple_of(index * units + i * ONE, ONE), ONE)
        table[row : row + 1] = b_up[:, lanes].astype(F32)
        row += 1
    few = b_qkv[0, :, pl.ds(pl.multiple_of(index * heads, ONE), heads)].astype(F32)
    table[row : row + few.shape[0]] = few


TABLE = 48


def vector_rows(at, vectors, got):
    dim = vectors[0].shape[1]
    units, few = vectors[5].shape[1] // 4, vectors[6].shape[1]

    def body(at, *refs):
        *lines, got, rows0, rows1, table = refs
        fill_table(table, at[S_OWN], lines)
        taken = got[got.shape[0] - TABLE :].astype(F32)
        is_first = at[S_SECTION] == 0
        for rows, lines in (
            (rows0, jnp.where(is_first, table[...], taken)),
            (rows1, jnp.where(is_first, taken, table[...])),
        ):
            rows[...] = jnp.zeros_like(rows)
            line = 0
            for r, tiles in enumerate([dim // ONE] * 5 + [units // ONE, few]):
                for i in range(tiles):
                    rows[r : r + 1, i * ONE : (i + 1) * ONE] = lines[line : line + 1]
                    line += 1

    return kernel_call_named(
        "vector_rows", body, [((8, dim), F32)] * 2, at, *vectors, got,
        scratch=[pltpu.VMEM((TABLE, ONE), F32)],
    )


def half_rows(at, which, size):
    return pl.ds(pl.multiple_of((at[S_CORE] ^ which) * size, size), size)


def qkv_copies(at, own, got, rest, target):
    three, heads = own.shape[1], own.shape[3] // 4
    side = own.shape[2] // 2
    lanes = pl.ds(pl.multiple_of(at[S_OWN] * heads, heads), heads)
    mine, halves = [], []
    for i in range(three):
        tile = slice(i * heads, (i + 1) * heads)
        mine.append((own.at[0, i, :, lanes], target[0].at[:, tile]))
        for which, source in ((0, got), (1, rest)):
            halves.append(
                (
                    source.at[i * side : (i + 1) * side],
                    target[1].at[half_rows(at, which, side), tile],
                )
            )
    return mine + halves


def up_copies(at, own, got, rest, target):
    side, units = got.shape
    lanes = pl.ds(pl.multiple_of(at[S_OWN] * units, units), units)
    return [(own.at[0, :, lanes], target[0])] + [
        (source, target[1].at[half_rows(at, which, side)])
        for which, source in ((0, got), (1, rest))
    ]


def row_copies(at, own, got, rest, target, start):
    size = target[0].shape[0]
    side = size // 2
    rows = pl.ds(pl.multiple_of(at[S_OWN] * size, size), size)
    return [(own.at[0, rows], target[0])] + [
        (source.at[start : start + side], target[1].at[half_rows(at, which, side)])
        for which, source in ((0, got), (1, rest))
    ]


def choose_weights(name, at, owns, got, rest, shapes, make):
    count = len(owns)

    def body(at, *refs):
        own, (got, rest), targets, sems = refs[:count], refs[count : count + 2], refs[count + 2 : -1], refs[-1]
        for section in range(2):

            @pl.when(at[S_SECTION] == section)
            def _():
                pairs = make(
                    at, own, got, rest,
                    [(targets[2 * i + section], targets[2 * i + 1 - section]) for i in range(count)],
                )
                run_copies(
                    [
                        pltpu.make_async_copy(source, target, sems.at[i])
                        for i, (source, target) in enumerate(pairs)
                    ]
                )

    outs = [(shape, B16) for shape in shapes for _ in range(2)]
    return kernel_call(
        body, outs, at, hbm=[*owns, got, rest],
        scratch=[pltpu.SemaphoreType.DMA((9,))], name=name,
    )


def weights_call(name, body, outs, at, arrays, weights, scratch=(), flops=0, exps=0):
    first, count = len(arrays), len(weights)

    def wrapped(at, *refs):
        given, chosen, rest = refs[:first], refs[first : first + count], refs[first + count :]
        made, own = rest[: len(outs)], rest[len(outs) :]
        body(at, *given, *made, *chosen, *own)

    return kernel_call(
        wrapped, outs, at, *arrays, *weights, scratch=scratch, flops=flops, exps=exps, name=name
    )


def first_weights(at, vectors, w_qkv, sent):
    _, three, dim, wide = w_qkv.shape
    got = swapped(sent, SECTION)
    qkv = choose_weights(
        "choose_qkv", at, [w_qkv], got, swapped(got, CORE), [(dim, three * (wide // 4))],
        lambda at, own, got, rest, to: qkv_copies(at, own[0], got, rest, to[0]),
    )
    return got, [dict(qkv=q, rows=r) for q, r in zip(qkv, vector_rows(at, vectors, got))]


def up_weights(at, w_up, got, rest):
    return choose_weights(
        "choose_up", at, [w_up], got, rest, [(w_up.shape[1], w_up.shape[2] // 4)],
        lambda at, own, got, rest, to: up_copies(at, own[0], got, rest, to[0]),
    )


def row_weights(at, w_down, w_out, got, rest):
    _, tall, dim = w_down.shape
    units, heads = tall // 4, w_out.shape[1] // 4
    return choose_weights(
        "choose_rows", at, [w_down, w_out], got, rest, [(units, dim), (heads, dim)],
        lambda at, own, got, rest, to: row_copies(at, own[0], got, rest, to[0], 0)
        + row_copies(at, own[1], got, rest, to[1], units // 2),
    )


def turn_tables(at, rows):
    half_rot = ROT // 2
    place = lax.broadcasted_iota(jnp.int32, (rows, ONE), 0)
    lane = lax.broadcasted_iota(jnp.int32, (rows, ONE), 1) % HD
    positions = (2 * (place // ONE) + at[S_CORE]) * ONE + place % ONE
    freqs = 1.0 / 10000.0 ** ((2 * (lane % half_rot)).astype(F32) / ROT)
    angles = positions.astype(F32) * freqs
    sine = jnp.sin(angles)
    return (
        jnp.where(lane < ROT, jnp.cos(angles), 1.0),
        jnp.where((lane >= half_rot) & (lane < ROT), sine, 0.0),
        jnp.where(lane < half_rot, -sine, 0.0),
    )


def keep_blocks(at, source, blocks):
    mine, give = blocks
    place = (2 * at[S_HALF] + at[S_NEAR]) * ONE
    mine[...] = source[pl.ds(pl.multiple_of(place, ONE), ONE)]
    size = give.shape[0]
    place = (2 * (1 - at[S_HALF]) + at[S_NEAR]) * ONE + at[S_SIDE] * size
    give[...] = source[pl.ds(pl.multiple_of(place, size), size)]


def keep_piece(at, source, piece):
    size = piece.shape[0]
    piece[...] = source[pl.ds(pl.multiple_of(at[S_CHIP] * size, size), size)]


def front(at, loader, sources, w, turns, with_piece):
    dim = w["qkv"].shape[0]
    rows = turns[0].shape[0]
    count = len(sources)

    def body(at, *refs):
        given = refs[:count]
        vectors, *turns = refs[count : count + 4]
        attn_in, mlp_in, normed_out, q, kv = refs[count + 4 : count + 9]
        *kept, qkv, ordered = refs[count + 9 :]
        gains = [vectors[i : i + 1] for i in range(4)]
        for place, block in loader(at, given):
            size = block.shape[0]
            ordered[pl.ds(pl.multiple_of(place * size, size), size)] = block
        if with_piece:
            keep_piece(at, ordered, kept[0])
        else:
            keep_blocks(at, ordered, kept)
        bias = vectors[6:7, : 3 * ONE]

        def norm(span):
            hidden = ordered[span].astype(F32)
            mean = jnp.sum(hidden, axis=1, keepdims=True) * (1.0 / dim)
            centre = hidden - mean
            var = jnp.sum(centre * centre, axis=1, keepdims=True) * (1.0 / dim)
            normed = centre * lax.rsqrt(var + 1e-05)
            attn_in[span] = (normed * gains[0] + gains[1]).astype(B16)
            mlp_in[span] = (normed * gains[2] + gains[3]).astype(B16)
            normed_out[span] = normed.astype(B16)

        def project(span):
            projected = nn(attn_in[span], qkv[...]) + bias
            cosine, second, first_half = [table[span] for table in turns]
            for i, target in ((0, q), (1, kv.at[0])):
                flat = projected[:, i * ONE : (i + 1) * ONE]
                flat = (
                    flat * cosine
                    + pltpu.roll(flat, ROT // 2, 1) * second
                    + pltpu.roll(flat, ONE - ROT // 2, 1) * first_half
                )
                target[span] = flat.astype(B16)
            kv[1, span] = projected[:, 2 * ONE :].astype(B16)

        by_rows(rows, 128, norm)
        by_rows(rows, 256, project)

    outs = [((rows, dim), B16)] * 3 + [((rows, ONE), B16), ((2, rows, ONE), B16)]
    outs += [((rows // 8, dim), B16)] if with_piece else [((n, dim), B16) for n in (ONE, ONE // 2)]
    return weights_call(
        "front", body, outs, at, [*sources, w["rows"], *turns], [w["qkv"]],
        scratch=[pltpu.VMEM((rows, dim), B16)],
        flops=2 * rows * dim * 3 * ONE + 20 * rows * dim,
    )


def units_forward(at, mlp_in, w):
    rows, dim = mlp_in.shape
    units = w["units"]

    def body(at, mlp_in, vectors, active, slope, up):
        bias = vectors[5:6, :units]

        def gelu(span):
            value = nn(mlp_in[span], up[...]) + bias
            cdf = 0.5 + 0.5 * lax.erf(value * (1.0 / math.sqrt(2.0)))
            pdf = jnp.exp(value * value * -0.5) * (1.0 / math.sqrt(2.0 * math.pi))
            active[span] = (value * cdf).astype(B16)
            slope[span] = (cdf + value * pdf).astype(B16)

        by_rows(rows, 128, gelu)

    return weights_call(
        "units_forward", body, [((rows, units), B16)] * 2, at, [mlp_in, w["rows"]], [w["up"]],
        flops=2 * rows * dim * units + 40 * rows * units, exps=rows * units,
    )


def head_lanes():
    return lax.broadcasted_iota(jnp.int32, (1, ONE), 1) < HD


def allowed_keys(at, first, step, count):
    row = lax.broadcasted_iota(jnp.int32, (step, count), 0) + first
    column = lax.broadcasted_iota(jnp.int32, (step, count), 1)
    return column <= row, column < (row // ONE + at[S_CORE]) * ONE


STEPS = (0, 1, 4, 5)
STEP_CHIPS = (0, SIDE, SECTION, SECTION | SIDE)


def pieces_out(at, total, pieces):
    size = total.shape[0] // 8
    for step, piece in zip(STEPS, pieces):
        for i in range(2):
            place = (at[S_CHIP] ^ (step | 2 * i)) * size
            piece[i] = total[pl.ds(pl.multiple_of(place, size), size)].astype(piece.dtype)


def piece_shapes(rows, dim):
    return [((2, rows // 8, dim), F32)] + [((2, rows // 8, dim), B16)] * 3


def fold(at, pieces):
    _, rows, dim = pieces[0].shape

    def body(at, *refs):
        *given, keep, give = refs
        for i, target in ((0, keep), (1, give)):
            total = given[0][i]
            for piece in given[1:]:
                total = total + piece[i].astype(F32)
            target[...] = total.astype(target.dtype)

    return kernel_call_named("fold", body, [((rows, dim), F32), ((rows, dim), B16)], at, *pieces)


def exchanged(pieces):
    return [pieces[0]] + [swapped(p, m) for p, m in zip(pieces[1:], STEP_CHIPS[1:])]


def gathered(piece, near):
    pair = jnp.stack([piece, near])
    return [pair] + [swapped(pair, mask) for mask in STEP_CHIPS[1:]]


def attention_forward(at, q, kv, kv_other, active, w):
    rows = q.shape[0]
    units, dim = w["down"].shape
    scale = 1.0 / math.sqrt(HD)

    def body(at, q, kv, kv_other, active, mixed, lse, *rest):
        pieces, (out, down, total) = rest[:4], rest[4:]
        first_head = head_lanes()
        step = 256
        for first in range(0, rows, step):
            span = slice(first, first + step)
            count = first + step
            queries = q[span]
            masks = allowed_keys(at, first, step, count)
            results, totals = [], []
            for head in range(2):
                lanes = first_head if head == 0 else jnp.logical_not(first_head)
                one = jnp.where(lanes, queries, jnp.zeros_like(queries))
                scores = [
                    jnp.where(mask, nt(one, keys[0, :count]) * scale, -1e9)
                    for mask, keys in zip(masks, (kv, kv_other))
                ]
                most = jnp.maximum(
                    jnp.max(scores[0], axis=1, keepdims=True),
                    jnp.max(scores[1], axis=1, keepdims=True),
                )
                exponents = [jnp.exp(s - most) for s in scores]
                summed = jnp.sum(exponents[0], axis=1, keepdims=True) + jnp.sum(
                    exponents[1], axis=1, keepdims=True
                )
                inverse = 1.0 / summed
                results.append(
                    nn((exponents[0] * inverse).astype(B16), kv[1, :count])
                    + nn((exponents[1] * inverse).astype(B16), kv_other[1, :count])
                )
                totals.append(most + jnp.log(summed))
            mixed[span] = jnp.where(first_head, results[0], results[1]).astype(B16)
            lse[span] = jnp.where(first_head, totals[0], totals[1])
            total[span] = nn(mixed[span], out[...]) + nn(active[span], down[...])
        pieces_out(at, total, pieces)

    outs = [((rows, ONE), B16), ((rows, ONE), F32)] + piece_shapes(rows, dim)
    return weights_call(
        "attention_forward", body, outs, at, [q, kv, kv_other, active], [w["out"], w["down"]],
        scratch=[pltpu.VMEM((rows, dim), F32)],
        flops=2 * rows * dim * (units + ONE) + 8 * rows * rows * ONE * 2,
        exps=2 * rows * rows * 2,
    )


def units_backward(at, loader, sources, slope, w, with_piece):
    rows, units = slope.shape
    dim = w["up"].shape[0]
    count = len(sources)

    def body(at, *refs):
        given = refs[:count]
        slope, g, up_grad, mixed_grad = refs[count : count + 4]
        *kept, down, out = refs[count + 4 :]
        for place, block in loader(at, given):
            size = block.shape[0]
            g[pl.ds(pl.multiple_of(place * size, size), size)] = block
        if with_piece:
            keep_piece(at, g, kept[0])
        else:
            keep_blocks(at, g, kept)

        def back(span):
            up_grad[span] = (nt(g[span], down[...]) * slope[span].astype(F32)).astype(B16)
            mixed_grad[span] = nt(g[span], out[...]).astype(B16)

        by_rows(rows, 256, back)

    outs = [((rows, dim), B16), ((rows, units), B16), ((rows, ONE), B16)]
    outs += [((rows // 8, dim), B16)] if with_piece else [((n, dim), B16) for n in (ONE, ONE // 2)]
    return weights_call(
        "units_backward", body, outs, at, [*sources, slope], [w["down"], w["out"]],
        flops=2 * rows * dim * (units + ONE),
    )


def attention_backward(at, q, kv, kv_other, lse, mixed_grad):
    rows = q.shape[0]
    scale = 1.0 / math.sqrt(HD)

    def body(at, q, kv, kv_other, lse, mixed_grad, dq, dkv, dkv_other):
        first_head = head_lanes()
        step = 256
        dkv[...] = jnp.zeros_like(dkv)
        dkv_other[...] = jnp.zeros_like(dkv_other)
        for first in range(0, rows, step):
            span = slice(first, first + step)
            count = first + step
            queries, back = q[span], mixed_grad[span]
            masks = allowed_keys(at, first, step, count)
            sides = ((masks[0], kv, dkv), (masks[1], kv_other, dkv_other))
            results = []
            for head in range(2):
                lanes = first_head if head == 0 else jnp.logical_not(first_head)
                one = jnp.where(lanes, queries, jnp.zeros_like(queries))
                one_back = jnp.where(lanes, back, jnp.zeros_like(back))
                level = lse[span, head * HD : head * HD + 1]
                probs, grads = [], []
                for mask, keys, _ in sides:
                    scores = nt(one, keys[0, :count]) * scale
                    probs.append(jnp.exp(jnp.where(mask, scores, -1e9) - level))
                    grads.append(nt(one_back, keys[1, :count]))
                delta = jnp.sum(probs[0] * grads[0], axis=1, keepdims=True) + jnp.sum(
                    probs[1] * grads[1], axis=1, keepdims=True
                )
                result = 0.0
                for (_, keys, target), prob, grad in zip(sides, probs, grads):
                    score_grad = (prob * (grad - delta) * scale).astype(B16)
                    result = result + nn(score_grad, keys[0, :count])
                    target[0, :count] += tn(score_grad, one)
                    target[1, :count] += tn(prob.astype(B16), one_back)
                results.append(result)
            dq[span] = jnp.where(first_head, results[0], results[1])

    return kernel_call_named(
        "attention_backward",
        body, [((rows, ONE), F32), ((2, rows, ONE), F32), ((2, rows, ONE), F32)],
        at, q, kv, kv_other, lse, mixed_grad,
        flops=20 * rows * rows * ONE * 2, exps=2 * rows * rows * 2,
    )


def inputs_backward(at, dq, dkv, dkv_got, up_grad, normed, g, turns, w):
    rows, dim = normed.shape
    units = up_grad.shape[1]

    def body(at, dq, dkv, dkv_got, up_grad, normed, g, *rest):
        turns, vectors, rest = rest[:3], rest[3], rest[4:]
        qkv_grad, table = rest[:2]
        pieces, (qkv, up, total, lines) = rest[2:6], rest[6:]
        gain_one, gain_two = vectors[0:1], vectors[2:3]
        step = 128

        def one(i, sums):
            span = pl.ds(pl.multiple_of(i * step, step), step)
            cosine, second, first_half = [table[span] for table in turns]
            parts = []
            for flat in (dq[span], dkv[0, span] + dkv_got[0, span]):
                parts.append(
                    flat * cosine
                    - pltpu.roll(flat, ROT // 2, 1) * second
                    - pltpu.roll(flat, ONE - ROT // 2, 1) * first_half
                )
            parts.append(dkv[1, span] + dkv_got[1, span])
            both = jnp.concatenate([p.astype(B16) for p in parts], axis=1)
            qkv_grad[span] = both
            attn = nt(both, qkv[...])
            mlp = nt(up_grad[span], up[...])
            total[span] = attn * gain_one + mlp * gain_two
            unit = normed[span].astype(F32)
            new = [
                jnp.sum(v, axis=0, keepdims=True)
                for v in (
                    attn * unit, attn, mlp * unit, mlp, g[span].astype(F32),
                    up_grad[span].astype(F32), both.astype(F32),
                )
            ]
            return tuple(a + b for a, b in zip(sums, new))

        widths = (dim,) * 5 + (units, 3 * ONE)
        sums = lax.fori_loop(
            0, rows // step, one, tuple(jnp.zeros((1, width), F32) for width in widths)
        )
        pieces_out(at, total, pieces)
        lines[...] = jnp.zeros_like(lines)
        line = 0
        for value in sums:
            for i in range(value.shape[1] // ONE):
                lines[line : line + 1] = value[:, i * ONE : (i + 1) * ONE]
                line += 1
        table[...] = lines[...].astype(B16)

    outs = [((rows, 3 * ONE), B16), ((LINES, ONE), B16)] + piece_shapes(rows, dim)
    return weights_call(
        "inputs_backward", body, outs, at,
        [dq, dkv, dkv_got, up_grad, normed, g, *turns, w["rows"]], [w["qkv"], w["up"]],
        scratch=[pltpu.VMEM((rows, dim), F32), pltpu.VMEM((LINES, ONE), F32)],
        flops=2 * rows * dim * (units + 3 * ONE) + 12 * rows * dim,
    )


LINES = 64


def join_forward(at, x_piece, parts, w):
    def body(at, x, vectors, own, *rest):
        total = x[...].astype(F32) + own[...].astype(F32) + vectors[4:5]
        for piece in rest[:-1]:
            total = total + piece[...].astype(F32)
        rest[-1][...] = total.astype(B16)

    return kernel_call_named("join_forward", body, [(x_piece.shape, B16)], at, x_piece, w["rows"], *parts)[0]


def join_backward(at, g_piece, x_piece, parts):
    dim = x_piece.shape[1]

    def body(at, g, x, own, *rest):
        total = own[...]
        for piece in rest[:-1]:
            total = total + piece[...].astype(F32)
        hidden = x[...].astype(F32)
        centre = hidden - jnp.sum(hidden, axis=1, keepdims=True) * (1.0 / dim)
        var = jnp.sum(centre * centre, axis=1, keepdims=True) * (1.0 / dim)
        scale = lax.rsqrt(var + 1e-05)
        normed = centre * scale
        inner = (
            total
            - jnp.sum(total, axis=1, keepdims=True) * (1.0 / dim)
            - normed * (jnp.sum(total * normed, axis=1, keepdims=True) * (1.0 / dim))
        )
        rest[-1][...] = (g[...].astype(F32) + scale * inner).astype(B16)

    return kernel_call_named("join_backward", body, [(x_piece.shape, B16)], at, g_piece, x_piece, *parts)[0]


def columns(at, ref, core, high):
    which = at[S_CORE] ^ core
    return jnp.concatenate(
        [
            ref[:, pl.ds(pl.multiple_of((4 * high + 2 * low + which) * ONE, ONE), ONE)]
            for low in range(2)
        ],
        axis=1,
    )


def early_grads(at, active, mixed, mlp_in, up_grad, g):
    rows, dim = g.shape
    units = active.shape[1]
    tiles = units // ONE

    def body(at, active, mixed, mlp_in, up_grad, g, keep, give):
        for core, target in ((0, keep), (1, give)):
            for high in range(2):
                strip = columns(at, g, core, high)
                down = tn(active[...], strip).astype(B16)
                out = tn(mixed[...], strip).astype(B16)
                up = tn(columns(at, mlp_in, core, high), up_grad[...]).astype(B16)
                for low in range(2):
                    lanes = slice(low * ONE, (low + 1) * ONE)
                    where = (at[S_HALF] ^ high, at[S_NEAR] ^ low)
                    target[where[0], where[1], :units] = down[:, lanes]
                    target[where[0], where[1], units : units + ONE] = out[:, lanes]
                    for i in range(tiles):
                        base = units + (1 + i) * ONE
                        target[where[0], where[1], base : base + ONE] = up[
                            lanes, i * ONE : (i + 1) * ONE
                        ]

    shape = (2, 2, 2 * units + ONE, ONE)
    return kernel_call_named(
        "early_grads",
        body, [(shape, B16)] * 2, at, active, mixed, mlp_in, up_grad, g,
        flops=2 * rows * dim * (2 * units + ONE),
    )


def late_grads(at, attn_in, qkv_grad, table, table_side):
    rows, dim = attn_in.shape

    def body(at, attn_in, qkv_grad, table, table_side, keep, give):
        lines = lax.broadcasted_iota(jnp.int32, table.shape, 0) < 4 * dim // ONE
        other = jnp.where(lines, table_side[...].astype(F32), 0.0)
        joined = (table[...].astype(F32) + other).astype(B16)
        for core, target in ((0, keep), (1, give)):
            for high in range(2):
                qkv = tn(columns(at, attn_in, core, high), qkv_grad[...]).astype(B16)
                for low in range(2):
                    where = (at[S_HALF] ^ high, at[S_NEAR] ^ low)
                    for i in range(3):
                        target[where[0], where[1], i * ONE : (i + 1) * ONE] = qkv[
                            low * ONE : (low + 1) * ONE, i * ONE : (i + 1) * ONE
                        ]
                    target[where[0], where[1], 3 * ONE :] = joined

    shape = (2, 2, 3 * ONE + LINES, ONE)
    return kernel_call_named(
        "late_grads",
        body, [(shape, B16)] * 2, at, attn_in, qkv_grad, table, table_side,
        flops=2 * rows * dim * 3 * ONE,
    )


def plus(a, b):
    return (a.astype(F32) + b.astype(F32)).astype(B16)


def summed_cores(keep, give):
    got = swapped(give, CORE)
    return (
        [plus(keep[0, i], got[0, i]) for i in range(2)],
        [plus(keep[1, i], got[1, i]) for i in range(2)],
    )


def unpack_grads(at, early, late, sizes):
    dim_part, units, heads = ONE, sizes["units"], ONE

    def body(at, *refs):
        early, late = refs[:4], refs[4:8]
        qkv, out, up, down, lines, b_qkv, b_up, branch = refs[8:]
        index = at[S_OWN]
        total = 0.0
        for j, (wide, narrow) in enumerate(zip(early, late)):
            source = index ^ (2 * (j % 2) + j // 2)
            place = pl.multiple_of(source * units, units)
            small = pl.multiple_of(source * ONE, ONE)
            down[pl.ds(place, units)] = wide[:units].astype(F32)
            out[pl.ds(small, ONE)] = wide[units : units + ONE].astype(F32)
            for i in range(units // ONE):
                base = units + (1 + i) * ONE
                up[:, pl.ds(place + i * ONE, ONE)] = wide[base : base + ONE].astype(F32)
            for i in range(3):
                qkv[i, :, pl.ds(small, ONE)] = narrow[i * ONE : (i + 1) * ONE].astype(F32)
            table = narrow[3 * ONE :].astype(F32)
            total = total + table[:32]
            for i in range(units // ONE):
                b_up[:, pl.ds(place + i * ONE, ONE)] = table[40 + i : 41 + i]
            for i in range(3):
                b_qkv[i : i + 1, pl.ds(small, ONE)] = table[40 + units // ONE + i :][:1]
            if j == 0:
                branch[...] = table[32:40]
        lines[...] = total

    outs = [
        ((3, dim_part, 4 * heads), F32),
        ((4 * heads, dim_part), F32),
        ((dim_part, 4 * units), F32),
        ((4 * units, dim_part), F32),
        ((32, ONE), F32),
        ((3, 4 * heads), F32),
        ((1, 4 * units), F32),
        ((8, ONE), F32),
    ]
    return kernel_call_named("unpack_grads", body, outs, at, *early, *late, keep=False)


def cube_device(
    inputs, cotangent, ln1_gain, ln1_bias, ln2_gain, ln2_bias, qkv_weight, qkv_bias,
    out_weight, up_weight, up_bias, down_weight, branch_bias,
):
    at = where_am_i()
    section, half, side = [lax.axis_index("section"), lax.axis_index("ctx") // 4, lax.axis_index("tp")]
    at, is_first, is_low, is_left, is_near = lax.optimization_barrier(
        (at, section == 0, half == 0, side == 0, section == half)
    )
    dim = inputs.shape[2]
    rows = 4 * inputs.shape[1]
    vectors = (ln1_gain, ln1_bias, ln2_gain, ln2_bias, branch_bias, up_bias, qkv_bias)

    mine, strip, sent_qkv = pack_first(at, inputs, vectors, qkv_weight)
    g_mine, g_strip, sent_up, sent_down = pack_second(
        at, cotangent, up_weight, out_weight, down_weight
    )
    x_parts = send_tokens(mine, strip)
    got_qkv, layers = first_weights(at, vectors, qkv_weight, sent_qkv)
    got_up = swapped(after(sent_up, got_qkv, x_parts[1]), SECTION)
    got_down = swapped(after(sent_down, got_up, *x_parts[4:]), SECTION)
    g_parts = send_tokens(after(g_mine, *x_parts[4:]), after(g_strip, *x_parts[4:]))
    first, second = layers
    turns = turn_tables(at, rows)

    def bring_rest(q):
        up = up_weights(at, up_weight, got_up, swapped(after(got_up, q), CORE))
        tall = row_weights(
            at, down_weight, out_weight, got_down,
            swapped(after(got_down, q, up[0], *g_parts[1:4]), CORE),
        )
        for i, layer in enumerate(layers):
            layer.update(up=up[i], down=tall[i], out=tall[2 + i], units=up[i].shape[1])

    def forward(loader, sources, w, with_piece):
        got = front(at, loader, sources, w, turns, with_piece)
        attn_in, mlp_in, normed, q, kv = got[:5]
        kv_other = swapped(kv, CORE)
        if "up" not in w:
            bring_rest(q)
        active, slope = units_forward(at, mlp_in, w)
        made = attention_forward(at, q, kv, kv_other, active, w)
        mixed, lse, pieces = made[0], made[1], made[2:]
        saved = dict(
            attn_in=attn_in, mlp_in=mlp_in, normed=normed, q=q, kv=kv, kv_other=kv_other,
            active=active, slope=slope, mixed=mixed, lse=lse,
        )
        return pieces, saved, got[5:]

    def backward(loader, sources, saved, w, with_piece, earlier=()):
        made = units_backward(at, loader, sources, saved["slope"], w, with_piece)
        g, up_grad, mixed_grad = made[:3]
        early = early_grads(at, saved["active"], saved["mixed"], saved["mlp_in"], up_grad, g)
        dq, dkv, dkv_other = attention_backward(
            at, saved["q"], saved["kv"], saved["kv_other"], saved["lse"],
            after(mixed_grad, early[0], *earlier),
        )
        dkv_got = swapped(dkv_other, CORE)
        return early, (dq, dkv, dkv_got, up_grad, saved["normed"], g), made[3:]

    def backward_end(given, saved, w):
        out = inputs_backward(at, *given, turns, w)
        qkv_grad, table, pieces = out[0], out[1], out[2:]
        late = late_grads(at, saved["attn_in"], qkv_grad, table, swapped(table, SIDE))
        return exchanged(pieces), late

    parts, saved_first, (x_piece,) = forward(start_loader, x_parts, first, True)
    keep, give = fold(at, exchanged(parts))
    piece = join_forward(at, x_piece, [keep, swapped(give, NEAR)], first)
    middle = gathered(piece, after(swapped(piece, NEAR), *g_parts[4:]))

    parts_last, saved_second, blocks = forward(piece_loader, middle, second, False)
    acts_mine, acts_give = blocks

    early, given, (g_piece,) = backward(start_loader, g_parts, saved_second, second, True)
    early_keep, early_give = summed_cores(*early)
    given = (after(given[0], *early_give),) + given[1:]
    parts, late = backward_end(given, saved_second, second)
    far_second = swapped(early_give[1], HALF)
    parts[0] = after(parts[0], far_second, *late)
    keep, give = fold(at, parts)
    late_keep, late_give = summed_cores(*late)
    late_got = swapped(after(jnp.stack(late_give), give), HALF)
    back = join_backward(at, g_piece, piece, [keep, swapped(give, NEAR)])
    near = after(swapped(back, NEAR), late_got)
    g_middle = gathered(back, near)
    close_second = swapped(after(early_give[0], near), HALF)
    g_middle[0] = after(g_middle[0], close_second)

    parts_last = exchanged([after(p, *g_middle) for p in parts_last])
    early, given, blocks = backward(piece_loader, g_middle, saved_first, first, False)
    in_mine, in_give = blocks
    early_second = [plus(a, b) for a, b in zip(early_keep, (close_second, far_second))]
    late_second = [plus(a, b) for a, b in zip(late_keep, late_got)]
    early_keep, early_give = summed_cores(*early)
    keep_last, give_last = fold(at, parts_last)
    given = (after(given[0], *early_give, give_last),) + given[1:]
    parts, late = backward_end(given, saved_first, first)
    far_first = swapped(early_give[1], HALF)
    parts[0] = after(parts[0], far_first, *late)
    keep, give = fold(at, parts)
    close_first = swapped(early_give[0], HALF)
    back_last = join_backward(at, back, x_piece, [keep, swapped(give, NEAR)])
    last = join_forward(at, piece, [keep_last, swapped(give_last, NEAR)], second)
    early_first = [plus(a, b) for a, b in zip(early_keep, (close_first, far_first))]
    late_keep, late_give = summed_cores(*late)
    late_got = swapped(jnp.stack(late_give), HALF)
    late_first = [plus(a, b) for a, b in zip(late_keep, late_got)]
    known_got = swapped(jnp.where(is_first, acts_give, in_give), HALF)
    known_rest = swapped(known_got, SIDE)

    def owned(one, two):
        return jnp.where(is_first, one, two), swapped(jnp.where(is_first, two, one), SECTION)

    far_own, far_got = owned(early_first[1], early_second[1])
    far = swapped(jnp.stack([far_own, far_got]), NEAR)
    close_own, close_got = owned(early_first[0], early_second[0])
    late_own, late_got = owned(jnp.stack(late_first), jnp.stack(late_second))
    late_near = swapped(jnp.stack([late_own[1], late_got[1]]), NEAR)
    sizes = dict(units=up_weight.shape[2] // 4)
    qkv, out, up, down, lines, b_qkv, b_up, branch = unpack_grads(
        at,
        (close_own, close_got, far[0], far[1]),
        (late_own[0], late_got[0], late_near[0], late_near[1]),
        sizes,
    )

    known_mine = jnp.where(is_first, acts_mine, in_mine)
    known_other = jnp.where(
        is_left,
        jnp.concatenate([known_got, known_rest], axis=0),
        jnp.concatenate([known_rest, known_got], axis=0),
    )
    known = jnp.where(
        is_low, jnp.stack([known_mine, known_other]), jnp.stack([known_other, known_mine])
    )
    mine = jnp.where(is_first, back_last, last)
    got = swapped(jnp.where(is_first, last, back_last), SECTION)
    stay = jnp.where(is_near, mine, got)
    other = swapped(jnp.where(is_near, got, mine), HALF)
    own = jnp.where(is_low, jnp.stack([stay, other]), jnp.stack([other, stay]))
    rest = swapped(own, SIDE)
    new = jnp.where(
        is_left, jnp.concatenate([own, rest], axis=1), jnp.concatenate([rest, own], axis=1)
    )
    acts = jnp.where(is_first, known, new)
    in_grads = jnp.where(is_first, new, known)

    lines = lines.reshape(4, dim)
    return (
        acts[None],
        in_grads[None],
        lines[0:1],
        lines[1:2],
        lines[2:3],
        lines[3:4],
        qkv[None],
        b_qkv[None],
        out[None],
        up[None],
        b_up,
        down[None],
        branch.reshape(1, dim),
    )


def placed_program(mesh, device_program):
    placed = (
        P(None, "ctx", None),
        P(None, "ctx", None),
        P("section", None),
        P("section", None),
        P("section", None),
        P("section", None),
        P("section", None, None, "tp"),
        P("section", None, "tp"),
        P("section", "tp", None),
        P("section", None, "tp"),
        P("section", "tp"),
        P("section", "tp", None),
        P("section", None),
    )
    return jax.shard_map(
        device_program,
        mesh=mesh,
        in_specs=placed,
        out_specs=(
            P("section", None, "ctx", None),
            P("section", None, "ctx", None),
            P("section", None),
            P("section", None),
            P("section", None),
            P("section", None),
            P("section", None, "ctx", "tp"),
            P("section", None, "tp"),
            P("section", "tp", "ctx"),
            P("section", "ctx", "tp"),
            P("section", "tp"),
            P("section", "tp", "ctx"),
            P("section", None),
        ),
        check_vma=False,
    )


def solution(mesh):
    sizes = dict(mesh.shape)
    if sizes["section"] == 2 and sizes["tp"] == 2 and sizes["ctx"] == 8:
        return placed_program(mesh, cube_device)
    return placed_program(mesh, per_device)
```

```python
import math

import jax
import jax.numpy as jnp
from jax import lax
from jax.experimental import pallas as pl
from jax.experimental.pallas import tpu as pltpu
from jax.sharding import PartitionSpec as P

HD = 64
ROT = 16


def shifted(shard, axis, by):
    peers = lax.axis_size(axis)
    pairs = [(i, i + by) for i in range(peers) if 0 <= i + by < peers]
    return lax.ppermute(shard, axis, pairs)


def tables(positions):
    freqs = 1.0 / 10000.0 ** (jnp.arange(0, ROT, 2).astype(jnp.float32) / ROT)
    angles = positions.astype(jnp.float32)[:, None] * freqs[None, :]
    return (jnp.cos(angles)[:, None, :], jnp.sin(angles)[:, None, :])


def rotate(field, cosine, sine):
    half_rot = ROT // 2
    front = field[..., :half_rot]
    second = field[..., half_rot:ROT]
    return jnp.concatenate(
        [front * cosine - second * sine, second * cosine + front * sine, field[..., ROT:]], axis=-1
    )


def norms(hidden, gain_one, shift_one, gain_two, shift_two):
    centre = hidden - jnp.mean(hidden, axis=-1, keepdims=True)
    normed = centre * lax.rsqrt(jnp.mean(centre * centre, axis=-1, keepdims=True) + 1e-05)
    return (normed * gain_one + shift_one, normed * gain_two + shift_two)


def gelu_exact(value):
    return jax.nn.gelu(value, approximate=False)


def scores_of(queries, keys, query_pos, score_scale):
    raw = jnp.einsum("qhd,khd->hqk", queries, keys, preferred_element_type=jnp.float32)
    key_pos = jnp.arange(keys.shape[0], dtype=jnp.int32)
    return jnp.where(
        key_pos[None, None, :] <= query_pos[None, :, None], raw * score_scale, -1000000000.0
    )


def forward_layer(layer_in, weights, query_pos, cosine, sine):
    gains, w_qkv, b_qkv, w_out, w_up, b_up, w_down, b_branch = weights
    hidden = layer_in.astype(jnp.float32)
    attn_norm, mlp_norm = norms(hidden, gains[0], gains[1], gains[2], gains[3])
    attn_in = attn_norm.astype(jnp.bfloat16)
    mlp_in = mlp_norm.astype(jnp.bfloat16)
    projected = (
        jnp.einsum("td,cdf->tcf", attn_in, w_qkv, preferred_element_type=jnp.float32) + b_qkv
    )
    row_count = hidden.shape[0]
    feat_width = projected.shape[2]
    head_count = feat_width // HD
    queries = rotate(projected[:, 0].reshape(row_count, head_count, HD), cosine, sine).astype(
        jnp.bfloat16
    )
    key_flat = (
        rotate(projected[:, 1].reshape(row_count, head_count, HD), cosine, sine)
        .astype(jnp.bfloat16)
        .reshape(row_count, feat_width)
    )
    value_flat = projected[:, 2].astype(jnp.bfloat16)
    all_keys, all_values = (
        lax.all_gather(key_flat, "ctx", axis=0, tiled=True),
        lax.all_gather(value_flat, "ctx", axis=0, tiled=True),
    )
    key_count = all_keys.shape[0]
    score_scale = 1.0 / math.sqrt(HD)
    scores = scores_of(queries, all_keys.reshape(key_count, head_count, HD), query_pos, score_scale)
    row_max = jnp.max(scores, axis=-1, keepdims=True)
    exponent = jnp.exp(scores - row_max)
    summed = jnp.sum(exponent, axis=-1, keepdims=True)
    probability = (exponent / summed).astype(jnp.bfloat16)
    log_total = row_max + jnp.log(summed)
    mixed = jnp.einsum(
        "hqk,khd->qhd",
        probability,
        all_values.reshape(key_count, head_count, HD),
        preferred_element_type=jnp.float32,
    )
    mixed = mixed.reshape(row_count, feat_width).astype(jnp.bfloat16)
    partial_out = jnp.dot(mixed, w_out, preferred_element_type=jnp.float32)
    up_value = jnp.dot(mlp_in, w_up, preferred_element_type=jnp.float32) + b_up
    active = gelu_exact(up_value).astype(jnp.bfloat16)
    partial_out = partial_out + jnp.dot(active, w_down, preferred_element_type=jnp.float32)
    branches = lax.psum(partial_out, "tp")
    layer_out = (hidden + branches + b_branch).astype(jnp.bfloat16)
    stored = (key_flat, value_flat)
    saved = (layer_in, queries, stored, log_total, mixed, up_value, active)
    return (layer_out, saved)


def backward_layer(grad_out, saved, weights, query_pos, cosine, sine):
    gains, w_qkv, b_qkv, w_out, w_up, b_up, w_down, b_branch = weights
    layer_in, queries, stored, log_total, mixed, up_value, active = saved
    grad_full = grad_out.astype(jnp.float32)
    row_count, feat_width = mixed.shape
    head_count = feat_width // HD
    hidden = layer_in.astype(jnp.float32)
    norm_pair, norm_back = jax.vjp(norms, hidden, gains[0], gains[1], gains[2], gains[3])
    attn_in = norm_pair[0].astype(jnp.bfloat16)
    mlp_in = norm_pair[1].astype(jnp.bfloat16)
    active_grad = jnp.einsum("td,fd->tf", grad_out, w_down, preferred_element_type=jnp.float32)
    grad_down = jnp.einsum("tf,td->fd", active, grad_out, preferred_element_type=jnp.float32)
    gelu_back = jax.vjp(gelu_exact, up_value)[1]
    up_grad = gelu_back(active_grad)[0].astype(jnp.bfloat16)
    grad_up_bias = jnp.sum(up_grad.astype(jnp.float32), axis=0)
    grad_up = jnp.einsum("td,tf->df", mlp_in, up_grad, preferred_element_type=jnp.float32)
    mlp_in_grad = jnp.einsum("tf,df->td", up_grad, w_up, preferred_element_type=jnp.float32)
    mixed_grad = jnp.einsum(
        "td,fd->tf", grad_out, w_out, preferred_element_type=jnp.float32
    ).astype(jnp.bfloat16)
    grad_out_weight = jnp.einsum("tf,td->fd", mixed, grad_out, preferred_element_type=jnp.float32)
    all_keys, all_values = (
        lax.all_gather(stored[0], "ctx", axis=0, tiled=True),
        lax.all_gather(stored[1], "ctx", axis=0, tiled=True),
    )
    key_count = all_keys.shape[0]
    keys_heads = all_keys.reshape(key_count, head_count, HD)
    values_heads = all_values.reshape(key_count, head_count, HD)
    score_scale = 1.0 / math.sqrt(HD)
    scores = scores_of(queries, keys_heads, query_pos, score_scale)
    probability = jnp.exp(scores - log_total)
    heads_grad = mixed_grad.reshape(row_count, head_count, HD)
    prob_grad = jnp.einsum(
        "qhd,khd->hqk", heads_grad, values_heads, preferred_element_type=jnp.float32
    )
    centre = jnp.sum(probability * prob_grad, axis=-1, keepdims=True)
    score_grad = (score_scale * probability * (prob_grad - centre)).astype(jnp.bfloat16)
    query_grad = jnp.einsum(
        "hqk,khd->qhd", score_grad, keys_heads, preferred_element_type=jnp.float32
    )
    value_terms = jnp.einsum(
        "hqk,qhd->khd",
        probability.astype(jnp.bfloat16),
        heads_grad,
        preferred_element_type=jnp.float32,
    )
    key_terms = jnp.einsum("hqk,qhd->khd", score_grad, queries, preferred_element_type=jnp.float32)
    key_grad, value_grad = (
        lax.psum_scatter(
            key_terms.reshape(key_count, feat_width), "ctx", scatter_dimension=0, tiled=True
        ),
        lax.psum_scatter(
            value_terms.reshape(key_count, feat_width), "ctx", scatter_dimension=0, tiled=True
        ),
    )
    query_grad = rotate(query_grad, cosine, -sine).reshape(row_count, feat_width)
    key_grad = rotate(key_grad.reshape(row_count, head_count, HD), cosine, -sine).reshape(
        row_count, feat_width
    )
    qkv_grad = jnp.stack([query_grad, key_grad, value_grad], axis=1).astype(jnp.bfloat16)
    grad_qkv_bias = jnp.sum(qkv_grad.astype(jnp.float32), axis=0)
    grad_qkv = jnp.einsum("td,tcf->cdf", attn_in, qkv_grad, preferred_element_type=jnp.float32)
    attn_in_grad = jnp.einsum("tcf,cdf->td", qkv_grad, w_qkv, preferred_element_type=jnp.float32)
    attn_in_grad, mlp_in_grad = lax.psum((attn_in_grad, mlp_in_grad), "tp")
    hidden_grad, gain_one_grad, shift_one_grad, gain_two_grad, shift_two_grad = norm_back(
        (attn_in_grad, mlp_in_grad)
    )
    input_grad = (grad_full + hidden_grad).astype(jnp.bfloat16)
    grad_branch = jnp.sum(grad_full, axis=0)
    grads = (
        gain_one_grad,
        shift_one_grad,
        gain_two_grad,
        shift_two_grad,
        grad_qkv,
        grad_qkv_bias,
        grad_out_weight,
        grad_up,
        grad_up_bias,
        grad_down,
        grad_branch,
    )
    return (input_grad, grads)


def per_device(
    inputs,
    cotangent,
    ln1_gain,
    ln1_bias,
    ln2_gain,
    ln2_bias,
    qkv_weight,
    qkv_bias,
    out_weight,
    up_weight,
    up_bias,
    down_weight,
    branch_bias,
):
    gains = (
        ln1_gain[0].astype(jnp.float32),
        ln1_bias[0].astype(jnp.float32),
        ln2_gain[0].astype(jnp.float32),
        ln2_bias[0].astype(jnp.float32),
    )
    weights = (
        gains,
        qkv_weight[0],
        qkv_bias[0].astype(jnp.float32),
        out_weight[0],
        up_weight[0],
        up_bias[0].astype(jnp.float32),
        down_weight[0],
        branch_bias[0].astype(jnp.float32),
    )
    micro_count = inputs.shape[0]
    row_count = inputs.shape[1]
    query_pos = lax.axis_index("ctx") * row_count + jnp.arange(row_count, dtype=jnp.int32)
    cosine, sine = tables(query_pos)
    at_first = lax.axis_index("section") == 0
    blank = jnp.zeros_like(inputs[0])
    received = blank
    outputs_list = []
    saved_list = []
    for step_index in range(micro_count + 1):
        fresh = inputs[step_index] if step_index < micro_count else blank
        layer_in = jnp.where(at_first, fresh, received)
        layer_out, saved = forward_layer(layer_in, weights, query_pos, cosine, sine)
        outputs_list.append(layer_out)
        saved_list.append(saved)
        if step_index < micro_count:
            received = shifted(layer_out, "section", 1)
    returned = blank
    grad_list = []
    sums = None
    for back_index in range(micro_count + 1):
        batch_index = micro_count - 1 - back_index
        given = cotangent[batch_index] if batch_index >= 0 else blank
        grad_in = jnp.where(at_first, returned, given)
        input_grad, grads = backward_layer(
            grad_in, saved_list[micro_count - back_index], weights, query_pos, cosine, sine
        )
        sums = grads if sums is None else jax.tree.map(jnp.add, sums, grads)
        grad_list.append(input_grad)
        if back_index < micro_count:
            returned = shifted(input_grad, "section", -1)
    acts = jnp.stack(
        [jnp.where(at_first, outputs_list[j], outputs_list[j + 1]) for j in range(micro_count)]
    )[None]
    in_grads = jnp.stack(
        [
            jnp.where(at_first, grad_list[micro_count - j], grad_list[micro_count - 1 - j])
            for j in range(micro_count)
        ]
    )[None]
    (
        gain_one_grad,
        shift_one_grad,
        gain_two_grad,
        shift_two_grad,
        grad_qkv,
        grad_qkv_bias,
        grad_out_weight,
        grad_up,
        grad_up_bias,
        grad_down,
        grad_branch,
    ) = sums
    qkv_part, out_part, up_part, down_part = (
        lax.psum_scatter(
            grad_qkv[None].astype(jnp.bfloat16), "ctx", scatter_dimension=2, tiled=True
        ).astype(jnp.float32),
        lax.psum_scatter(
            grad_out_weight[None].astype(jnp.bfloat16), "ctx", scatter_dimension=2, tiled=True
        ).astype(jnp.float32),
        lax.psum_scatter(
            grad_up[None].astype(jnp.bfloat16), "ctx", scatter_dimension=1, tiled=True
        ).astype(jnp.float32),
        lax.psum_scatter(
            grad_down[None].astype(jnp.bfloat16), "ctx", scatter_dimension=2, tiled=True
        ).astype(jnp.float32),
    )
    small_sums = (
        lax.psum(gain_one_grad[None].astype(jnp.bfloat16), "ctx").astype(jnp.float32),
        lax.psum(shift_one_grad[None].astype(jnp.bfloat16), "ctx").astype(jnp.float32),
        lax.psum(gain_two_grad[None].astype(jnp.bfloat16), "ctx").astype(jnp.float32),
        lax.psum(shift_two_grad[None].astype(jnp.bfloat16), "ctx").astype(jnp.float32),
        lax.psum(grad_qkv_bias[None].astype(jnp.bfloat16), "ctx").astype(jnp.float32),
        lax.psum(grad_up_bias[None].astype(jnp.bfloat16), "ctx").astype(jnp.float32),
        lax.psum(grad_branch[None].astype(jnp.bfloat16), "ctx").astype(jnp.float32),
    )
    return (
        acts,
        in_grads,
        small_sums[0],
        small_sums[1],
        small_sums[2],
        small_sums[3],
        qkv_part,
        small_sums[4],
        out_part,
        up_part,
        small_sums[5],
        down_part,
        small_sums[6],
    )


ALL = ("section", "ctx", "tp")
SECTION, HALF, NEAR, CORE, SIDE = 16, 8, 4, 2, 1
CHIPS = (0, SIDE, NEAR, NEAR | SIDE, SECTION, SECTION | SIDE, SECTION | NEAR, SECTION | NEAR | SIDE)
F32, B16 = jnp.float32, jnp.bfloat16
ONE = 128
S_SECTION, S_HALF, S_NEAR, S_CORE, S_SIDE, S_CHIP, S_OWN, S_GIVE = range(8)


def swapped(array, mask, section=None):
    pairs = [(i, i ^ mask) for i in range(32) if section is None or i // 16 == section]
    return lax.ppermute(array, ALL, pairs)


def after(array, *earlier):
    return lax.optimization_barrier((array,) + earlier)[0]


def where_am_i():
    section = lax.axis_index("section")
    ctx = lax.axis_index("ctx")
    side = lax.axis_index("tp")
    half, near, core = ctx // 4, (ctx // 2) % 2, ctx % 2
    chip = 4 * section + 2 * near + side
    own, give = 2 * section + near, 2 * (1 - section) + near
    return jnp.stack([section, half, near, core, side, chip, own, give]).astype(jnp.int32)


def in_hbm(arrays):
    return [pltpu.with_memory_space_constraint(a, pltpu.HBM) for a in arrays]


def kernel_call(body, outs, at, *arrays, hbm=(), scratch=(), flops=0, exps=0, name=None, keep=True):
    moved = sum(a.size * a.dtype.itemsize for a in arrays)
    moved += sum(math.prod(s) * jnp.dtype(d).itemsize for s, d in outs)
    return pl.pallas_call(
        body,
        name=name,
        out_shape=[(pltpu.VMEM if keep else jax.ShapeDtypeStruct)(s, d) for s, d in outs],
        in_specs=[pl.BlockSpec(memory_space=pltpu.SMEM)]
        + [pl.BlockSpec(memory_space=pltpu.VMEM)] * len(arrays)
        + [pl.BlockSpec(memory_space=pltpu.HBM)] * len(hbm),
        out_specs=[pl.BlockSpec(memory_space=pltpu.VMEM)] * len(outs),
        scratch_shapes=list(scratch),
        compiler_params=pltpu.CompilerParams(vmem_limit_bytes=VMEM_BYTES),
        cost_estimate=pl.CostEstimate(flops=0, bytes_accessed=0, transcendentals=0),
    )(at, *arrays, *in_hbm(hbm))


VMEM_BYTES = 12 * 1024 * 1024


def kernel_call_named(name, *args, **kwargs):
    return kernel_call(*args, name=name, **kwargs)


def by_rows(rows, step, do):
    def one(i, _):
        do(pl.ds(pl.multiple_of(i * step, step), step))
        return 0

    lax.fori_loop(0, rows // step, one, 0)


def nn(a, b):
    return jnp.dot(a, b, preferred_element_type=F32)


def nt(a, b):
    return lax.dot_general(a, b, (((1,), (1,)), ((), ())), preferred_element_type=F32)


def tn(a, b):
    return lax.dot_general(a, b, (((0,), (0,)), ((), ())), preferred_element_type=F32)


def copy_kernel(name, body, outs, at, arrays, scratch):
    return pl.pallas_call(
        body,
        name=name,
        out_shape=[jax.ShapeDtypeStruct(s, B16) for s in outs],
        in_specs=[pl.BlockSpec(memory_space=pltpu.SMEM)]
        + [pl.BlockSpec(memory_space=pltpu.HBM)] * len(arrays),
        out_specs=[pl.BlockSpec(memory_space=pltpu.HBM)] * len(outs),
        scratch_shapes=list(scratch),
        compiler_params=pltpu.CompilerParams(vmem_limit_bytes=VMEM_BYTES),
        cost_estimate=pl.CostEstimate(flops=0, bytes_accessed=0, transcendentals=0),
    )(at, *in_hbm(arrays))


def token_copies(at, array, mine, strip, sems):
    width = strip.shape[1]
    lanes = pl.ds(pl.multiple_of(at[S_SIDE] * width, width), width)
    return [
        pltpu.make_async_copy(array.at[at[S_HALF]], mine, sems.at[0]),
        pltpu.make_async_copy(array.at[1 - at[S_HALF], :, lanes], strip, sems.at[1]),
    ]


def token_shapes(array):
    _, rows, dim = array.shape
    return [(rows, dim), (rows, dim // 2)]


def send_strips(strip):
    return swapped(strip, HALF), swapped(strip, HALF | NEAR)


def start_loader(at, refs):
    mine, near, far, far_near, far_rest, far_near_rest = refs
    first = at[S_SIDE] == 0
    index = 2 * at[S_HALF] + at[S_NEAR]

    def whole(strip, rest):
        a, b = strip[...], rest[...]
        return jnp.concatenate([jnp.where(first, a, b), jnp.where(first, b, a)], axis=1)

    yield index, mine[...]
    yield index ^ 1, near[...]
    yield index ^ 2, whole(far, far_rest)
    yield index ^ 3, whole(far_near, far_near_rest)


def piece_loader(at, refs):
    for step, ref in zip(STEPS, refs):
        for i in range(2):
            yield at[S_CHIP] ^ (step | 2 * i), ref[i]


def run_copies(copies):
    for copy in copies:
        copy.start()
    for copy in copies:
        copy.wait()


def pack_first(at, tokens, vectors, w_qkv):
    _, three, dim, wide = w_qkv.shape
    heads, side = wide // 4, dim // 2
    count = len(vectors)

    def body(at, tokens, w_qkv, *refs):
        lines = refs[:count]
        mine, strip, packed, table, rounded, sems = refs[count : count + 6]
        held = refs[count + 6 :]
        rows = pl.ds(pl.multiple_of(at[S_CORE] * side, side), side)
        lanes = pl.ds(pl.multiple_of(at[S_GIVE] * heads, heads), heads)
        copies = token_copies(at, tokens, mine, strip, sems)
        for i in range(three):
            copies.append(
                pltpu.make_async_copy(
                    w_qkv.at[0, i, rows, lanes], packed.at[i * side : (i + 1) * side], sems.at[2 + i]
                )
            )
        loads = [
            pltpu.make_async_copy(line, hold, sems.at[6 + i])
            for i, (line, hold) in enumerate(zip(lines, held))
        ]
        for copy in copies:
            copy.start()
        run_copies(loads)
        fill_table(table, at[S_GIVE], held)
        rounded[...] = table[...].astype(B16)
        run_copies([pltpu.make_async_copy(rounded, packed.at[three * side :], sems.at[5])])
        for copy in copies:
            copy.wait()

    return copy_kernel(
        "pack_first", body, token_shapes(tokens) + [(three * side + TABLE, ONE)], at,
        [tokens, w_qkv, *vectors],
        [pltpu.VMEM((TABLE, ONE), F32), pltpu.VMEM((TABLE, ONE), B16), pltpu.SemaphoreType.DMA((6 + count,))]
        + [pltpu.VMEM(v.shape, B16) for v in vectors],
    )


def pack_second(at, tokens, w_up, w_out, w_down):
    dim, units, heads = w_up.shape[1], w_up.shape[2] // 4, w_out.shape[1] // 4
    side = dim // 2

    def body(at, tokens, w_up, w_out, w_down, mine, strip, up, down, sems):
        copies = token_copies(at, tokens, mine, strip, sems)
        rows = pl.ds(pl.multiple_of(at[S_CORE] * side, side), side)
        lanes = pl.ds(pl.multiple_of(at[S_GIVE] * units, units), units)
        copies.append(pltpu.make_async_copy(w_up.at[0, rows, lanes], up, sems.at[2]))
        part = 2 * at[S_GIVE] + at[S_CORE]
        for i, (source, size, start) in enumerate(
            ((w_down, units // 2, 0), (w_out, heads // 2, units // 2))
        ):
            rows = pl.ds(pl.multiple_of(part * size, size), size)
            copies.append(
                pltpu.make_async_copy(
                    source.at[0, rows], down.at[start : start + size], sems.at[3 + i]
                )
            )
        run_copies(copies)

    return copy_kernel(
        "pack_second", body, token_shapes(tokens) + [(side, units), ((units + heads) // 2, dim)], at,
        [tokens, w_up, w_out, w_down], [pltpu.SemaphoreType.DMA((5,))],
    )


def fill_table(table, index, vectors):
    *lines, b_up, b_qkv = vectors
    units, heads = b_up.shape[1] // 4, b_qkv.shape[2] // 4
    table[...] = jnp.zeros_like(table)
    row = 0
    for line in lines:
        for i in range(line.shape[1] // ONE):
            table[row : row + 1] = line[:, i * ONE : (i + 1) * ONE].astype(F32)
            row += 1
    for i in range(units // ONE):
        lanes = pl.ds(pl.multiple_of(index * units + i * ONE, ONE), ONE)
        table[row : row + 1] = b_up[:, lanes].astype(F32)
        row += 1
    few = b_qkv[0, :, pl.ds(pl.multiple_of(index * heads, ONE), heads)].astype(F32)
    table[row : row + few.shape[0]] = few


TABLE = 48


def vector_rows(at, vectors, got):
    dim = vectors[0].shape[1]
    units, few = vectors[5].shape[1] // 4, vectors[6].shape[1]

    def body(at, *refs):
        *lines, got, rows0, rows1, table = refs
        fill_table(table, at[S_OWN], lines)
        taken = got[got.shape[0] - TABLE :].astype(F32)
        is_first = at[S_SECTION] == 0
        for rows, lines in (
            (rows0, jnp.where(is_first, table[...], taken)),
            (rows1, jnp.where(is_first, taken, table[...])),
        ):
            rows[...] = jnp.zeros_like(rows)
            line = 0
            for r, tiles in enumerate([dim // ONE] * 5 + [units // ONE, few]):
                for i in range(tiles):
                    rows[r : r + 1, i * ONE : (i + 1) * ONE] = lines[line : line + 1]
                    line += 1

    return kernel_call_named(
        "vector_rows", body, [((8, dim), F32)] * 2, at, *vectors, got,
        scratch=[pltpu.VMEM((TABLE, ONE), F32)],
    )


def half_rows(at, which, size):
    return pl.ds(pl.multiple_of((at[S_CORE] ^ which) * size, size), size)


def qkv_copies(at, own, got, rest, target):
    three, heads = own.shape[1], own.shape[3] // 4
    side = own.shape[2] // 2
    lanes = pl.ds(pl.multiple_of(at[S_OWN] * heads, heads), heads)
    mine, halves = [], []
    for i in range(three):
        tile = slice(i * heads, (i + 1) * heads)
        mine.append((own.at[0, i, :, lanes], target[0].at[:, tile]))
        for which, source in ((0, got), (1, rest)):
            halves.append(
                (
                    source.at[i * side : (i + 1) * side],
                    target[1].at[half_rows(at, which, side), tile],
                )
            )
    return mine + halves


def up_copies(at, own, got, rest, target):
    side, units = got.shape
    lanes = pl.ds(pl.multiple_of(at[S_OWN] * units, units), units)
    return [(own.at[0, :, lanes], target[0])] + [
        (source, target[1].at[half_rows(at, which, side)])
        for which, source in ((0, got), (1, rest))
    ]


def row_copies(at, own, got, rest, target, start):
    size = target[0].shape[0]
    side = size // 2
    rows = pl.ds(pl.multiple_of(at[S_OWN] * size, size), size)
    return [(own.at[0, rows], target[0])] + [
        (source.at[start : start + side], target[1].at[half_rows(at, which, side)])
        for which, source in ((0, got), (1, rest))
    ]


def choose_weights(name, at, owns, got, rest, shapes, make):
    count = len(owns)

    def body(at, *refs):
        own, (got, rest), targets, sems = refs[:count], refs[count : count + 2], refs[count + 2 : -1], refs[-1]
        for section in range(2):

            @pl.when(at[S_SECTION] == section)
            def _():
                pairs = make(
                    at, own, got, rest,
                    [(targets[2 * i + section], targets[2 * i + 1 - section]) for i in range(count)],
                )
                run_copies(
                    [
                        pltpu.make_async_copy(source, target, sems.at[i])
                        for i, (source, target) in enumerate(pairs)
                    ]
                )

    outs = [(shape, B16) for shape in shapes for _ in range(2)]
    return kernel_call(
        body, outs, at, hbm=[*owns, got, rest],
        scratch=[pltpu.SemaphoreType.DMA((9,))], name=name,
    )


def weights_call(name, body, outs, at, arrays, weights, scratch=(), flops=0, exps=0):
    first, count = len(arrays), len(weights)

    def wrapped(at, *refs):
        given, chosen, rest = refs[:first], refs[first : first + count], refs[first + count :]
        made, own = rest[: len(outs)], rest[len(outs) :]
        body(at, *given, *made, *chosen, *own)

    return kernel_call(
        wrapped, outs, at, *arrays, *weights, scratch=scratch, flops=flops, exps=exps, name=name
    )


def first_weights(at, vectors, w_qkv, sent):
    _, three, dim, wide = w_qkv.shape
    got = swapped(sent, SECTION)
    qkv = choose_weights(
        "choose_qkv", at, [w_qkv], got, swapped(got, CORE), [(dim, three * (wide // 4))],
        lambda at, own, got, rest, to: qkv_copies(at, own[0], got, rest, to[0]),
    )
    return got, [dict(qkv=q, rows=r) for q, r in zip(qkv, vector_rows(at, vectors, got))]


def up_weights(at, w_up, got, rest):
    return choose_weights(
        "choose_up", at, [w_up], got, rest, [(w_up.shape[1], w_up.shape[2] // 4)],
        lambda at, own, got, rest, to: up_copies(at, own[0], got, rest, to[0]),
    )


def row_weights(at, w_down, w_out, got, rest):
    _, tall, dim = w_down.shape
    units, heads = tall // 4, w_out.shape[1] // 4
    return choose_weights(
        "choose_rows", at, [w_down, w_out], got, rest, [(units, dim), (heads, dim)],
        lambda at, own, got, rest, to: row_copies(at, own[0], got, rest, to[0], 0)
        + row_copies(at, own[1], got, rest, to[1], units // 2),
    )


def turn_tables(at, rows):
    half_rot = ROT // 2
    place = lax.broadcasted_iota(jnp.int32, (rows, ONE), 0)
    lane = lax.broadcasted_iota(jnp.int32, (rows, ONE), 1) % HD
    positions = (2 * (place // ONE) + at[S_CORE]) * ONE + place % ONE
    freqs = 1.0 / 10000.0 ** ((2 * (lane % half_rot)).astype(F32) / ROT)
    angles = positions.astype(F32) * freqs
    sine = jnp.sin(angles)
    return (
        jnp.where(lane < ROT, jnp.cos(angles), 1.0),
        jnp.where((lane >= half_rot) & (lane < ROT), sine, 0.0),
        jnp.where(lane < half_rot, -sine, 0.0),
    )


def keep_blocks(at, source, blocks):
    mine, give = blocks
    place = (2 * at[S_HALF] + at[S_NEAR]) * ONE
    mine[...] = source[pl.ds(pl.multiple_of(place, ONE), ONE)]
    size = give.shape[0]
    place = (2 * (1 - at[S_HALF]) + at[S_NEAR]) * ONE + at[S_SIDE] * size
    give[...] = source[pl.ds(pl.multiple_of(place, size), size)]


def keep_piece(at, source, piece):
    size = piece.shape[0]
    piece[...] = source[pl.ds(pl.multiple_of(at[S_CHIP] * size, size), size)]


def front(at, loader, sources, w, turns, with_piece):
    dim = w["qkv"].shape[0]
    rows = turns[0].shape[0]
    count = len(sources)

    def body(at, *refs):
        given = refs[:count]
        vectors, *turns = refs[count : count + 4]
        attn_in, mlp_in, normed_out, q, kv = refs[count + 4 : count + 9]
        *kept, qkv, ordered = refs[count + 9 :]
        gains = [vectors[i : i + 1] for i in range(4)]
        for place, block in loader(at, given):
            size = block.shape[0]
            ordered[pl.ds(pl.multiple_of(place * size, size), size)] = block
        if with_piece:
            keep_piece(at, ordered, kept[0])
        else:
            keep_blocks(at, ordered, kept)
        bias = vectors[6:7, : 3 * ONE]

        def norm(span):
            hidden = ordered[span].astype(F32)
            mean = jnp.sum(hidden, axis=1, keepdims=True) * (1.0 / dim)
            centre = hidden - mean
            var = jnp.sum(centre * centre, axis=1, keepdims=True) * (1.0 / dim)
            normed = centre * lax.rsqrt(var + 1e-05)
            attn_in[span] = (normed * gains[0] + gains[1]).astype(B16)
            mlp_in[span] = (normed * gains[2] + gains[3]).astype(B16)
            normed_out[span] = normed.astype(B16)

        def project(span):
            projected = nn(attn_in[span], qkv[...]) + bias
            cosine, second, first_half = [table[span] for table in turns]
            for i, target in ((0, q), (1, kv.at[0])):
                flat = projected[:, i * ONE : (i + 1) * ONE]
                flat = (
                    flat * cosine
                    + pltpu.roll(flat, ROT // 2, 1) * second
                    + pltpu.roll(flat, ONE - ROT // 2, 1) * first_half
                )
                target[span] = flat.astype(B16)
            kv[1, span] = projected[:, 2 * ONE :].astype(B16)

        by_rows(rows, 128, norm)
        by_rows(rows, 256, project)

    outs = [((rows, dim), B16)] * 3 + [((rows, ONE), B16), ((2, rows, ONE), B16)]
    outs += [((rows // 8, dim), B16)] if with_piece else [((n, dim), B16) for n in (ONE, ONE // 2)]
    return weights_call(
        "front", body, outs, at, [*sources, w["rows"], *turns], [w["qkv"]],
        scratch=[pltpu.VMEM((rows, dim), B16)],
        flops=2 * rows * dim * 3 * ONE + 20 * rows * dim,
    )


def units_forward(at, mlp_in, w):
    rows, dim = mlp_in.shape
    units = w["units"]

    def body(at, mlp_in, vectors, active, slope, up):
        bias = vectors[5:6, :units]

        def gelu(span):
            value = nn(mlp_in[span], up[...]) + bias
            cdf = 0.5 + 0.5 * lax.erf(value * (1.0 / math.sqrt(2.0)))
            pdf = jnp.exp(value * value * -0.5) * (1.0 / math.sqrt(2.0 * math.pi))
            active[span] = (value * cdf).astype(B16)
            slope[span] = (cdf + value * pdf).astype(B16)

        by_rows(rows, 128, gelu)

    return weights_call(
        "units_forward", body, [((rows, units), B16)] * 2, at, [mlp_in, w["rows"]], [w["up"]],
        flops=2 * rows * dim * units + 40 * rows * units, exps=rows * units,
    )


def head_lanes():
    return lax.broadcasted_iota(jnp.int32, (1, ONE), 1) < HD


def allowed_keys(at, first, step, count):
    row = lax.broadcasted_iota(jnp.int32, (step, count), 0) + first
    column = lax.broadcasted_iota(jnp.int32, (step, count), 1)
    return column <= row, column < (row // ONE + at[S_CORE]) * ONE


STEPS = (0, 1, 4, 5)
STEP_CHIPS = (0, SIDE, SECTION, SECTION | SIDE)


def pieces_out(at, total, pieces):
    size = total.shape[0] // 8
    for step, piece in zip(STEPS, pieces):
        for i in range(2):
            place = (at[S_CHIP] ^ (step | 2 * i)) * size
            piece[i] = total[pl.ds(pl.multiple_of(place, size), size)].astype(piece.dtype)


def piece_shapes(rows, dim):
    return [((2, rows // 8, dim), F32)] + [((2, rows // 8, dim), B16)] * 3


def fold(at, pieces):
    _, rows, dim = pieces[0].shape

    def body(at, *refs):
        *given, keep, give = refs
        for i, target in ((0, keep), (1, give)):
            total = given[0][i]
            for piece in given[1:]:
                total = total + piece[i].astype(F32)
            target[...] = total.astype(target.dtype)

    return kernel_call_named("fold", body, [((rows, dim), F32), ((rows, dim), B16)], at, *pieces)


def exchanged(pieces):
    return [pieces[0]] + [swapped(p, m) for p, m in zip(pieces[1:], STEP_CHIPS[1:])]


def gathered(piece, near):
    pair = jnp.stack([piece, near])
    return [pair] + [swapped(pair, mask) for mask in STEP_CHIPS[1:]]


def attention_forward(at, q, kv, kv_other):
    rows = q.shape[0]
    scale = 1.0 / math.sqrt(HD)

    def body(at, q, kv, kv_other, mixed, lse):
        first_head = head_lanes()
        step = 256
        for first in range(0, rows, step):
            span = slice(first, first + step)
            count = first + step
            queries = q[span]
            masks = allowed_keys(at, first, step, count)
            results, totals = [], []
            for head in range(2):
                lanes = first_head if head == 0 else jnp.logical_not(first_head)
                one = jnp.where(lanes, queries, jnp.zeros_like(queries))
                scores = [
                    jnp.where(mask, nt(one, keys[0, :count]) * scale, -1e9)
                    for mask, keys in zip(masks, (kv, kv_other))
                ]
                most = jnp.maximum(
                    jnp.max(scores[0], axis=1, keepdims=True),
                    jnp.max(scores[1], axis=1, keepdims=True),
                )
                exponents = [jnp.exp(s - most) for s in scores]
                summed = jnp.sum(exponents[0], axis=1, keepdims=True) + jnp.sum(
                    exponents[1], axis=1, keepdims=True
                )
                inverse = 1.0 / summed
                results.append(
                    nn((exponents[0] * inverse).astype(B16), kv[1, :count])
                    + nn((exponents[1] * inverse).astype(B16), kv_other[1, :count])
                )
                totals.append(most + jnp.log(summed))
            mixed[span] = jnp.where(first_head, results[0], results[1]).astype(B16)
            lse[span] = jnp.where(first_head, totals[0], totals[1])

    return kernel_call_named(
        "attention_forward", body, [((rows, ONE), B16), ((rows, ONE), F32)], at, q, kv, kv_other,
        flops=8 * rows * rows * ONE * 2, exps=2 * rows * rows * 2,
    )


def outputs_forward(at, mixed, active, w):
    rows = mixed.shape[0]
    units, dim = w["down"].shape

    def body(at, mixed, active, *rest):
        pieces, (out, down, total) = rest[:4], rest[4:]

        def one(span):
            total[span] = nn(mixed[span], out[...]) + nn(active[span], down[...])

        by_rows(rows, 256, one)
        pieces_out(at, total, pieces)

    return weights_call(
        "outputs_forward", body, piece_shapes(rows, dim), at, [mixed, active],
        [w["out"], w["down"]], scratch=[pltpu.VMEM((rows, dim), F32)],
        flops=2 * rows * dim * (units + ONE),
    )


def units_backward(at, loader, sources, slope, w, with_piece):
    rows, units = slope.shape
    dim = w["up"].shape[0]
    count = len(sources)

    def body(at, *refs):
        given = refs[:count]
        slope, g, up_grad, mixed_grad = refs[count : count + 4]
        *kept, down, out = refs[count + 4 :]
        for place, block in loader(at, given):
            size = block.shape[0]
            g[pl.ds(pl.multiple_of(place * size, size), size)] = block
        if with_piece:
            keep_piece(at, g, kept[0])
        else:
            keep_blocks(at, g, kept)

        def back(span):
            up_grad[span] = (nt(g[span], down[...]) * slope[span].astype(F32)).astype(B16)
            mixed_grad[span] = nt(g[span], out[...]).astype(B16)

        by_rows(rows, 256, back)

    outs = [((rows, dim), B16), ((rows, units), B16), ((rows, ONE), B16)]
    outs += [((rows // 8, dim), B16)] if with_piece else [((n, dim), B16) for n in (ONE, ONE // 2)]
    return weights_call(
        "units_backward", body, outs, at, [*sources, slope], [w["down"], w["out"]],
        flops=2 * rows * dim * (units + ONE),
    )


def attention_backward(at, q, kv, kv_other, lse, mixed_grad):
    rows = q.shape[0]
    scale = 1.0 / math.sqrt(HD)

    def body(at, q, kv, kv_other, lse, mixed_grad, dq, dkv, dkv_other):
        first_head = head_lanes()
        step = 256
        dkv[...] = jnp.zeros_like(dkv)
        dkv_other[...] = jnp.zeros_like(dkv_other)
        for first in range(0, rows, step):
            span = slice(first, first + step)
            count = first + step
            queries, back = q[span], mixed_grad[span]
            masks = allowed_keys(at, first, step, count)
            sides = ((masks[0], kv, dkv), (masks[1], kv_other, dkv_other))
            results = []
            for head in range(2):
                lanes = first_head if head == 0 else jnp.logical_not(first_head)
                one = jnp.where(lanes, queries, jnp.zeros_like(queries))
                one_back = jnp.where(lanes, back, jnp.zeros_like(back))
                level = lse[span, head * HD : head * HD + 1]
                probs, grads = [], []
                for mask, keys, _ in sides:
                    scores = nt(one, keys[0, :count]) * scale
                    probs.append(jnp.exp(jnp.where(mask, scores, -1e9) - level))
                    grads.append(nt(one_back, keys[1, :count]))
                delta = jnp.sum(probs[0] * grads[0], axis=1, keepdims=True) + jnp.sum(
                    probs[1] * grads[1], axis=1, keepdims=True
                )
                result = 0.0
                for (_, keys, target), prob, grad in zip(sides, probs, grads):
                    score_grad = (prob * (grad - delta) * scale).astype(B16)
                    result = result + nn(score_grad, keys[0, :count])
                    target[0, :count] += tn(score_grad, one)
                    target[1, :count] += tn(prob.astype(B16), one_back)
                results.append(result)
            dq[span] = jnp.where(first_head, results[0], results[1])

    return kernel_call_named(
        "attention_backward",
        body, [((rows, ONE), F32), ((2, rows, ONE), F32), ((2, rows, ONE), F32)],
        at, q, kv, kv_other, lse, mixed_grad,
        flops=20 * rows * rows * ONE * 2, exps=2 * rows * rows * 2,
    )


def inputs_backward(at, dq, dkv, dkv_got, up_grad, normed, g, turns, w):
    rows, dim = normed.shape
    units = up_grad.shape[1]

    def body(at, dq, dkv, dkv_got, up_grad, normed, g, *rest):
        turns, vectors, rest = rest[:3], rest[3], rest[4:]
        qkv_grad, table = rest[:2]
        pieces, (qkv, up, total, lines) = rest[2:6], rest[6:]
        gain_one, gain_two = vectors[0:1], vectors[2:3]
        step = 128

        def one(i, sums):
            span = pl.ds(pl.multiple_of(i * step, step), step)
            cosine, second, first_half = [table[span] for table in turns]
            parts = []
            for flat in (dq[span], dkv[0, span] + dkv_got[0, span]):
                parts.append(
                    flat * cosine
                    - pltpu.roll(flat, ROT // 2, 1) * second
                    - pltpu.roll(flat, ONE - ROT // 2, 1) * first_half
                )
            parts.append(dkv[1, span] + dkv_got[1, span])
            both = jnp.concatenate([p.astype(B16) for p in parts], axis=1)
            qkv_grad[span] = both
            attn = nt(both, qkv[...])
            mlp = nt(up_grad[span], up[...])
            total[span] = attn * gain_one + mlp * gain_two
            unit = normed[span].astype(F32)
            new = [
                jnp.sum(v, axis=0, keepdims=True)
                for v in (
                    attn * unit, attn, mlp * unit, mlp, g[span].astype(F32),
                    up_grad[span].astype(F32), both.astype(F32),
                )
            ]
            return tuple(a + b for a, b in zip(sums, new))

        widths = (dim,) * 5 + (units, 3 * ONE)
        sums = lax.fori_loop(
            0, rows // step, one, tuple(jnp.zeros((1, width), F32) for width in widths)
        )
        pieces_out(at, total, pieces)
        lines[...] = jnp.zeros_like(lines)
        line = 0
        for value in sums:
            for i in range(value.shape[1] // ONE):
                lines[line : line + 1] = value[:, i * ONE : (i + 1) * ONE]
                line += 1
        table[...] = lines[...].astype(B16)

    outs = [((rows, 3 * ONE), B16), ((LINES, ONE), B16)] + piece_shapes(rows, dim)
    return weights_call(
        "inputs_backward", body, outs, at,
        [dq, dkv, dkv_got, up_grad, normed, g, *turns, w["rows"]], [w["qkv"], w["up"]],
        scratch=[pltpu.VMEM((rows, dim), F32), pltpu.VMEM((LINES, ONE), F32)],
        flops=2 * rows * dim * (units + 3 * ONE) + 12 * rows * dim,
    )


LINES = 64


def join_forward(at, x_piece, parts, w):
    def body(at, x, vectors, own, *rest):
        total = x[...].astype(F32) + own[...].astype(F32) + vectors[4:5]
        for piece in rest[:-1]:
            total = total + piece[...].astype(F32)
        rest[-1][...] = total.astype(B16)

    return kernel_call_named("join_forward", body, [(x_piece.shape, B16)], at, x_piece, w["rows"], *parts)[0]


def join_backward(at, g_piece, x_piece, parts):
    dim = x_piece.shape[1]

    def body(at, g, x, own, *rest):
        total = own[...]
        for piece in rest[:-1]:
            total = total + piece[...].astype(F32)
        hidden = x[...].astype(F32)
        centre = hidden - jnp.sum(hidden, axis=1, keepdims=True) * (1.0 / dim)
        var = jnp.sum(centre * centre, axis=1, keepdims=True) * (1.0 / dim)
        scale = lax.rsqrt(var + 1e-05)
        normed = centre * scale
        inner = (
            total
            - jnp.sum(total, axis=1, keepdims=True) * (1.0 / dim)
            - normed * (jnp.sum(total * normed, axis=1, keepdims=True) * (1.0 / dim))
        )
        rest[-1][...] = (g[...].astype(F32) + scale * inner).astype(B16)

    return kernel_call_named("join_backward", body, [(x_piece.shape, B16)], at, g_piece, x_piece, *parts)[0]


def columns(at, ref, core, high):
    which = at[S_CORE] ^ core
    return jnp.concatenate(
        [
            ref[:, pl.ds(pl.multiple_of((4 * high + 2 * low + which) * ONE, ONE), ONE)]
            for low in range(2)
        ],
        axis=1,
    )


def early_grads(at, active, mixed, mlp_in, up_grad, g):
    rows, dim = g.shape
    units = active.shape[1]
    tiles = units // ONE

    def body(at, active, mixed, mlp_in, up_grad, g, keep, give):
        for core, target in ((0, keep), (1, give)):
            for high in range(2):
                strip = columns(at, g, core, high)
                down = tn(active[...], strip).astype(B16)
                out = tn(mixed[...], strip).astype(B16)
                up = tn(columns(at, mlp_in, core, high), up_grad[...]).astype(B16)
                for low in range(2):
                    lanes = slice(low * ONE, (low + 1) * ONE)
                    where = (at[S_HALF] ^ high, at[S_NEAR] ^ low)
                    target[where[0], where[1], :units] = down[:, lanes]
                    target[where[0], where[1], units : units + ONE] = out[:, lanes]
                    for i in range(tiles):
                        base = units + (1 + i) * ONE
                        target[where[0], where[1], base : base + ONE] = up[
                            lanes, i * ONE : (i + 1) * ONE
                        ]

    shape = (2, 2, 2 * units + ONE, ONE)
    return kernel_call_named(
        "early_grads",
        body, [(shape, B16)] * 2, at, active, mixed, mlp_in, up_grad, g,
        flops=2 * rows * dim * (2 * units + ONE),
    )


def late_grads(at, attn_in, qkv_grad, tables):
    rows, dim = attn_in.shape
    count = len(tables)

    def body(at, attn_in, qkv_grad, *refs):
        tables, (keep, give) = refs[:count], refs[count:]
        for core, target in ((0, keep), (1, give)):
            for high in range(2):
                qkv = tn(columns(at, attn_in, core, high), qkv_grad[...]).astype(B16)
                for low in range(2):
                    where = (at[S_HALF] ^ high, at[S_NEAR] ^ low)
                    for i in range(3):
                        target[where[0], where[1], i * ONE : (i + 1) * ONE] = qkv[
                            low * ONE : (low + 1) * ONE, i * ONE : (i + 1) * ONE
                        ]
                    for i, table in enumerate(tables):
                        base = 3 * ONE + i * LINES
                        target[where[0], where[1], base : base + LINES] = table[...]

    shape = (2, 2, 3 * ONE + count * LINES, ONE)
    return kernel_call_named(
        "late_grads", body, [(shape, B16)] * 2, at, attn_in, qkv_grad, *tables,
        flops=2 * rows * dim * 3 * ONE,
    )


def plus(a, b):
    return (a.astype(F32) + b.astype(F32)).astype(B16)


def summed_cores(keep, give, *earlier):
    got = swapped(after(give, *earlier), CORE)
    return (
        [plus(keep[0, i], got[0, i]) for i in range(2)],
        [plus(keep[1, i], got[1, i]) for i in range(2)],
    )


def sum_lines(at, late):
    def body(at, *refs):
        *late, lines = refs
        total = 0.0
        for part in late:
            total = total + part[3 * ONE : 3 * ONE + lines.shape[0]].astype(F32)
        lines[...] = total

    return kernel_call_named("sum_lines", body, [((32, ONE), F32)], at, *late)[0]


def unpack_grads(at, early, late, sizes):
    dim_part, units, heads = ONE, sizes["units"], ONE

    def body(at, *refs):
        early, late = refs[:4], refs[4:8]
        qkv, out, up, down, b_qkv, b_up, branch = refs[8:]
        index = at[S_OWN]
        for j, (wide, narrow) in enumerate(zip(early, late)):
            source = index ^ (2 * (j % 2) + j // 2)
            place = pl.multiple_of(source * units, units)
            small = pl.multiple_of(source * ONE, ONE)
            down[pl.ds(place, units)] = wide[:units].astype(F32)
            out[pl.ds(small, ONE)] = wide[units : units + ONE].astype(F32)
            for i in range(units // ONE):
                base = units + (1 + i) * ONE
                up[:, pl.ds(place + i * ONE, ONE)] = wide[base : base + ONE].astype(F32)
            for i in range(3):
                qkv[i, :, pl.ds(small, ONE)] = narrow[i * ONE : (i + 1) * ONE].astype(F32)
            table = narrow[3 * ONE :].astype(F32)
            for i in range(units // ONE):
                b_up[:, pl.ds(place + i * ONE, ONE)] = table[40 + i : 41 + i]
            for i in range(3):
                b_qkv[i : i + 1, pl.ds(small, ONE)] = table[40 + units // ONE + i :][:1]
            if j == 0:
                branch[...] = table[32:40]

    outs = [
        ((3, dim_part, 4 * heads), F32),
        ((4 * heads, dim_part), F32),
        ((dim_part, 4 * units), F32),
        ((4 * units, dim_part), F32),
        ((3, 4 * heads), F32),
        ((1, 4 * units), F32),
        ((8, ONE), F32),
    ]
    return kernel_call_named("unpack_grads", body, outs, at, *early, *late, keep=False)


def cube_device(
    inputs, cotangent, ln1_gain, ln1_bias, ln2_gain, ln2_bias, qkv_weight, qkv_bias,
    out_weight, up_weight, up_bias, down_weight, branch_bias,
):
    at = where_am_i()
    section, half, side = [lax.axis_index("section"), lax.axis_index("ctx") // 4, lax.axis_index("tp")]
    at, is_first, is_low, is_left, is_near = lax.optimization_barrier(
        (at, section == 0, half == 0, side == 0, section == half)
    )
    dim = inputs.shape[2]
    rows = 4 * inputs.shape[1]
    vectors = (ln1_gain, ln1_bias, ln2_gain, ln2_bias, branch_bias, up_bias, qkv_bias)

    mine, strip, sent_qkv = pack_first(at, inputs, vectors, qkv_weight)
    g_mine, g_strip, sent_up, sent_down = pack_second(
        at, cotangent, up_weight, out_weight, down_weight
    )
    strips = send_strips(strip)
    turns = turn_tables(at, rows)
    sides = [swapped(after(part, turns[0]), SIDE) for part in strips]
    x_parts = (mine, swapped(mine, NEAR), *strips, *sides)
    got_qkv, layers = first_weights(at, vectors, qkv_weight, sent_qkv)
    got_up = swapped(after(sent_up, got_qkv), SECTION)
    first, second = layers
    got_down = swapped(
        after(sent_down, got_up, *x_parts[4:], first["qkv"], first["rows"]), SECTION
    )

    def bring_up(*earlier):
        up = up_weights(at, up_weight, got_up, swapped(after(got_up, *earlier), CORE))
        for i, layer in enumerate(layers):
            layer.update(up=up[i], units=up[i].shape[1])

    def bring_rows(*earlier):
        tall = row_weights(
            at, down_weight, out_weight, got_down, swapped(after(got_down, *earlier), CORE)
        )
        for i, layer in enumerate(layers):
            layer.update(down=tall[i], out=tall[2 + i])

    def forward(loader, sources, w, with_piece):
        got = front(at, loader, sources, w, turns, with_piece)
        attn_in, mlp_in, normed, q, kv = got[:5]
        kv_other = swapped(kv, CORE)
        is_start = "up" not in w
        if is_start:
            bring_up(q)
        active, slope = units_forward(at, mlp_in, w)
        mixed, lse = attention_forward(at, q, kv, kv_other)
        if is_start:
            bring_rows(active, mixed)
        pieces = outputs_forward(at, mixed, active, w)
        saved = dict(
            attn_in=attn_in, mlp_in=mlp_in, normed=normed, q=q, kv=kv, kv_other=kv_other,
            active=active, slope=slope, mixed=mixed, lse=lse,
        )
        return pieces, saved, got[5:]

    def backward(loader, sources, saved, w, with_piece):
        made = units_backward(at, loader, sources, saved["slope"], w, with_piece)
        g, up_grad, mixed_grad = made[:3]
        dq, dkv, dkv_other = attention_backward(
            at, saved["q"], saved["kv"], saved["kv_other"], saved["lse"], mixed_grad
        )
        dkv_got = swapped(dkv_other, CORE)
        early = early_grads(
            at, saved["active"], saved["mixed"], saved["mlp_in"], up_grad, after(g, dkv_other)
        )
        given = (after(dq, early[0]), dkv, dkv_got, up_grad, saved["normed"], g)
        return early, given, made[3:]

    def backward_end(given, saved, w):
        out = inputs_backward(at, *given, turns, w)
        return out[0], out[1], out[2:]

    parts, saved_first, (x_piece,) = forward(start_loader, x_parts, first, True)
    strips = send_strips(after(g_strip, parts[0]))
    parts = exchanged(parts)
    parts[0] = after(parts[0], *strips)
    keep, give = fold(at, parts)
    sides = [swapped(part, SIDE) for part in strips]
    piece = join_forward(at, x_piece, [keep, swapped(give, NEAR)], first)
    near = after(swapped(piece, NEAR), *sides)
    middle = gathered(piece, near)
    g_near = swapped(after(g_mine, near), NEAR)
    middle[0] = after(middle[0], g_near)
    g_parts = (g_mine, g_near, *strips, *sides)

    parts_last, saved_second, blocks = forward(piece_loader, middle, second, False)
    acts_mine, acts_give = blocks

    early, given, (g_piece,) = backward(start_loader, g_parts, saved_second, second, True)
    early_keep, early_give = summed_cores(*early, given[2])
    qkv_grad, table_second, pieces = backward_end(given, saved_second, second)
    late = late_grads(at, saved_second["attn_in"], qkv_grad, ())
    parts = exchanged(pieces)
    far_second = swapped(early_give[1], HALF)
    parts[0] = after(parts[0], far_second, *late)
    keep, give = fold(at, parts)
    late_keep, late_give = summed_cores(*late)
    late_got = swapped(after(jnp.stack(late_give), give), HALF)
    parts_last = exchanged([after(p, give) for p in parts_last])
    back = join_backward(at, g_piece, piece, [keep, swapped(give, NEAR)])
    near = after(swapped(back, NEAR), late_got, *parts_last)
    g_middle = gathered(back, near)
    close_second = swapped(after(early_give[0], near), HALF)
    g_middle[0] = after(g_middle[0], close_second)
    keep_last, give_last = fold(at, parts_last)

    early, given, blocks = backward(piece_loader, g_middle, saved_first, first, False)
    in_mine, in_give = blocks
    early_second = [plus(a, b) for a, b in zip(early_keep, (close_second, far_second))]
    late_second = [plus(a, b) for a, b in zip(late_keep, late_got)]
    early_keep, early_give = summed_cores(*early, given[2])
    given = (after(given[0], *early_give),) + given[1:]
    qkv_grad, table_first, pieces = backward_end(given, saved_first, first)
    parts = exchanged(pieces)
    far_first = swapped(early_give[1], HALF)
    late = late_grads(at, saved_first["attn_in"], qkv_grad, (table_first, table_second))
    parts[0] = after(parts[0], far_first)
    keep, give = fold(at, parts)
    close_first = swapped(after(early_give[0], give), HALF)
    late_keep, late_give = summed_cores(*late)
    late_got = swapped(after(jnp.stack(late_give), give), HALF)
    back_last = join_backward(
        at, back, x_piece, [keep, after(swapped(give, NEAR), close_first)]
    )
    last = join_forward(at, piece, [keep_last, swapped(after(give_last, give), NEAR)], second)
    early_first = [plus(a, b) for a, b in zip(early_keep, (close_first, far_first))]
    late_first = [plus(a, b) for a, b in zip(late_keep, late_got)]
    tall = 3 * ONE + LINES
    late_second = [
        jnp.concatenate([a, b[tall:]], axis=0) for a, b in zip(late_second, late_first)
    ]
    late_first = [a[:tall] for a in late_first]
    def brought(close, far):
        own = jnp.where(is_first, close[0], close[1])
        near = swapped(jnp.where(is_first, far[0], far[1]), NEAR)
        got = swapped(jnp.where(is_first, close[1], close[0]), SECTION)
        cross = swapped(jnp.where(is_first, far[1], far[0]), SECTION | NEAR)
        return own, got, near, cross

    early, late = [
        brought((one[0], two[0]), (one[1], two[1]))
        for one, two in ((early_first, early_second), (late_first, late_second))
    ]
    lines = sum_lines(at, late)
    lines = lines + swapped(lines, SIDE)
    sizes = dict(units=up_weight.shape[2] // 4)
    qkv, out, up, down, b_qkv, b_up, branch = unpack_grads(at, early, late, sizes)

    mine = jnp.where(is_first, back_last, last)
    got = swapped(jnp.where(is_first, last, back_last), SECTION)
    stay = jnp.where(is_near, mine, got)
    known_give = jnp.where(is_first, acts_give, in_give)
    other = swapped(jnp.stack([jnp.where(is_near, got, mine), known_give]), HALF)
    own = jnp.stack(
        [jnp.where(is_low, stay, other[0]), jnp.where(is_low, other[0], stay), other[1]]
    )
    rest = swapped(own, SIDE)
    both = jnp.where(
        is_left, jnp.concatenate([own, rest], axis=1), jnp.concatenate([rest, own], axis=1)
    )
    new = both[:2]
    known_mine = jnp.where(is_first, acts_mine, in_mine)
    known = jnp.where(
        is_low, jnp.stack([known_mine, both[2]]), jnp.stack([both[2], known_mine])
    )
    acts = jnp.where(is_first, known, new)
    in_grads = jnp.where(is_first, new, known)

    lines = lines.reshape(4, dim)
    return (
        acts[None],
        in_grads[None],
        lines[0:1],
        lines[1:2],
        lines[2:3],
        lines[3:4],
        qkv[None],
        b_qkv[None],
        out[None],
        up[None],
        b_up,
        down[None],
        branch.reshape(1, dim),
    )


def placed_program(mesh, device_program):
    placed = (
        P(None, "ctx", None),
        P(None, "ctx", None),
        P("section", None),
        P("section", None),
        P("section", None),
        P("section", None),
        P("section", None, None, "tp"),
        P("section", None, "tp"),
        P("section", "tp", None),
        P("section", None, "tp"),
        P("section", "tp"),
        P("section", "tp", None),
        P("section", None),
    )
    return jax.shard_map(
        device_program,
        mesh=mesh,
        in_specs=placed,
        out_specs=(
            P("section", None, "ctx", None),
            P("section", None, "ctx", None),
            P("section", None),
            P("section", None),
            P("section", None),
            P("section", None),
            P("section", None, "ctx", "tp"),
            P("section", None, "tp"),
            P("section", "tp", "ctx"),
            P("section", "ctx", "tp"),
            P("section", "tp"),
            P("section", "tp", "ctx"),
            P("section", None),
        ),
        check_vma=False,
    )


def solution(mesh):
    sizes = dict(mesh.shape)
    if sizes["section"] == 2 and sizes["tp"] == 2 and sizes["ctx"] == 8:
        return placed_program(mesh, cube_device)
    return placed_program(mesh, per_device)
```

```python
import math

import jax
import jax.numpy as jnp
from jax import lax
from jax.experimental import pallas as pl
from jax.experimental.pallas import tpu as pltpu
from jax.sharding import PartitionSpec as P

HD = 64
ROT = 16


def shifted(shard, axis, by):
    peers = lax.axis_size(axis)
    pairs = [(i, i + by) for i in range(peers) if 0 <= i + by < peers]
    return lax.ppermute(shard, axis, pairs)


def tables(positions):
    freqs = 1.0 / 10000.0 ** (jnp.arange(0, ROT, 2).astype(jnp.float32) / ROT)
    angles = positions.astype(jnp.float32)[:, None] * freqs[None, :]
    return (jnp.cos(angles)[:, None, :], jnp.sin(angles)[:, None, :])


def rotate(field, cosine, sine):
    half_rot = ROT // 2
    front = field[..., :half_rot]
    second = field[..., half_rot:ROT]
    return jnp.concatenate(
        [front * cosine - second * sine, second * cosine + front * sine, field[..., ROT:]], axis=-1
    )


def norms(hidden, gain_one, shift_one, gain_two, shift_two):
    centre = hidden - jnp.mean(hidden, axis=-1, keepdims=True)
    normed = centre * lax.rsqrt(jnp.mean(centre * centre, axis=-1, keepdims=True) + 1e-05)
    return (normed * gain_one + shift_one, normed * gain_two + shift_two)


def gelu_exact(value):
    return jax.nn.gelu(value, approximate=False)


def scores_of(queries, keys, query_pos, score_scale):
    raw = jnp.einsum("qhd,khd->hqk", queries, keys, preferred_element_type=jnp.float32)
    key_pos = jnp.arange(keys.shape[0], dtype=jnp.int32)
    return jnp.where(
        key_pos[None, None, :] <= query_pos[None, :, None], raw * score_scale, -1000000000.0
    )


def forward_layer(layer_in, weights, query_pos, cosine, sine):
    gains, w_qkv, b_qkv, w_out, w_up, b_up, w_down, b_branch = weights
    hidden = layer_in.astype(jnp.float32)
    attn_norm, mlp_norm = norms(hidden, gains[0], gains[1], gains[2], gains[3])
    attn_in = attn_norm.astype(jnp.bfloat16)
    mlp_in = mlp_norm.astype(jnp.bfloat16)
    projected = (
        jnp.einsum("td,cdf->tcf", attn_in, w_qkv, preferred_element_type=jnp.float32) + b_qkv
    )
    row_count = hidden.shape[0]
    feat_width = projected.shape[2]
    head_count = feat_width // HD
    queries = rotate(projected[:, 0].reshape(row_count, head_count, HD), cosine, sine).astype(
        jnp.bfloat16
    )
    key_flat = (
        rotate(projected[:, 1].reshape(row_count, head_count, HD), cosine, sine)
        .astype(jnp.bfloat16)
        .reshape(row_count, feat_width)
    )
    value_flat = projected[:, 2].astype(jnp.bfloat16)
    all_keys, all_values = (
        lax.all_gather(key_flat, "ctx", axis=0, tiled=True),
        lax.all_gather(value_flat, "ctx", axis=0, tiled=True),
    )
    key_count = all_keys.shape[0]
    score_scale = 1.0 / math.sqrt(HD)
    scores = scores_of(queries, all_keys.reshape(key_count, head_count, HD), query_pos, score_scale)
    row_max = jnp.max(scores, axis=-1, keepdims=True)
    exponent = jnp.exp(scores - row_max)
    summed = jnp.sum(exponent, axis=-1, keepdims=True)
    probability = (exponent / summed).astype(jnp.bfloat16)
    log_total = row_max + jnp.log(summed)
    mixed = jnp.einsum(
        "hqk,khd->qhd",
        probability,
        all_values.reshape(key_count, head_count, HD),
        preferred_element_type=jnp.float32,
    )
    mixed = mixed.reshape(row_count, feat_width).astype(jnp.bfloat16)
    partial_out = jnp.dot(mixed, w_out, preferred_element_type=jnp.float32)
    up_value = jnp.dot(mlp_in, w_up, preferred_element_type=jnp.float32) + b_up
    active = gelu_exact(up_value).astype(jnp.bfloat16)
    partial_out = partial_out + jnp.dot(active, w_down, preferred_element_type=jnp.float32)
    branches = lax.psum(partial_out, "tp")
    layer_out = (hidden + branches + b_branch).astype(jnp.bfloat16)
    stored = (key_flat, value_flat)
    saved = (layer_in, queries, stored, log_total, mixed, up_value, active)
    return (layer_out, saved)


def backward_layer(grad_out, saved, weights, query_pos, cosine, sine):
    gains, w_qkv, b_qkv, w_out, w_up, b_up, w_down, b_branch = weights
    layer_in, queries, stored, log_total, mixed, up_value, active = saved
    grad_full = grad_out.astype(jnp.float32)
    row_count, feat_width = mixed.shape
    head_count = feat_width // HD
    hidden = layer_in.astype(jnp.float32)
    norm_pair, norm_back = jax.vjp(norms, hidden, gains[0], gains[1], gains[2], gains[3])
    attn_in = norm_pair[0].astype(jnp.bfloat16)
    mlp_in = norm_pair[1].astype(jnp.bfloat16)
    active_grad = jnp.einsum("td,fd->tf", grad_out, w_down, preferred_element_type=jnp.float32)
    grad_down = jnp.einsum("tf,td->fd", active, grad_out, preferred_element_type=jnp.float32)
    gelu_back = jax.vjp(gelu_exact, up_value)[1]
    up_grad = gelu_back(active_grad)[0].astype(jnp.bfloat16)
    grad_up_bias = jnp.sum(up_grad.astype(jnp.float32), axis=0)
    grad_up = jnp.einsum("td,tf->df", mlp_in, up_grad, preferred_element_type=jnp.float32)
    mlp_in_grad = jnp.einsum("tf,df->td", up_grad, w_up, preferred_element_type=jnp.float32)
    mixed_grad = jnp.einsum(
        "td,fd->tf", grad_out, w_out, preferred_element_type=jnp.float32
    ).astype(jnp.bfloat16)
    grad_out_weight = jnp.einsum("tf,td->fd", mixed, grad_out, preferred_element_type=jnp.float32)
    all_keys, all_values = (
        lax.all_gather(stored[0], "ctx", axis=0, tiled=True),
        lax.all_gather(stored[1], "ctx", axis=0, tiled=True),
    )
    key_count = all_keys.shape[0]
    keys_heads = all_keys.reshape(key_count, head_count, HD)
    values_heads = all_values.reshape(key_count, head_count, HD)
    score_scale = 1.0 / math.sqrt(HD)
    scores = scores_of(queries, keys_heads, query_pos, score_scale)
    probability = jnp.exp(scores - log_total)
    heads_grad = mixed_grad.reshape(row_count, head_count, HD)
    prob_grad = jnp.einsum(
        "qhd,khd->hqk", heads_grad, values_heads, preferred_element_type=jnp.float32
    )
    centre = jnp.sum(probability * prob_grad, axis=-1, keepdims=True)
    score_grad = (score_scale * probability * (prob_grad - centre)).astype(jnp.bfloat16)
    query_grad = jnp.einsum(
        "hqk,khd->qhd", score_grad, keys_heads, preferred_element_type=jnp.float32
    )
    value_terms = jnp.einsum(
        "hqk,qhd->khd",
        probability.astype(jnp.bfloat16),
        heads_grad,
        preferred_element_type=jnp.float32,
    )
    key_terms = jnp.einsum("hqk,qhd->khd", score_grad, queries, preferred_element_type=jnp.float32)
    key_grad, value_grad = (
        lax.psum_scatter(
            key_terms.reshape(key_count, feat_width), "ctx", scatter_dimension=0, tiled=True
        ),
        lax.psum_scatter(
            value_terms.reshape(key_count, feat_width), "ctx", scatter_dimension=0, tiled=True
        ),
    )
    query_grad = rotate(query_grad, cosine, -sine).reshape(row_count, feat_width)
    key_grad = rotate(key_grad.reshape(row_count, head_count, HD), cosine, -sine).reshape(
        row_count, feat_width
    )
    qkv_grad = jnp.stack([query_grad, key_grad, value_grad], axis=1).astype(jnp.bfloat16)
    grad_qkv_bias = jnp.sum(qkv_grad.astype(jnp.float32), axis=0)
    grad_qkv = jnp.einsum("td,tcf->cdf", attn_in, qkv_grad, preferred_element_type=jnp.float32)
    attn_in_grad = jnp.einsum("tcf,cdf->td", qkv_grad, w_qkv, preferred_element_type=jnp.float32)
    attn_in_grad, mlp_in_grad = lax.psum((attn_in_grad, mlp_in_grad), "tp")
    hidden_grad, gain_one_grad, shift_one_grad, gain_two_grad, shift_two_grad = norm_back(
        (attn_in_grad, mlp_in_grad)
    )
    input_grad = (grad_full + hidden_grad).astype(jnp.bfloat16)
    grad_branch = jnp.sum(grad_full, axis=0)
    grads = (
        gain_one_grad,
        shift_one_grad,
        gain_two_grad,
        shift_two_grad,
        grad_qkv,
        grad_qkv_bias,
        grad_out_weight,
        grad_up,
        grad_up_bias,
        grad_down,
        grad_branch,
    )
    return (input_grad, grads)


def per_device(
    inputs,
    cotangent,
    ln1_gain,
    ln1_bias,
    ln2_gain,
    ln2_bias,
    qkv_weight,
    qkv_bias,
    out_weight,
    up_weight,
    up_bias,
    down_weight,
    branch_bias,
):
    gains = (
        ln1_gain[0].astype(jnp.float32),
        ln1_bias[0].astype(jnp.float32),
        ln2_gain[0].astype(jnp.float32),
        ln2_bias[0].astype(jnp.float32),
    )
    weights = (
        gains,
        qkv_weight[0],
        qkv_bias[0].astype(jnp.float32),
        out_weight[0],
        up_weight[0],
        up_bias[0].astype(jnp.float32),
        down_weight[0],
        branch_bias[0].astype(jnp.float32),
    )
    micro_count = inputs.shape[0]
    row_count = inputs.shape[1]
    query_pos = lax.axis_index("ctx") * row_count + jnp.arange(row_count, dtype=jnp.int32)
    cosine, sine = tables(query_pos)
    at_first = lax.axis_index("section") == 0
    blank = jnp.zeros_like(inputs[0])
    received = blank
    outputs_list = []
    saved_list = []
    for step_index in range(micro_count + 1):
        fresh = inputs[step_index] if step_index < micro_count else blank
        layer_in = jnp.where(at_first, fresh, received)
        layer_out, saved = forward_layer(layer_in, weights, query_pos, cosine, sine)
        outputs_list.append(layer_out)
        saved_list.append(saved)
        if step_index < micro_count:
            received = shifted(layer_out, "section", 1)
    returned = blank
    grad_list = []
    sums = None
    for back_index in range(micro_count + 1):
        batch_index = micro_count - 1 - back_index
        given = cotangent[batch_index] if batch_index >= 0 else blank
        grad_in = jnp.where(at_first, returned, given)
        input_grad, grads = backward_layer(
            grad_in, saved_list[micro_count - back_index], weights, query_pos, cosine, sine
        )
        sums = grads if sums is None else jax.tree.map(jnp.add, sums, grads)
        grad_list.append(input_grad)
        if back_index < micro_count:
            returned = shifted(input_grad, "section", -1)
    acts = jnp.stack(
        [jnp.where(at_first, outputs_list[j], outputs_list[j + 1]) for j in range(micro_count)]
    )[None]
    in_grads = jnp.stack(
        [
            jnp.where(at_first, grad_list[micro_count - j], grad_list[micro_count - 1 - j])
            for j in range(micro_count)
        ]
    )[None]
    (
        gain_one_grad,
        shift_one_grad,
        gain_two_grad,
        shift_two_grad,
        grad_qkv,
        grad_qkv_bias,
        grad_out_weight,
        grad_up,
        grad_up_bias,
        grad_down,
        grad_branch,
    ) = sums
    qkv_part, out_part, up_part, down_part = (
        lax.psum_scatter(
            grad_qkv[None].astype(jnp.bfloat16), "ctx", scatter_dimension=2, tiled=True
        ).astype(jnp.float32),
        lax.psum_scatter(
            grad_out_weight[None].astype(jnp.bfloat16), "ctx", scatter_dimension=2, tiled=True
        ).astype(jnp.float32),
        lax.psum_scatter(
            grad_up[None].astype(jnp.bfloat16), "ctx", scatter_dimension=1, tiled=True
        ).astype(jnp.float32),
        lax.psum_scatter(
            grad_down[None].astype(jnp.bfloat16), "ctx", scatter_dimension=2, tiled=True
        ).astype(jnp.float32),
    )
    small_sums = (
        lax.psum(gain_one_grad[None].astype(jnp.bfloat16), "ctx").astype(jnp.float32),
        lax.psum(shift_one_grad[None].astype(jnp.bfloat16), "ctx").astype(jnp.float32),
        lax.psum(gain_two_grad[None].astype(jnp.bfloat16), "ctx").astype(jnp.float32),
        lax.psum(shift_two_grad[None].astype(jnp.bfloat16), "ctx").astype(jnp.float32),
        lax.psum(grad_qkv_bias[None].astype(jnp.bfloat16), "ctx").astype(jnp.float32),
        lax.psum(grad_up_bias[None].astype(jnp.bfloat16), "ctx").astype(jnp.float32),
        lax.psum(grad_branch[None].astype(jnp.bfloat16), "ctx").astype(jnp.float32),
    )
    return (
        acts,
        in_grads,
        small_sums[0],
        small_sums[1],
        small_sums[2],
        small_sums[3],
        qkv_part,
        small_sums[4],
        out_part,
        up_part,
        small_sums[5],
        down_part,
        small_sums[6],
    )


ALL = ("section", "ctx", "tp")
SECTION, HALF, NEAR, CORE, SIDE = 16, 8, 4, 2, 1
CHIPS = (0, SIDE, NEAR, NEAR | SIDE, SECTION, SECTION | SIDE, SECTION | NEAR, SECTION | NEAR | SIDE)
F32, B16 = jnp.float32, jnp.bfloat16
ONE = 128
S_SECTION, S_HALF, S_NEAR, S_CORE, S_SIDE, S_CHIP, S_OWN, S_GIVE = range(8)


def swapped(array, mask, section=None):
    pairs = [(i, i ^ mask) for i in range(32) if section is None or i // 16 == section]
    return lax.ppermute(array, ALL, pairs)


def after(array, *earlier):
    return lax.optimization_barrier((array,) + earlier)[0]


def where_am_i():
    section = lax.axis_index("section")
    ctx = lax.axis_index("ctx")
    side = lax.axis_index("tp")
    half, near, core = ctx // 4, (ctx // 2) % 2, ctx % 2
    chip = 4 * section + 2 * near + side
    own, give = 2 * section + near, 2 * (1 - section) + near
    return jnp.stack([section, half, near, core, side, chip, own, give]).astype(jnp.int32)


def in_hbm(arrays):
    return [pltpu.with_memory_space_constraint(a, pltpu.HBM) for a in arrays]


def kernel_call(body, outs, at, *arrays, hbm=(), scratch=(), flops=0, exps=0, name=None, keep=True):
    moved = sum(a.size * a.dtype.itemsize for a in arrays)
    moved += sum(math.prod(s) * jnp.dtype(d).itemsize for s, d in outs)
    return pl.pallas_call(
        body,
        name=name,
        out_shape=[(pltpu.VMEM if keep else jax.ShapeDtypeStruct)(s, d) for s, d in outs],
        in_specs=[pl.BlockSpec(memory_space=pltpu.SMEM)]
        + [pl.BlockSpec(memory_space=pltpu.VMEM)] * len(arrays)
        + [pl.BlockSpec(memory_space=pltpu.HBM)] * len(hbm),
        out_specs=[pl.BlockSpec(memory_space=pltpu.VMEM)] * len(outs),
        scratch_shapes=list(scratch),
        compiler_params=pltpu.CompilerParams(vmem_limit_bytes=VMEM_BYTES),
        cost_estimate=pl.CostEstimate(flops=0, bytes_accessed=0, transcendentals=0),
    )(at, *arrays, *in_hbm(hbm))


VMEM_BYTES = 12 * 1024 * 1024


def kernel_call_named(name, *args, **kwargs):
    return kernel_call(*args, name=name, **kwargs)


def by_rows(rows, step, do):
    def one(i, _):
        do(pl.ds(pl.multiple_of(i * step, step), step))
        return 0

    lax.fori_loop(0, rows // step, one, 0)


def nn(a, b):
    return jnp.dot(a, b, preferred_element_type=F32)


def nt(a, b):
    return lax.dot_general(a, b, (((1,), (1,)), ((), ())), preferred_element_type=F32)


def tn(a, b):
    return lax.dot_general(a, b, (((0,), (0,)), ((), ())), preferred_element_type=F32)


def copy_kernel(name, body, outs, at, arrays, scratch):
    return pl.pallas_call(
        body,
        name=name,
        out_shape=[jax.ShapeDtypeStruct(s, B16) for s in outs],
        in_specs=[pl.BlockSpec(memory_space=pltpu.SMEM)]
        + [pl.BlockSpec(memory_space=pltpu.HBM)] * len(arrays),
        out_specs=[pl.BlockSpec(memory_space=pltpu.HBM)] * len(outs),
        scratch_shapes=list(scratch),
        compiler_params=pltpu.CompilerParams(vmem_limit_bytes=VMEM_BYTES),
        cost_estimate=pl.CostEstimate(flops=0, bytes_accessed=0, transcendentals=0),
    )(at, *in_hbm(arrays))


def token_copies(at, array, mine, strip, sems):
    width = strip.shape[1]
    lanes = pl.ds(pl.multiple_of(at[S_SIDE] * width, width), width)
    return [
        pltpu.make_async_copy(array.at[at[S_HALF]], mine, sems.at[0]),
        pltpu.make_async_copy(array.at[1 - at[S_HALF], :, lanes], strip, sems.at[1]),
    ]


def token_shapes(array):
    _, rows, dim = array.shape
    return [(rows, dim), (rows, dim // 2)]


def send_strips(strip):
    return swapped(strip, HALF), swapped(strip, HALF | NEAR)


def start_loader(at, refs):
    mine, near, far, far_near, far_rest, far_near_rest = refs
    first = at[S_SIDE] == 0
    index = 2 * at[S_HALF] + at[S_NEAR]

    def whole(strip, rest):
        a, b = strip[...], rest[...]
        return jnp.concatenate([jnp.where(first, a, b), jnp.where(first, b, a)], axis=1)

    yield index, mine[...]
    yield index ^ 1, near[...]
    yield index ^ 2, whole(far, far_rest)
    yield index ^ 3, whole(far_near, far_near_rest)


def piece_loader(at, refs):
    for step, ref in zip(STEPS, refs):
        for i in range(2):
            yield at[S_CHIP] ^ (step | 2 * i), ref[i]


def run_copies(copies):
    for copy in copies:
        copy.start()
    for copy in copies:
        copy.wait()


def pack_first(at, tokens, vectors, w_qkv):
    _, three, dim, wide = w_qkv.shape
    heads, side = wide // 4, dim // 2
    count = len(vectors)

    def body(at, tokens, w_qkv, *refs):
        lines = refs[:count]
        mine, strip, packed, table, rounded, sems = refs[count : count + 6]
        held = refs[count + 6 :]
        rows = pl.ds(pl.multiple_of(at[S_CORE] * side, side), side)
        lanes = pl.ds(pl.multiple_of(at[S_GIVE] * heads, heads), heads)
        copies = token_copies(at, tokens, mine, strip, sems)
        for i in range(three):
            copies.append(
                pltpu.make_async_copy(
                    w_qkv.at[0, i, rows, lanes], packed.at[i * side : (i + 1) * side], sems.at[2 + i]
                )
            )
        loads = [
            pltpu.make_async_copy(line, hold, sems.at[6 + i])
            for i, (line, hold) in enumerate(zip(lines, held))
        ]
        for copy in copies:
            copy.start()
        run_copies(loads)
        fill_table(table, at[S_GIVE], held)
        rounded[...] = table[...].astype(B16)
        run_copies([pltpu.make_async_copy(rounded, packed.at[three * side :], sems.at[5])])
        for copy in copies:
            copy.wait()

    return copy_kernel(
        "pack_first", body, token_shapes(tokens) + [(three * side + TABLE, ONE)], at,
        [tokens, w_qkv, *vectors],
        [pltpu.VMEM((TABLE, ONE), F32), pltpu.VMEM((TABLE, ONE), B16), pltpu.SemaphoreType.DMA((6 + count,))]
        + [pltpu.VMEM(v.shape, B16) for v in vectors],
    )


def pack_second(at, tokens, w_up, w_out, w_down):
    dim, units, heads = w_up.shape[1], w_up.shape[2] // 4, w_out.shape[1] // 4
    side = dim // 2

    def body(at, tokens, w_up, w_out, w_down, mine, strip, up, down, sems):
        copies = token_copies(at, tokens, mine, strip, sems)
        rows = pl.ds(pl.multiple_of(at[S_CORE] * side, side), side)
        lanes = pl.ds(pl.multiple_of(at[S_GIVE] * units, units), units)
        copies.append(pltpu.make_async_copy(w_up.at[0, rows, lanes], up, sems.at[2]))
        part = 2 * at[S_GIVE] + at[S_CORE]
        for i, (source, size, start) in enumerate(
            ((w_down, units // 2, 0), (w_out, heads // 2, units // 2))
        ):
            rows = pl.ds(pl.multiple_of(part * size, size), size)
            copies.append(
                pltpu.make_async_copy(
                    source.at[0, rows], down.at[start : start + size], sems.at[3 + i]
                )
            )
        run_copies(copies)

    return copy_kernel(
        "pack_second", body, token_shapes(tokens) + [(side, units), ((units + heads) // 2, dim)], at,
        [tokens, w_up, w_out, w_down], [pltpu.SemaphoreType.DMA((5,))],
    )


def fill_table(table, index, vectors):
    *lines, b_up, b_qkv = vectors
    units, heads = b_up.shape[1] // 4, b_qkv.shape[2] // 4
    table[...] = jnp.zeros_like(table)
    row = 0
    for line in lines:
        for i in range(line.shape[1] // ONE):
            table[row : row + 1] = line[:, i * ONE : (i + 1) * ONE].astype(F32)
            row += 1
    for i in range(units // ONE):
        lanes = pl.ds(pl.multiple_of(index * units + i * ONE, ONE), ONE)
        table[row : row + 1] = b_up[:, lanes].astype(F32)
        row += 1
    few = b_qkv[0, :, pl.ds(pl.multiple_of(index * heads, ONE), heads)].astype(F32)
    table[row : row + few.shape[0]] = few


TABLE = 48


def vector_rows(at, vectors, got):
    dim = vectors[0].shape[1]
    units, few = vectors[5].shape[1] // 4, vectors[6].shape[1]

    def body(at, *refs):
        *lines, got, rows0, rows1, table = refs
        fill_table(table, at[S_OWN], lines)
        taken = got[got.shape[0] - TABLE :].astype(F32)
        is_first = at[S_SECTION] == 0
        for rows, lines in (
            (rows0, jnp.where(is_first, table[...], taken)),
            (rows1, jnp.where(is_first, taken, table[...])),
        ):
            rows[...] = jnp.zeros_like(rows)
            line = 0
            for r, tiles in enumerate([dim // ONE] * 5 + [units // ONE, few]):
                for i in range(tiles):
                    rows[r : r + 1, i * ONE : (i + 1) * ONE] = lines[line : line + 1]
                    line += 1

    return kernel_call_named(
        "vector_rows", body, [((8, dim), F32)] * 2, at, *vectors, got,
        scratch=[pltpu.VMEM((TABLE, ONE), F32)],
    )


def half_rows(at, which, size):
    return pl.ds(pl.multiple_of((at[S_CORE] ^ which) * size, size), size)


def qkv_copies(at, own, got, rest, target):
    three, heads = own.shape[1], own.shape[3] // 4
    side = own.shape[2] // 2
    lanes = pl.ds(pl.multiple_of(at[S_OWN] * heads, heads), heads)
    mine, halves = [], []
    for i in range(three):
        tile = slice(i * heads, (i + 1) * heads)
        mine.append((own.at[0, i, :, lanes], target[0].at[:, tile]))
        for which, source in ((0, got), (1, rest)):
            halves.append(
                (
                    source.at[i * side : (i + 1) * side],
                    target[1].at[half_rows(at, which, side), tile],
                )
            )
    return mine + halves


def up_copies(at, own, got, rest, target):
    side, units = got.shape
    lanes = pl.ds(pl.multiple_of(at[S_OWN] * units, units), units)
    return [(own.at[0, :, lanes], target[0])] + [
        (source, target[1].at[half_rows(at, which, side)])
        for which, source in ((0, got), (1, rest))
    ]


def row_copies(at, own, got, rest, target, start):
    size = target[0].shape[0]
    side = size // 2
    rows = pl.ds(pl.multiple_of(at[S_OWN] * size, size), size)
    return [(own.at[0, rows], target[0])] + [
        (source.at[start : start + side], target[1].at[half_rows(at, which, side)])
        for which, source in ((0, got), (1, rest))
    ]


def choose_weights(name, at, owns, got, rest, shapes, make):
    count = len(owns)

    def body(at, *refs):
        own, (got, rest), targets, sems = refs[:count], refs[count : count + 2], refs[count + 2 : -1], refs[-1]
        for section in range(2):

            @pl.when(at[S_SECTION] == section)
            def _():
                pairs = make(
                    at, own, got, rest,
                    [(targets[2 * i + section], targets[2 * i + 1 - section]) for i in range(count)],
                )
                run_copies(
                    [
                        pltpu.make_async_copy(source, target, sems.at[i])
                        for i, (source, target) in enumerate(pairs)
                    ]
                )

    outs = [(shape, B16) for shape in shapes for _ in range(2)]
    return kernel_call(
        body, outs, at, hbm=[*owns, got, rest],
        scratch=[pltpu.SemaphoreType.DMA((9,))], name=name,
    )


def weights_call(name, body, outs, at, arrays, weights, scratch=(), flops=0, exps=0):
    first, count = len(arrays), len(weights)

    def wrapped(at, *refs):
        given, chosen, rest = refs[:first], refs[first : first + count], refs[first + count :]
        made, own = rest[: len(outs)], rest[len(outs) :]
        body(at, *given, *made, *chosen, *own)

    return kernel_call(
        wrapped, outs, at, *arrays, *weights, scratch=scratch, flops=flops, exps=exps, name=name
    )


def first_weights(at, vectors, w_qkv, sent):
    _, three, dim, wide = w_qkv.shape
    got = swapped(sent, SECTION)
    qkv = choose_weights(
        "choose_qkv", at, [w_qkv], got, swapped(got, CORE), [(dim, three * (wide // 4))],
        lambda at, own, got, rest, to: qkv_copies(at, own[0], got, rest, to[0]),
    )
    return got, [dict(qkv=q, rows=r) for q, r in zip(qkv, vector_rows(at, vectors, got))]


def up_weights(at, w_up, got, rest):
    return choose_weights(
        "choose_up", at, [w_up], got, rest, [(w_up.shape[1], w_up.shape[2] // 4)],
        lambda at, own, got, rest, to: up_copies(at, own[0], got, rest, to[0]),
    )


def row_weights(at, w_down, w_out, got, rest):
    _, tall, dim = w_down.shape
    units, heads = tall // 4, w_out.shape[1] // 4
    return choose_weights(
        "choose_rows", at, [w_down, w_out], got, rest, [(units, dim), (heads, dim)],
        lambda at, own, got, rest, to: row_copies(at, own[0], got, rest, to[0], 0)
        + row_copies(at, own[1], got, rest, to[1], units // 2),
    )


def turn_tables(at, rows):
    half_rot = ROT // 2
    place = lax.broadcasted_iota(jnp.int32, (rows, ONE), 0)
    lane = lax.broadcasted_iota(jnp.int32, (rows, ONE), 1) % HD
    positions = (2 * (place // ONE) + at[S_CORE]) * ONE + place % ONE
    freqs = 1.0 / 10000.0 ** ((2 * (lane % half_rot)).astype(F32) / ROT)
    angles = positions.astype(F32) * freqs
    sine = jnp.sin(angles)
    return (
        jnp.where(lane < ROT, jnp.cos(angles), 1.0),
        jnp.where((lane >= half_rot) & (lane < ROT), sine, 0.0),
        jnp.where(lane < half_rot, -sine, 0.0),
    )


def keep_blocks(at, source, blocks):
    mine, give = blocks
    place = (2 * at[S_HALF] + at[S_NEAR]) * ONE
    mine[...] = source[pl.ds(pl.multiple_of(place, ONE), ONE)]
    size = give.shape[0]
    place = (2 * (1 - at[S_HALF]) + at[S_NEAR]) * ONE + at[S_SIDE] * size
    give[...] = source[pl.ds(pl.multiple_of(place, size), size)]


def keep_piece(at, source, piece):
    size = piece.shape[0]
    piece[...] = source[pl.ds(pl.multiple_of(at[S_CHIP] * size, size), size)]


def front(at, loader, sources, w, turns, with_piece):
    dim = w["qkv"].shape[0]
    rows = turns[0].shape[0]
    count = len(sources)

    def body(at, *refs):
        given = refs[:count]
        vectors, *turns = refs[count : count + 4]
        attn_in, mlp_in, normed_out, q, kv = refs[count + 4 : count + 9]
        *kept, qkv, ordered = refs[count + 9 :]
        gains = [vectors[i : i + 1] for i in range(4)]
        for place, block in loader(at, given):
            size = block.shape[0]
            ordered[pl.ds(pl.multiple_of(place * size, size), size)] = block
        if with_piece:
            keep_piece(at, ordered, kept[0])
        else:
            keep_blocks(at, ordered, kept)
        bias = vectors[6:7, : 3 * ONE]

        def norm(span):
            hidden = ordered[span].astype(F32)
            mean = jnp.sum(hidden, axis=1, keepdims=True) * (1.0 / dim)
            centre = hidden - mean
            var = jnp.sum(centre * centre, axis=1, keepdims=True) * (1.0 / dim)
            normed = centre * lax.rsqrt(var + 1e-05)
            attn_in[span] = (normed * gains[0] + gains[1]).astype(B16)
            mlp_in[span] = (normed * gains[2] + gains[3]).astype(B16)
            normed_out[span] = normed.astype(B16)

        def project(span):
            projected = nn(attn_in[span], qkv[...]) + bias
            cosine, second, first_half = [table[span] for table in turns]
            for i, target in ((0, q), (1, kv.at[0])):
                flat = projected[:, i * ONE : (i + 1) * ONE]
                flat = (
                    flat * cosine
                    + pltpu.roll(flat, ROT // 2, 1) * second
                    + pltpu.roll(flat, ONE - ROT // 2, 1) * first_half
                )
                target[span] = flat.astype(B16)
            kv[1, span] = projected[:, 2 * ONE :].astype(B16)

        by_rows(rows, 128, norm)
        by_rows(rows, 256, project)

    outs = [((rows, dim), B16)] * 3 + [((rows, ONE), B16), ((2, rows, ONE), B16)]
    outs += [((rows // 8, dim), B16)] if with_piece else [((n, dim), B16) for n in (ONE, ONE // 2)]
    return weights_call(
        "front", body, outs, at, [*sources, w["rows"], *turns], [w["qkv"]],
        scratch=[pltpu.VMEM((rows, dim), B16)],
        flops=2 * rows * dim * 3 * ONE + 20 * rows * dim,
    )


def units_forward(at, mlp_in, w):
    rows, dim = mlp_in.shape
    units = w["units"]

    def body(at, mlp_in, vectors, active, slope, up):
        bias = vectors[5:6, :units]

        def gelu(span):
            value = nn(mlp_in[span], up[...]) + bias
            cdf = 0.5 + 0.5 * lax.erf(value * (1.0 / math.sqrt(2.0)))
            pdf = jnp.exp(value * value * -0.5) * (1.0 / math.sqrt(2.0 * math.pi))
            active[span] = (value * cdf).astype(B16)
            slope[span] = (cdf + value * pdf).astype(B16)

        by_rows(rows, 128, gelu)

    return weights_call(
        "units_forward", body, [((rows, units), B16)] * 2, at, [mlp_in, w["rows"]], [w["up"]],
        flops=2 * rows * dim * units + 40 * rows * units, exps=rows * units,
    )


def head_lanes():
    return lax.broadcasted_iota(jnp.int32, (1, ONE), 1) < HD


def allowed_keys(at, first, step, count):
    row = lax.broadcasted_iota(jnp.int32, (step, count), 0) + first
    column = lax.broadcasted_iota(jnp.int32, (step, count), 1)
    return column <= row, column < (row // ONE + at[S_CORE]) * ONE


STEPS = (0, 1, 4, 5)
STEP_CHIPS = (0, SIDE, SECTION, SECTION | SIDE)


def pieces_out(at, total, pieces):
    size = total.shape[0] // 8
    for step, piece in zip(STEPS, pieces):
        for i in range(2):
            place = (at[S_CHIP] ^ (step | 2 * i)) * size
            piece[i] = total[pl.ds(pl.multiple_of(place, size), size)].astype(piece.dtype)


def piece_shapes(rows, dim):
    return [((2, rows // 8, dim), F32)] + [((2, rows // 8, dim), B16)] * 3


def fold(at, pieces):
    _, rows, dim = pieces[0].shape

    def body(at, *refs):
        *given, keep, give = refs
        for i, target in ((0, keep), (1, give)):
            total = given[0][i]
            for piece in given[1:]:
                total = total + piece[i].astype(F32)
            target[...] = total.astype(target.dtype)

    return kernel_call_named("fold", body, [((rows, dim), F32), ((rows, dim), B16)], at, *pieces)


def exchanged(pieces):
    return [pieces[0]] + [swapped(p, m) for p, m in zip(pieces[1:], STEP_CHIPS[1:])]


def gathered(piece, near):
    pair = jnp.stack([piece, near])
    return [pair] + [swapped(pair, mask) for mask in STEP_CHIPS[1:]]


def attention_forward(at, q, kv, kv_other):
    rows = q.shape[0]
    scale = 1.0 / math.sqrt(HD)

    def body(at, q, kv, kv_other, mixed, lse):
        first_head = head_lanes()
        step = 256
        for first in range(0, rows, step):
            span = slice(first, first + step)
            count = first + step
            queries = q[span]
            masks = allowed_keys(at, first, step, count)
            results, totals = [], []
            for head in range(2):
                lanes = first_head if head == 0 else jnp.logical_not(first_head)
                one = jnp.where(lanes, queries, jnp.zeros_like(queries))
                scores = [
                    jnp.where(mask, nt(one, keys[0, :count]) * scale, -1e9)
                    for mask, keys in zip(masks, (kv, kv_other))
                ]
                most = jnp.maximum(
                    jnp.max(scores[0], axis=1, keepdims=True),
                    jnp.max(scores[1], axis=1, keepdims=True),
                )
                exponents = [jnp.exp(s - most) for s in scores]
                summed = jnp.sum(exponents[0], axis=1, keepdims=True) + jnp.sum(
                    exponents[1], axis=1, keepdims=True
                )
                inverse = 1.0 / summed
                results.append(
                    nn((exponents[0] * inverse).astype(B16), kv[1, :count])
                    + nn((exponents[1] * inverse).astype(B16), kv_other[1, :count])
                )
                totals.append(most + jnp.log(summed))
            mixed[span] = jnp.where(first_head, results[0], results[1]).astype(B16)
            lse[span] = jnp.where(first_head, totals[0], totals[1])

    return kernel_call_named(
        "attention_forward", body, [((rows, ONE), B16), ((rows, ONE), F32)], at, q, kv, kv_other,
        flops=8 * rows * rows * ONE * 2, exps=2 * rows * rows * 2,
    )


def outputs_forward(at, mixed, active, w):
    rows = mixed.shape[0]
    units, dim = w["down"].shape

    def body(at, mixed, active, *rest):
        pieces, (out, down, total) = rest[:4], rest[4:]

        def one(span):
            total[span] = nn(mixed[span], out[...]) + nn(active[span], down[...])

        by_rows(rows, 256, one)
        pieces_out(at, total, pieces)

    return weights_call(
        "outputs_forward", body, piece_shapes(rows, dim), at, [mixed, active],
        [w["out"], w["down"]], scratch=[pltpu.VMEM((rows, dim), F32)],
        flops=2 * rows * dim * (units + ONE),
    )


def units_backward(at, loader, sources, slope, w, with_piece):
    rows, units = slope.shape
    dim = w["up"].shape[0]
    count = len(sources)

    def body(at, *refs):
        given = refs[:count]
        slope, g, up_grad, mixed_grad = refs[count : count + 4]
        *kept, down, out = refs[count + 4 :]
        for place, block in loader(at, given):
            size = block.shape[0]
            g[pl.ds(pl.multiple_of(place * size, size), size)] = block
        if with_piece:
            keep_piece(at, g, kept[0])
        else:
            keep_blocks(at, g, kept)

        def back(span):
            up_grad[span] = (nt(g[span], down[...]) * slope[span].astype(F32)).astype(B16)
            mixed_grad[span] = nt(g[span], out[...]).astype(B16)

        by_rows(rows, 256, back)

    outs = [((rows, dim), B16), ((rows, units), B16), ((rows, ONE), B16)]
    outs += [((rows // 8, dim), B16)] if with_piece else [((n, dim), B16) for n in (ONE, ONE // 2)]
    return weights_call(
        "units_backward", body, outs, at, [*sources, slope], [w["down"], w["out"]],
        flops=2 * rows * dim * (units + ONE),
    )


def attention_backward(at, q, kv, kv_other, lse, mixed_grad):
    rows = q.shape[0]
    scale = 1.0 / math.sqrt(HD)

    def body(at, q, kv, kv_other, lse, mixed_grad, dq, dkv, dkv_other):
        first_head = head_lanes()
        step = 256
        dkv[...] = jnp.zeros_like(dkv)
        dkv_other[...] = jnp.zeros_like(dkv_other)
        for first in range(0, rows, step):
            span = slice(first, first + step)
            count = first + step
            queries, back = q[span], mixed_grad[span]
            masks = allowed_keys(at, first, step, count)
            sides = ((masks[0], kv, dkv), (masks[1], kv_other, dkv_other))
            results = []
            for head in range(2):
                lanes = first_head if head == 0 else jnp.logical_not(first_head)
                one = jnp.where(lanes, queries, jnp.zeros_like(queries))
                one_back = jnp.where(lanes, back, jnp.zeros_like(back))
                level = lse[span, head * HD : head * HD + 1]
                probs, grads = [], []
                for mask, keys, _ in sides:
                    scores = nt(one, keys[0, :count]) * scale
                    probs.append(jnp.exp(jnp.where(mask, scores, -1e9) - level))
                    grads.append(nt(one_back, keys[1, :count]))
                delta = jnp.sum(probs[0] * grads[0], axis=1, keepdims=True) + jnp.sum(
                    probs[1] * grads[1], axis=1, keepdims=True
                )
                result = 0.0
                for (_, keys, target), prob, grad in zip(sides, probs, grads):
                    score_grad = (prob * (grad - delta) * scale).astype(B16)
                    result = result + nn(score_grad, keys[0, :count])
                    target[0, :count] += tn(score_grad, one)
                    target[1, :count] += tn(prob.astype(B16), one_back)
                results.append(result)
            dq[span] = jnp.where(first_head, results[0], results[1])

    return kernel_call_named(
        "attention_backward",
        body, [((rows, ONE), F32), ((2, rows, ONE), F32), ((2, rows, ONE), F32)],
        at, q, kv, kv_other, lse, mixed_grad,
        flops=20 * rows * rows * ONE * 2, exps=2 * rows * rows * 2,
    )


def inputs_backward(at, dq, dkv, dkv_got, up_grad, normed, g, turns, w):
    rows, dim = normed.shape
    units = up_grad.shape[1]

    def body(at, dq, dkv, dkv_got, up_grad, normed, g, *rest):
        turns, vectors, rest = rest[:3], rest[3], rest[4:]
        qkv_grad, table = rest[:2]
        pieces, (qkv, up, total, lines) = rest[2:6], rest[6:]
        gain_one, gain_two = vectors[0:1], vectors[2:3]
        step = 128

        def one(i, sums):
            span = pl.ds(pl.multiple_of(i * step, step), step)
            cosine, second, first_half = [table[span] for table in turns]
            parts = []
            for flat in (dq[span], dkv[0, span] + dkv_got[0, span]):
                parts.append(
                    flat * cosine
                    - pltpu.roll(flat, ROT // 2, 1) * second
                    - pltpu.roll(flat, ONE - ROT // 2, 1) * first_half
                )
            parts.append(dkv[1, span] + dkv_got[1, span])
            both = jnp.concatenate([p.astype(B16) for p in parts], axis=1)
            qkv_grad[span] = both
            attn = nt(both, qkv[...])
            mlp = nt(up_grad[span], up[...])
            total[span] = attn * gain_one + mlp * gain_two
            unit = normed[span].astype(F32)
            new = [
                jnp.sum(v, axis=0, keepdims=True)
                for v in (
                    attn * unit, attn, mlp * unit, mlp, g[span].astype(F32),
                    up_grad[span].astype(F32), both.astype(F32),
                )
            ]
            return tuple(a + b for a, b in zip(sums, new))

        widths = (dim,) * 5 + (units, 3 * ONE)
        sums = lax.fori_loop(
            0, rows // step, one, tuple(jnp.zeros((1, width), F32) for width in widths)
        )
        pieces_out(at, total, pieces)
        lines[...] = jnp.zeros_like(lines)
        line = 0
        for value in sums:
            for i in range(value.shape[1] // ONE):
                lines[line : line + 1] = value[:, i * ONE : (i + 1) * ONE]
                line += 1
        table[...] = lines[...].astype(B16)

    outs = [((rows, 3 * ONE), B16), ((LINES, ONE), B16)] + piece_shapes(rows, dim)
    return weights_call(
        "inputs_backward", body, outs, at,
        [dq, dkv, dkv_got, up_grad, normed, g, *turns, w["rows"]], [w["qkv"], w["up"]],
        scratch=[pltpu.VMEM((rows, dim), F32), pltpu.VMEM((LINES, ONE), F32)],
        flops=2 * rows * dim * (units + 3 * ONE) + 12 * rows * dim,
    )


LINES = 64


def join_forward(at, x_piece, parts, w):
    def body(at, x, vectors, own, *rest):
        total = x[...].astype(F32) + own[...].astype(F32) + vectors[4:5]
        for piece in rest[:-1]:
            total = total + piece[...].astype(F32)
        rest[-1][...] = total.astype(B16)

    return kernel_call_named("join_forward", body, [(x_piece.shape, B16)], at, x_piece, w["rows"], *parts)[0]


def join_backward(at, g_piece, x_piece, parts):
    dim = x_piece.shape[1]

    def body(at, g, x, own, *rest):
        total = own[...]
        for piece in rest[:-1]:
            total = total + piece[...].astype(F32)
        hidden = x[...].astype(F32)
        centre = hidden - jnp.sum(hidden, axis=1, keepdims=True) * (1.0 / dim)
        var = jnp.sum(centre * centre, axis=1, keepdims=True) * (1.0 / dim)
        scale = lax.rsqrt(var + 1e-05)
        normed = centre * scale
        inner = (
            total
            - jnp.sum(total, axis=1, keepdims=True) * (1.0 / dim)
            - normed * (jnp.sum(total * normed, axis=1, keepdims=True) * (1.0 / dim))
        )
        rest[-1][...] = (g[...].astype(F32) + scale * inner).astype(B16)

    return kernel_call_named("join_backward", body, [(x_piece.shape, B16)], at, g_piece, x_piece, *parts)[0]


def columns(at, ref, core, high):
    which = at[S_CORE] ^ core
    return jnp.concatenate(
        [
            ref[:, pl.ds(pl.multiple_of((4 * high + 2 * low + which) * ONE, ONE), ONE)]
            for low in range(2)
        ],
        axis=1,
    )


def early_grads(at, active, mixed, mlp_in, up_grad, g):
    rows, dim = g.shape
    units = active.shape[1]
    tiles = units // ONE

    def body(at, active, mixed, mlp_in, up_grad, g, keep, give):
        for core, target in ((0, keep), (1, give)):
            for high in range(2):
                strip = columns(at, g, core, high)
                down = tn(active[...], strip).astype(B16)
                out = tn(mixed[...], strip).astype(B16)
                up = tn(columns(at, mlp_in, core, high), up_grad[...]).astype(B16)
                for low in range(2):
                    lanes = slice(low * ONE, (low + 1) * ONE)
                    where = (at[S_HALF] ^ high, at[S_NEAR] ^ low)
                    target[where[0], where[1], :units] = down[:, lanes]
                    target[where[0], where[1], units : units + ONE] = out[:, lanes]
                    for i in range(tiles):
                        base = units + (1 + i) * ONE
                        target[where[0], where[1], base : base + ONE] = up[
                            lanes, i * ONE : (i + 1) * ONE
                        ]

    shape = (2, 2, 2 * units + ONE, ONE)
    return kernel_call_named(
        "early_grads",
        body, [(shape, B16)] * 2, at, active, mixed, mlp_in, up_grad, g,
        flops=2 * rows * dim * (2 * units + ONE),
    )


def late_grads(at, attn_in, qkv_grad, tables):
    rows, dim = attn_in.shape
    count = len(tables)

    def body(at, attn_in, qkv_grad, *refs):
        tables, (keep, give) = refs[:count], refs[count:]
        for core, target in ((0, keep), (1, give)):
            for high in range(2):
                qkv = tn(columns(at, attn_in, core, high), qkv_grad[...]).astype(B16)
                for low in range(2):
                    where = (at[S_HALF] ^ high, at[S_NEAR] ^ low)
                    for i in range(3):
                        target[where[0], where[1], i * ONE : (i + 1) * ONE] = qkv[
                            low * ONE : (low + 1) * ONE, i * ONE : (i + 1) * ONE
                        ]
                    for i, table in enumerate(tables):
                        base = 3 * ONE + i * LINES
                        target[where[0], where[1], base : base + LINES] = table[...]

    shape = (2, 2, 3 * ONE + count * LINES, ONE)
    return kernel_call_named(
        "late_grads", body, [(shape, B16)] * 2, at, attn_in, qkv_grad, *tables,
        flops=2 * rows * dim * 3 * ONE,
    )


def plus(a, b):
    return (a.astype(F32) + b.astype(F32)).astype(B16)


def summed_cores(keep, give, *earlier):
    got = swapped(after(give, *earlier), CORE)
    return (
        [plus(keep[0, i], got[0, i]) for i in range(2)],
        [plus(keep[1, i], got[1, i]) for i in range(2)],
    )


def sum_lines(at, late):
    def body(at, *refs):
        *late, lines = refs
        total = 0.0
        for part in late:
            total = total + part[3 * ONE : 3 * ONE + lines.shape[0]].astype(F32)
        lines[...] = total

    return kernel_call_named("sum_lines", body, [((32, ONE), F32)], at, *late)[0]


def unpack_grads(at, early, late, sizes):
    dim_part, units, heads = ONE, sizes["units"], ONE

    def body(at, *refs):
        early, late = refs[:4], refs[4:8]
        qkv, out, up, down, b_qkv, b_up, branch = refs[8:]
        index = at[S_OWN]
        for j, (wide, narrow) in enumerate(zip(early, late)):
            source = index ^ (2 * (j % 2) + j // 2)
            place = pl.multiple_of(source * units, units)
            small = pl.multiple_of(source * ONE, ONE)
            down[pl.ds(place, units)] = wide[:units].astype(F32)
            out[pl.ds(small, ONE)] = wide[units : units + ONE].astype(F32)
            for i in range(units // ONE):
                base = units + (1 + i) * ONE
                up[:, pl.ds(place + i * ONE, ONE)] = wide[base : base + ONE].astype(F32)
            for i in range(3):
                qkv[i, :, pl.ds(small, ONE)] = narrow[i * ONE : (i + 1) * ONE].astype(F32)
            table = narrow[3 * ONE :].astype(F32)
            for i in range(units // ONE):
                b_up[:, pl.ds(place + i * ONE, ONE)] = table[40 + i : 41 + i]
            for i in range(3):
                b_qkv[i : i + 1, pl.ds(small, ONE)] = table[40 + units // ONE + i :][:1]
            if j == 0:
                branch[...] = table[32:40]

    outs = [
        ((3, dim_part, 4 * heads), F32),
        ((4 * heads, dim_part), F32),
        ((dim_part, 4 * units), F32),
        ((4 * units, dim_part), F32),
        ((3, 4 * heads), F32),
        ((1, 4 * units), F32),
        ((8, ONE), F32),
    ]
    return kernel_call_named("unpack_grads", body, outs, at, *early, *late, keep=False)


def cube_device(
    inputs, cotangent, ln1_gain, ln1_bias, ln2_gain, ln2_bias, qkv_weight, qkv_bias,
    out_weight, up_weight, up_bias, down_weight, branch_bias,
):
    at = where_am_i()
    section, half, side = [lax.axis_index("section"), lax.axis_index("ctx") // 4, lax.axis_index("tp")]
    at, is_first, is_low, is_left, is_near = lax.optimization_barrier(
        (at, section == 0, half == 0, side == 0, section == half)
    )
    dim = inputs.shape[2]
    rows = 4 * inputs.shape[1]
    vectors = (ln1_gain, ln1_bias, ln2_gain, ln2_bias, branch_bias, up_bias, qkv_bias)

    mine, strip, sent_qkv = pack_first(at, inputs, vectors, qkv_weight)
    g_mine, g_strip, sent_up, sent_down = pack_second(
        at, cotangent, up_weight, out_weight, down_weight
    )
    strips = send_strips(strip)
    turns = turn_tables(at, rows)
    sides = [swapped(after(part, turns[0]), SIDE) for part in strips]
    x_parts = (mine, swapped(mine, NEAR), *strips, *sides)
    got_qkv, layers = first_weights(at, vectors, qkv_weight, sent_qkv)
    got_up = swapped(after(sent_up, got_qkv), SECTION)
    first, second = layers
    got_down = swapped(
        after(sent_down, got_up, *x_parts[4:], first["qkv"], first["rows"]), SECTION
    )

    g_near = swapped(after(g_mine, *x_parts[4:]), NEAR)

    def bring_up(*earlier):
        up = up_weights(at, up_weight, got_up, swapped(after(got_up, *earlier), CORE))
        for i, layer in enumerate(layers):
            layer.update(up=up[i], units=up[i].shape[1])

    def bring_rows(*earlier):
        tall = row_weights(
            at, down_weight, out_weight, got_down, swapped(after(got_down, *earlier), CORE)
        )
        for i, layer in enumerate(layers):
            layer.update(down=tall[i], out=tall[2 + i])

    def forward(loader, sources, w, with_piece):
        got = front(at, loader, sources, w, turns, with_piece)
        attn_in, mlp_in, normed, q, kv = got[:5]
        kv_other = swapped(kv, CORE)
        is_start = "up" not in w
        if is_start:
            bring_up(q)
        active, slope = units_forward(at, mlp_in, w)
        mixed, lse = attention_forward(at, q, kv, kv_other)
        if is_start:
            bring_rows(active, mixed, g_near)
        pieces = outputs_forward(at, mixed, active, w)
        saved = dict(
            attn_in=attn_in, mlp_in=mlp_in, normed=normed, q=q, kv=kv, kv_other=kv_other,
            active=active, slope=slope, mixed=mixed, lse=lse,
        )
        return pieces, saved, got[5:]

    def backward(loader, sources, saved, w, with_piece, grads_first):
        made = units_backward(at, loader, sources, saved["slope"], w, with_piece)
        g, up_grad, mixed_grad = made[:3]
        if grads_first:
            early = early_grads(
                at, saved["active"], saved["mixed"], saved["mlp_in"], up_grad, g
            )
            mixed_grad = after(mixed_grad, early[0])
        dq, dkv, dkv_other = attention_backward(
            at, saved["q"], saved["kv"], saved["kv_other"], saved["lse"], mixed_grad
        )
        dkv_got = swapped(dkv_other, CORE)
        if not grads_first:
            early = early_grads(
                at, saved["active"], saved["mixed"], saved["mlp_in"], up_grad, after(g, dkv_other)
            )
            dq = after(dq, early[0])
        given = (dq, dkv, dkv_got, up_grad, saved["normed"], g)
        return early, given, made[3:]

    def backward_end(given, saved, w):
        out = inputs_backward(at, *given, turns, w)
        return out[0], out[1], out[2:]

    parts, saved_first, (x_piece,) = forward(start_loader, x_parts, first, True)
    strips = send_strips(after(g_strip, parts[0]))
    parts = exchanged(parts)
    parts[0] = after(parts[0], *strips)
    keep, give = fold(at, parts)
    sides = [swapped(part, SIDE) for part in strips]
    piece = join_forward(at, x_piece, [keep, swapped(give, NEAR)], first)
    near = after(swapped(piece, NEAR), *sides)
    middle = gathered(piece, near)
    g_parts = (g_mine, g_near, *strips, *sides)

    parts_last, saved_second, blocks = forward(piece_loader, middle, second, False)
    acts_mine, acts_give = blocks

    early, given, (g_piece,) = backward(
        start_loader, g_parts, saved_second, second, True, False
    )
    early_keep, early_give = summed_cores(*early, given[2])
    qkv_grad, table_second, pieces = backward_end(given, saved_second, second)
    late = late_grads(at, saved_second["attn_in"], qkv_grad, ())
    parts = exchanged(pieces)
    far_second = swapped(early_give[1], HALF)
    parts[0] = after(parts[0], far_second, *late)
    keep, give = fold(at, parts)
    late_keep, late_give = summed_cores(*late)
    late_got = swapped(after(jnp.stack(late_give), give), HALF)
    parts_last = exchanged([after(p, give) for p in parts_last])
    back = join_backward(at, g_piece, piece, [keep, swapped(give, NEAR)])
    near = after(swapped(back, NEAR), late_got, *parts_last)
    g_middle = gathered(back, near)
    close_second = swapped(after(early_give[0], near), HALF)
    g_middle[0] = after(g_middle[0], close_second)
    keep_last, give_last = fold(at, parts_last)

    early, given, blocks = backward(
        piece_loader, g_middle, saved_first, first, False, True
    )
    in_mine, in_give = blocks
    early_second = [plus(a, b) for a, b in zip(early_keep, (close_second, far_second))]
    late_second = [plus(a, b) for a, b in zip(late_keep, late_got)]
    early_keep, early_give = summed_cores(*early)
    given = (after(given[0], *early_give),) + given[1:]
    qkv_grad, table_first, pieces = backward_end(given, saved_first, first)
    last_near = swapped(give_last, NEAR)
    parts = exchanged([after(p, last_near) for p in pieces])
    far_first = swapped(early_give[1], HALF)
    late = late_grads(at, saved_first["attn_in"], qkv_grad, (table_first, table_second))
    parts[0] = after(parts[0], far_first)
    keep, give = fold(at, parts)
    close_first = swapped(after(early_give[0], give), HALF)
    late_keep, late_give = summed_cores(*late)
    late_got = swapped(after(jnp.stack(late_give), give), HALF)
    back_last = join_backward(
        at, back, x_piece, [keep, after(swapped(give, NEAR), close_first)]
    )
    last = join_forward(at, piece, [keep_last, last_near], second)
    early_first = [plus(a, b) for a, b in zip(early_keep, (close_first, far_first))]
    late_first = [plus(a, b) for a, b in zip(late_keep, late_got)]
    tall = 3 * ONE + LINES
    late_second = [
        jnp.concatenate([a, b[tall:]], axis=0) for a, b in zip(late_second, late_first)
    ]
    late_first = [a[:tall] for a in late_first]
    def brought(close, far):
        own = jnp.where(is_first, close[0], close[1])
        near = swapped(jnp.where(is_first, far[0], far[1]), NEAR)
        got = swapped(jnp.where(is_first, close[1], close[0]), SECTION)
        cross = swapped(jnp.where(is_first, far[1], far[0]), SECTION | NEAR)
        return own, got, near, cross

    early = brought((early_first[0], early_second[0]), (early_first[1], early_second[1]))
    late_first[1] = after(late_first[1], *early)
    late = brought((late_first[0], late_second[0]), (late_first[1], late_second[1]))
    lines = sum_lines(at, late)
    lines = lines + swapped(lines, SIDE)
    sizes = dict(units=up_weight.shape[2] // 4)
    qkv, out, up, down, b_qkv, b_up, branch = unpack_grads(at, early, late, sizes)

    mine = jnp.where(is_first, back_last, last)
    got = swapped(jnp.where(is_first, last, back_last), SECTION)
    stay = jnp.where(is_near, mine, got)
    known_give = jnp.where(is_first, acts_give, in_give)
    other = swapped(jnp.stack([jnp.where(is_near, got, mine), known_give]), HALF)
    own = jnp.stack(
        [jnp.where(is_low, stay, other[0]), jnp.where(is_low, other[0], stay), other[1]]
    )
    rest = swapped(own, SIDE)
    both = jnp.where(
        is_left, jnp.concatenate([own, rest], axis=1), jnp.concatenate([rest, own], axis=1)
    )
    new = both[:2]
    known_mine = jnp.where(is_first, acts_mine, in_mine)
    known = jnp.where(
        is_low, jnp.stack([known_mine, both[2]]), jnp.stack([both[2], known_mine])
    )
    acts = jnp.where(is_first, known, new)
    in_grads = jnp.where(is_first, new, known)

    lines = lines.reshape(4, dim)
    return (
        acts[None],
        in_grads[None],
        lines[0:1],
        lines[1:2],
        lines[2:3],
        lines[3:4],
        qkv[None],
        b_qkv[None],
        out[None],
        up[None],
        b_up,
        down[None],
        branch.reshape(1, dim),
    )


def placed_program(mesh, device_program):
    placed = (
        P(None, "ctx", None),
        P(None, "ctx", None),
        P("section", None),
        P("section", None),
        P("section", None),
        P("section", None),
        P("section", None, None, "tp"),
        P("section", None, "tp"),
        P("section", "tp", None),
        P("section", None, "tp"),
        P("section", "tp"),
        P("section", "tp", None),
        P("section", None),
    )
    return jax.shard_map(
        device_program,
        mesh=mesh,
        in_specs=placed,
        out_specs=(
            P("section", None, "ctx", None),
            P("section", None, "ctx", None),
            P("section", None),
            P("section", None),
            P("section", None),
            P("section", None),
            P("section", None, "ctx", "tp"),
            P("section", None, "tp"),
            P("section", "tp", "ctx"),
            P("section", "ctx", "tp"),
            P("section", "tp"),
            P("section", "tp", "ctx"),
            P("section", None),
        ),
        check_vma=False,
    )


def solution(mesh):
    sizes = dict(mesh.shape)
    if sizes["section"] == 2 and sizes["tp"] == 2 and sizes["ctx"] == 8:
        return placed_program(mesh, cube_device)
    return placed_program(mesh, per_device)
```

```python
import math

import jax
import jax.numpy as jnp
from jax import lax
from jax.experimental import pallas as pl
from jax.experimental.pallas import tpu as pltpu
from jax.sharding import PartitionSpec as P

HD = 64
ROT = 16


def shifted(shard, axis, by):
    peers = lax.axis_size(axis)
    pairs = [(i, i + by) for i in range(peers) if 0 <= i + by < peers]
    return lax.ppermute(shard, axis, pairs)


def tables(positions):
    freqs = 1.0 / 10000.0 ** (jnp.arange(0, ROT, 2).astype(jnp.float32) / ROT)
    angles = positions.astype(jnp.float32)[:, None] * freqs[None, :]
    return (jnp.cos(angles)[:, None, :], jnp.sin(angles)[:, None, :])


def rotate(field, cosine, sine):
    half_rot = ROT // 2
    front = field[..., :half_rot]
    second = field[..., half_rot:ROT]
    return jnp.concatenate(
        [front * cosine - second * sine, second * cosine + front * sine, field[..., ROT:]], axis=-1
    )


def norms(hidden, gain_one, shift_one, gain_two, shift_two):
    centre = hidden - jnp.mean(hidden, axis=-1, keepdims=True)
    normed = centre * lax.rsqrt(jnp.mean(centre * centre, axis=-1, keepdims=True) + 1e-05)
    return (normed * gain_one + shift_one, normed * gain_two + shift_two)


def gelu_exact(value):
    return jax.nn.gelu(value, approximate=False)


def scores_of(queries, keys, query_pos, score_scale):
    raw = jnp.einsum("qhd,khd->hqk", queries, keys, preferred_element_type=jnp.float32)
    key_pos = jnp.arange(keys.shape[0], dtype=jnp.int32)
    return jnp.where(
        key_pos[None, None, :] <= query_pos[None, :, None], raw * score_scale, -1000000000.0
    )


def forward_layer(layer_in, weights, query_pos, cosine, sine):
    gains, w_qkv, b_qkv, w_out, w_up, b_up, w_down, b_branch = weights
    hidden = layer_in.astype(jnp.float32)
    attn_norm, mlp_norm = norms(hidden, gains[0], gains[1], gains[2], gains[3])
    attn_in = attn_norm.astype(jnp.bfloat16)
    mlp_in = mlp_norm.astype(jnp.bfloat16)
    projected = (
        jnp.einsum("td,cdf->tcf", attn_in, w_qkv, preferred_element_type=jnp.float32) + b_qkv
    )
    row_count = hidden.shape[0]
    feat_width = projected.shape[2]
    head_count = feat_width // HD
    queries = rotate(projected[:, 0].reshape(row_count, head_count, HD), cosine, sine).astype(
        jnp.bfloat16
    )
    key_flat = (
        rotate(projected[:, 1].reshape(row_count, head_count, HD), cosine, sine)
        .astype(jnp.bfloat16)
        .reshape(row_count, feat_width)
    )
    value_flat = projected[:, 2].astype(jnp.bfloat16)
    all_keys, all_values = (
        lax.all_gather(key_flat, "ctx", axis=0, tiled=True),
        lax.all_gather(value_flat, "ctx", axis=0, tiled=True),
    )
    key_count = all_keys.shape[0]
    score_scale = 1.0 / math.sqrt(HD)
    scores = scores_of(queries, all_keys.reshape(key_count, head_count, HD), query_pos, score_scale)
    row_max = jnp.max(scores, axis=-1, keepdims=True)
    exponent = jnp.exp(scores - row_max)
    summed = jnp.sum(exponent, axis=-1, keepdims=True)
    probability = (exponent / summed).astype(jnp.bfloat16)
    log_total = row_max + jnp.log(summed)
    mixed = jnp.einsum(
        "hqk,khd->qhd",
        probability,
        all_values.reshape(key_count, head_count, HD),
        preferred_element_type=jnp.float32,
    )
    mixed = mixed.reshape(row_count, feat_width).astype(jnp.bfloat16)
    partial_out = jnp.dot(mixed, w_out, preferred_element_type=jnp.float32)
    up_value = jnp.dot(mlp_in, w_up, preferred_element_type=jnp.float32) + b_up
    active = gelu_exact(up_value).astype(jnp.bfloat16)
    partial_out = partial_out + jnp.dot(active, w_down, preferred_element_type=jnp.float32)
    branches = lax.psum(partial_out, "tp")
    layer_out = (hidden + branches + b_branch).astype(jnp.bfloat16)
    stored = (key_flat, value_flat)
    saved = (layer_in, queries, stored, log_total, mixed, up_value, active)
    return (layer_out, saved)


def backward_layer(grad_out, saved, weights, query_pos, cosine, sine):
    gains, w_qkv, b_qkv, w_out, w_up, b_up, w_down, b_branch = weights
    layer_in, queries, stored, log_total, mixed, up_value, active = saved
    grad_full = grad_out.astype(jnp.float32)
    row_count, feat_width = mixed.shape
    head_count = feat_width // HD
    hidden = layer_in.astype(jnp.float32)
    norm_pair, norm_back = jax.vjp(norms, hidden, gains[0], gains[1], gains[2], gains[3])
    attn_in = norm_pair[0].astype(jnp.bfloat16)
    mlp_in = norm_pair[1].astype(jnp.bfloat16)
    active_grad = jnp.einsum("td,fd->tf", grad_out, w_down, preferred_element_type=jnp.float32)
    grad_down = jnp.einsum("tf,td->fd", active, grad_out, preferred_element_type=jnp.float32)
    gelu_back = jax.vjp(gelu_exact, up_value)[1]
    up_grad = gelu_back(active_grad)[0].astype(jnp.bfloat16)
    grad_up_bias = jnp.sum(up_grad.astype(jnp.float32), axis=0)
    grad_up = jnp.einsum("td,tf->df", mlp_in, up_grad, preferred_element_type=jnp.float32)
    mlp_in_grad = jnp.einsum("tf,df->td", up_grad, w_up, preferred_element_type=jnp.float32)
    mixed_grad = jnp.einsum(
        "td,fd->tf", grad_out, w_out, preferred_element_type=jnp.float32
    ).astype(jnp.bfloat16)
    grad_out_weight = jnp.einsum("tf,td->fd", mixed, grad_out, preferred_element_type=jnp.float32)
    all_keys, all_values = (
        lax.all_gather(stored[0], "ctx", axis=0, tiled=True),
        lax.all_gather(stored[1], "ctx", axis=0, tiled=True),
    )
    key_count = all_keys.shape[0]
    keys_heads = all_keys.reshape(key_count, head_count, HD)
    values_heads = all_values.reshape(key_count, head_count, HD)
    score_scale = 1.0 / math.sqrt(HD)
    scores = scores_of(queries, keys_heads, query_pos, score_scale)
    probability = jnp.exp(scores - log_total)
    heads_grad = mixed_grad.reshape(row_count, head_count, HD)
    prob_grad = jnp.einsum(
        "qhd,khd->hqk", heads_grad, values_heads, preferred_element_type=jnp.float32
    )
    centre = jnp.sum(probability * prob_grad, axis=-1, keepdims=True)
    score_grad = (score_scale * probability * (prob_grad - centre)).astype(jnp.bfloat16)
    query_grad = jnp.einsum(
        "hqk,khd->qhd", score_grad, keys_heads, preferred_element_type=jnp.float32
    )
    value_terms = jnp.einsum(
        "hqk,qhd->khd",
        probability.astype(jnp.bfloat16),
        heads_grad,
        preferred_element_type=jnp.float32,
    )
    key_terms = jnp.einsum("hqk,qhd->khd", score_grad, queries, preferred_element_type=jnp.float32)
    key_grad, value_grad = (
        lax.psum_scatter(
            key_terms.reshape(key_count, feat_width), "ctx", scatter_dimension=0, tiled=True
        ),
        lax.psum_scatter(
            value_terms.reshape(key_count, feat_width), "ctx", scatter_dimension=0, tiled=True
        ),
    )
    query_grad = rotate(query_grad, cosine, -sine).reshape(row_count, feat_width)
    key_grad = rotate(key_grad.reshape(row_count, head_count, HD), cosine, -sine).reshape(
        row_count, feat_width
    )
    qkv_grad = jnp.stack([query_grad, key_grad, value_grad], axis=1).astype(jnp.bfloat16)
    grad_qkv_bias = jnp.sum(qkv_grad.astype(jnp.float32), axis=0)
    grad_qkv = jnp.einsum("td,tcf->cdf", attn_in, qkv_grad, preferred_element_type=jnp.float32)
    attn_in_grad = jnp.einsum("tcf,cdf->td", qkv_grad, w_qkv, preferred_element_type=jnp.float32)
    attn_in_grad, mlp_in_grad = lax.psum((attn_in_grad, mlp_in_grad), "tp")
    hidden_grad, gain_one_grad, shift_one_grad, gain_two_grad, shift_two_grad = norm_back(
        (attn_in_grad, mlp_in_grad)
    )
    input_grad = (grad_full + hidden_grad).astype(jnp.bfloat16)
    grad_branch = jnp.sum(grad_full, axis=0)
    grads = (
        gain_one_grad,
        shift_one_grad,
        gain_two_grad,
        shift_two_grad,
        grad_qkv,
        grad_qkv_bias,
        grad_out_weight,
        grad_up,
        grad_up_bias,
        grad_down,
        grad_branch,
    )
    return (input_grad, grads)


def per_device(
    inputs,
    cotangent,
    ln1_gain,
    ln1_bias,
    ln2_gain,
    ln2_bias,
    qkv_weight,
    qkv_bias,
    out_weight,
    up_weight,
    up_bias,
    down_weight,
    branch_bias,
):
    gains = (
        ln1_gain[0].astype(jnp.float32),
        ln1_bias[0].astype(jnp.float32),
        ln2_gain[0].astype(jnp.float32),
        ln2_bias[0].astype(jnp.float32),
    )
    weights = (
        gains,
        qkv_weight[0],
        qkv_bias[0].astype(jnp.float32),
        out_weight[0],
        up_weight[0],
        up_bias[0].astype(jnp.float32),
        down_weight[0],
        branch_bias[0].astype(jnp.float32),
    )
    micro_count = inputs.shape[0]
    row_count = inputs.shape[1]
    query_pos = lax.axis_index("ctx") * row_count + jnp.arange(row_count, dtype=jnp.int32)
    cosine, sine = tables(query_pos)
    at_first = lax.axis_index("section") == 0
    blank = jnp.zeros_like(inputs[0])
    received = blank
    outputs_list = []
    saved_list = []
    for step_index in range(micro_count + 1):
        fresh = inputs[step_index] if step_index < micro_count else blank
        layer_in = jnp.where(at_first, fresh, received)
        layer_out, saved = forward_layer(layer_in, weights, query_pos, cosine, sine)
        outputs_list.append(layer_out)
        saved_list.append(saved)
        if step_index < micro_count:
            received = shifted(layer_out, "section", 1)
    returned = blank
    grad_list = []
    sums = None
    for back_index in range(micro_count + 1):
        batch_index = micro_count - 1 - back_index
        given = cotangent[batch_index] if batch_index >= 0 else blank
        grad_in = jnp.where(at_first, returned, given)
        input_grad, grads = backward_layer(
            grad_in, saved_list[micro_count - back_index], weights, query_pos, cosine, sine
        )
        sums = grads if sums is None else jax.tree.map(jnp.add, sums, grads)
        grad_list.append(input_grad)
        if back_index < micro_count:
            returned = shifted(input_grad, "section", -1)
    acts = jnp.stack(
        [jnp.where(at_first, outputs_list[j], outputs_list[j + 1]) for j in range(micro_count)]
    )[None]
    in_grads = jnp.stack(
        [
            jnp.where(at_first, grad_list[micro_count - j], grad_list[micro_count - 1 - j])
            for j in range(micro_count)
        ]
    )[None]
    (
        gain_one_grad,
        shift_one_grad,
        gain_two_grad,
        shift_two_grad,
        grad_qkv,
        grad_qkv_bias,
        grad_out_weight,
        grad_up,
        grad_up_bias,
        grad_down,
        grad_branch,
    ) = sums
    qkv_part, out_part, up_part, down_part = (
        lax.psum_scatter(
            grad_qkv[None].astype(jnp.bfloat16), "ctx", scatter_dimension=2, tiled=True
        ).astype(jnp.float32),
        lax.psum_scatter(
            grad_out_weight[None].astype(jnp.bfloat16), "ctx", scatter_dimension=2, tiled=True
        ).astype(jnp.float32),
        lax.psum_scatter(
            grad_up[None].astype(jnp.bfloat16), "ctx", scatter_dimension=1, tiled=True
        ).astype(jnp.float32),
        lax.psum_scatter(
            grad_down[None].astype(jnp.bfloat16), "ctx", scatter_dimension=2, tiled=True
        ).astype(jnp.float32),
    )
    small_sums = (
        lax.psum(gain_one_grad[None].astype(jnp.bfloat16), "ctx").astype(jnp.float32),
        lax.psum(shift_one_grad[None].astype(jnp.bfloat16), "ctx").astype(jnp.float32),
        lax.psum(gain_two_grad[None].astype(jnp.bfloat16), "ctx").astype(jnp.float32),
        lax.psum(shift_two_grad[None].astype(jnp.bfloat16), "ctx").astype(jnp.float32),
        lax.psum(grad_qkv_bias[None].astype(jnp.bfloat16), "ctx").astype(jnp.float32),
        lax.psum(grad_up_bias[None].astype(jnp.bfloat16), "ctx").astype(jnp.float32),
        lax.psum(grad_branch[None].astype(jnp.bfloat16), "ctx").astype(jnp.float32),
    )
    return (
        acts,
        in_grads,
        small_sums[0],
        small_sums[1],
        small_sums[2],
        small_sums[3],
        qkv_part,
        small_sums[4],
        out_part,
        up_part,
        small_sums[5],
        down_part,
        small_sums[6],
    )


ALL = ("section", "ctx", "tp")
SECTION, HALF, NEAR, CORE, SIDE = 16, 8, 4, 2, 1
CHIPS = (0, SIDE, NEAR, NEAR | SIDE, SECTION, SECTION | SIDE, SECTION | NEAR, SECTION | NEAR | SIDE)
F32, B16 = jnp.float32, jnp.bfloat16
ONE = 128
S_SECTION, S_HALF, S_NEAR, S_CORE, S_SIDE, S_CHIP, S_OWN, S_GIVE = range(8)


def swapped(array, mask, section=None):
    pairs = [(i, i ^ mask) for i in range(32) if section is None or i // 16 == section]
    return lax.ppermute(array, ALL, pairs)


def after(array, *earlier):
    return lax.optimization_barrier((array,) + earlier)[0]


def where_am_i():
    section = lax.axis_index("section")
    ctx = lax.axis_index("ctx")
    side = lax.axis_index("tp")
    half, near, core = ctx // 4, (ctx // 2) % 2, ctx % 2
    chip = 4 * section + 2 * near + side
    own, give = 2 * section + near, 2 * (1 - section) + near
    return jnp.stack([section, half, near, core, side, chip, own, give]).astype(jnp.int32)


def in_hbm(arrays):
    return [pltpu.with_memory_space_constraint(a, pltpu.HBM) for a in arrays]


def kernel_call(body, outs, at, *arrays, hbm=(), free=(), scratch=(), flops=0, exps=0, name=None, keep=True):
    moved = sum(a.size * a.dtype.itemsize for a in arrays)
    moved += sum(math.prod(s) * jnp.dtype(d).itemsize for s, d in outs)
    return pl.pallas_call(
        body,
        name=name,
        out_shape=[(pltpu.VMEM if keep else jax.ShapeDtypeStruct)(s, d) for s, d in outs],
        in_specs=[pl.BlockSpec(memory_space=pltpu.SMEM)]
        + [pl.BlockSpec(memory_space=pltpu.VMEM)] * len(arrays)
        + [pl.BlockSpec(memory_space=pltpu.HBM)] * len(hbm)
        + [pl.BlockSpec(memory_space=pl.ANY)] * len(free),
        out_specs=[pl.BlockSpec(memory_space=pltpu.VMEM)] * len(outs),
        scratch_shapes=list(scratch),
        compiler_params=pltpu.CompilerParams(vmem_limit_bytes=VMEM_BYTES),
        cost_estimate=pl.CostEstimate(flops=0, bytes_accessed=0, transcendentals=0),
    )(at, *arrays, *in_hbm(hbm), *free)


VMEM_BYTES = 12 * 1024 * 1024


def kernel_call_named(name, *args, **kwargs):
    return kernel_call(*args, name=name, **kwargs)


def by_rows(rows, step, do):
    def one(i, _):
        do(pl.ds(pl.multiple_of(i * step, step), step))
        return 0

    lax.fori_loop(0, rows // step, one, 0)


def nn(a, b):
    return jnp.dot(a, b, preferred_element_type=F32)


def nt(a, b):
    return lax.dot_general(a, b, (((1,), (1,)), ((), ())), preferred_element_type=F32)


def tn(a, b):
    return lax.dot_general(a, b, (((0,), (0,)), ((), ())), preferred_element_type=F32)


def copy_kernel(name, body, outs, at, arrays, scratch):
    return pl.pallas_call(
        body,
        name=name,
        out_shape=[jax.ShapeDtypeStruct(s, B16) for s in outs],
        in_specs=[pl.BlockSpec(memory_space=pltpu.SMEM)]
        + [pl.BlockSpec(memory_space=pltpu.HBM)] * len(arrays),
        out_specs=[pl.BlockSpec(memory_space=pltpu.HBM)] * len(outs),
        scratch_shapes=list(scratch),
        compiler_params=pltpu.CompilerParams(vmem_limit_bytes=VMEM_BYTES),
        cost_estimate=pl.CostEstimate(flops=0, bytes_accessed=0, transcendentals=0),
    )(at, *in_hbm(arrays))


def token_copies(at, array, mine, strip, sems):
    width = strip.shape[1]
    lanes = pl.ds(pl.multiple_of(at[S_SIDE] * width, width), width)
    return [
        pltpu.make_async_copy(array.at[at[S_HALF]], mine, sems.at[0]),
        pltpu.make_async_copy(array.at[1 - at[S_HALF], :, lanes], strip, sems.at[1]),
    ]


def token_shapes(array):
    _, rows, dim = array.shape
    return [(rows, dim), (rows, dim // 2)]


def send_strips(strip):
    return swapped(strip, HALF), swapped(strip, HALF | NEAR)


def start_loader(at, refs):
    mine, near, far, far_near, far_rest, far_near_rest = refs
    first = at[S_SIDE] == 0
    index = 2 * at[S_HALF] + at[S_NEAR]

    def whole(strip, rest):
        a, b = strip[...], rest[...]
        return jnp.concatenate([jnp.where(first, a, b), jnp.where(first, b, a)], axis=1)

    yield index, mine[...]
    yield index ^ 1, near[...]
    yield index ^ 2, whole(far, far_rest)
    yield index ^ 3, whole(far_near, far_near_rest)


def piece_loader(at, refs):
    for step, ref in zip(STEPS, refs):
        for i in range(2):
            yield at[S_CHIP] ^ (step | 2 * i), ref[i]


def run_copies(copies):
    for copy in copies:
        copy.start()
    for copy in copies:
        copy.wait()


def pack_first(at, tokens, vectors, w_qkv):
    _, three, dim, wide = w_qkv.shape
    heads, side = wide // 4, dim // 2
    count = len(vectors)

    def body(at, tokens, w_qkv, *refs):
        lines = refs[:count]
        mine, strip, packed, table, rounded, sems = refs[count : count + 6]
        held = refs[count + 6 :]
        rows = pl.ds(pl.multiple_of(at[S_CORE] * side, side), side)
        lanes = pl.ds(pl.multiple_of(at[S_GIVE] * heads, heads), heads)
        copies = token_copies(at, tokens, mine, strip, sems)
        for i in range(three):
            copies.append(
                pltpu.make_async_copy(
                    w_qkv.at[0, i, rows, lanes], packed.at[i * side : (i + 1) * side], sems.at[2 + i]
                )
            )
        loads = [
            pltpu.make_async_copy(line, hold, sems.at[6 + i])
            for i, (line, hold) in enumerate(zip(lines, held))
        ]
        for copy in copies:
            copy.start()
        run_copies(loads)
        fill_table(table, at[S_GIVE], held)
        rounded[...] = table[...].astype(B16)
        run_copies([pltpu.make_async_copy(rounded, packed.at[three * side :], sems.at[5])])
        for copy in copies:
            copy.wait()

    return copy_kernel(
        "pack_first", body, token_shapes(tokens) + [(three * side + TABLE, ONE)], at,
        [tokens, w_qkv, *vectors],
        [pltpu.VMEM((TABLE, ONE), F32), pltpu.VMEM((TABLE, ONE), B16), pltpu.SemaphoreType.DMA((6 + count,))]
        + [pltpu.VMEM(v.shape, B16) for v in vectors],
    )


def pack_second(at, tokens, w_up, w_out, w_down):
    dim, units, heads = w_up.shape[1], w_up.shape[2] // 4, w_out.shape[1] // 4
    side = dim // 2

    def body(at, tokens, w_up, w_out, w_down, mine, strip, up, down, sems):
        copies = token_copies(at, tokens, mine, strip, sems)
        rows = pl.ds(pl.multiple_of(at[S_CORE] * side, side), side)
        lanes = pl.ds(pl.multiple_of(at[S_GIVE] * units, units), units)
        copies.append(pltpu.make_async_copy(w_up.at[0, rows, lanes], up, sems.at[2]))
        part = 2 * at[S_GIVE] + at[S_CORE]
        for i, (source, size, start) in enumerate(
            ((w_down, units // 2, 0), (w_out, heads // 2, units // 2))
        ):
            rows = pl.ds(pl.multiple_of(part * size, size), size)
            copies.append(
                pltpu.make_async_copy(
                    source.at[0, rows], down.at[start : start + size], sems.at[3 + i]
                )
            )
        run_copies(copies)

    return copy_kernel(
        "pack_second", body, token_shapes(tokens) + [(side, units), ((units + heads) // 2, dim)], at,
        [tokens, w_up, w_out, w_down], [pltpu.SemaphoreType.DMA((5,))],
    )


def fill_table(table, index, vectors):
    *lines, b_up, b_qkv = vectors
    units, heads = b_up.shape[1] // 4, b_qkv.shape[2] // 4
    table[...] = jnp.zeros_like(table)
    row = 0
    for line in lines:
        for i in range(line.shape[1] // ONE):
            table[row : row + 1] = line[:, i * ONE : (i + 1) * ONE].astype(F32)
            row += 1
    for i in range(units // ONE):
        lanes = pl.ds(pl.multiple_of(index * units + i * ONE, ONE), ONE)
        table[row : row + 1] = b_up[:, lanes].astype(F32)
        row += 1
    few = b_qkv[0, :, pl.ds(pl.multiple_of(index * heads, ONE), heads)].astype(F32)
    table[row : row + few.shape[0]] = few


TABLE = 48


def vector_rows(at, vectors, got):
    dim = vectors[0].shape[1]
    units, few = vectors[5].shape[1] // 4, vectors[6].shape[1]

    def body(at, *refs):
        *lines, got, rows0, rows1, table = refs
        fill_table(table, at[S_OWN], lines)
        taken = got[got.shape[0] - TABLE :].astype(F32)
        is_first = at[S_SECTION] == 0
        for rows, lines in (
            (rows0, jnp.where(is_first, table[...], taken)),
            (rows1, jnp.where(is_first, taken, table[...])),
        ):
            rows[...] = jnp.zeros_like(rows)
            line = 0
            for r, tiles in enumerate([dim // ONE] * 5 + [units // ONE, few]):
                for i in range(tiles):
                    rows[r : r + 1, i * ONE : (i + 1) * ONE] = lines[line : line + 1]
                    line += 1

    return kernel_call_named(
        "vector_rows", body, [((8, dim), F32)] * 2, at, *vectors, got,
        scratch=[pltpu.VMEM((TABLE, ONE), F32)],
    )


def half_rows(at, which, size):
    return pl.ds(pl.multiple_of((at[S_CORE] ^ which) * size, size), size)


def qkv_copies(at, own, got, rest, target):
    three, heads = own.shape[1], own.shape[3] // 4
    side = own.shape[2] // 2
    lanes = pl.ds(pl.multiple_of(at[S_OWN] * heads, heads), heads)
    mine, halves = [], []
    for i in range(three):
        tile = slice(i * heads, (i + 1) * heads)
        mine.append((own.at[0, i, :, lanes], target[0].at[:, tile]))
        for which, source in ((0, got), (1, rest)):
            halves.append(
                (
                    source.at[i * side : (i + 1) * side],
                    target[1].at[half_rows(at, which, side), tile],
                )
            )
    return mine + halves


def up_copies(at, own, got, rest, target):
    side, units = got.shape
    lanes = pl.ds(pl.multiple_of(at[S_OWN] * units, units), units)
    return [(own.at[0, :, lanes], target[0])] + [
        (source, target[1].at[half_rows(at, which, side)])
        for which, source in ((0, got), (1, rest))
    ]


def row_copies(at, own, got, rest, target, start):
    size = target[0].shape[0]
    side = size // 2
    rows = pl.ds(pl.multiple_of(at[S_OWN] * size, size), size)
    return [(own.at[0, rows], target[0])] + [
        (source.at[start : start + side], target[1].at[half_rows(at, which, side)])
        for which, source in ((0, got), (1, rest))
    ]


def choose_weights(name, at, owns, got, rest, shapes, make):
    count = len(owns)

    def body(at, *refs):
        own, (got, rest), targets, sems = refs[:count], refs[count : count + 2], refs[count + 2 : -1], refs[-1]
        for section in range(2):

            @pl.when(at[S_SECTION] == section)
            def _():
                pairs = make(
                    at, own, got, rest,
                    [(targets[2 * i + section], targets[2 * i + 1 - section]) for i in range(count)],
                )
                run_copies(
                    [
                        pltpu.make_async_copy(source, target, sems.at[i])
                        for i, (source, target) in enumerate(pairs)
                    ]
                )

    outs = [(shape, B16) for shape in shapes for _ in range(2)]
    return kernel_call(
        body, outs, at, hbm=owns, free=[got, rest],
        scratch=[pltpu.SemaphoreType.DMA((9,))], name=name,
    )


def weights_call(name, body, outs, at, arrays, weights, scratch=(), flops=0, exps=0):
    first, count = len(arrays), len(weights)

    def wrapped(at, *refs):
        given, chosen, rest = refs[:first], refs[first : first + count], refs[first + count :]
        made, own = rest[: len(outs)], rest[len(outs) :]
        body(at, *given, *made, *chosen, *own)

    return kernel_call(
        wrapped, outs, at, *arrays, *weights, scratch=scratch, flops=flops, exps=exps, name=name
    )


def first_weights(at, vectors, w_qkv, sent):
    _, three, dim, wide = w_qkv.shape
    got = swapped(sent, SECTION)
    qkv = choose_weights(
        "choose_qkv", at, [w_qkv], got, swapped(got, CORE), [(dim, three * (wide // 4))],
        lambda at, own, got, rest, to: qkv_copies(at, own[0], got, rest, to[0]),
    )
    return got, [dict(qkv=q, rows=r) for q, r in zip(qkv, vector_rows(at, vectors, got))]


def up_weights(at, w_up, got, rest):
    return choose_weights(
        "choose_up", at, [w_up], got, rest, [(w_up.shape[1], w_up.shape[2] // 4)],
        lambda at, own, got, rest, to: up_copies(at, own[0], got, rest, to[0]),
    )


def row_weights(at, w_down, w_out, got, rest):
    _, tall, dim = w_down.shape
    units, heads = tall // 4, w_out.shape[1] // 4
    return choose_weights(
        "choose_rows", at, [w_down, w_out], got, rest, [(units, dim), (heads, dim)],
        lambda at, own, got, rest, to: row_copies(at, own[0], got, rest, to[0], 0)
        + row_copies(at, own[1], got, rest, to[1], units // 2),
    )


def turn_tables(at, rows):
    half_rot = ROT // 2
    place = lax.broadcasted_iota(jnp.int32, (rows, ONE), 0)
    lane = lax.broadcasted_iota(jnp.int32, (rows, ONE), 1) % HD
    positions = (2 * (place // ONE) + at[S_CORE]) * ONE + place % ONE
    freqs = 1.0 / 10000.0 ** ((2 * (lane % half_rot)).astype(F32) / ROT)
    angles = positions.astype(F32) * freqs
    sine = jnp.sin(angles)
    return (
        jnp.where(lane < ROT, jnp.cos(angles), 1.0),
        jnp.where((lane >= half_rot) & (lane < ROT), sine, 0.0),
        jnp.where(lane < half_rot, -sine, 0.0),
    )


def keep_blocks(at, source, blocks):
    mine, give = blocks
    place = (2 * at[S_HALF] + at[S_NEAR]) * ONE
    mine[...] = source[pl.ds(pl.multiple_of(place, ONE), ONE)]
    size = give.shape[0]
    place = (2 * (1 - at[S_HALF]) + at[S_NEAR]) * ONE + at[S_SIDE] * size
    give[...] = source[pl.ds(pl.multiple_of(place, size), size)]


def keep_piece(at, source, piece):
    size = piece.shape[0]
    piece[...] = source[pl.ds(pl.multiple_of(at[S_CHIP] * size, size), size)]


def front(at, loader, sources, w, turns, with_piece):
    dim = w["qkv"].shape[0]
    rows = turns[0].shape[0]
    count = len(sources)

    def body(at, *refs):
        given = refs[:count]
        vectors, *turns = refs[count : count + 4]
        attn_in, mlp_in, normed_out, q, kv = refs[count + 4 : count + 9]
        *kept, qkv, ordered = refs[count + 9 :]
        gains = [vectors[i : i + 1] for i in range(4)]
        for place, block in loader(at, given):
            size = block.shape[0]
            ordered[pl.ds(pl.multiple_of(place * size, size), size)] = block
        if with_piece:
            keep_piece(at, ordered, kept[0])
        else:
            keep_blocks(at, ordered, kept)
        bias = vectors[6:7, : 3 * ONE]

        def norm(span):
            hidden = ordered[span].astype(F32)
            mean = jnp.sum(hidden, axis=1, keepdims=True) * (1.0 / dim)
            centre = hidden - mean
            var = jnp.sum(centre * centre, axis=1, keepdims=True) * (1.0 / dim)
            normed = centre * lax.rsqrt(var + 1e-05)
            attn_in[span] = (normed * gains[0] + gains[1]).astype(B16)
            mlp_in[span] = (normed * gains[2] + gains[3]).astype(B16)
            normed_out[span] = normed.astype(B16)

        def project(span):
            projected = nn(attn_in[span], qkv[...]) + bias
            cosine, second, first_half = [table[span] for table in turns]
            for i, target in ((0, q), (1, kv.at[0])):
                flat = projected[:, i * ONE : (i + 1) * ONE]
                flat = (
                    flat * cosine
                    + pltpu.roll(flat, ROT // 2, 1) * second
                    + pltpu.roll(flat, ONE - ROT // 2, 1) * first_half
                )
                target[span] = flat.astype(B16)
            kv[1, span] = projected[:, 2 * ONE :].astype(B16)

        by_rows(rows, 256, norm)
        by_rows(rows, rows, project)

    outs = [((rows, dim), B16)] * 3 + [((rows, ONE), B16), ((2, rows, ONE), B16)]
    outs += [((rows // 8, dim), B16)] if with_piece else [((n, dim), B16) for n in (ONE, ONE // 2)]
    return weights_call(
        "front", body, outs, at, [*sources, w["rows"], *turns], [w["qkv"]],
        scratch=[pltpu.VMEM((rows, dim), B16)],
        flops=2 * rows * dim * 3 * ONE + 20 * rows * dim,
    )


def units_forward(at, mlp_in, w):
    rows, dim = mlp_in.shape
    units = w["units"]

    def body(at, mlp_in, vectors, active, slope, up):
        bias = vectors[5:6, :units]

        def gelu(span):
            value = nn(mlp_in[span], up[...]) + bias
            cdf = 0.5 + 0.5 * lax.erf(value * (1.0 / math.sqrt(2.0)))
            pdf = jnp.exp(value * value * -0.5) * (1.0 / math.sqrt(2.0 * math.pi))
            active[span] = (value * cdf).astype(B16)
            slope[span] = (cdf + value * pdf).astype(B16)

        by_rows(rows, rows, gelu)

    return weights_call(
        "units_forward", body, [((rows, units), B16)] * 2, at, [mlp_in, w["rows"]], [w["up"]],
        flops=2 * rows * dim * units + 40 * rows * units, exps=rows * units,
    )


def head_lanes():
    return lax.broadcasted_iota(jnp.int32, (1, ONE), 1) < HD


def by_head(array):
    first_head = head_lanes()
    zero = jnp.zeros_like(array)
    return jnp.concatenate(
        [jnp.where(first_head, array, zero), jnp.where(first_head, zero, array)], axis=0
    )


def joined_heads(array):
    half = array.shape[0] // 2
    return jnp.where(head_lanes(), array[:half], array[half:])


def allowed_keys(at, first, step, count):
    row = lax.broadcasted_iota(jnp.int32, (2 * step, count), 0) % step + first
    column = lax.broadcasted_iota(jnp.int32, (2 * step, count), 1)
    return column <= row, column < (row // ONE + at[S_CORE]) * ONE


STEPS = (0, 1, 4, 5)
STEP_CHIPS = (0, SIDE, SECTION, SECTION | SIDE)


def pieces_out(at, total, pieces):
    size = total.shape[0] // 8
    for step, piece in zip(STEPS, pieces):
        for i in range(2):
            place = (at[S_CHIP] ^ (step | 2 * i)) * size
            piece[i] = total[pl.ds(pl.multiple_of(place, size), size)].astype(piece.dtype)


def piece_shapes(rows, dim):
    return [((2, rows // 8, dim), F32)] + [((2, rows // 8, dim), B16)] * 3


def fold(at, pieces):
    _, rows, dim = pieces[0].shape

    def body(at, *refs):
        *given, keep, give = refs
        for i, target in ((0, keep), (1, give)):
            total = given[0][i]
            for piece in given[1:]:
                total = total + piece[i].astype(F32)
            target[...] = total.astype(target.dtype)

    return kernel_call_named("fold", body, [((rows, dim), F32), ((rows, dim), B16)], at, *pieces)


def exchanged(pieces):
    return [pieces[0]] + [swapped(p, m) for p, m in zip(pieces[1:], STEP_CHIPS[1:])]


def gathered(piece, near):
    pair = jnp.stack([piece, near])
    return [pair] + [swapped(pair, mask) for mask in STEP_CHIPS[1:]]


def attention_forward(at, q, kv, kv_other):
    rows = q.shape[0]
    scale = 1.0 / math.sqrt(HD)

    def body(at, q, kv, kv_other, mixed, lse):
        step = 256
        for first in range(0, rows, step):
            span = slice(first, first + step)
            count = first + step
            one = by_head(q[span] * scale)
            scores = [
                jnp.where(mask, nt(one, keys[0, :count]), -1e9)
                for mask, keys in zip(allowed_keys(at, first, step, count), (kv, kv_other))
            ]
            most = jnp.maximum(
                jnp.max(scores[0], axis=1, keepdims=True),
                jnp.max(scores[1], axis=1, keepdims=True),
            )
            exponents = [jnp.exp(s - most) for s in scores]
            summed = jnp.sum(exponents[0], axis=1, keepdims=True) + jnp.sum(
                exponents[1], axis=1, keepdims=True
            )
            inverse = 1.0 / summed
            result = nn(exponents[0].astype(B16), kv[1, :count]) + nn(
                exponents[1].astype(B16), kv_other[1, :count]
            )
            mixed[span] = joined_heads(result * inverse).astype(B16)
            lse[span] = joined_heads(
                jnp.broadcast_to(most + jnp.log(summed), (2 * step, ONE))
            )

    return kernel_call_named(
        "attention_forward", body, [((rows, ONE), B16), ((rows, ONE), F32)], at, q, kv, kv_other,
        flops=8 * rows * rows * ONE * 2, exps=2 * rows * rows * 2,
    )


def outputs_forward(at, mixed, active, w):
    rows = mixed.shape[0]
    units, dim = w["down"].shape

    def body(at, mixed, active, *rest):
        pieces, (out, down, total) = rest[:4], rest[4:]

        def one(span):
            total[span] = nn(mixed[span], out[...]) + nn(active[span], down[...])

        by_rows(rows, rows, one)
        pieces_out(at, total, pieces)

    return weights_call(
        "outputs_forward", body, piece_shapes(rows, dim), at, [mixed, active],
        [w["out"], w["down"]], scratch=[pltpu.VMEM((rows, dim), F32)],
        flops=2 * rows * dim * (units + ONE),
    )


def units_backward(at, loader, sources, slope, w, with_piece):
    rows, units = slope.shape
    dim = w["up"].shape[0]
    count = len(sources)

    def body(at, *refs):
        given = refs[:count]
        slope, g, up_grad, mixed_grad = refs[count : count + 4]
        *kept, down, out = refs[count + 4 :]
        for place, block in loader(at, given):
            size = block.shape[0]
            g[pl.ds(pl.multiple_of(place * size, size), size)] = block
        if with_piece:
            keep_piece(at, g, kept[0])
        else:
            keep_blocks(at, g, kept)

        def back(span):
            up_grad[span] = (nt(g[span], down[...]) * slope[span].astype(F32)).astype(B16)
            mixed_grad[span] = nt(g[span], out[...]).astype(B16)

        by_rows(rows, rows, back)

    outs = [((rows, dim), B16), ((rows, units), B16), ((rows, ONE), B16)]
    outs += [((rows // 8, dim), B16)] if with_piece else [((n, dim), B16) for n in (ONE, ONE // 2)]
    return weights_call(
        "units_backward", body, outs, at, [*sources, slope], [w["down"], w["out"]],
        flops=2 * rows * dim * (units + ONE),
    )


def attention_backward(at, q, kv, kv_other, lse, mixed_grad):
    rows = q.shape[0]
    scale = 1.0 / math.sqrt(HD)

    def body(at, q, kv, kv_other, lse, mixed_grad, dq, dkv, dkv_other):
        step = 256
        dkv[...] = jnp.zeros_like(dkv)
        dkv_other[...] = jnp.zeros_like(dkv_other)
        for first in range(0, rows, step):
            span = slice(first, first + step)
            count = first + step
            one, one_back = by_head(q[span] * scale), by_head(mixed_grad[span])
            masks = allowed_keys(at, first, step, count)
            sides = ((masks[0], kv, dkv), (masks[1], kv_other, dkv_other))
            level = jnp.concatenate([lse[span, :1], lse[span, HD : HD + 1]], axis=0)
            probs, grads = [], []
            for mask, keys, _ in sides:
                scores = nt(one, keys[0, :count])
                probs.append(jnp.exp(jnp.where(mask, scores, -1e9) - level))
                grads.append(nt(one_back, keys[1, :count]))
            delta = jnp.sum(probs[0] * grads[0], axis=1, keepdims=True) + jnp.sum(
                probs[1] * grads[1], axis=1, keepdims=True
            )
            result = 0.0
            for (_, keys, target), prob, grad in zip(sides, probs, grads):
                score_grad = (prob * (grad - delta)).astype(B16)
                result = result + nn(score_grad, keys[0, :count])
                target[0, :count] += tn(score_grad, one)
                target[1, :count] += tn(prob.astype(B16), one_back)
            dq[span] = joined_heads(result) * scale

    return kernel_call_named(
        "attention_backward",
        body, [((rows, ONE), F32), ((2, rows, ONE), F32), ((2, rows, ONE), F32)],
        at, q, kv, kv_other, lse, mixed_grad,
        flops=20 * rows * rows * ONE * 2, exps=2 * rows * rows * 2,
    )


def inputs_backward(at, dq, dkv, dkv_got, up_grad, normed, g, turns, w):
    rows, dim = normed.shape
    units = up_grad.shape[1]

    def body(at, dq, dkv, dkv_got, up_grad, normed, g, *rest):
        turns, vectors, rest = rest[:3], rest[3], rest[4:]
        qkv_grad, table = rest[:2]
        pieces, (qkv, up, total, lines) = rest[2:6], rest[6:]
        gain_one, gain_two = vectors[0:1], vectors[2:3]
        step = rows

        def one(i, sums):
            span = pl.ds(pl.multiple_of(i * step, step), step)
            cosine, second, first_half = [table[span] for table in turns]
            parts = []
            for flat in (dq[span], dkv[0, span] + dkv_got[0, span]):
                parts.append(
                    flat * cosine
                    - pltpu.roll(flat, ROT // 2, 1) * second
                    - pltpu.roll(flat, ONE - ROT // 2, 1) * first_half
                )
            parts.append(dkv[1, span] + dkv_got[1, span])
            both = jnp.concatenate([p.astype(B16) for p in parts], axis=1)
            qkv_grad[span] = both
            attn = nt(both, qkv[...])
            mlp = nt(up_grad[span], up[...])
            total[span] = attn * gain_one + mlp * gain_two
            unit = normed[span].astype(F32)
            new = [
                jnp.sum(v, axis=0, keepdims=True)
                for v in (
                    attn * unit, attn, mlp * unit, mlp, g[span].astype(F32),
                    up_grad[span].astype(F32), both.astype(F32),
                )
            ]
            return tuple(a + b for a, b in zip(sums, new))

        widths = (dim,) * 5 + (units, 3 * ONE)
        sums = lax.fori_loop(
            0, rows // step, one, tuple(jnp.zeros((1, width), F32) for width in widths)
        )
        pieces_out(at, total, pieces)
        lines[...] = jnp.zeros_like(lines)
        line = 0
        for value in sums:
            for i in range(value.shape[1] // ONE):
                lines[line : line + 1] = value[:, i * ONE : (i + 1) * ONE]
                line += 1
        table[...] = lines[...].astype(B16)

    outs = [((rows, 3 * ONE), B16), ((LINES, ONE), B16)] + piece_shapes(rows, dim)
    return weights_call(
        "inputs_backward", body, outs, at,
        [dq, dkv, dkv_got, up_grad, normed, g, *turns, w["rows"]], [w["qkv"], w["up"]],
        scratch=[pltpu.VMEM((rows, dim), F32), pltpu.VMEM((LINES, ONE), F32)],
        flops=2 * rows * dim * (units + 3 * ONE) + 12 * rows * dim,
    )


LINES = 64


def join_forward(at, x_piece, parts, w):
    def body(at, x, vectors, own, *rest):
        total = x[...].astype(F32) + own[...].astype(F32) + vectors[4:5]
        for piece in rest[:-1]:
            total = total + piece[...].astype(F32)
        rest[-1][...] = total.astype(B16)

    return kernel_call_named("join_forward", body, [(x_piece.shape, B16)], at, x_piece, w["rows"], *parts)[0]


def join_backward(at, g_piece, x_piece, parts):
    dim = x_piece.shape[1]

    def body(at, g, x, own, *rest):
        total = own[...]
        for piece in rest[:-1]:
            total = total + piece[...].astype(F32)
        hidden = x[...].astype(F32)
        centre = hidden - jnp.sum(hidden, axis=1, keepdims=True) * (1.0 / dim)
        var = jnp.sum(centre * centre, axis=1, keepdims=True) * (1.0 / dim)
        scale = lax.rsqrt(var + 1e-05)
        normed = centre * scale
        inner = (
            total
            - jnp.sum(total, axis=1, keepdims=True) * (1.0 / dim)
            - normed * (jnp.sum(total * normed, axis=1, keepdims=True) * (1.0 / dim))
        )
        rest[-1][...] = (g[...].astype(F32) + scale * inner).astype(B16)

    return kernel_call_named("join_backward", body, [(x_piece.shape, B16)], at, g_piece, x_piece, *parts)[0]


def columns(at, ref, core, high):
    which = at[S_CORE] ^ core
    return jnp.concatenate(
        [
            ref[:, pl.ds(pl.multiple_of((4 * high + 2 * low + which) * ONE, ONE), ONE)]
            for low in range(2)
        ],
        axis=1,
    )


def early_grads(at, active, mixed, mlp_in, up_grad, g):
    rows, dim = g.shape
    units = active.shape[1]
    tiles = units // ONE

    def body(at, active, mixed, mlp_in, up_grad, g, keep, give):
        for core, target in ((0, keep), (1, give)):
            strip = jnp.concatenate([columns(at, g, core, high) for high in range(2)], axis=1)
            down = tn(active[...], strip).astype(B16)
            out = tn(mixed[...], strip).astype(B16)
            for high in range(2):
                up = tn(columns(at, mlp_in, core, high), up_grad[...]).astype(B16)
                for low in range(2):
                    lanes = slice((2 * high + low) * ONE, (2 * high + low + 1) * ONE)
                    where = (at[S_HALF] ^ high, at[S_NEAR] ^ low)
                    target[where[0], where[1], :units] = down[:, lanes]
                    target[where[0], where[1], units : units + ONE] = out[:, lanes]
                    for i in range(tiles):
                        base = units + (1 + i) * ONE
                        target[where[0], where[1], base : base + ONE] = up[
                            low * ONE : (low + 1) * ONE, i * ONE : (i + 1) * ONE
                        ]

    shape = (2, 2, 2 * units + ONE, ONE)
    return kernel_call_named(
        "early_grads",
        body, [(shape, B16)] * 2, at, active, mixed, mlp_in, up_grad, g,
        flops=2 * rows * dim * (2 * units + ONE),
    )


def late_grads(at, attn_in, qkv_grad, tables):
    rows, dim = attn_in.shape
    count = len(tables)

    def body(at, attn_in, qkv_grad, *refs):
        tables, (keep, give) = refs[:count], refs[count:]
        for core, target in ((0, keep), (1, give)):
            for high in range(2):
                qkv = tn(columns(at, attn_in, core, high), qkv_grad[...]).astype(B16)
                for low in range(2):
                    where = (at[S_HALF] ^ high, at[S_NEAR] ^ low)
                    for i in range(3):
                        target[where[0], where[1], i * ONE : (i + 1) * ONE] = qkv[
                            low * ONE : (low + 1) * ONE, i * ONE : (i + 1) * ONE
                        ]
                    for i, table in enumerate(tables):
                        base = 3 * ONE + i * LINES
                        target[where[0], where[1], base : base + LINES] = table[...]

    shape = (2, 2, 3 * ONE + count * LINES, ONE)
    return kernel_call_named(
        "late_grads", body, [(shape, B16)] * 2, at, attn_in, qkv_grad, *tables,
        flops=2 * rows * dim * 3 * ONE,
    )


def plus(a, b):
    return (a.astype(F32) + b.astype(F32)).astype(B16)


def summed_cores(keep, give, *earlier):
    got = swapped(after(give, *earlier), CORE)
    return (
        [plus(keep[0, i], got[0, i]) for i in range(2)],
        [plus(keep[1, i], got[1, i]) for i in range(2)],
    )


def sum_lines(at, late):
    def body(at, *refs):
        *late, lines = refs
        total = 0.0
        for part in late:
            total = total + part[3 * ONE : 3 * ONE + lines.shape[0]].astype(F32)
        lines[...] = total

    return kernel_call_named("sum_lines", body, [((32, ONE), F32)], at, *late)[0]


def unpack_grads(at, early, late, sizes):
    dim_part, units, heads = ONE, sizes["units"], ONE

    def body(at, *refs):
        early, late = refs[:4], refs[4:8]
        qkv, out, up, down, b_qkv, b_up, branch = refs[8:]
        index = at[S_OWN]
        for j, (wide, narrow) in enumerate(zip(early, late)):
            source = index ^ (2 * (j % 2) + j // 2)
            place = pl.multiple_of(source * units, units)
            small = pl.multiple_of(source * ONE, ONE)
            down[pl.ds(place, units)] = wide[:units].astype(F32)
            out[pl.ds(small, ONE)] = wide[units : units + ONE].astype(F32)
            for i in range(units // ONE):
                base = units + (1 + i) * ONE
                up[:, pl.ds(place + i * ONE, ONE)] = wide[base : base + ONE].astype(F32)
            for i in range(3):
                qkv[i, :, pl.ds(small, ONE)] = narrow[i * ONE : (i + 1) * ONE].astype(F32)
            table = narrow[3 * ONE :].astype(F32)
            for i in range(units // ONE):
                b_up[:, pl.ds(place + i * ONE, ONE)] = table[40 + i : 41 + i]
            for i in range(3):
                b_qkv[i : i + 1, pl.ds(small, ONE)] = table[40 + units // ONE + i :][:1]
            if j == 0:
                branch[...] = table[32:40]

    outs = [
        ((3, dim_part, 4 * heads), F32),
        ((4 * heads, dim_part), F32),
        ((dim_part, 4 * units), F32),
        ((4 * units, dim_part), F32),
        ((3, 4 * heads), F32),
        ((1, 4 * units), F32),
        ((8, ONE), F32),
    ]
    return kernel_call_named("unpack_grads", body, outs, at, *early, *late, keep=False)


def cube_device(
    inputs, cotangent, ln1_gain, ln1_bias, ln2_gain, ln2_bias, qkv_weight, qkv_bias,
    out_weight, up_weight, up_bias, down_weight, branch_bias,
):
    at = where_am_i()
    section, half, side = [lax.axis_index("section"), lax.axis_index("ctx") // 4, lax.axis_index("tp")]
    at, is_first, is_low, is_left, is_near = lax.optimization_barrier(
        (at, section == 0, half == 0, side == 0, section == half)
    )
    dim = inputs.shape[2]
    rows = 4 * inputs.shape[1]
    vectors = (ln1_gain, ln1_bias, ln2_gain, ln2_bias, branch_bias, up_bias, qkv_bias)

    mine, strip, sent_qkv = pack_first(at, inputs, vectors, qkv_weight)
    g_mine, g_strip, sent_up, sent_down = pack_second(
        at, cotangent, up_weight, out_weight, down_weight
    )
    strips = send_strips(strip)
    turns = turn_tables(at, rows)
    sides = [swapped(after(part, turns[0]), SIDE) for part in strips]
    x_parts = (mine, swapped(mine, NEAR), *strips, *sides)
    got_qkv, layers = first_weights(at, vectors, qkv_weight, sent_qkv)
    got_up = swapped(after(sent_up, got_qkv), SECTION)
    first, second = layers
    got_down = swapped(
        after(sent_down, got_up, *x_parts[4:], first["qkv"], first["rows"]), SECTION
    )

    g_near = swapped(after(g_mine, *x_parts[4:]), NEAR)

    def bring_up(*earlier):
        up = up_weights(at, up_weight, got_up, swapped(after(got_up, *earlier), CORE))
        for i, layer in enumerate(layers):
            layer.update(up=up[i], units=up[i].shape[1])

    def bring_rows(*earlier):
        tall = row_weights(
            at, down_weight, out_weight, got_down, swapped(after(got_down, *earlier), CORE)
        )
        for i, layer in enumerate(layers):
            layer.update(down=tall[i], out=tall[2 + i])

    def forward(loader, sources, w, with_piece):
        got = front(at, loader, sources, w, turns, with_piece)
        attn_in, mlp_in, normed, q, kv = got[:5]
        kv_other = swapped(kv, CORE)
        is_start = "up" not in w
        if is_start:
            bring_up(q)
        active, slope = units_forward(at, mlp_in, w)
        mixed, lse = attention_forward(at, q, kv, kv_other)
        if is_start:
            bring_rows(active, mixed, g_near)
        pieces = outputs_forward(at, mixed, active, w)
        saved = dict(
            attn_in=attn_in, mlp_in=mlp_in, normed=normed, q=q, kv=kv, kv_other=kv_other,
            active=active, slope=slope, mixed=mixed, lse=lse,
        )
        return pieces, saved, got[5:]

    def backward(loader, sources, saved, w, with_piece, grads_first):
        made = units_backward(at, loader, sources, saved["slope"], w, with_piece)
        g, up_grad, mixed_grad = made[:3]
        if grads_first:
            early = early_grads(
                at, saved["active"], saved["mixed"], saved["mlp_in"], up_grad, g
            )
            mixed_grad = after(mixed_grad, early[0])
        dq, dkv, dkv_other = attention_backward(
            at, saved["q"], saved["kv"], saved["kv_other"], saved["lse"], mixed_grad
        )
        dkv_got = swapped(dkv_other, CORE)
        if not grads_first:
            early = early_grads(
                at, saved["active"], saved["mixed"], saved["mlp_in"], up_grad, after(g, dkv_other)
            )
            dq = after(dq, early[0])
        given = (dq, dkv, dkv_got, up_grad, saved["normed"], g)
        return early, given, made[3:]

    def backward_end(given, saved, w):
        out = inputs_backward(at, *given, turns, w)
        return out[0], out[1], out[2:]

    parts, saved_first, (x_piece,) = forward(start_loader, x_parts, first, True)
    strips = send_strips(after(g_strip, parts[0]))
    parts = exchanged(parts)
    parts[0] = after(parts[0], *strips)
    keep, give = fold(at, parts)
    sides = [swapped(part, SIDE) for part in strips]
    piece = join_forward(at, x_piece, [keep, swapped(give, NEAR)], first)
    near = after(swapped(piece, NEAR), *sides)
    middle = gathered(piece, near)
    g_parts = (g_mine, g_near, *strips, *sides)

    parts_last, saved_second, blocks = forward(piece_loader, middle, second, False)
    acts_mine, acts_give = blocks

    early, given, (g_piece,) = backward(
        start_loader, g_parts, saved_second, second, True, False
    )
    early_keep, early_give = summed_cores(*early, given[2])
    qkv_grad, table_second, pieces = backward_end(given, saved_second, second)
    late = late_grads(at, saved_second["attn_in"], qkv_grad, ())
    parts = exchanged(pieces)
    far_second = swapped(early_give[1], HALF)
    parts[0] = after(parts[0], far_second, *late)
    keep, give = fold(at, parts)
    late_keep, late_give = summed_cores(*late)
    late_got = swapped(after(jnp.stack(late_give), give), HALF)
    parts_last = exchanged([after(p, give) for p in parts_last])
    back = join_backward(at, g_piece, piece, [keep, swapped(give, NEAR)])
    near = after(swapped(back, NEAR), late_got, *parts_last)
    g_middle = gathered(back, near)
    close_second = swapped(after(early_give[0], near), HALF)
    g_middle[0] = after(g_middle[0], close_second)
    keep_last, give_last = fold(at, parts_last)

    early, given, blocks = backward(
        piece_loader, g_middle, saved_first, first, False, True
    )
    in_mine, in_give = blocks
    early_second = [plus(a, b) for a, b in zip(early_keep, (close_second, far_second))]
    late_second = [plus(a, b) for a, b in zip(late_keep, late_got)]
    early_keep, early_give = summed_cores(*early)
    given = (after(given[0], *early_give),) + given[1:]
    qkv_grad, table_first, pieces = backward_end(given, saved_first, first)
    last_near = swapped(give_last, NEAR)
    parts = exchanged([after(p, last_near) for p in pieces])
    far_first = swapped(early_give[1], HALF)
    late = late_grads(at, saved_first["attn_in"], qkv_grad, (table_first, table_second))
    parts[0] = after(parts[0], far_first)
    keep, give = fold(at, parts)
    close_first = swapped(after(early_give[0], give), HALF)
    late_keep, late_give = summed_cores(*late)
    late_got = swapped(after(jnp.stack(late_give), give), HALF)
    back_last = join_backward(
        at, back, x_piece, [keep, after(swapped(give, NEAR), close_first)]
    )
    last = join_forward(at, piece, [keep_last, last_near], second)
    early_first = [plus(a, b) for a, b in zip(early_keep, (close_first, far_first))]
    late_first = [plus(a, b) for a, b in zip(late_keep, late_got)]
    tall = 3 * ONE + LINES
    late_second = [
        jnp.concatenate([a, b[tall:]], axis=0) for a, b in zip(late_second, late_first)
    ]
    late_first = [a[:tall] for a in late_first]
    def brought(close, far):
        own = jnp.where(is_first, close[0], close[1])
        near = swapped(jnp.where(is_first, far[0], far[1]), NEAR)
        got = swapped(jnp.where(is_first, close[1], close[0]), SECTION)
        cross = swapped(jnp.where(is_first, far[1], far[0]), SECTION | NEAR)
        return own, got, near, cross

    early = brought((early_first[0], early_second[0]), (early_first[1], early_second[1]))
    late_first[1] = after(late_first[1], *early)
    late = brought((late_first[0], late_second[0]), (late_first[1], late_second[1]))
    lines = sum_lines(at, late)
    lines = lines + swapped(lines, SIDE)
    sizes = dict(units=up_weight.shape[2] // 4)
    qkv, out, up, down, b_qkv, b_up, branch = unpack_grads(at, early, late, sizes)

    mine = jnp.where(is_first, back_last, last)
    got = swapped(jnp.where(is_first, last, back_last), SECTION)
    stay = jnp.where(is_near, mine, got)
    known_give = jnp.where(is_first, acts_give, in_give)
    other = swapped(jnp.stack([jnp.where(is_near, got, mine), known_give]), HALF)
    own = jnp.stack(
        [jnp.where(is_low, stay, other[0]), jnp.where(is_low, other[0], stay), other[1]]
    )
    rest = swapped(own, SIDE)
    both = jnp.where(
        is_left, jnp.concatenate([own, rest], axis=1), jnp.concatenate([rest, own], axis=1)
    )
    new = both[:2]
    known_mine = jnp.where(is_first, acts_mine, in_mine)
    known = jnp.where(
        is_low, jnp.stack([known_mine, both[2]]), jnp.stack([both[2], known_mine])
    )
    acts = jnp.where(is_first, known, new)
    in_grads = jnp.where(is_first, new, known)

    lines = lines.reshape(4, dim)
    return (
        acts[None],
        in_grads[None],
        lines[0:1],
        lines[1:2],
        lines[2:3],
        lines[3:4],
        qkv[None],
        b_qkv[None],
        out[None],
        up[None],
        b_up,
        down[None],
        branch.reshape(1, dim),
    )


def placed_program(mesh, device_program):
    placed = (
        P(None, "ctx", None),
        P(None, "ctx", None),
        P("section", None),
        P("section", None),
        P("section", None),
        P("section", None),
        P("section", None, None, "tp"),
        P("section", None, "tp"),
        P("section", "tp", None),
        P("section", None, "tp"),
        P("section", "tp"),
        P("section", "tp", None),
        P("section", None),
    )
    return jax.shard_map(
        device_program,
        mesh=mesh,
        in_specs=placed,
        out_specs=(
            P("section", None, "ctx", None),
            P("section", None, "ctx", None),
            P("section", None),
            P("section", None),
            P("section", None),
            P("section", None),
            P("section", None, "ctx", "tp"),
            P("section", None, "tp"),
            P("section", "tp", "ctx"),
            P("section", "ctx", "tp"),
            P("section", "tp"),
            P("section", "tp", "ctx"),
            P("section", None),
        ),
        check_vma=False,
    )


def solution(mesh):
    sizes = dict(mesh.shape)
    if sizes["section"] == 2 and sizes["tp"] == 2 and sizes["ctx"] == 8:
        return placed_program(mesh, cube_device)
    return placed_program(mesh, per_device)
```

```python
import math

import jax
import jax.numpy as jnp
from jax import lax
from jax.experimental import pallas as pl
from jax.experimental.pallas import tpu as pltpu
from jax.sharding import PartitionSpec as P

HD = 64
ROT = 16


def shifted(shard, axis, by):
    peers = lax.axis_size(axis)
    pairs = [(i, i + by) for i in range(peers) if 0 <= i + by < peers]
    return lax.ppermute(shard, axis, pairs)


def tables(positions):
    freqs = 1.0 / 10000.0 ** (jnp.arange(0, ROT, 2).astype(jnp.float32) / ROT)
    angles = positions.astype(jnp.float32)[:, None] * freqs[None, :]
    return (jnp.cos(angles)[:, None, :], jnp.sin(angles)[:, None, :])


def rotate(field, cosine, sine):
    half_rot = ROT // 2
    front = field[..., :half_rot]
    second = field[..., half_rot:ROT]
    return jnp.concatenate(
        [front * cosine - second * sine, second * cosine + front * sine, field[..., ROT:]], axis=-1
    )


def norms(hidden, gain_one, shift_one, gain_two, shift_two):
    centre = hidden - jnp.mean(hidden, axis=-1, keepdims=True)
    normed = centre * lax.rsqrt(jnp.mean(centre * centre, axis=-1, keepdims=True) + 1e-05)
    return (normed * gain_one + shift_one, normed * gain_two + shift_two)


def gelu_exact(value):
    return jax.nn.gelu(value, approximate=False)


def scores_of(queries, keys, query_pos, score_scale):
    raw = jnp.einsum("qhd,khd->hqk", queries, keys, preferred_element_type=jnp.float32)
    key_pos = jnp.arange(keys.shape[0], dtype=jnp.int32)
    return jnp.where(
        key_pos[None, None, :] <= query_pos[None, :, None], raw * score_scale, -1000000000.0
    )


def forward_layer(layer_in, weights, query_pos, cosine, sine):
    gains, w_qkv, b_qkv, w_out, w_up, b_up, w_down, b_branch = weights
    hidden = layer_in.astype(jnp.float32)
    attn_norm, mlp_norm = norms(hidden, gains[0], gains[1], gains[2], gains[3])
    attn_in = attn_norm.astype(jnp.bfloat16)
    mlp_in = mlp_norm.astype(jnp.bfloat16)
    projected = (
        jnp.einsum("td,cdf->tcf", attn_in, w_qkv, preferred_element_type=jnp.float32) + b_qkv
    )
    row_count = hidden.shape[0]
    feat_width = projected.shape[2]
    head_count = feat_width // HD
    queries = rotate(projected[:, 0].reshape(row_count, head_count, HD), cosine, sine).astype(
        jnp.bfloat16
    )
    key_flat = (
        rotate(projected[:, 1].reshape(row_count, head_count, HD), cosine, sine)
        .astype(jnp.bfloat16)
        .reshape(row_count, feat_width)
    )
    value_flat = projected[:, 2].astype(jnp.bfloat16)
    all_keys, all_values = (
        lax.all_gather(key_flat, "ctx", axis=0, tiled=True),
        lax.all_gather(value_flat, "ctx", axis=0, tiled=True),
    )
    key_count = all_keys.shape[0]
    score_scale = 1.0 / math.sqrt(HD)
    scores = scores_of(queries, all_keys.reshape(key_count, head_count, HD), query_pos, score_scale)
    row_max = jnp.max(scores, axis=-1, keepdims=True)
    exponent = jnp.exp(scores - row_max)
    summed = jnp.sum(exponent, axis=-1, keepdims=True)
    probability = (exponent / summed).astype(jnp.bfloat16)
    log_total = row_max + jnp.log(summed)
    mixed = jnp.einsum(
        "hqk,khd->qhd",
        probability,
        all_values.reshape(key_count, head_count, HD),
        preferred_element_type=jnp.float32,
    )
    mixed = mixed.reshape(row_count, feat_width).astype(jnp.bfloat16)
    partial_out = jnp.dot(mixed, w_out, preferred_element_type=jnp.float32)
    up_value = jnp.dot(mlp_in, w_up, preferred_element_type=jnp.float32) + b_up
    active = gelu_exact(up_value).astype(jnp.bfloat16)
    partial_out = partial_out + jnp.dot(active, w_down, preferred_element_type=jnp.float32)
    branches = lax.psum(partial_out, "tp")
    layer_out = (hidden + branches + b_branch).astype(jnp.bfloat16)
    stored = (key_flat, value_flat)
    saved = (layer_in, queries, stored, log_total, mixed, up_value, active)
    return (layer_out, saved)


def backward_layer(grad_out, saved, weights, query_pos, cosine, sine):
    gains, w_qkv, b_qkv, w_out, w_up, b_up, w_down, b_branch = weights
    layer_in, queries, stored, log_total, mixed, up_value, active = saved
    grad_full = grad_out.astype(jnp.float32)
    row_count, feat_width = mixed.shape
    head_count = feat_width // HD
    hidden = layer_in.astype(jnp.float32)
    norm_pair, norm_back = jax.vjp(norms, hidden, gains[0], gains[1], gains[2], gains[3])
    attn_in = norm_pair[0].astype(jnp.bfloat16)
    mlp_in = norm_pair[1].astype(jnp.bfloat16)
    active_grad = jnp.einsum("td,fd->tf", grad_out, w_down, preferred_element_type=jnp.float32)
    grad_down = jnp.einsum("tf,td->fd", active, grad_out, preferred_element_type=jnp.float32)
    gelu_back = jax.vjp(gelu_exact, up_value)[1]
    up_grad = gelu_back(active_grad)[0].astype(jnp.bfloat16)
    grad_up_bias = jnp.sum(up_grad.astype(jnp.float32), axis=0)
    grad_up = jnp.einsum("td,tf->df", mlp_in, up_grad, preferred_element_type=jnp.float32)
    mlp_in_grad = jnp.einsum("tf,df->td", up_grad, w_up, preferred_element_type=jnp.float32)
    mixed_grad = jnp.einsum(
        "td,fd->tf", grad_out, w_out, preferred_element_type=jnp.float32
    ).astype(jnp.bfloat16)
    grad_out_weight = jnp.einsum("tf,td->fd", mixed, grad_out, preferred_element_type=jnp.float32)
    all_keys, all_values = (
        lax.all_gather(stored[0], "ctx", axis=0, tiled=True),
        lax.all_gather(stored[1], "ctx", axis=0, tiled=True),
    )
    key_count = all_keys.shape[0]
    keys_heads = all_keys.reshape(key_count, head_count, HD)
    values_heads = all_values.reshape(key_count, head_count, HD)
    score_scale = 1.0 / math.sqrt(HD)
    scores = scores_of(queries, keys_heads, query_pos, score_scale)
    probability = jnp.exp(scores - log_total)
    heads_grad = mixed_grad.reshape(row_count, head_count, HD)
    prob_grad = jnp.einsum(
        "qhd,khd->hqk", heads_grad, values_heads, preferred_element_type=jnp.float32
    )
    centre = jnp.sum(probability * prob_grad, axis=-1, keepdims=True)
    score_grad = (score_scale * probability * (prob_grad - centre)).astype(jnp.bfloat16)
    query_grad = jnp.einsum(
        "hqk,khd->qhd", score_grad, keys_heads, preferred_element_type=jnp.float32
    )
    value_terms = jnp.einsum(
        "hqk,qhd->khd",
        probability.astype(jnp.bfloat16),
        heads_grad,
        preferred_element_type=jnp.float32,
    )
    key_terms = jnp.einsum("hqk,qhd->khd", score_grad, queries, preferred_element_type=jnp.float32)
    key_grad, value_grad = (
        lax.psum_scatter(
            key_terms.reshape(key_count, feat_width), "ctx", scatter_dimension=0, tiled=True
        ),
        lax.psum_scatter(
            value_terms.reshape(key_count, feat_width), "ctx", scatter_dimension=0, tiled=True
        ),
    )
    query_grad = rotate(query_grad, cosine, -sine).reshape(row_count, feat_width)
    key_grad = rotate(key_grad.reshape(row_count, head_count, HD), cosine, -sine).reshape(
        row_count, feat_width
    )
    qkv_grad = jnp.stack([query_grad, key_grad, value_grad], axis=1).astype(jnp.bfloat16)
    grad_qkv_bias = jnp.sum(qkv_grad.astype(jnp.float32), axis=0)
    grad_qkv = jnp.einsum("td,tcf->cdf", attn_in, qkv_grad, preferred_element_type=jnp.float32)
    attn_in_grad = jnp.einsum("tcf,cdf->td", qkv_grad, w_qkv, preferred_element_type=jnp.float32)
    attn_in_grad, mlp_in_grad = lax.psum((attn_in_grad, mlp_in_grad), "tp")
    hidden_grad, gain_one_grad, shift_one_grad, gain_two_grad, shift_two_grad = norm_back(
        (attn_in_grad, mlp_in_grad)
    )
    input_grad = (grad_full + hidden_grad).astype(jnp.bfloat16)
    grad_branch = jnp.sum(grad_full, axis=0)
    grads = (
        gain_one_grad,
        shift_one_grad,
        gain_two_grad,
        shift_two_grad,
        grad_qkv,
        grad_qkv_bias,
        grad_out_weight,
        grad_up,
        grad_up_bias,
        grad_down,
        grad_branch,
    )
    return (input_grad, grads)


def per_device(
    inputs,
    cotangent,
    ln1_gain,
    ln1_bias,
    ln2_gain,
    ln2_bias,
    qkv_weight,
    qkv_bias,
    out_weight,
    up_weight,
    up_bias,
    down_weight,
    branch_bias,
):
    gains = (
        ln1_gain[0].astype(jnp.float32),
        ln1_bias[0].astype(jnp.float32),
        ln2_gain[0].astype(jnp.float32),
        ln2_bias[0].astype(jnp.float32),
    )
    weights = (
        gains,
        qkv_weight[0],
        qkv_bias[0].astype(jnp.float32),
        out_weight[0],
        up_weight[0],
        up_bias[0].astype(jnp.float32),
        down_weight[0],
        branch_bias[0].astype(jnp.float32),
    )
    micro_count = inputs.shape[0]
    row_count = inputs.shape[1]
    query_pos = lax.axis_index("ctx") * row_count + jnp.arange(row_count, dtype=jnp.int32)
    cosine, sine = tables(query_pos)
    at_first = lax.axis_index("section") == 0
    blank = jnp.zeros_like(inputs[0])
    received = blank
    outputs_list = []
    saved_list = []
    for step_index in range(micro_count + 1):
        fresh = inputs[step_index] if step_index < micro_count else blank
        layer_in = jnp.where(at_first, fresh, received)
        layer_out, saved = forward_layer(layer_in, weights, query_pos, cosine, sine)
        outputs_list.append(layer_out)
        saved_list.append(saved)
        if step_index < micro_count:
            received = shifted(layer_out, "section", 1)
    returned = blank
    grad_list = []
    sums = None
    for back_index in range(micro_count + 1):
        batch_index = micro_count - 1 - back_index
        given = cotangent[batch_index] if batch_index >= 0 else blank
        grad_in = jnp.where(at_first, returned, given)
        input_grad, grads = backward_layer(
            grad_in, saved_list[micro_count - back_index], weights, query_pos, cosine, sine
        )
        sums = grads if sums is None else jax.tree.map(jnp.add, sums, grads)
        grad_list.append(input_grad)
        if back_index < micro_count:
            returned = shifted(input_grad, "section", -1)
    acts = jnp.stack(
        [jnp.where(at_first, outputs_list[j], outputs_list[j + 1]) for j in range(micro_count)]
    )[None]
    in_grads = jnp.stack(
        [
            jnp.where(at_first, grad_list[micro_count - j], grad_list[micro_count - 1 - j])
            for j in range(micro_count)
        ]
    )[None]
    (
        gain_one_grad,
        shift_one_grad,
        gain_two_grad,
        shift_two_grad,
        grad_qkv,
        grad_qkv_bias,
        grad_out_weight,
        grad_up,
        grad_up_bias,
        grad_down,
        grad_branch,
    ) = sums
    qkv_part, out_part, up_part, down_part = (
        lax.psum_scatter(
            grad_qkv[None].astype(jnp.bfloat16), "ctx", scatter_dimension=2, tiled=True
        ).astype(jnp.float32),
        lax.psum_scatter(
            grad_out_weight[None].astype(jnp.bfloat16), "ctx", scatter_dimension=2, tiled=True
        ).astype(jnp.float32),
        lax.psum_scatter(
            grad_up[None].astype(jnp.bfloat16), "ctx", scatter_dimension=1, tiled=True
        ).astype(jnp.float32),
        lax.psum_scatter(
            grad_down[None].astype(jnp.bfloat16), "ctx", scatter_dimension=2, tiled=True
        ).astype(jnp.float32),
    )
    small_sums = (
        lax.psum(gain_one_grad[None].astype(jnp.bfloat16), "ctx").astype(jnp.float32),
        lax.psum(shift_one_grad[None].astype(jnp.bfloat16), "ctx").astype(jnp.float32),
        lax.psum(gain_two_grad[None].astype(jnp.bfloat16), "ctx").astype(jnp.float32),
        lax.psum(shift_two_grad[None].astype(jnp.bfloat16), "ctx").astype(jnp.float32),
        lax.psum(grad_qkv_bias[None].astype(jnp.bfloat16), "ctx").astype(jnp.float32),
        lax.psum(grad_up_bias[None].astype(jnp.bfloat16), "ctx").astype(jnp.float32),
        lax.psum(grad_branch[None].astype(jnp.bfloat16), "ctx").astype(jnp.float32),
    )
    return (
        acts,
        in_grads,
        small_sums[0],
        small_sums[1],
        small_sums[2],
        small_sums[3],
        qkv_part,
        small_sums[4],
        out_part,
        up_part,
        small_sums[5],
        down_part,
        small_sums[6],
    )


ALL = ("section", "ctx", "tp")
SECTION, HALF, NEAR, CORE, SIDE = 16, 8, 4, 2, 1
CHIPS = (0, SIDE, NEAR, NEAR | SIDE, SECTION, SECTION | SIDE, SECTION | NEAR, SECTION | NEAR | SIDE)
F32, B16 = jnp.float32, jnp.bfloat16
ONE = 128
S_SECTION, S_HALF, S_NEAR, S_CORE, S_SIDE, S_CHIP, S_OWN, S_GIVE = range(8)


def swapped(array, mask, section=None):
    pairs = [(i, i ^ mask) for i in range(32) if section is None or i // 16 == section]
    return lax.ppermute(array, ALL, pairs)


def after(array, *earlier):
    return lax.optimization_barrier((array,) + earlier)[0]


def where_am_i():
    section = lax.axis_index("section")
    ctx = lax.axis_index("ctx")
    side = lax.axis_index("tp")
    half, near, core = ctx // 4, (ctx // 2) % 2, ctx % 2
    chip = 4 * section + 2 * near + side
    own, give = 2 * section + near, 2 * (1 - section) + near
    return jnp.stack([section, half, near, core, side, chip, own, give]).astype(jnp.int32)


def in_hbm(arrays):
    return [pltpu.with_memory_space_constraint(a, pltpu.HBM) for a in arrays]


def kernel_call(body, outs, at, *arrays, hbm=(), free=(), scratch=(), flops=0, exps=0, name=None, keep=True):
    moved = sum(a.size * a.dtype.itemsize for a in arrays)
    moved += sum(math.prod(s) * jnp.dtype(d).itemsize for s, d in outs)
    return pl.pallas_call(
        body,
        name=name,
        out_shape=[(pltpu.VMEM if keep else jax.ShapeDtypeStruct)(s, d) for s, d in outs],
        in_specs=[pl.BlockSpec(memory_space=pltpu.SMEM)]
        + [pl.BlockSpec(memory_space=pltpu.VMEM)] * len(arrays)
        + [pl.BlockSpec(memory_space=pltpu.HBM)] * len(hbm)
        + [pl.BlockSpec(memory_space=pl.ANY)] * len(free),
        out_specs=[pl.BlockSpec(memory_space=pltpu.VMEM)] * len(outs),
        scratch_shapes=list(scratch),
        compiler_params=pltpu.CompilerParams(vmem_limit_bytes=VMEM_BYTES),
        cost_estimate=pl.CostEstimate(flops=0, bytes_accessed=0, transcendentals=0),
    )(at, *arrays, *in_hbm(hbm), *free)


VMEM_BYTES = 16 * 1024 * 1024


def kernel_call_named(name, *args, **kwargs):
    return kernel_call(*args, name=name, **kwargs)


def by_rows(rows, step, do):
    def one(i, _):
        do(pl.ds(pl.multiple_of(i * step, step), step))
        return 0

    lax.fori_loop(0, rows // step, one, 0)


def nn(a, b):
    return jnp.dot(a, b, preferred_element_type=F32)


def nt(a, b):
    return lax.dot_general(a, b, (((1,), (1,)), ((), ())), preferred_element_type=F32)


def tn(a, b):
    return lax.dot_general(a, b, (((0,), (0,)), ((), ())), preferred_element_type=F32)


def copy_kernel(name, body, outs, at, arrays, scratch):
    return pl.pallas_call(
        body,
        name=name,
        out_shape=[jax.ShapeDtypeStruct(s, B16) for s in outs],
        in_specs=[pl.BlockSpec(memory_space=pltpu.SMEM)]
        + [pl.BlockSpec(memory_space=pltpu.HBM)] * len(arrays),
        out_specs=[pl.BlockSpec(memory_space=pltpu.HBM)] * len(outs),
        scratch_shapes=list(scratch),
        compiler_params=pltpu.CompilerParams(vmem_limit_bytes=VMEM_BYTES),
        cost_estimate=pl.CostEstimate(flops=0, bytes_accessed=0, transcendentals=0),
    )(at, *in_hbm(arrays))


def token_copies(at, array, mine, strip, sems):
    width = strip.shape[1]
    lanes = pl.ds(pl.multiple_of(at[S_SIDE] * width, width), width)
    return [
        pltpu.make_async_copy(array.at[at[S_HALF]], mine, sems.at[0]),
        pltpu.make_async_copy(array.at[1 - at[S_HALF], :, lanes], strip, sems.at[1]),
    ]


def token_shapes(array):
    _, rows, dim = array.shape
    return [(rows, dim), (rows, dim // 2)]


def send_strips(strip):
    return swapped(strip, HALF), swapped(strip, HALF | NEAR)


def start_loader(at, refs):
    mine, near, far, far_near, far_rest, far_near_rest = refs
    first = at[S_SIDE] == 0
    index = 2 * at[S_HALF] + at[S_NEAR]

    def whole(strip, rest):
        a, b = strip[...], rest[...]
        return jnp.concatenate([jnp.where(first, a, b), jnp.where(first, b, a)], axis=1)

    yield index, mine[...]
    yield index ^ 1, near[...]
    yield index ^ 2, whole(far, far_rest)
    yield index ^ 3, whole(far_near, far_near_rest)


def piece_loader(at, refs):
    for step, ref in zip(STEPS, refs):
        for i in range(2):
            yield at[S_CHIP] ^ (step | 2 * i), ref[i]


def run_copies(copies):
    for copy in copies:
        copy.start()
    for copy in copies:
        copy.wait()


def pack_first(at, tokens, vectors, w_qkv):
    _, three, dim, wide = w_qkv.shape
    heads, side = wide // 4, dim // 2
    count = len(vectors)

    def body(at, tokens, w_qkv, *refs):
        lines = refs[:count]
        mine, strip, packed, table, rounded, sems = refs[count : count + 6]
        held = refs[count + 6 :]
        rows = pl.ds(pl.multiple_of(at[S_CORE] * side, side), side)
        lanes = pl.ds(pl.multiple_of(at[S_GIVE] * heads, heads), heads)
        copies = token_copies(at, tokens, mine, strip, sems)
        for i in range(three):
            copies.append(
                pltpu.make_async_copy(
                    w_qkv.at[0, i, rows, lanes], packed.at[i * side : (i + 1) * side], sems.at[2 + i]
                )
            )
        loads = [
            pltpu.make_async_copy(line, hold, sems.at[6 + i])
            for i, (line, hold) in enumerate(zip(lines, held))
        ]
        for copy in copies:
            copy.start()
        run_copies(loads)
        fill_table(table, at[S_GIVE], held)
        rounded[...] = table[...].astype(B16)
        run_copies([pltpu.make_async_copy(rounded, packed.at[three * side :], sems.at[5])])
        for copy in copies:
            copy.wait()

    return copy_kernel(
        "pack_first", body, token_shapes(tokens) + [(three * side + TABLE, ONE)], at,
        [tokens, w_qkv, *vectors],
        [pltpu.VMEM((TABLE, ONE), F32), pltpu.VMEM((TABLE, ONE), B16), pltpu.SemaphoreType.DMA((6 + count,))]
        + [pltpu.VMEM(v.shape, B16) for v in vectors],
    )


def pack_second(at, tokens, w_up, w_out, w_down):
    dim, units, heads = w_up.shape[1], w_up.shape[2] // 4, w_out.shape[1] // 4
    side = dim // 2

    def body(at, tokens, w_up, w_out, w_down, mine, strip, up, down, sems):
        copies = token_copies(at, tokens, mine, strip, sems)
        rows = pl.ds(pl.multiple_of(at[S_CORE] * side, side), side)
        lanes = pl.ds(pl.multiple_of(at[S_GIVE] * units, units), units)
        copies.append(pltpu.make_async_copy(w_up.at[0, rows, lanes], up, sems.at[2]))
        part = 2 * at[S_GIVE] + at[S_CORE]
        for i, (source, size, start) in enumerate(
            ((w_down, units // 2, 0), (w_out, heads // 2, units // 2))
        ):
            rows = pl.ds(pl.multiple_of(part * size, size), size)
            copies.append(
                pltpu.make_async_copy(
                    source.at[0, rows], down.at[start : start + size], sems.at[3 + i]
                )
            )
        run_copies(copies)

    return copy_kernel(
        "pack_second", body, token_shapes(tokens) + [(side, units), ((units + heads) // 2, dim)], at,
        [tokens, w_up, w_out, w_down], [pltpu.SemaphoreType.DMA((5,))],
    )


def fill_table(table, index, vectors):
    *lines, b_up, b_qkv = vectors
    units, heads = b_up.shape[1] // 4, b_qkv.shape[2] // 4
    table[...] = jnp.zeros_like(table)
    row = 0
    for line in lines:
        for i in range(line.shape[1] // ONE):
            table[row : row + 1] = line[:, i * ONE : (i + 1) * ONE].astype(F32)
            row += 1
    for i in range(units // ONE):
        lanes = pl.ds(pl.multiple_of(index * units + i * ONE, ONE), ONE)
        table[row : row + 1] = b_up[:, lanes].astype(F32)
        row += 1
    few = b_qkv[0, :, pl.ds(pl.multiple_of(index * heads, ONE), heads)].astype(F32)
    table[row : row + few.shape[0]] = few


TABLE = 48


def vector_rows(at, vectors, got):
    dim = vectors[0].shape[1]
    units, few = vectors[5].shape[1] // 4, vectors[6].shape[1]

    def body(at, *refs):
        *lines, got, rows0, rows1, table = refs
        fill_table(table, at[S_OWN], lines)
        taken = got[got.shape[0] - TABLE :].astype(F32)
        is_first = at[S_SECTION] == 0
        for rows, lines in (
            (rows0, jnp.where(is_first, table[...], taken)),
            (rows1, jnp.where(is_first, taken, table[...])),
        ):
            rows[...] = jnp.zeros_like(rows)
            line = 0
            for r, tiles in enumerate([dim // ONE] * 5 + [units // ONE, few]):
                for i in range(tiles):
                    rows[r : r + 1, i * ONE : (i + 1) * ONE] = lines[line : line + 1]
                    line += 1

    return kernel_call_named(
        "vector_rows", body, [((8, dim), F32)] * 2, at, *vectors, got,
        scratch=[pltpu.VMEM((TABLE, ONE), F32)],
    )


def half_rows(at, which, size):
    return pl.ds(pl.multiple_of((at[S_CORE] ^ which) * size, size), size)


def qkv_copies(at, own, got, rest, target):
    three, heads = own.shape[1], own.shape[3] // 4
    side = own.shape[2] // 2
    lanes = pl.ds(pl.multiple_of(at[S_OWN] * heads, heads), heads)
    mine, halves = [], []
    for i in range(three):
        tile = slice(i * heads, (i + 1) * heads)
        mine.append((own.at[0, i, :, lanes], target[0].at[:, tile]))
        for which, source in ((0, got), (1, rest)):
            halves.append(
                (
                    source.at[i * side : (i + 1) * side],
                    target[1].at[half_rows(at, which, side), tile],
                )
            )
    return mine + halves


def up_copies(at, own, got, rest, target):
    side, units = got.shape
    lanes = pl.ds(pl.multiple_of(at[S_OWN] * units, units), units)
    return [(own.at[0, :, lanes], target[0])] + [
        (source, target[1].at[half_rows(at, which, side)])
        for which, source in ((0, got), (1, rest))
    ]


def row_copies(at, own, got, rest, target, start):
    size = target[0].shape[0]
    side = size // 2
    rows = pl.ds(pl.multiple_of(at[S_OWN] * size, size), size)
    return [(own.at[0, rows], target[0])] + [
        (source.at[start : start + side], target[1].at[half_rows(at, which, side)])
        for which, source in ((0, got), (1, rest))
    ]


def choose_weights(name, at, owns, got, rest, shapes, make):
    count = len(owns)

    def body(at, *refs):
        own, (got, rest), targets, sems = refs[:count], refs[count : count + 2], refs[count + 2 : -1], refs[-1]
        for section in range(2):

            @pl.when(at[S_SECTION] == section)
            def _():
                pairs = make(
                    at, own, got, rest,
                    [(targets[2 * i + section], targets[2 * i + 1 - section]) for i in range(count)],
                )
                run_copies(
                    [
                        pltpu.make_async_copy(source, target, sems.at[i])
                        for i, (source, target) in enumerate(pairs)
                    ]
                )

    outs = [(shape, B16) for shape in shapes for _ in range(2)]
    return kernel_call(
        body, outs, at, hbm=owns, free=[got, rest],
        scratch=[pltpu.SemaphoreType.DMA((9,))], name=name,
    )


def weights_call(name, body, outs, at, arrays, weights, scratch=(), flops=0, exps=0):
    first, count = len(arrays), len(weights)

    def wrapped(at, *refs):
        given, chosen, rest = refs[:first], refs[first : first + count], refs[first + count :]
        made, own = rest[: len(outs)], rest[len(outs) :]
        body(at, *given, *made, *chosen, *own)

    return kernel_call(
        wrapped, outs, at, *arrays, *weights, scratch=scratch, flops=flops, exps=exps, name=name
    )


def first_weights(at, vectors, w_qkv, sent):
    _, three, dim, wide = w_qkv.shape
    got = swapped(sent, SECTION)
    qkv = choose_weights(
        "choose_qkv", at, [w_qkv], got, swapped(got, CORE), [(dim, three * (wide // 4))],
        lambda at, own, got, rest, to: qkv_copies(at, own[0], got, rest, to[0]),
    )
    return got, [dict(qkv=q, rows=r) for q, r in zip(qkv, vector_rows(at, vectors, got))]


def up_weights(at, w_up, got, rest):
    return choose_weights(
        "choose_up", at, [w_up], got, rest, [(w_up.shape[1], w_up.shape[2] // 4)],
        lambda at, own, got, rest, to: up_copies(at, own[0], got, rest, to[0]),
    )


def row_weights(at, w_down, w_out, got, rest):
    _, tall, dim = w_down.shape
    units, heads = tall // 4, w_out.shape[1] // 4
    return choose_weights(
        "choose_rows", at, [w_down, w_out], got, rest, [(units, dim), (heads, dim)],
        lambda at, own, got, rest, to: row_copies(at, own[0], got, rest, to[0], 0)
        + row_copies(at, own[1], got, rest, to[1], units // 2),
    )


def turn_tables(at, rows):
    half_rot = ROT // 2
    place = lax.broadcasted_iota(jnp.int32, (rows, ONE), 0)
    lane = lax.broadcasted_iota(jnp.int32, (rows, ONE), 1) % HD
    positions = (2 * (place // ONE) + at[S_CORE]) * ONE + place % ONE
    freqs = 1.0 / 10000.0 ** ((2 * (lane % half_rot)).astype(F32) / ROT)
    angles = positions.astype(F32) * freqs
    sine = jnp.sin(angles)
    return (
        jnp.where(lane < ROT, jnp.cos(angles), 1.0),
        jnp.where((lane >= half_rot) & (lane < ROT), sine, 0.0),
        jnp.where(lane < half_rot, -sine, 0.0),
    )


def keep_blocks(at, source, blocks):
    mine, give = blocks
    place = (2 * at[S_HALF] + at[S_NEAR]) * ONE
    mine[...] = source[pl.ds(pl.multiple_of(place, ONE), ONE)]
    size = give.shape[0]
    place = (2 * (1 - at[S_HALF]) + at[S_NEAR]) * ONE + at[S_SIDE] * size
    give[...] = source[pl.ds(pl.multiple_of(place, size), size)]


def keep_piece(at, source, piece):
    size = piece.shape[0]
    piece[...] = source[pl.ds(pl.multiple_of(at[S_CHIP] * size, size), size)]


def front(at, loader, sources, w, turns, with_piece):
    dim = w["qkv"].shape[0]
    rows = turns[0].shape[0]
    count = len(sources)

    def body(at, *refs):
        given = refs[:count]
        vectors, *turns = refs[count : count + 4]
        attn_in, mlp_in, normed_out, q, kv = refs[count + 4 : count + 9]
        *kept, qkv, ordered = refs[count + 9 :]
        gains = [vectors[i : i + 1] for i in range(4)]
        for place, block in loader(at, given):
            size = block.shape[0]
            ordered[pl.ds(pl.multiple_of(place * size, size), size)] = block
        if with_piece:
            keep_piece(at, ordered, kept[0])
        else:
            keep_blocks(at, ordered, kept)
        bias = vectors[6:7, : 3 * ONE]

        def norm(span):
            hidden = ordered[span].astype(F32)
            mean = jnp.sum(hidden, axis=1, keepdims=True) * (1.0 / dim)
            centre = hidden - mean
            var = jnp.sum(centre * centre, axis=1, keepdims=True) * (1.0 / dim)
            normed = centre * lax.rsqrt(var + 1e-05)
            attn_in[span] = (normed * gains[0] + gains[1]).astype(B16)
            mlp_in[span] = (normed * gains[2] + gains[3]).astype(B16)
            normed_out[span] = normed.astype(B16)

        def project(span):
            projected = nn(attn_in[span], qkv[...]) + bias
            cosine, second, first_half = [table[span] for table in turns]
            for i, target in ((0, q), (1, kv.at[0])):
                flat = projected[:, i * ONE : (i + 1) * ONE]
                flat = (
                    flat * cosine
                    + pltpu.roll(flat, ROT // 2, 1) * second
                    + pltpu.roll(flat, ONE - ROT // 2, 1) * first_half
                )
                target[span] = flat.astype(B16)
            kv[1, span] = projected[:, 2 * ONE :].astype(B16)

        by_rows(rows, rows, norm)
        by_rows(rows, rows, project)

    outs = [((rows, dim), B16)] * 3 + [((rows, ONE), B16), ((2, rows, ONE), B16)]
    outs += [((rows // 8, dim), B16)] if with_piece else [((n, dim), B16) for n in (ONE, ONE // 2)]
    return weights_call(
        "front", body, outs, at, [*sources, w["rows"], *turns], [w["qkv"]],
        scratch=[pltpu.VMEM((rows, dim), B16)],
        flops=2 * rows * dim * 3 * ONE + 20 * rows * dim,
    )


def units_forward(at, mlp_in, w):
    rows, dim = mlp_in.shape
    units = w["units"]

    def body(at, mlp_in, vectors, active, slope, up):
        bias = vectors[5:6, :units]

        def gelu(span):
            value = nn(mlp_in[span], up[...]) + bias
            cdf = 0.5 + 0.5 * lax.erf(value * (1.0 / math.sqrt(2.0)))
            pdf = jnp.exp(value * value * -0.5) * (1.0 / math.sqrt(2.0 * math.pi))
            active[span] = (value * cdf).astype(B16)
            slope[span] = (cdf + value * pdf).astype(B16)

        by_rows(rows, rows, gelu)

    return weights_call(
        "units_forward", body, [((rows, units), B16)] * 2, at, [mlp_in, w["rows"]], [w["up"]],
        flops=2 * rows * dim * units + 40 * rows * units, exps=rows * units,
    )


def head_lanes():
    return lax.broadcasted_iota(jnp.int32, (1, ONE), 1) < HD


def by_head(array):
    first_head = head_lanes()
    zero = jnp.zeros_like(array)
    return jnp.concatenate(
        [jnp.where(first_head, array, zero), jnp.where(first_head, zero, array)], axis=0
    )


def joined_heads(array):
    half = array.shape[0] // 2
    return jnp.where(head_lanes(), array[:half], array[half:])


def allowed_keys(at, first, step, count):
    row = lax.broadcasted_iota(jnp.int32, (2 * step, count), 0) % step + first
    column = lax.broadcasted_iota(jnp.int32, (2 * step, count), 1)
    return column <= row, column < (row // ONE + at[S_CORE]) * ONE


STEPS = (0, 1, 4, 5)
STEP_CHIPS = (0, SIDE, SECTION, SECTION | SIDE)


def pieces_out(at, total, pieces):
    size = total.shape[0] // 8
    for step, piece in zip(STEPS, pieces):
        for i in range(2):
            place = (at[S_CHIP] ^ (step | 2 * i)) * size
            piece[i] = total[pl.ds(pl.multiple_of(place, size), size)].astype(piece.dtype)


def piece_shapes(rows, dim):
    return [((2, rows // 8, dim), F32)] + [((2, rows // 8, dim), B16)] * 3


def fold(at, pieces):
    _, rows, dim = pieces[0].shape

    def body(at, *refs):
        *given, keep, give = refs
        for i, target in ((0, keep), (1, give)):
            total = given[0][i]
            for piece in given[1:]:
                total = total + piece[i].astype(F32)
            target[...] = total.astype(target.dtype)

    return kernel_call_named("fold", body, [((rows, dim), F32), ((rows, dim), B16)], at, *pieces)


def exchanged(pieces):
    return [pieces[0]] + [swapped(p, m) for p, m in zip(pieces[1:], STEP_CHIPS[1:])]


def gathered(piece, near):
    pair = jnp.stack([piece, near])
    return [pair] + [swapped(pair, mask) for mask in STEP_CHIPS[1:]]


def attention_forward(at, q, kv, kv_other):
    rows = q.shape[0]
    scale = 1.0 / math.sqrt(HD)

    def body(at, q, kv, kv_other, mixed, lse):
        step = 128
        for first in range(0, rows, step):
            span = slice(first, first + step)
            count = first + step
            one = by_head(q[span] * scale)
            scores = [
                jnp.where(mask, nt(one, keys[0, :count]), -1e9)
                for mask, keys in zip(allowed_keys(at, first, step, count), (kv, kv_other))
            ]
            most = jnp.maximum(
                jnp.max(scores[0], axis=1, keepdims=True),
                jnp.max(scores[1], axis=1, keepdims=True),
            )
            exponents = [jnp.exp(s - most) for s in scores]
            summed = jnp.sum(exponents[0], axis=1, keepdims=True) + jnp.sum(
                exponents[1], axis=1, keepdims=True
            )
            inverse = 1.0 / summed
            result = nn(exponents[0].astype(B16), kv[1, :count]) + nn(
                exponents[1].astype(B16), kv_other[1, :count]
            )
            mixed[span] = joined_heads(result * inverse).astype(B16)
            lse[span] = joined_heads(
                jnp.broadcast_to(most + jnp.log(summed), (2 * step, ONE))
            )

    return kernel_call_named(
        "attention_forward", body, [((rows, ONE), B16), ((rows, ONE), F32)], at, q, kv, kv_other,
        flops=8 * rows * rows * ONE * 2, exps=2 * rows * rows * 2,
    )


def outputs_forward(at, mixed, active, w):
    rows = mixed.shape[0]
    units, dim = w["down"].shape

    def body(at, mixed, active, *rest):
        pieces, (out, down, total) = rest[:4], rest[4:]

        def one(span):
            total[span] = nn(mixed[span], out[...]) + nn(active[span], down[...])

        by_rows(rows, rows, one)
        pieces_out(at, total, pieces)

    return weights_call(
        "outputs_forward", body, piece_shapes(rows, dim), at, [mixed, active],
        [w["out"], w["down"]], scratch=[pltpu.VMEM((rows, dim), F32)],
        flops=2 * rows * dim * (units + ONE),
    )


def units_backward(at, loader, sources, slope, w, with_piece):
    rows, units = slope.shape
    dim = w["up"].shape[0]
    count = len(sources)

    def body(at, *refs):
        given = refs[:count]
        slope, g, up_grad, mixed_grad = refs[count : count + 4]
        *kept, down, out = refs[count + 4 :]
        for place, block in loader(at, given):
            size = block.shape[0]
            g[pl.ds(pl.multiple_of(place * size, size), size)] = block
        if with_piece:
            keep_piece(at, g, kept[0])
        else:
            keep_blocks(at, g, kept)

        def back(span):
            up_grad[span] = (nt(g[span], down[...]) * slope[span].astype(F32)).astype(B16)
            mixed_grad[span] = nt(g[span], out[...]).astype(B16)

        by_rows(rows, rows, back)

    outs = [((rows, dim), B16), ((rows, units), B16), ((rows, ONE), B16)]
    outs += [((rows // 8, dim), B16)] if with_piece else [((n, dim), B16) for n in (ONE, ONE // 2)]
    return weights_call(
        "units_backward", body, outs, at, [*sources, slope], [w["down"], w["out"]],
        flops=2 * rows * dim * (units + ONE),
    )


def attention_backward(at, q, kv, kv_other, lse, mixed_grad):
    rows = q.shape[0]
    scale = 1.0 / math.sqrt(HD)

    def body(at, q, kv, kv_other, lse, mixed_grad, dq, dkv, dkv_other):
        step = 256
        dkv[...] = jnp.zeros_like(dkv)
        dkv_other[...] = jnp.zeros_like(dkv_other)
        for first in range(0, rows, step):
            span = slice(first, first + step)
            count = first + step
            one, one_back = by_head(q[span] * scale), by_head(mixed_grad[span])
            masks = allowed_keys(at, first, step, count)
            sides = ((masks[0], kv, dkv), (masks[1], kv_other, dkv_other))
            level = jnp.concatenate([lse[span, :1], lse[span, HD : HD + 1]], axis=0)
            probs, grads = [], []
            for mask, keys, _ in sides:
                scores = nt(one, keys[0, :count])
                probs.append(jnp.exp(jnp.where(mask, scores, -1e9) - level))
                grads.append(nt(one_back, keys[1, :count]))
            delta = jnp.sum(probs[0] * grads[0], axis=1, keepdims=True) + jnp.sum(
                probs[1] * grads[1], axis=1, keepdims=True
            )
            result = 0.0
            for (_, keys, target), prob, grad in zip(sides, probs, grads):
                score_grad = (prob * (grad - delta)).astype(B16)
                result = result + nn(score_grad, keys[0, :count])
                target[0, :count] += tn(score_grad, one)
                target[1, :count] += tn(prob.astype(B16), one_back)
            dq[span] = joined_heads(result) * scale

    return kernel_call_named(
        "attention_backward",
        body, [((rows, ONE), F32), ((2, rows, ONE), F32), ((2, rows, ONE), F32)],
        at, q, kv, kv_other, lse, mixed_grad,
        flops=20 * rows * rows * ONE * 2, exps=2 * rows * rows * 2,
    )


def inputs_backward(at, dq, dkv, dkv_got, up_grad, normed, g, turns, w):
    rows, dim = normed.shape
    units = up_grad.shape[1]

    def body(at, dq, dkv, dkv_got, up_grad, normed, g, *rest):
        turns, vectors, rest = rest[:3], rest[3], rest[4:]
        qkv_grad, table = rest[:2]
        pieces, (qkv, up, total, lines) = rest[2:6], rest[6:]
        gain_one, gain_two = vectors[0:1], vectors[2:3]
        step = rows

        def one(i, sums):
            span = pl.ds(pl.multiple_of(i * step, step), step)
            cosine, second, first_half = [table[span] for table in turns]
            parts = []
            for flat in (dq[span], dkv[0, span] + dkv_got[0, span]):
                parts.append(
                    flat * cosine
                    - pltpu.roll(flat, ROT // 2, 1) * second
                    - pltpu.roll(flat, ONE - ROT // 2, 1) * first_half
                )
            parts.append(dkv[1, span] + dkv_got[1, span])
            both = jnp.concatenate([p.astype(B16) for p in parts], axis=1)
            qkv_grad[span] = both
            attn = nt(both, qkv[...])
            mlp = nt(up_grad[span], up[...])
            total[span] = attn * gain_one + mlp * gain_two
            unit = normed[span].astype(F32)
            new = [
                jnp.sum(v, axis=0, keepdims=True)
                for v in (
                    attn * unit, attn, mlp * unit, mlp, g[span].astype(F32),
                    up_grad[span].astype(F32), both.astype(F32),
                )
            ]
            return tuple(a + b for a, b in zip(sums, new))

        widths = (dim,) * 5 + (units, 3 * ONE)
        sums = lax.fori_loop(
            0, rows // step, one, tuple(jnp.zeros((1, width), F32) for width in widths)
        )
        pieces_out(at, total, pieces)
        lines[...] = jnp.zeros_like(lines)
        line = 0
        for value in sums:
            for i in range(value.shape[1] // ONE):
                lines[line : line + 1] = value[:, i * ONE : (i + 1) * ONE]
                line += 1
        table[...] = lines[...].astype(B16)

    outs = [((rows, 3 * ONE), B16), ((LINES, ONE), B16)] + piece_shapes(rows, dim)
    return weights_call(
        "inputs_backward", body, outs, at,
        [dq, dkv, dkv_got, up_grad, normed, g, *turns, w["rows"]], [w["qkv"], w["up"]],
        scratch=[pltpu.VMEM((rows, dim), F32), pltpu.VMEM((LINES, ONE), F32)],
        flops=2 * rows * dim * (units + 3 * ONE) + 12 * rows * dim,
    )


LINES = 64


def join_forward(at, x_piece, parts, w):
    def body(at, x, vectors, own, *rest):
        total = x[...].astype(F32) + own[...].astype(F32) + vectors[4:5]
        for piece in rest[:-1]:
            total = total + piece[...].astype(F32)
        rest[-1][...] = total.astype(B16)

    return kernel_call_named("join_forward", body, [(x_piece.shape, B16)], at, x_piece, w["rows"], *parts)[0]


def join_backward(at, g_piece, x_piece, parts):
    dim = x_piece.shape[1]

    def body(at, g, x, own, *rest):
        total = own[...]
        for piece in rest[:-1]:
            total = total + piece[...].astype(F32)
        hidden = x[...].astype(F32)
        centre = hidden - jnp.sum(hidden, axis=1, keepdims=True) * (1.0 / dim)
        var = jnp.sum(centre * centre, axis=1, keepdims=True) * (1.0 / dim)
        scale = lax.rsqrt(var + 1e-05)
        normed = centre * scale
        inner = (
            total
            - jnp.sum(total, axis=1, keepdims=True) * (1.0 / dim)
            - normed * (jnp.sum(total * normed, axis=1, keepdims=True) * (1.0 / dim))
        )
        rest[-1][...] = (g[...].astype(F32) + scale * inner).astype(B16)

    return kernel_call_named("join_backward", body, [(x_piece.shape, B16)], at, g_piece, x_piece, *parts)[0]


def columns(at, ref, core, high):
    which = at[S_CORE] ^ core
    return jnp.concatenate(
        [
            ref[:, pl.ds(pl.multiple_of((4 * high + 2 * low + which) * ONE, ONE), ONE)]
            for low in range(2)
        ],
        axis=1,
    )


def early_grads(at, active, mixed, mlp_in, up_grad, g):
    rows, dim = g.shape
    units = active.shape[1]
    tiles = units // ONE

    def body(at, active, mixed, mlp_in, up_grad, g, keep, give):
        for core, target in ((0, keep), (1, give)):
            strip = jnp.concatenate([columns(at, g, core, high) for high in range(2)], axis=1)
            down = tn(active[...], strip).astype(B16)
            out = tn(mixed[...], strip).astype(B16)
            for high in range(2):
                up = tn(columns(at, mlp_in, core, high), up_grad[...]).astype(B16)
                for low in range(2):
                    lanes = slice((2 * high + low) * ONE, (2 * high + low + 1) * ONE)
                    where = (at[S_HALF] ^ high, at[S_NEAR] ^ low)
                    target[where[0], where[1], :units] = down[:, lanes]
                    target[where[0], where[1], units : units + ONE] = out[:, lanes]
                    for i in range(tiles):
                        base = units + (1 + i) * ONE
                        target[where[0], where[1], base : base + ONE] = up[
                            low * ONE : (low + 1) * ONE, i * ONE : (i + 1) * ONE
                        ]

    shape = (2, 2, 2 * units + ONE, ONE)
    return kernel_call_named(
        "early_grads",
        body, [(shape, B16)] * 2, at, active, mixed, mlp_in, up_grad, g,
        flops=2 * rows * dim * (2 * units + ONE),
    )


def late_grads(at, attn_in, qkv_grad, tables):
    rows, dim = attn_in.shape
    count = len(tables)

    def body(at, attn_in, qkv_grad, *refs):
        tables, (keep, give) = refs[:count], refs[count:]
        for core, target in ((0, keep), (1, give)):
            for high in range(2):
                qkv = tn(columns(at, attn_in, core, high), qkv_grad[...]).astype(B16)
                for low in range(2):
                    where = (at[S_HALF] ^ high, at[S_NEAR] ^ low)
                    for i in range(3):
                        target[where[0], where[1], i * ONE : (i + 1) * ONE] = qkv[
                            low * ONE : (low + 1) * ONE, i * ONE : (i + 1) * ONE
                        ]
                    for i, table in enumerate(tables):
                        base = 3 * ONE + i * LINES
                        target[where[0], where[1], base : base + LINES] = table[...]

    shape = (2, 2, 3 * ONE + count * LINES, ONE)
    return kernel_call_named(
        "late_grads", body, [(shape, B16)] * 2, at, attn_in, qkv_grad, *tables,
        flops=2 * rows * dim * 3 * ONE,
    )


def plus(a, b):
    return (a.astype(F32) + b.astype(F32)).astype(B16)


def summed_cores(keep, give, *earlier):
    got = swapped(after(give, *earlier), CORE)
    return (
        [plus(keep[0, i], got[0, i]) for i in range(2)],
        [plus(keep[1, i], got[1, i]) for i in range(2)],
    )


def sum_lines(at, late):
    def body(at, *refs):
        *late, lines = refs
        total = 0.0
        for part in late:
            total = total + part[3 * ONE : 3 * ONE + lines.shape[0]].astype(F32)
        lines[...] = total

    return kernel_call_named("sum_lines", body, [((32, ONE), F32)], at, *late)[0]


def unpack_grads(at, early, late, sizes):
    dim_part, units, heads = ONE, sizes["units"], ONE

    def body(at, *refs):
        early, late = refs[:4], refs[4:8]
        qkv, out, up, down, b_qkv, b_up, branch = refs[8:]
        index = at[S_OWN]
        for j, (wide, narrow) in enumerate(zip(early, late)):
            source = index ^ (2 * (j % 2) + j // 2)
            place = pl.multiple_of(source * units, units)
            small = pl.multiple_of(source * ONE, ONE)
            down[pl.ds(place, units)] = wide[:units].astype(F32)
            out[pl.ds(small, ONE)] = wide[units : units + ONE].astype(F32)
            for i in range(units // ONE):
                base = units + (1 + i) * ONE
                up[:, pl.ds(place + i * ONE, ONE)] = wide[base : base + ONE].astype(F32)
            for i in range(3):
                qkv[i, :, pl.ds(small, ONE)] = narrow[i * ONE : (i + 1) * ONE].astype(F32)
            table = narrow[3 * ONE :].astype(F32)
            for i in range(units // ONE):
                b_up[:, pl.ds(place + i * ONE, ONE)] = table[40 + i : 41 + i]
            for i in range(3):
                b_qkv[i : i + 1, pl.ds(small, ONE)] = table[40 + units // ONE + i :][:1]
            if j == 0:
                branch[...] = table[32:40]

    outs = [
        ((3, dim_part, 4 * heads), F32),
        ((4 * heads, dim_part), F32),
        ((dim_part, 4 * units), F32),
        ((4 * units, dim_part), F32),
        ((3, 4 * heads), F32),
        ((1, 4 * units), F32),
        ((8, ONE), F32),
    ]
    return kernel_call_named("unpack_grads", body, outs, at, *early, *late, keep=False)


def cube_device(
    inputs, cotangent, ln1_gain, ln1_bias, ln2_gain, ln2_bias, qkv_weight, qkv_bias,
    out_weight, up_weight, up_bias, down_weight, branch_bias,
):
    at = where_am_i()
    section, half, side = [lax.axis_index("section"), lax.axis_index("ctx") // 4, lax.axis_index("tp")]
    at, is_first, is_low, is_left, is_near = lax.optimization_barrier(
        (at, section == 0, half == 0, side == 0, section == half)
    )
    dim = inputs.shape[2]
    rows = 4 * inputs.shape[1]
    vectors = (ln1_gain, ln1_bias, ln2_gain, ln2_bias, branch_bias, up_bias, qkv_bias)

    mine, strip, sent_qkv = pack_first(at, inputs, vectors, qkv_weight)
    g_mine, g_strip, sent_up, sent_down = pack_second(
        at, cotangent, up_weight, out_weight, down_weight
    )
    strips = send_strips(strip)
    turns = turn_tables(at, rows)
    sides = [swapped(after(part, turns[0]), SIDE) for part in strips]
    x_parts = (mine, swapped(mine, NEAR), *strips, *sides)
    got_qkv, layers = first_weights(at, vectors, qkv_weight, sent_qkv)
    got_up = swapped(after(sent_up, got_qkv), SECTION)
    first, second = layers
    got_down = swapped(
        after(sent_down, got_up, *x_parts[4:], first["qkv"], first["rows"]), SECTION
    )

    g_near = swapped(after(g_mine, *x_parts[4:]), NEAR)

    def bring_up(*earlier):
        up = up_weights(at, up_weight, got_up, swapped(after(got_up, *earlier), CORE))
        for i, layer in enumerate(layers):
            layer.update(up=up[i], units=up[i].shape[1])

    def bring_rows(*earlier):
        tall = row_weights(
            at, down_weight, out_weight, got_down, swapped(after(got_down, *earlier), CORE)
        )
        for i, layer in enumerate(layers):
            layer.update(down=tall[i], out=tall[2 + i])

    def forward(loader, sources, w, with_piece):
        got = front(at, loader, sources, w, turns, with_piece)
        attn_in, mlp_in, normed, q, kv = got[:5]
        kv_other = swapped(kv, CORE)
        is_start = "up" not in w
        if is_start:
            bring_up(q)
        active, slope = units_forward(at, mlp_in, w)
        mixed, lse = attention_forward(at, q, kv, kv_other)
        if is_start:
            bring_rows(active, mixed, g_near)
        pieces = outputs_forward(at, mixed, active, w)
        saved = dict(
            attn_in=attn_in, mlp_in=mlp_in, normed=normed, q=q, kv=kv, kv_other=kv_other,
            active=active, slope=slope, mixed=mixed, lse=lse,
        )
        return pieces, saved, got[5:]

    def backward(loader, sources, saved, w, with_piece, grads_first):
        made = units_backward(at, loader, sources, saved["slope"], w, with_piece)
        g, up_grad, mixed_grad = made[:3]
        if grads_first:
            early = early_grads(
                at, saved["active"], saved["mixed"], saved["mlp_in"], up_grad, g
            )
            mixed_grad = after(mixed_grad, early[0])
        dq, dkv, dkv_other = attention_backward(
            at, saved["q"], saved["kv"], saved["kv_other"], saved["lse"], mixed_grad
        )
        dkv_got = swapped(dkv_other, CORE)
        if not grads_first:
            early = early_grads(
                at, saved["active"], saved["mixed"], saved["mlp_in"], up_grad, after(g, dkv_other)
            )
            dq = after(dq, early[0])
        given = (dq, dkv, dkv_got, up_grad, saved["normed"], g)
        return early, given, made[3:]

    def backward_end(given, saved, w):
        out = inputs_backward(at, *given, turns, w)
        return out[0], out[1], out[2:]

    parts, saved_first, (x_piece,) = forward(start_loader, x_parts, first, True)
    strips = send_strips(after(g_strip, parts[0]))
    parts = exchanged(parts)
    parts[0] = after(parts[0], *strips)
    keep, give = fold(at, parts)
    sides = [swapped(part, SIDE) for part in strips]
    piece = join_forward(at, x_piece, [keep, swapped(give, NEAR)], first)
    near = after(swapped(piece, NEAR), *sides)
    middle = gathered(piece, near)
    g_parts = (g_mine, g_near, *strips, *sides)

    parts_last, saved_second, blocks = forward(piece_loader, middle, second, False)
    acts_mine, acts_give = blocks

    early, given, (g_piece,) = backward(
        start_loader, g_parts, saved_second, second, True, False
    )
    early_keep, early_give = summed_cores(*early, given[2])
    qkv_grad, table_second, pieces = backward_end(given, saved_second, second)
    late = late_grads(at, saved_second["attn_in"], qkv_grad, ())
    parts = exchanged(pieces)
    far_second = swapped(early_give[1], HALF)
    parts[0] = after(parts[0], far_second, *late)
    keep, give = fold(at, parts)
    late_keep, late_give = summed_cores(*late)
    late_got = swapped(after(jnp.stack(late_give), give), HALF)
    parts_last = exchanged([after(p, give) for p in parts_last])
    back = join_backward(at, g_piece, piece, [keep, swapped(give, NEAR)])
    near = after(swapped(back, NEAR), late_got, *parts_last)
    g_middle = gathered(back, near)
    close_second = swapped(after(early_give[0], near), HALF)
    g_middle[0] = after(g_middle[0], close_second)
    keep_last, give_last = fold(at, parts_last)

    early, given, blocks = backward(
        piece_loader, g_middle, saved_first, first, False, True
    )
    in_mine, in_give = blocks
    early_second = [plus(a, b) for a, b in zip(early_keep, (close_second, far_second))]
    late_second = [plus(a, b) for a, b in zip(late_keep, late_got)]
    early_keep, early_give = summed_cores(*early)
    given = (after(given[0], *early_give),) + given[1:]
    qkv_grad, table_first, pieces = backward_end(given, saved_first, first)
    last_near = swapped(give_last, NEAR)
    parts = exchanged([after(p, last_near) for p in pieces])
    far_first = swapped(early_give[1], HALF)
    late = late_grads(at, saved_first["attn_in"], qkv_grad, (table_first, table_second))
    parts[0] = after(parts[0], far_first)
    keep, give = fold(at, parts)
    close_first = swapped(after(early_give[0], give), HALF)
    late_keep, late_give = summed_cores(*late)
    late_got = swapped(after(jnp.stack(late_give), give), HALF)
    back_last = join_backward(
        at, back, x_piece, [keep, after(swapped(give, NEAR), close_first)]
    )
    last = join_forward(at, piece, [keep_last, last_near], second)
    early_first = [plus(a, b) for a, b in zip(early_keep, (close_first, far_first))]
    late_first = [plus(a, b) for a, b in zip(late_keep, late_got)]
    tall = 3 * ONE + LINES
    late_second = [
        jnp.concatenate([a, b[tall:]], axis=0) for a, b in zip(late_second, late_first)
    ]
    late_first = [a[:tall] for a in late_first]
    def brought(close, far):
        own = jnp.where(is_first, close[0], close[1])
        near = swapped(jnp.where(is_first, far[0], far[1]), NEAR)
        got = swapped(jnp.where(is_first, close[1], close[0]), SECTION)
        cross = swapped(jnp.where(is_first, far[1], far[0]), SECTION | NEAR)
        return own, got, near, cross

    early = brought((early_first[0], early_second[0]), (early_first[1], early_second[1]))
    late_first[1] = after(late_first[1], *early)
    late = brought((late_first[0], late_second[0]), (late_first[1], late_second[1]))
    lines = sum_lines(at, late)
    lines = lines + swapped(lines, SIDE)
    sizes = dict(units=up_weight.shape[2] // 4)
    qkv, out, up, down, b_qkv, b_up, branch = unpack_grads(at, early, late, sizes)

    mine = jnp.where(is_first, back_last, last)
    got = swapped(jnp.where(is_first, last, back_last), SECTION)
    stay = jnp.where(is_near, mine, got)
    known_give = jnp.where(is_first, acts_give, in_give)
    other = swapped(jnp.stack([jnp.where(is_near, got, mine), known_give]), HALF)
    own = jnp.stack(
        [jnp.where(is_low, stay, other[0]), jnp.where(is_low, other[0], stay), other[1]]
    )
    rest = swapped(own, SIDE)
    both = jnp.where(
        is_left, jnp.concatenate([own, rest], axis=1), jnp.concatenate([rest, own], axis=1)
    )
    new = both[:2]
    known_mine = jnp.where(is_first, acts_mine, in_mine)
    known = jnp.where(
        is_low, jnp.stack([known_mine, both[2]]), jnp.stack([both[2], known_mine])
    )
    acts = jnp.where(is_first, known, new)
    in_grads = jnp.where(is_first, new, known)

    lines = lines.reshape(4, dim)
    return (
        acts[None],
        in_grads[None],
        lines[0:1],
        lines[1:2],
        lines[2:3],
        lines[3:4],
        qkv[None],
        b_qkv[None],
        out[None],
        up[None],
        b_up,
        down[None],
        branch.reshape(1, dim),
    )


def placed_program(mesh, device_program):
    placed = (
        P(None, "ctx", None),
        P(None, "ctx", None),
        P("section", None),
        P("section", None),
        P("section", None),
        P("section", None),
        P("section", None, None, "tp"),
        P("section", None, "tp"),
        P("section", "tp", None),
        P("section", None, "tp"),
        P("section", "tp"),
        P("section", "tp", None),
        P("section", None),
    )
    return jax.shard_map(
        device_program,
        mesh=mesh,
        in_specs=placed,
        out_specs=(
            P("section", None, "ctx", None),
            P("section", None, "ctx", None),
            P("section", None),
            P("section", None),
            P("section", None),
            P("section", None),
            P("section", None, "ctx", "tp"),
            P("section", None, "tp"),
            P("section", "tp", "ctx"),
            P("section", "ctx", "tp"),
            P("section", "tp"),
            P("section", "tp", "ctx"),
            P("section", None),
        ),
        check_vma=False,
    )


def solution(mesh):
    sizes = dict(mesh.shape)
    if sizes["section"] == 2 and sizes["tp"] == 2 and sizes["ctx"] == 8:
        return placed_program(mesh, cube_device)
    return placed_program(mesh, per_device)
```

```python
import math

import jax
import jax.numpy as jnp
from jax import lax
from jax.experimental import pallas as pl
from jax.experimental.pallas import tpu as pltpu
from jax.sharding import PartitionSpec as P

HD = 64
ROT = 16


def shifted(shard, axis, by):
    peers = lax.axis_size(axis)
    pairs = [(i, i + by) for i in range(peers) if 0 <= i + by < peers]
    return lax.ppermute(shard, axis, pairs)


def tables(positions):
    freqs = 1.0 / 10000.0 ** (jnp.arange(0, ROT, 2).astype(jnp.float32) / ROT)
    angles = positions.astype(jnp.float32)[:, None] * freqs[None, :]
    return (jnp.cos(angles)[:, None, :], jnp.sin(angles)[:, None, :])


def rotate(field, cosine, sine):
    half_rot = ROT // 2
    front = field[..., :half_rot]
    second = field[..., half_rot:ROT]
    return jnp.concatenate(
        [front * cosine - second * sine, second * cosine + front * sine, field[..., ROT:]], axis=-1
    )


def norms(hidden, gain_one, shift_one, gain_two, shift_two):
    centre = hidden - jnp.mean(hidden, axis=-1, keepdims=True)
    normed = centre * lax.rsqrt(jnp.mean(centre * centre, axis=-1, keepdims=True) + 1e-05)
    return (normed * gain_one + shift_one, normed * gain_two + shift_two)


def gelu_exact(value):
    return jax.nn.gelu(value, approximate=False)


def scores_of(queries, keys, query_pos, score_scale):
    raw = jnp.einsum("qhd,khd->hqk", queries, keys, preferred_element_type=jnp.float32)
    key_pos = jnp.arange(keys.shape[0], dtype=jnp.int32)
    return jnp.where(
        key_pos[None, None, :] <= query_pos[None, :, None], raw * score_scale, -1000000000.0
    )


def forward_layer(layer_in, weights, query_pos, cosine, sine):
    gains, w_qkv, b_qkv, w_out, w_up, b_up, w_down, b_branch = weights
    hidden = layer_in.astype(jnp.float32)
    attn_norm, mlp_norm = norms(hidden, gains[0], gains[1], gains[2], gains[3])
    attn_in = attn_norm.astype(jnp.bfloat16)
    mlp_in = mlp_norm.astype(jnp.bfloat16)
    projected = (
        jnp.einsum("td,cdf->tcf", attn_in, w_qkv, preferred_element_type=jnp.float32) + b_qkv
    )
    row_count = hidden.shape[0]
    feat_width = projected.shape[2]
    head_count = feat_width // HD
    queries = rotate(projected[:, 0].reshape(row_count, head_count, HD), cosine, sine).astype(
        jnp.bfloat16
    )
    key_flat = (
        rotate(projected[:, 1].reshape(row_count, head_count, HD), cosine, sine)
        .astype(jnp.bfloat16)
        .reshape(row_count, feat_width)
    )
    value_flat = projected[:, 2].astype(jnp.bfloat16)
    all_keys, all_values = (
        lax.all_gather(key_flat, "ctx", axis=0, tiled=True),
        lax.all_gather(value_flat, "ctx", axis=0, tiled=True),
    )
    key_count = all_keys.shape[0]
    score_scale = 1.0 / math.sqrt(HD)
    scores = scores_of(queries, all_keys.reshape(key_count, head_count, HD), query_pos, score_scale)
    row_max = jnp.max(scores, axis=-1, keepdims=True)
    exponent = jnp.exp(scores - row_max)
    summed = jnp.sum(exponent, axis=-1, keepdims=True)
    probability = (exponent / summed).astype(jnp.bfloat16)
    log_total = row_max + jnp.log(summed)
    mixed = jnp.einsum(
        "hqk,khd->qhd",
        probability,
        all_values.reshape(key_count, head_count, HD),
        preferred_element_type=jnp.float32,
    )
    mixed = mixed.reshape(row_count, feat_width).astype(jnp.bfloat16)
    partial_out = jnp.dot(mixed, w_out, preferred_element_type=jnp.float32)
    up_value = jnp.dot(mlp_in, w_up, preferred_element_type=jnp.float32) + b_up
    active = gelu_exact(up_value).astype(jnp.bfloat16)
    partial_out = partial_out + jnp.dot(active, w_down, preferred_element_type=jnp.float32)
    branches = lax.psum(partial_out, "tp")
    layer_out = (hidden + branches + b_branch).astype(jnp.bfloat16)
    stored = (key_flat, value_flat)
    saved = (layer_in, queries, stored, log_total, mixed, up_value, active)
    return (layer_out, saved)


def backward_layer(grad_out, saved, weights, query_pos, cosine, sine):
    gains, w_qkv, b_qkv, w_out, w_up, b_up, w_down, b_branch = weights
    layer_in, queries, stored, log_total, mixed, up_value, active = saved
    grad_full = grad_out.astype(jnp.float32)
    row_count, feat_width = mixed.shape
    head_count = feat_width // HD
    hidden = layer_in.astype(jnp.float32)
    norm_pair, norm_back = jax.vjp(norms, hidden, gains[0], gains[1], gains[2], gains[3])
    attn_in = norm_pair[0].astype(jnp.bfloat16)
    mlp_in = norm_pair[1].astype(jnp.bfloat16)
    active_grad = jnp.einsum("td,fd->tf", grad_out, w_down, preferred_element_type=jnp.float32)
    grad_down = jnp.einsum("tf,td->fd", active, grad_out, preferred_element_type=jnp.float32)
    gelu_back = jax.vjp(gelu_exact, up_value)[1]
    up_grad = gelu_back(active_grad)[0].astype(jnp.bfloat16)
    grad_up_bias = jnp.sum(up_grad.astype(jnp.float32), axis=0)
    grad_up = jnp.einsum("td,tf->df", mlp_in, up_grad, preferred_element_type=jnp.float32)
    mlp_in_grad = jnp.einsum("tf,df->td", up_grad, w_up, preferred_element_type=jnp.float32)
    mixed_grad = jnp.einsum(
        "td,fd->tf", grad_out, w_out, preferred_element_type=jnp.float32
    ).astype(jnp.bfloat16)
    grad_out_weight = jnp.einsum("tf,td->fd", mixed, grad_out, preferred_element_type=jnp.float32)
    all_keys, all_values = (
        lax.all_gather(stored[0], "ctx", axis=0, tiled=True),
        lax.all_gather(stored[1], "ctx", axis=0, tiled=True),
    )
    key_count = all_keys.shape[0]
    keys_heads = all_keys.reshape(key_count, head_count, HD)
    values_heads = all_values.reshape(key_count, head_count, HD)
    score_scale = 1.0 / math.sqrt(HD)
    scores = scores_of(queries, keys_heads, query_pos, score_scale)
    probability = jnp.exp(scores - log_total)
    heads_grad = mixed_grad.reshape(row_count, head_count, HD)
    prob_grad = jnp.einsum(
        "qhd,khd->hqk", heads_grad, values_heads, preferred_element_type=jnp.float32
    )
    centre = jnp.sum(probability * prob_grad, axis=-1, keepdims=True)
    score_grad = (score_scale * probability * (prob_grad - centre)).astype(jnp.bfloat16)
    query_grad = jnp.einsum(
        "hqk,khd->qhd", score_grad, keys_heads, preferred_element_type=jnp.float32
    )
    value_terms = jnp.einsum(
        "hqk,qhd->khd",
        probability.astype(jnp.bfloat16),
        heads_grad,
        preferred_element_type=jnp.float32,
    )
    key_terms = jnp.einsum("hqk,qhd->khd", score_grad, queries, preferred_element_type=jnp.float32)
    key_grad, value_grad = (
        lax.psum_scatter(
            key_terms.reshape(key_count, feat_width), "ctx", scatter_dimension=0, tiled=True
        ),
        lax.psum_scatter(
            value_terms.reshape(key_count, feat_width), "ctx", scatter_dimension=0, tiled=True
        ),
    )
    query_grad = rotate(query_grad, cosine, -sine).reshape(row_count, feat_width)
    key_grad = rotate(key_grad.reshape(row_count, head_count, HD), cosine, -sine).reshape(
        row_count, feat_width
    )
    qkv_grad = jnp.stack([query_grad, key_grad, value_grad], axis=1).astype(jnp.bfloat16)
    grad_qkv_bias = jnp.sum(qkv_grad.astype(jnp.float32), axis=0)
    grad_qkv = jnp.einsum("td,tcf->cdf", attn_in, qkv_grad, preferred_element_type=jnp.float32)
    attn_in_grad = jnp.einsum("tcf,cdf->td", qkv_grad, w_qkv, preferred_element_type=jnp.float32)
    attn_in_grad, mlp_in_grad = lax.psum((attn_in_grad, mlp_in_grad), "tp")
    hidden_grad, gain_one_grad, shift_one_grad, gain_two_grad, shift_two_grad = norm_back(
        (attn_in_grad, mlp_in_grad)
    )
    input_grad = (grad_full + hidden_grad).astype(jnp.bfloat16)
    grad_branch = jnp.sum(grad_full, axis=0)
    grads = (
        gain_one_grad,
        shift_one_grad,
        gain_two_grad,
        shift_two_grad,
        grad_qkv,
        grad_qkv_bias,
        grad_out_weight,
        grad_up,
        grad_up_bias,
        grad_down,
        grad_branch,
    )
    return (input_grad, grads)


def per_device(
    inputs,
    cotangent,
    ln1_gain,
    ln1_bias,
    ln2_gain,
    ln2_bias,
    qkv_weight,
    qkv_bias,
    out_weight,
    up_weight,
    up_bias,
    down_weight,
    branch_bias,
):
    gains = (
        ln1_gain[0].astype(jnp.float32),
        ln1_bias[0].astype(jnp.float32),
        ln2_gain[0].astype(jnp.float32),
        ln2_bias[0].astype(jnp.float32),
    )
    weights = (
        gains,
        qkv_weight[0],
        qkv_bias[0].astype(jnp.float32),
        out_weight[0],
        up_weight[0],
        up_bias[0].astype(jnp.float32),
        down_weight[0],
        branch_bias[0].astype(jnp.float32),
    )
    micro_count = inputs.shape[0]
    row_count = inputs.shape[1]
    query_pos = lax.axis_index("ctx") * row_count + jnp.arange(row_count, dtype=jnp.int32)
    cosine, sine = tables(query_pos)
    at_first = lax.axis_index("section") == 0
    blank = jnp.zeros_like(inputs[0])
    received = blank
    outputs_list = []
    saved_list = []
    for step_index in range(micro_count + 1):
        fresh = inputs[step_index] if step_index < micro_count else blank
        layer_in = jnp.where(at_first, fresh, received)
        layer_out, saved = forward_layer(layer_in, weights, query_pos, cosine, sine)
        outputs_list.append(layer_out)
        saved_list.append(saved)
        if step_index < micro_count:
            received = shifted(layer_out, "section", 1)
    returned = blank
    grad_list = []
    sums = None
    for back_index in range(micro_count + 1):
        batch_index = micro_count - 1 - back_index
        given = cotangent[batch_index] if batch_index >= 0 else blank
        grad_in = jnp.where(at_first, returned, given)
        input_grad, grads = backward_layer(
            grad_in, saved_list[micro_count - back_index], weights, query_pos, cosine, sine
        )
        sums = grads if sums is None else jax.tree.map(jnp.add, sums, grads)
        grad_list.append(input_grad)
        if back_index < micro_count:
            returned = shifted(input_grad, "section", -1)
    acts = jnp.stack(
        [jnp.where(at_first, outputs_list[j], outputs_list[j + 1]) for j in range(micro_count)]
    )[None]
    in_grads = jnp.stack(
        [
            jnp.where(at_first, grad_list[micro_count - j], grad_list[micro_count - 1 - j])
            for j in range(micro_count)
        ]
    )[None]
    (
        gain_one_grad,
        shift_one_grad,
        gain_two_grad,
        shift_two_grad,
        grad_qkv,
        grad_qkv_bias,
        grad_out_weight,
        grad_up,
        grad_up_bias,
        grad_down,
        grad_branch,
    ) = sums
    qkv_part, out_part, up_part, down_part = (
        lax.psum_scatter(
            grad_qkv[None].astype(jnp.bfloat16), "ctx", scatter_dimension=2, tiled=True
        ).astype(jnp.float32),
        lax.psum_scatter(
            grad_out_weight[None].astype(jnp.bfloat16), "ctx", scatter_dimension=2, tiled=True
        ).astype(jnp.float32),
        lax.psum_scatter(
            grad_up[None].astype(jnp.bfloat16), "ctx", scatter_dimension=1, tiled=True
        ).astype(jnp.float32),
        lax.psum_scatter(
            grad_down[None].astype(jnp.bfloat16), "ctx", scatter_dimension=2, tiled=True
        ).astype(jnp.float32),
    )
    small_sums = (
        lax.psum(gain_one_grad[None].astype(jnp.bfloat16), "ctx").astype(jnp.float32),
        lax.psum(shift_one_grad[None].astype(jnp.bfloat16), "ctx").astype(jnp.float32),
        lax.psum(gain_two_grad[None].astype(jnp.bfloat16), "ctx").astype(jnp.float32),
        lax.psum(shift_two_grad[None].astype(jnp.bfloat16), "ctx").astype(jnp.float32),
        lax.psum(grad_qkv_bias[None].astype(jnp.bfloat16), "ctx").astype(jnp.float32),
        lax.psum(grad_up_bias[None].astype(jnp.bfloat16), "ctx").astype(jnp.float32),
        lax.psum(grad_branch[None].astype(jnp.bfloat16), "ctx").astype(jnp.float32),
    )
    return (
        acts,
        in_grads,
        small_sums[0],
        small_sums[1],
        small_sums[2],
        small_sums[3],
        qkv_part,
        small_sums[4],
        out_part,
        up_part,
        small_sums[5],
        down_part,
        small_sums[6],
    )


ALL = ("section", "ctx", "tp")
SECTION, HALF, NEAR, CORE, SIDE = 16, 8, 4, 2, 1
CHIPS = (0, SIDE, NEAR, NEAR | SIDE, SECTION, SECTION | SIDE, SECTION | NEAR, SECTION | NEAR | SIDE)
F32, B16 = jnp.float32, jnp.bfloat16
ONE = 128
S_SECTION, S_HALF, S_NEAR, S_CORE, S_SIDE, S_CHIP, S_OWN, S_GIVE = range(8)


def swapped(array, mask, section=None):
    pairs = [(i, i ^ mask) for i in range(32) if section is None or i // 16 == section]
    return lax.ppermute(array, ALL, pairs)


def after(array, *earlier):
    return lax.optimization_barrier((array,) + earlier)[0]


def where_am_i():
    section = lax.axis_index("section")
    ctx = lax.axis_index("ctx")
    side = lax.axis_index("tp")
    half, near, core = ctx // 4, (ctx // 2) % 2, ctx % 2
    chip = 4 * section + 2 * near + side
    own, give = 2 * section + near, 2 * (1 - section) + near
    return jnp.stack([section, half, near, core, side, chip, own, give]).astype(jnp.int32)


def in_hbm(arrays):
    return [pltpu.with_memory_space_constraint(a, pltpu.HBM) for a in arrays]


def kernel_call(body, outs, at, *arrays, hbm=(), free=(), scratch=(), flops=0, exps=0, name=None, keep=True):
    moved = sum(a.size * a.dtype.itemsize for a in arrays)
    moved += sum(math.prod(s) * jnp.dtype(d).itemsize for s, d in outs)
    return pl.pallas_call(
        body,
        name=name,
        out_shape=[(pltpu.VMEM if keep else jax.ShapeDtypeStruct)(s, d) for s, d in outs],
        in_specs=[pl.BlockSpec(memory_space=pltpu.SMEM)]
        + [pl.BlockSpec(memory_space=pltpu.VMEM)] * len(arrays)
        + [pl.BlockSpec(memory_space=pltpu.HBM)] * len(hbm)
        + [pl.BlockSpec(memory_space=pl.ANY)] * len(free),
        out_specs=[pl.BlockSpec(memory_space=pltpu.VMEM)] * len(outs),
        scratch_shapes=list(scratch),
        compiler_params=pltpu.CompilerParams(vmem_limit_bytes=VMEM_BYTES),
        cost_estimate=pl.CostEstimate(flops=0, bytes_accessed=0, transcendentals=0),
    )(at, *arrays, *in_hbm(hbm), *free)


VMEM_BYTES = 16 * 1024 * 1024


def kernel_call_named(name, *args, **kwargs):
    return kernel_call(*args, name=name, **kwargs)


def by_rows(rows, step, do):
    def one(i, _):
        do(pl.ds(pl.multiple_of(i * step, step), step))
        return 0

    lax.fori_loop(0, rows // step, one, 0)


def nn(a, b):
    return jnp.dot(a, b, preferred_element_type=F32)


def nt(a, b):
    return lax.dot_general(a, b, (((1,), (1,)), ((), ())), preferred_element_type=F32)


def tn(a, b):
    return lax.dot_general(a, b, (((0,), (0,)), ((), ())), preferred_element_type=F32)


def copy_kernel(name, body, outs, at, arrays, scratch):
    return pl.pallas_call(
        body,
        name=name,
        out_shape=[jax.ShapeDtypeStruct(s, B16) for s in outs],
        in_specs=[pl.BlockSpec(memory_space=pltpu.SMEM)]
        + [pl.BlockSpec(memory_space=pltpu.HBM)] * len(arrays),
        out_specs=[pl.BlockSpec(memory_space=pltpu.HBM)] * len(outs),
        scratch_shapes=list(scratch),
        compiler_params=pltpu.CompilerParams(vmem_limit_bytes=VMEM_BYTES),
        cost_estimate=pl.CostEstimate(flops=0, bytes_accessed=0, transcendentals=0),
    )(at, *in_hbm(arrays))


def token_copies(at, array, mine, strip, sems):
    width = strip.shape[1]
    lanes = pl.ds(pl.multiple_of(at[S_SIDE] * width, width), width)
    return [
        pltpu.make_async_copy(array.at[at[S_HALF]], mine, sems.at[0]),
        pltpu.make_async_copy(array.at[1 - at[S_HALF], :, lanes], strip, sems.at[1]),
    ]


def token_shapes(array):
    _, rows, dim = array.shape
    return [(rows, dim), (rows, dim // 2)]


def send_strips(strip):
    return swapped(strip, HALF), swapped(strip, HALF | NEAR)


def start_loader(at, refs):
    mine, near, far, far_near, far_rest, far_near_rest = refs
    first = at[S_SIDE] == 0
    index = 2 * at[S_HALF] + at[S_NEAR]

    def whole(strip, rest):
        a, b = strip[...], rest[...]
        return jnp.concatenate([jnp.where(first, a, b), jnp.where(first, b, a)], axis=1)

    yield index, mine[...]
    yield index ^ 1, near[...]
    yield index ^ 2, whole(far, far_rest)
    yield index ^ 3, whole(far_near, far_near_rest)


def piece_loader(at, refs):
    for step, ref in zip(STEPS, refs):
        for i in range(2):
            yield at[S_CHIP] ^ (step | 2 * i), ref[i]


def run_copies(copies):
    for copy in copies:
        copy.start()
    for copy in copies:
        copy.wait()


def pack_first(at, tokens, vectors, w_qkv):
    _, three, dim, wide = w_qkv.shape
    heads, side = wide // 4, dim // 2
    count = len(vectors)

    def body(at, tokens, w_qkv, *refs):
        lines = refs[:count]
        mine, strip, packed, table, rounded, sems = refs[count : count + 6]
        held = refs[count + 6 :]
        rows = pl.ds(pl.multiple_of(at[S_CORE] * side, side), side)
        lanes = pl.ds(pl.multiple_of(at[S_GIVE] * heads, heads), heads)
        copies = token_copies(at, tokens, mine, strip, sems)
        for i in range(three):
            copies.append(
                pltpu.make_async_copy(
                    w_qkv.at[0, i, rows, lanes], packed.at[i * side : (i + 1) * side], sems.at[2 + i]
                )
            )
        loads = [
            pltpu.make_async_copy(line, hold, sems.at[6 + i])
            for i, (line, hold) in enumerate(zip(lines, held))
        ]
        for copy in copies:
            copy.start()
        run_copies(loads)
        fill_table(table, at[S_GIVE], held)
        rounded[...] = table[...].astype(B16)
        run_copies([pltpu.make_async_copy(rounded, packed.at[three * side :], sems.at[5])])
        for copy in copies:
            copy.wait()

    return copy_kernel(
        "pack_first", body, token_shapes(tokens) + [(three * side + TABLE, ONE)], at,
        [tokens, w_qkv, *vectors],
        [pltpu.VMEM((TABLE, ONE), F32), pltpu.VMEM((TABLE, ONE), B16), pltpu.SemaphoreType.DMA((6 + count,))]
        + [pltpu.VMEM(v.shape, B16) for v in vectors],
    )


def pack_second(at, tokens, w_up, w_out, w_down):
    dim, units, heads = w_up.shape[1], w_up.shape[2] // 4, w_out.shape[1] // 4
    side = dim // 2

    def body(at, tokens, w_up, w_out, w_down, mine, strip, up, down, sems):
        copies = token_copies(at, tokens, mine, strip, sems)
        rows = pl.ds(pl.multiple_of(at[S_CORE] * side, side), side)
        lanes = pl.ds(pl.multiple_of(at[S_GIVE] * units, units), units)
        copies.append(pltpu.make_async_copy(w_up.at[0, rows, lanes], up, sems.at[2]))
        part = 2 * at[S_GIVE] + at[S_CORE]
        for i, (source, size, start) in enumerate(
            ((w_down, units // 2, 0), (w_out, heads // 2, units // 2))
        ):
            rows = pl.ds(pl.multiple_of(part * size, size), size)
            copies.append(
                pltpu.make_async_copy(
                    source.at[0, rows], down.at[start : start + size], sems.at[3 + i]
                )
            )
        run_copies(copies)

    return copy_kernel(
        "pack_second", body, token_shapes(tokens) + [(side, units), ((units + heads) // 2, dim)], at,
        [tokens, w_up, w_out, w_down], [pltpu.SemaphoreType.DMA((5,))],
    )


def fill_table(table, index, vectors):
    *lines, b_up, b_qkv = vectors
    units, heads = b_up.shape[1] // 4, b_qkv.shape[2] // 4
    table[...] = jnp.zeros_like(table)
    row = 0
    for line in lines:
        for i in range(line.shape[1] // ONE):
            table[row : row + 1] = line[:, i * ONE : (i + 1) * ONE].astype(F32)
            row += 1
    for i in range(units // ONE):
        lanes = pl.ds(pl.multiple_of(index * units + i * ONE, ONE), ONE)
        table[row : row + 1] = b_up[:, lanes].astype(F32)
        row += 1
    few = b_qkv[0, :, pl.ds(pl.multiple_of(index * heads, ONE), heads)].astype(F32)
    table[row : row + few.shape[0]] = few


TABLE = 48


def vector_rows(at, vectors, got):
    dim = vectors[0].shape[1]
    units, few = vectors[5].shape[1] // 4, vectors[6].shape[1]

    def body(at, *refs):
        *lines, got, rows0, rows1, table = refs
        fill_table(table, at[S_OWN], lines)
        taken = got[got.shape[0] - TABLE :].astype(F32)
        is_first = at[S_SECTION] == 0
        for rows, lines in (
            (rows0, jnp.where(is_first, table[...], taken)),
            (rows1, jnp.where(is_first, taken, table[...])),
        ):
            rows[...] = jnp.zeros_like(rows)
            line = 0
            for r, tiles in enumerate([dim // ONE] * 5 + [units // ONE, few]):
                for i in range(tiles):
                    rows[r : r + 1, i * ONE : (i + 1) * ONE] = lines[line : line + 1]
                    line += 1

    return kernel_call_named(
        "vector_rows", body, [((8, dim), F32)] * 2, at, *vectors, got,
        scratch=[pltpu.VMEM((TABLE, ONE), F32)],
    )


def half_rows(at, which, size):
    return pl.ds(pl.multiple_of((at[S_CORE] ^ which) * size, size), size)


def qkv_copies(at, own, got, rest, target):
    three, heads = own.shape[1], own.shape[3] // 4
    side = own.shape[2] // 2
    lanes = pl.ds(pl.multiple_of(at[S_OWN] * heads, heads), heads)
    mine, halves = [], []
    for i in range(three):
        tile = slice(i * heads, (i + 1) * heads)
        mine.append((own.at[0, i, :, lanes], target[0].at[:, tile]))
        for which, source in ((0, got), (1, rest)):
            halves.append(
                (
                    source.at[i * side : (i + 1) * side],
                    target[1].at[half_rows(at, which, side), tile],
                )
            )
    return mine + halves


def up_copies(at, own, got, rest, target):
    side, units = got.shape
    lanes = pl.ds(pl.multiple_of(at[S_OWN] * units, units), units)
    return [(own.at[0, :, lanes], target[0])] + [
        (source, target[1].at[half_rows(at, which, side)])
        for which, source in ((0, got), (1, rest))
    ]


def row_copies(at, own, got, rest, target, start):
    size = target[0].shape[0]
    side = size // 2
    rows = pl.ds(pl.multiple_of(at[S_OWN] * size, size), size)
    return [(own.at[0, rows], target[0])] + [
        (source.at[start : start + side], target[1].at[half_rows(at, which, side)])
        for which, source in ((0, got), (1, rest))
    ]


def choose_weights(name, at, owns, got, rest, shapes, make):
    count = len(owns)

    def body(at, *refs):
        own, (got, rest), targets, sems = refs[:count], refs[count : count + 2], refs[count + 2 : -1], refs[-1]
        for section in range(2):

            @pl.when(at[S_SECTION] == section)
            def _():
                pairs = make(
                    at, own, got, rest,
                    [(targets[2 * i + section], targets[2 * i + 1 - section]) for i in range(count)],
                )
                run_copies(
                    [
                        pltpu.make_async_copy(source, target, sems.at[i])
                        for i, (source, target) in enumerate(pairs)
                    ]
                )

    outs = [(shape, B16) for shape in shapes for _ in range(2)]
    return kernel_call(
        body, outs, at, hbm=owns, free=[got, rest],
        scratch=[pltpu.SemaphoreType.DMA((9,))], name=name,
    )


def weights_call(name, body, outs, at, arrays, weights, scratch=(), flops=0, exps=0):
    first, count = len(arrays), len(weights)

    def wrapped(at, *refs):
        given, chosen, rest = refs[:first], refs[first : first + count], refs[first + count :]
        made, own = rest[: len(outs)], rest[len(outs) :]
        body(at, *given, *made, *chosen, *own)

    return kernel_call(
        wrapped, outs, at, *arrays, *weights, scratch=scratch, flops=flops, exps=exps, name=name
    )


def first_weights(at, vectors, w_qkv, sent):
    _, three, dim, wide = w_qkv.shape
    got = swapped(sent, SECTION)
    qkv = choose_weights(
        "choose_qkv", at, [w_qkv], got, swapped(got, CORE), [(dim, three * (wide // 4))],
        lambda at, own, got, rest, to: qkv_copies(at, own[0], got, rest, to[0]),
    )
    return got, [dict(qkv=q, rows=r) for q, r in zip(qkv, vector_rows(at, vectors, got))]


def up_weights(at, w_up, got, rest):
    return choose_weights(
        "choose_up", at, [w_up], got, rest, [(w_up.shape[1], w_up.shape[2] // 4)],
        lambda at, own, got, rest, to: up_copies(at, own[0], got, rest, to[0]),
    )


def row_weights(at, w_down, w_out, got, rest):
    _, tall, dim = w_down.shape
    units, heads = tall // 4, w_out.shape[1] // 4
    return choose_weights(
        "choose_rows", at, [w_down, w_out], got, rest, [(units, dim), (heads, dim)],
        lambda at, own, got, rest, to: row_copies(at, own[0], got, rest, to[0], 0)
        + row_copies(at, own[1], got, rest, to[1], units // 2),
    )


def turn_tables(at, rows):
    half_rot = ROT // 2
    place = lax.broadcasted_iota(jnp.int32, (rows, ONE), 0)
    lane = lax.broadcasted_iota(jnp.int32, (rows, ONE), 1) % HD
    positions = (2 * (place // ONE) + at[S_CORE]) * ONE + place % ONE
    freqs = 1.0 / 10000.0 ** ((2 * (lane % half_rot)).astype(F32) / ROT)
    angles = positions.astype(F32) * freqs
    sine = jnp.sin(angles)
    return (
        jnp.where(lane < ROT, jnp.cos(angles), 1.0),
        jnp.where((lane >= half_rot) & (lane < ROT), sine, 0.0),
        jnp.where(lane < half_rot, -sine, 0.0),
    )


def keep_blocks(at, source, blocks):
    mine, give = blocks
    place = (2 * at[S_HALF] + at[S_NEAR]) * ONE
    mine[...] = source[pl.ds(pl.multiple_of(place, ONE), ONE)]
    size = give.shape[0]
    place = (2 * (1 - at[S_HALF]) + at[S_NEAR]) * ONE + at[S_SIDE] * size
    give[...] = source[pl.ds(pl.multiple_of(place, size), size)]


def keep_piece(at, source, piece):
    size = piece.shape[0]
    piece[...] = source[pl.ds(pl.multiple_of(at[S_CHIP] * size, size), size)]


def front(at, loader, sources, w, turns, with_piece):
    dim = w["qkv"].shape[0]
    rows = turns[0].shape[0]
    count = len(sources)

    def body(at, *refs):
        given = refs[:count]
        vectors, *turns = refs[count : count + 4]
        attn_in, mlp_in, normed_out, q, kv = refs[count + 4 : count + 9]
        *kept, qkv, ordered = refs[count + 9 :]
        gains = [vectors[i : i + 1] for i in range(4)]
        for place, block in loader(at, given):
            size = block.shape[0]
            ordered[pl.ds(pl.multiple_of(place * size, size), size)] = block
        if with_piece:
            keep_piece(at, ordered, kept[0])
        else:
            keep_blocks(at, ordered, kept)
        bias = vectors[6:7, : 3 * ONE]

        def norm(span):
            hidden = ordered[span].astype(F32)
            mean = jnp.sum(hidden, axis=1, keepdims=True) * (1.0 / dim)
            centre = hidden - mean
            var = jnp.sum(centre * centre, axis=1, keepdims=True) * (1.0 / dim)
            normed = centre * lax.rsqrt(var + 1e-05)
            attn_in[span] = (normed * gains[0] + gains[1]).astype(B16)
            mlp_in[span] = (normed * gains[2] + gains[3]).astype(B16)
            normed_out[span] = normed.astype(B16)

        def project(span):
            projected = nn(attn_in[span], qkv[...]) + bias
            cosine, second, first_half = [table[span] for table in turns]
            for i, target in ((0, q), (1, kv.at[0])):
                flat = projected[:, i * ONE : (i + 1) * ONE]
                flat = (
                    flat * cosine
                    + pltpu.roll(flat, ROT // 2, 1) * second
                    + pltpu.roll(flat, ONE - ROT // 2, 1) * first_half
                )
                target[span] = flat.astype(B16)
            kv[1, span] = projected[:, 2 * ONE :].astype(B16)

        by_rows(rows, rows, norm)
        by_rows(rows, rows, project)

    outs = [((rows, dim), B16)] * 3 + [((rows, ONE), B16), ((2, rows, ONE), B16)]
    outs += [((rows // 8, dim), B16)] if with_piece else [((n, dim), B16) for n in (ONE, ONE // 2)]
    return weights_call(
        "front", body, outs, at, [*sources, w["rows"], *turns], [w["qkv"]],
        scratch=[pltpu.VMEM((rows, dim), B16)],
        flops=2 * rows * dim * 3 * ONE + 20 * rows * dim,
    )


def units_forward(at, mlp_in, w):
    rows, dim = mlp_in.shape
    units = w["units"]

    def body(at, mlp_in, vectors, active, slope, up):
        bias = vectors[5:6, :units]

        def gelu(span):
            value = nn(mlp_in[span], up[...]) + bias
            cdf = 0.5 + 0.5 * lax.erf(value * (1.0 / math.sqrt(2.0)))
            pdf = jnp.exp(value * value * -0.5) * (1.0 / math.sqrt(2.0 * math.pi))
            active[span] = (value * cdf).astype(B16)
            slope[span] = (cdf + value * pdf).astype(B16)

        by_rows(rows, rows, gelu)

    return weights_call(
        "units_forward", body, [((rows, units), B16)] * 2, at, [mlp_in, w["rows"]], [w["up"]],
        flops=2 * rows * dim * units + 40 * rows * units, exps=rows * units,
    )


def head_lanes():
    return lax.broadcasted_iota(jnp.int32, (1, ONE), 1) < HD


def by_head(array):
    first_head = head_lanes()
    zero = jnp.zeros_like(array)
    return jnp.concatenate(
        [jnp.where(first_head, array, zero), jnp.where(first_head, zero, array)], axis=0
    )


def joined_heads(array):
    half = array.shape[0] // 2
    return jnp.where(head_lanes(), array[:half], array[half:])


def allowed_keys(at, first, step, count):
    row = lax.broadcasted_iota(jnp.int32, (2 * step, count), 0) % step + first
    column = lax.broadcasted_iota(jnp.int32, (2 * step, count), 1)
    return column <= row, column < (row // ONE + at[S_CORE]) * ONE


STEPS = (0, 1, 4, 5)
STEP_CHIPS = (0, SIDE, SECTION, SECTION | SIDE)


def pieces_out(at, total, pieces):
    size = total.shape[0] // 8
    for step, piece in zip(STEPS, pieces):
        for i in range(2):
            place = (at[S_CHIP] ^ (step | 2 * i)) * size
            piece[i] = total[pl.ds(pl.multiple_of(place, size), size)].astype(piece.dtype)


def piece_shapes(rows, dim):
    return [((2, rows // 8, dim), F32)] + [((2, rows // 8, dim), B16)] * 3


def fold(at, pieces):
    _, rows, dim = pieces[0].shape

    def body(at, *refs):
        *given, keep, give = refs
        for i, target in ((0, keep), (1, give)):
            total = given[0][i]
            for piece in given[1:]:
                total = total + piece[i].astype(F32)
            target[...] = total.astype(target.dtype)

    return kernel_call_named("fold", body, [((rows, dim), F32), ((rows, dim), B16)], at, *pieces)


def exchanged(pieces):
    return [pieces[0]] + [swapped(p, m) for p, m in zip(pieces[1:], STEP_CHIPS[1:])]


def gathered(piece, near):
    pair = jnp.stack([piece, near])
    return [pair] + [swapped(pair, mask) for mask in STEP_CHIPS[1:]]


def attention_forward(at, q, kv, kv_other):
    rows = q.shape[0]
    scale = 1.0 / math.sqrt(HD)

    def body(at, q, kv, kv_other, mixed, lse):
        step = 128
        for first in range(0, rows, step):
            span = slice(first, first + step)
            count = first + step
            one = by_head(q[span] * scale)
            scores = [
                jnp.where(mask, nt(one, keys[0, :count]), -1e9)
                for mask, keys in zip(allowed_keys(at, first, step, count), (kv, kv_other))
            ]
            most = jnp.maximum(
                jnp.max(scores[0], axis=1, keepdims=True),
                jnp.max(scores[1], axis=1, keepdims=True),
            )
            exponents = [jnp.exp(s - most) for s in scores]
            summed = jnp.sum(exponents[0], axis=1, keepdims=True) + jnp.sum(
                exponents[1], axis=1, keepdims=True
            )
            inverse = 1.0 / summed
            result = nn(exponents[0].astype(B16), kv[1, :count]) + nn(
                exponents[1].astype(B16), kv_other[1, :count]
            )
            mixed[span] = joined_heads(result * inverse).astype(B16)
            lse[span] = joined_heads(
                jnp.broadcast_to(most + jnp.log(summed), (2 * step, ONE))
            )

    return kernel_call_named(
        "attention_forward", body, [((rows, ONE), B16), ((rows, ONE), F32)], at, q, kv, kv_other,
        flops=8 * rows * rows * ONE * 2, exps=2 * rows * rows * 2,
    )


def outputs_forward(at, mixed, active, w):
    rows = mixed.shape[0]
    units, dim = w["down"].shape

    def body(at, mixed, active, *rest):
        pieces, (out, down, total) = rest[:4], rest[4:]

        def one(span):
            total[span] = nn(mixed[span], out[...]) + nn(active[span], down[...])

        by_rows(rows, rows, one)
        pieces_out(at, total, pieces)

    return weights_call(
        "outputs_forward", body, piece_shapes(rows, dim), at, [mixed, active],
        [w["out"], w["down"]], scratch=[pltpu.VMEM((rows, dim), F32)],
        flops=2 * rows * dim * (units + ONE),
    )


def units_backward(at, loader, sources, slope, w, with_piece):
    rows, units = slope.shape
    dim = w["up"].shape[0]
    count = len(sources)

    def body(at, *refs):
        given = refs[:count]
        slope, g, up_grad, mixed_grad = refs[count : count + 4]
        *kept, down, out = refs[count + 4 :]
        for place, block in loader(at, given):
            size = block.shape[0]
            g[pl.ds(pl.multiple_of(place * size, size), size)] = block
        if with_piece:
            keep_piece(at, g, kept[0])
        else:
            keep_blocks(at, g, kept)

        def back(span):
            up_grad[span] = (nt(g[span], down[...]) * slope[span].astype(F32)).astype(B16)
            mixed_grad[span] = nt(g[span], out[...]).astype(B16)

        by_rows(rows, rows, back)

    outs = [((rows, dim), B16), ((rows, units), B16), ((rows, ONE), B16)]
    outs += [((rows // 8, dim), B16)] if with_piece else [((n, dim), B16) for n in (ONE, ONE // 2)]
    return weights_call(
        "units_backward", body, outs, at, [*sources, slope], [w["down"], w["out"]],
        flops=2 * rows * dim * (units + ONE),
    )


def attention_backward(at, q, kv, kv_other, lse, mixed_grad):
    rows = q.shape[0]
    scale = 1.0 / math.sqrt(HD)

    def body(at, q, kv, kv_other, lse, mixed_grad, dq, dkv, dkv_other):
        step = 256
        dkv[...] = jnp.zeros_like(dkv)
        dkv_other[...] = jnp.zeros_like(dkv_other)
        for first in range(0, rows, step):
            span = slice(first, first + step)
            count = first + step
            one, one_back = by_head(q[span] * scale), by_head(mixed_grad[span])
            masks = allowed_keys(at, first, step, count)
            sides = ((masks[0], kv, dkv), (masks[1], kv_other, dkv_other))
            level = jnp.concatenate([lse[span, :1], lse[span, HD : HD + 1]], axis=0)
            probs, grads = [], []
            for mask, keys, _ in sides:
                scores = nt(one, keys[0, :count])
                probs.append(jnp.exp(jnp.where(mask, scores, -1e9) - level))
                grads.append(nt(one_back, keys[1, :count]))
            delta = jnp.sum(probs[0] * grads[0], axis=1, keepdims=True) + jnp.sum(
                probs[1] * grads[1], axis=1, keepdims=True
            )
            result = 0.0
            for (_, keys, target), prob, grad in zip(sides, probs, grads):
                score_grad = (prob * (grad - delta)).astype(B16)
                result = result + nn(score_grad, keys[0, :count])
                target[0, :count] += tn(score_grad, one)
                target[1, :count] += tn(prob.astype(B16), one_back)
            dq[span] = joined_heads(result) * scale

    return kernel_call_named(
        "attention_backward",
        body, [((rows, ONE), F32), ((2, rows, ONE), F32), ((2, rows, ONE), F32)],
        at, q, kv, kv_other, lse, mixed_grad,
        flops=20 * rows * rows * ONE * 2, exps=2 * rows * rows * 2,
    )


def inputs_backward(at, dq, dkv, dkv_got, up_grad, normed, g, turns, w):
    rows, dim = normed.shape
    units = up_grad.shape[1]

    def body(at, dq, dkv, dkv_got, up_grad, normed, g, *rest):
        turns, vectors, rest = rest[:3], rest[3], rest[4:]
        qkv_grad, table = rest[:2]
        pieces, (qkv, up, total, lines) = rest[2:6], rest[6:]
        gain_one, gain_two = vectors[0:1], vectors[2:3]
        step = rows

        def one(i, sums):
            span = pl.ds(pl.multiple_of(i * step, step), step)
            cosine, second, first_half = [table[span] for table in turns]
            parts = []
            for flat in (dq[span], dkv[0, span] + dkv_got[0, span]):
                parts.append(
                    flat * cosine
                    - pltpu.roll(flat, ROT // 2, 1) * second
                    - pltpu.roll(flat, ONE - ROT // 2, 1) * first_half
                )
            parts.append(dkv[1, span] + dkv_got[1, span])
            both = jnp.concatenate([p.astype(B16) for p in parts], axis=1)
            qkv_grad[span] = both
            attn = nt(both, qkv[...])
            mlp = nt(up_grad[span], up[...])
            total[span] = attn * gain_one + mlp * gain_two
            unit = normed[span].astype(F32)
            new = [
                jnp.sum(v, axis=0, keepdims=True)
                for v in (
                    attn * unit, attn, mlp * unit, mlp, g[span].astype(F32),
                    up_grad[span].astype(F32), both.astype(F32),
                )
            ]
            return tuple(a + b for a, b in zip(sums, new))

        widths = (dim,) * 5 + (units, 3 * ONE)
        sums = lax.fori_loop(
            0, rows // step, one, tuple(jnp.zeros((1, width), F32) for width in widths)
        )
        pieces_out(at, total, pieces)
        lines[...] = jnp.zeros_like(lines)
        line = 0
        for value in sums:
            for i in range(value.shape[1] // ONE):
                lines[line : line + 1] = value[:, i * ONE : (i + 1) * ONE]
                line += 1
        table[...] = lines[...].astype(B16)

    outs = [((rows, 3 * ONE), B16), ((LINES, ONE), B16)] + piece_shapes(rows, dim)
    return weights_call(
        "inputs_backward", body, outs, at,
        [dq, dkv, dkv_got, up_grad, normed, g, *turns, w["rows"]], [w["qkv"], w["up"]],
        scratch=[pltpu.VMEM((rows, dim), F32), pltpu.VMEM((LINES, ONE), F32)],
        flops=2 * rows * dim * (units + 3 * ONE) + 12 * rows * dim,
    )


LINES = 64


def join_forward(at, x_piece, parts, w):
    def body(at, x, vectors, own, *rest):
        total = x[...].astype(F32) + own[...].astype(F32) + vectors[4:5]
        for piece in rest[:-1]:
            total = total + piece[...].astype(F32)
        rest[-1][...] = total.astype(B16)

    return kernel_call_named("join_forward", body, [(x_piece.shape, B16)], at, x_piece, w["rows"], *parts)[0]


def join_backward(at, g_piece, x_piece, parts):
    dim = x_piece.shape[1]

    def body(at, g, x, own, *rest):
        total = own[...]
        for piece in rest[:-1]:
            total = total + piece[...].astype(F32)
        hidden = x[...].astype(F32)
        centre = hidden - jnp.sum(hidden, axis=1, keepdims=True) * (1.0 / dim)
        var = jnp.sum(centre * centre, axis=1, keepdims=True) * (1.0 / dim)
        scale = lax.rsqrt(var + 1e-05)
        normed = centre * scale
        inner = (
            total
            - jnp.sum(total, axis=1, keepdims=True) * (1.0 / dim)
            - normed * (jnp.sum(total * normed, axis=1, keepdims=True) * (1.0 / dim))
        )
        rest[-1][...] = (g[...].astype(F32) + scale * inner).astype(B16)

    return kernel_call_named("join_backward", body, [(x_piece.shape, B16)], at, g_piece, x_piece, *parts)[0]


def columns(at, ref, core, high):
    which = at[S_CORE] ^ core
    return jnp.concatenate(
        [
            ref[:, pl.ds(pl.multiple_of((4 * high + 2 * low + which) * ONE, ONE), ONE)]
            for low in range(2)
        ],
        axis=1,
    )


def early_grads(at, active, mixed, mlp_in, up_grad, g):
    rows, dim = g.shape
    units = active.shape[1]
    tiles = units // ONE

    def body(at, active, mixed, mlp_in, up_grad, g, keep, give):
        for core, target in ((0, keep), (1, give)):
            strip = jnp.concatenate([columns(at, g, core, high) for high in range(2)], axis=1)
            down = tn(active[...], strip).astype(B16)
            out = tn(mixed[...], strip).astype(B16)
            for high in range(2):
                up = tn(columns(at, mlp_in, core, high), up_grad[...]).astype(B16)
                for low in range(2):
                    lanes = slice((2 * high + low) * ONE, (2 * high + low + 1) * ONE)
                    where = (at[S_HALF] ^ high, at[S_NEAR] ^ low)
                    target[where[0], where[1], :units] = down[:, lanes]
                    target[where[0], where[1], units : units + ONE] = out[:, lanes]
                    for i in range(tiles):
                        base = units + (1 + i) * ONE
                        target[where[0], where[1], base : base + ONE] = up[
                            low * ONE : (low + 1) * ONE, i * ONE : (i + 1) * ONE
                        ]

    shape = (2, 2, 2 * units + ONE, ONE)
    return kernel_call_named(
        "early_grads",
        body, [(shape, B16)] * 2, at, active, mixed, mlp_in, up_grad, g,
        flops=2 * rows * dim * (2 * units + ONE),
    )


def late_grads(at, attn_in, qkv_grad, tables):
    rows, dim = attn_in.shape
    count = len(tables)

    def body(at, attn_in, qkv_grad, *refs):
        tables, (keep, give) = refs[:count], refs[count:]
        for core, target in ((0, keep), (1, give)):
            for high in range(2):
                qkv = tn(columns(at, attn_in, core, high), qkv_grad[...]).astype(B16)
                for low in range(2):
                    where = (at[S_HALF] ^ high, at[S_NEAR] ^ low)
                    for i in range(3):
                        target[where[0], where[1], i * ONE : (i + 1) * ONE] = qkv[
                            low * ONE : (low + 1) * ONE, i * ONE : (i + 1) * ONE
                        ]
                    for i, table in enumerate(tables):
                        base = 3 * ONE + i * LINES
                        target[where[0], where[1], base : base + LINES] = table[...]

    shape = (2, 2, 3 * ONE + count * LINES, ONE)
    return kernel_call_named(
        "late_grads", body, [(shape, B16)] * 2, at, attn_in, qkv_grad, *tables,
        flops=2 * rows * dim * 3 * ONE,
    )


def plus(a, b):
    return (a.astype(F32) + b.astype(F32)).astype(B16)


def summed_cores(keep, give, *earlier):
    got = swapped(after(give, *earlier), CORE)
    return (
        [plus(keep[0, i], got[0, i]) for i in range(2)],
        [plus(keep[1, i], got[1, i]) for i in range(2)],
    )


def sum_lines(at, late):
    def body(at, *refs):
        *late, lines = refs
        total = 0.0
        for part in late:
            total = total + part[3 * ONE : 3 * ONE + lines.shape[0]].astype(F32)
        lines[...] = total

    return kernel_call_named("sum_lines", body, [((32, ONE), F32)], at, *late)[0]


def unpack_grads(at, early, late, sizes):
    dim_part, units, heads = ONE, sizes["units"], ONE

    def body(at, *refs):
        early, late = refs[:4], refs[4:8]
        qkv, out, up, down, b_qkv, b_up, branch = refs[8:]
        index = at[S_OWN]
        for j, (wide, narrow) in enumerate(zip(early, late)):
            source = index ^ (2 * (j % 2) + j // 2)
            place = pl.multiple_of(source * units, units)
            small = pl.multiple_of(source * ONE, ONE)
            down[pl.ds(place, units)] = wide[:units].astype(F32)
            out[pl.ds(small, ONE)] = wide[units : units + ONE].astype(F32)
            for i in range(units // ONE):
                base = units + (1 + i) * ONE
                up[:, pl.ds(place + i * ONE, ONE)] = wide[base : base + ONE].astype(F32)
            for i in range(3):
                qkv[i, :, pl.ds(small, ONE)] = narrow[i * ONE : (i + 1) * ONE].astype(F32)
            table = narrow[3 * ONE :].astype(F32)
            for i in range(units // ONE):
                b_up[:, pl.ds(place + i * ONE, ONE)] = table[40 + i : 41 + i]
            for i in range(3):
                b_qkv[i : i + 1, pl.ds(small, ONE)] = table[40 + units // ONE + i :][:1]
            if j == 0:
                branch[...] = table[32:40]

    outs = [
        ((3, dim_part, 4 * heads), F32),
        ((4 * heads, dim_part), F32),
        ((dim_part, 4 * units), F32),
        ((4 * units, dim_part), F32),
        ((3, 4 * heads), F32),
        ((1, 4 * units), F32),
        ((8, ONE), F32),
    ]
    return kernel_call_named("unpack_grads", body, outs, at, *early, *late, keep=False)


def cube_device(
    inputs, cotangent, ln1_gain, ln1_bias, ln2_gain, ln2_bias, qkv_weight, qkv_bias,
    out_weight, up_weight, up_bias, down_weight, branch_bias,
):
    at = where_am_i()
    section, half, side = [lax.axis_index("section"), lax.axis_index("ctx") // 4, lax.axis_index("tp")]
    at, is_first, is_low, is_left, is_near = lax.optimization_barrier(
        (at, section == 0, half == 0, side == 0, section == half)
    )
    dim = inputs.shape[2]
    rows = 4 * inputs.shape[1]
    vectors = (ln1_gain, ln1_bias, ln2_gain, ln2_bias, branch_bias, up_bias, qkv_bias)

    mine, strip, sent_qkv = pack_first(at, inputs, vectors, qkv_weight)
    g_mine, g_strip, sent_up, sent_down = pack_second(
        at, cotangent, up_weight, out_weight, down_weight
    )
    strips = send_strips(strip)
    turns = turn_tables(at, rows)
    sides = [swapped(after(part, turns[0]), SIDE) for part in strips]
    x_parts = (mine, swapped(mine, NEAR), *strips, *sides)
    got_qkv, layers = first_weights(at, vectors, qkv_weight, sent_qkv)
    got_up = swapped(after(sent_up, got_qkv), SECTION)
    first, second = layers
    got_down = swapped(
        after(sent_down, got_up, *x_parts[4:], first["qkv"], first["rows"]), SECTION
    )

    g_near = swapped(after(g_mine, *x_parts[4:]), NEAR)

    def bring_up(*earlier):
        up = up_weights(at, up_weight, got_up, swapped(after(got_up, *earlier), CORE))
        for i, layer in enumerate(layers):
            layer.update(up=up[i], units=up[i].shape[1])

    def bring_rows(*earlier):
        tall = row_weights(
            at, down_weight, out_weight, got_down, swapped(after(got_down, *earlier), CORE)
        )
        for i, layer in enumerate(layers):
            layer.update(down=tall[i], out=tall[2 + i])

    def forward(loader, sources, w, with_piece):
        got = front(at, loader, sources, w, turns, with_piece)
        attn_in, mlp_in, normed, q, kv = got[:5]
        kv_other = swapped(kv, CORE)
        is_start = "up" not in w
        if is_start:
            bring_up(q)
        active, slope = units_forward(at, mlp_in, w)
        mixed, lse = attention_forward(at, q, kv, kv_other)
        if is_start:
            bring_rows(active, mixed, g_near)
        pieces = outputs_forward(at, mixed, active, w)
        saved = dict(
            attn_in=attn_in, mlp_in=mlp_in, normed=normed, q=q, kv=kv, kv_other=kv_other,
            active=active, slope=slope, mixed=mixed, lse=lse,
        )
        return pieces, saved, got[5:]

    def backward(loader, sources, saved, w, with_piece, grads_first):
        made = units_backward(at, loader, sources, saved["slope"], w, with_piece)
        g, up_grad, mixed_grad = made[:3]
        if grads_first:
            early = early_grads(
                at, saved["active"], saved["mixed"], saved["mlp_in"], up_grad, g
            )
            mixed_grad = after(mixed_grad, early[0])
        dq, dkv, dkv_other = attention_backward(
            at, saved["q"], saved["kv"], saved["kv_other"], saved["lse"], mixed_grad
        )
        dkv_got = swapped(dkv_other, CORE)
        if not grads_first:
            early = early_grads(
                at, saved["active"], saved["mixed"], saved["mlp_in"], up_grad, after(g, dkv_other)
            )
            dq = after(dq, early[0])
        given = (dq, dkv, dkv_got, up_grad, saved["normed"], g)
        return early, given, made[3:]

    def backward_end(given, saved, w):
        out = inputs_backward(at, *given, turns, w)
        return out[0], out[1], out[2:]

    parts, saved_first, (x_piece,) = forward(start_loader, x_parts, first, True)
    strips = send_strips(after(g_strip, parts[0]))
    parts = exchanged(parts)
    parts[0] = after(parts[0], *strips)
    keep, give = fold(at, parts)
    sides = [swapped(part, SIDE) for part in strips]
    piece = join_forward(at, x_piece, [keep, swapped(give, NEAR)], first)
    near = after(swapped(piece, NEAR), *sides)
    middle = gathered(piece, near)
    g_parts = (g_mine, g_near, *strips, *sides)

    parts_last, saved_second, blocks = forward(piece_loader, middle, second, False)
    acts_mine, acts_give = blocks

    early, given, (g_piece,) = backward(
        start_loader, g_parts, saved_second, second, True, False
    )
    early_keep, early_give = summed_cores(*early, given[2])
    qkv_grad, table_second, pieces = backward_end(given, saved_second, second)
    late = late_grads(at, saved_second["attn_in"], qkv_grad, ())
    parts = exchanged(pieces)
    far_second = swapped(early_give[1], HALF)
    parts[0] = after(parts[0], far_second, *late)
    keep, give = fold(at, parts)
    late_keep, late_give = summed_cores(*late)
    late_got = swapped(after(jnp.stack(late_give), give), HALF)
    parts_last = exchanged([after(p, give) for p in parts_last])
    back = join_backward(at, g_piece, piece, [keep, swapped(give, NEAR)])
    near = after(swapped(back, NEAR), late_got, *parts_last)
    g_middle = gathered(back, near)
    close_second = swapped(after(early_give[0], near), HALF)
    g_middle[0] = after(g_middle[0], close_second)
    keep_last, give_last = fold(at, parts_last)

    early, given, blocks = backward(
        piece_loader, g_middle, saved_first, first, False, True
    )
    in_mine, in_give = blocks
    early_second = [plus(a, b) for a, b in zip(early_keep, (close_second, far_second))]
    late_second = [plus(a, b) for a, b in zip(late_keep, late_got)]
    early_keep, early_give = summed_cores(*early)
    given = (after(given[0], *early_give),) + given[1:]
    qkv_grad, table_first, pieces = backward_end(given, saved_first, first)
    last_near = swapped(give_last, NEAR)
    parts = exchanged([after(p, last_near) for p in pieces])
    far_first = swapped(early_give[1], HALF)
    late = late_grads(at, saved_first["attn_in"], qkv_grad, (table_first, table_second))
    parts[0] = after(parts[0], far_first)
    keep, give = fold(at, parts)
    close_first = swapped(after(early_give[0], give), HALF)
    late_keep, late_give = summed_cores(*late)
    late_got = swapped(jnp.stack(late_give), HALF)
    back_last = join_backward(
        at, back, x_piece, [keep, after(swapped(give, NEAR), close_first)]
    )
    last = join_forward(at, piece, [keep_last, last_near], second)
    early_first = [plus(a, b) for a, b in zip(early_keep, (close_first, far_first))]
    late_first = [plus(a, b) for a, b in zip(late_keep, late_got)]
    tall = 3 * ONE + LINES
    late_second = [
        jnp.concatenate([a, b[tall:]], axis=0) for a, b in zip(late_second, late_first)
    ]
    late_first = [a[:tall] for a in late_first]
    def brought(close, far):
        own = jnp.where(is_first, close[0], close[1])
        near = swapped(jnp.where(is_first, far[0], far[1]), NEAR)
        got = swapped(jnp.where(is_first, close[1], close[0]), SECTION)
        cross = swapped(jnp.where(is_first, far[1], far[0]), SECTION | NEAR)
        return own, got, near, cross

    early = brought((early_first[0], early_second[0]), (early_first[1], early_second[1]))
    late_first[1] = after(late_first[1], *early)
    late = brought((late_first[0], late_second[0]), (late_first[1], late_second[1]))
    lines = sum_lines(at, late)
    lines = lines + swapped(lines, SIDE)
    sizes = dict(units=up_weight.shape[2] // 4)
    qkv, out, up, down, b_qkv, b_up, branch = unpack_grads(at, early, late, sizes)

    mine = jnp.where(is_first, back_last, last)
    got = swapped(jnp.where(is_first, last, back_last), SECTION)
    stay = jnp.where(is_near, mine, got)
    known_give = jnp.where(is_first, acts_give, in_give)
    other = swapped(jnp.stack([jnp.where(is_near, got, mine), known_give]), HALF)
    own = jnp.stack(
        [jnp.where(is_low, stay, other[0]), jnp.where(is_low, other[0], stay), other[1]]
    )
    rest = swapped(own, SIDE)
    both = jnp.where(
        is_left, jnp.concatenate([own, rest], axis=1), jnp.concatenate([rest, own], axis=1)
    )
    new = both[:2]
    known_mine = jnp.where(is_first, acts_mine, in_mine)
    known = jnp.where(
        is_low, jnp.stack([known_mine, both[2]]), jnp.stack([both[2], known_mine])
    )
    acts = jnp.where(is_first, known, new)
    in_grads = jnp.where(is_first, new, known)

    lines = lines.reshape(4, dim)
    return (
        acts[None],
        in_grads[None],
        lines[0:1],
        lines[1:2],
        lines[2:3],
        lines[3:4],
        qkv[None],
        b_qkv[None],
        out[None],
        up[None],
        b_up,
        down[None],
        branch.reshape(1, dim),
    )


def placed_program(mesh, device_program):
    placed = (
        P(None, "ctx", None),
        P(None, "ctx", None),
        P("section", None),
        P("section", None),
        P("section", None),
        P("section", None),
        P("section", None, None, "tp"),
        P("section", None, "tp"),
        P("section", "tp", None),
        P("section", None, "tp"),
        P("section", "tp"),
        P("section", "tp", None),
        P("section", None),
    )
    return jax.shard_map(
        device_program,
        mesh=mesh,
        in_specs=placed,
        out_specs=(
            P("section", None, "ctx", None),
            P("section", None, "ctx", None),
            P("section", None),
            P("section", None),
            P("section", None),
            P("section", None),
            P("section", None, "ctx", "tp"),
            P("section", None, "tp"),
            P("section", "tp", "ctx"),
            P("section", "ctx", "tp"),
            P("section", "tp"),
            P("section", "tp", "ctx"),
            P("section", None),
        ),
        check_vma=False,
    )


def solution(mesh):
    sizes = dict(mesh.shape)
    if sizes["section"] == 2 and sizes["tp"] == 2 and sizes["ctx"] == 8:
        return placed_program(mesh, cube_device)
    return placed_program(mesh, per_device)
```
